32 devices in a mesh: batch: 4 (over y, core), space: 8 (over z, x).
Axes of the slice: x: 2, y: 2, z: 4, core: 2. Of those that a mesh axis runs over, the one named last changes fastest.
Arguments:
- features: bfloat16 [3, 32, 8, 16, 1024], P(None, 'batch', 'space'), may hold values from -30 to 30
- view_ids: int32 [3, 32], P(None, 'batch'), may hold values from 0 to 1, as said below
- w_reduce: bfloat16 [1024, 256], replicated, may hold values from -0.1875 to 0.1875
- w_spatial: bfloat16 [2304, 256], replicated, may hold values from -0.125 to 0.125
- w_expand: bfloat16 [256, 1024], replicated, may hold values from -0.375 to 0.375
- w_narrow: bfloat16 [1024, 512], replicated, may hold values from -0.1875 to 0.1875
- w_stride: bfloat16 [4608, 512], replicated, may hold values from -0.09375 to 0.09375
- w_widen: bfloat16 [512, 2048], replicated, may hold values from -0.25 to 0.25
- w_shortcut: bfloat16 [1024, 2048], replicated, may hold values from -0.1875 to 0.1875
- gain_reduce: float32 [256], replicated, may hold values from 0.5 to 1.5
- offset_reduce: float32 [256], replicated, may hold values from -3 to 3
- gain_spatial: float32 [256], replicated, may hold values from 0.5 to 1.5
- offset_spatial: float32 [256], replicated, may hold values from -3 to 3
- gain_expand: float32 [1024], replicated, may hold values from 0.5 to 1.5
- offset_expand: float32 [1024], replicated, may hold values from -3 to 3
- gain_narrow: float32 [512], replicated, may hold values from 0.5 to 1.5
- offset_narrow: float32 [512], replicated, may hold values from -3 to 3
- gain_stride: float32 [512], replicated, may hold values from 0.5 to 1.5
- offset_stride: float32 [512], replicated, may hold values from -3 to 3
- gain_widen: float32 [2048], replicated, may hold values from 0.5 to 1.5
- offset_widen: float32 [2048], replicated, may hold values from -3 to 3
- gain_shortcut: float32 [2048], replicated, may hold values from 0.5 to 1.5
- offset_shortcut: float32 [2048], replicated, may hold values from -3 to 3
- cotangent: bfloat16 [3, 32, 4, 8, 2048], P(None, ('batch', 'space')), may hold values from -6 to 6
Outputs:
- mapped: bfloat16 [3, 32, 4, 8, 2048], P(None, ('batch', 'space'))
- grad_features: bfloat16 [3, 32, 8, 16, 1024], P(None, 'batch', 'space')
- grad_w_reduce: float32 [1024, 256], P('space')
- grad_w_spatial: float32 [2304, 256], P('space')
- grad_w_expand: float32 [256, 1024], P('space')
- grad_w_narrow: float32 [1024, 512], P('space')
- grad_w_stride: float32 [4608, 512], P('space')
- grad_w_widen: float32 [512, 2048], P('space')
- grad_w_shortcut: float32 [1024, 2048], P('space')
- grad_gain_reduce: float32 [256], replicated
- grad_offset_reduce: float32 [256], replicated
- grad_gain_spatial: float32 [256], replicated
- grad_offset_spatial: float32 [256], replicated
- grad_gain_expand: float32 [1024], replicated
- grad_offset_expand: float32 [1024], replicated
- grad_gain_narrow: float32 [512], replicated
- grad_offset_narrow: float32 [512], replicated
- grad_gain_stride: float32 [512], replicated
- grad_offset_stride: float32 [512], replicated
- grad_gain_widen: float32 [2048], replicated
- grad_offset_widen: float32 [2048], replicated
- grad_gain_shortcut: float32 [2048], replicated
- grad_offset_shortcut: float32 [2048], replicated
The draws below stay inside these ranges and needn't reach their ends.
Inputs may be any that keep to these rules, and one draw needn't show every extreme that they name: `view_ids`: in every micro-batch exactly 16 maps carry each view.
All inputs are finite; a program needn't handle non-finite values.
Results may differ from the reference program's by a relative error of at most 0.025.
Values may be sent and summed in bfloat16 or wider, within the bound.
No kernel may reach another device: no remote copies, remote signals or barrier semaphores. Data moves between devices by JAX's collectives and lax.ppermute only.
A program may use at most 256 MiB of HBM per device.

```python
import jax
import jax.numpy as jnp
from jax import lax

C_IN = 1024
C_MID = 256
C_WIDE = 512
C_OUT = 2048
NVIEW = 2
MICRO = 3
COLS = 16
HEIGHT = 8
MAPS = 32


def view_table(key):
    keys = jax.random.split(jax.random.fold_in(key, 11), MICRO)
    order = jax.vmap(lambda sub_key: jax.random.permutation(sub_key, MAPS))(keys)
    return (order % NVIEW).astype(jnp.int32)


def draw_view_ids(key, part):
    return view_table(key)


def draw_features(key, part):
    labels = view_table(key)
    key = jax.random.fold_in(key, 5)
    base_key, shift_key, scale_key = jax.random.split(key, 3)
    layout = (MICRO, MAPS, HEIGHT, COLS, C_IN)
    base = jnp.clip(jax.random.normal(base_key, layout, jnp.float32), -6.0, 6.0)
    row_scale = 1.0 + 2.0 * jnp.arange(HEIGHT, dtype=jnp.float32) / max(HEIGHT - 1, 1)
    view_scale = jax.random.uniform(scale_key, (NVIEW,), jnp.float32, 0.5, 1.5)
    shift = jnp.clip(0.8 * jax.random.normal(shift_key, (NVIEW, C_IN), jnp.float32), -2.0, 2.0)
    scale = row_scale[None, None, :, None, None] * jnp.take(view_scale, labels, axis=0)[:, :, None, None, None]
    return (base * scale + jnp.take(shift, labels, axis=0)[:, :, None, None, :]).astype(jnp.bfloat16)


def block_levels(own_key, dims, pieces, least, high):
    level, own = 1.0, jax.random.fold_in(own_key, 6)
    for position, blocks in pieces:
        draws = jnp.exp(jax.random.uniform(jax.random.fold_in(own, position), (blocks,), jnp.float32, least / len(pieces), high / len(pieces)))
        level = level * jnp.repeat(draws, dims[position] // blocks).reshape([-1 if axis == position else 1 for axis in range(len(dims))])
    return level


def scatter_about(own_key, dims, deviation, bound, cuts=(), kind=jnp.bfloat16):
    entries = deviation * jax.random.normal(own_key, dims, jnp.float32)
    if cuts:
        entries = entries * block_levels(own_key, dims, cuts, -0.22, 0.18)
    return jnp.clip(entries, -bound, bound).astype(kind)


def setup_inputs(seed: int = 0) -> dict:
    arg_keys = jax.random.split(jax.random.key(seed), 25)
    features = draw_features(jax.random.fold_in(arg_keys[24], 71), 0)
    view_ids = draw_view_ids(jax.random.fold_in(arg_keys[24], 71), 0)
    w_reduce = scatter_about(arg_keys[2], (C_IN, C_MID), C_IN ** -0.5, 0.1875)
    w_spatial = scatter_about(arg_keys[3], (9 * C_MID, C_MID), (9 * C_MID) ** -0.5, 0.125)
    w_expand = scatter_about(arg_keys[4], (C_MID, C_IN), C_MID ** -0.5, 0.375)
    w_narrow = scatter_about(arg_keys[5], (C_IN, C_WIDE), C_IN ** -0.5, 0.1875)
    w_stride = scatter_about(arg_keys[6], (9 * C_WIDE, C_WIDE), (9 * C_WIDE) ** -0.5, 0.09375)
    w_widen = scatter_about(arg_keys[7], (C_WIDE, C_OUT), C_WIDE ** -0.5, 0.25)
    w_shortcut = scatter_about(arg_keys[8], (C_IN, C_OUT), C_IN ** -0.5, 0.1875)
    gain_reduce = jnp.clip(jax.random.uniform(arg_keys[9], (C_MID,), jnp.float32, 0.5, 1.5), 0.5, 1.5)
    offset_reduce = scatter_about(arg_keys[10], (C_MID,), 0.5, 3.0, (), jnp.float32)
    gain_spatial = jnp.clip(jax.random.uniform(arg_keys[11], (C_MID,), jnp.float32, 0.5, 1.5), 0.5, 1.5)
    offset_spatial = scatter_about(arg_keys[12], (C_MID,), 0.5, 3.0, (), jnp.float32)
    gain_expand = jnp.clip(jax.random.uniform(arg_keys[13], (C_IN,), jnp.float32, 0.5, 1.5), 0.5, 1.5)
    offset_expand = scatter_about(arg_keys[14], (C_IN,), 0.5, 3.0, (), jnp.float32)
    gain_narrow = jnp.clip(jax.random.uniform(arg_keys[15], (C_WIDE,), jnp.float32, 0.5, 1.5), 0.5, 1.5)
    offset_narrow = scatter_about(arg_keys[16], (C_WIDE,), 0.5, 3.0, (), jnp.float32)
    gain_stride = jnp.clip(jax.random.uniform(arg_keys[17], (C_WIDE,), jnp.float32, 0.5, 1.5), 0.5, 1.5)
    offset_stride = scatter_about(arg_keys[18], (C_WIDE,), 0.5, 3.0, (), jnp.float32)
    gain_widen = jnp.clip(jax.random.uniform(arg_keys[19], (C_OUT,), jnp.float32, 0.5, 1.5), 0.5, 1.5)
    offset_widen = scatter_about(arg_keys[20], (C_OUT,), 0.5, 3.0, (), jnp.float32)
    gain_shortcut = jnp.clip(jax.random.uniform(arg_keys[21], (C_OUT,), jnp.float32, 0.5, 1.5), 0.5, 1.5)
    offset_shortcut = scatter_about(arg_keys[22], (C_OUT,), 0.5, 3.0, (), jnp.float32)
    cotangent = scatter_about(arg_keys[23], (MICRO, MAPS, HEIGHT // 2, COLS // 2, C_OUT), 1.0, 6.0, ((1, 32),))
    return dict(features=features, view_ids=view_ids, w_reduce=w_reduce, w_spatial=w_spatial, w_expand=w_expand, w_narrow=w_narrow, w_stride=w_stride, w_widen=w_widen, w_shortcut=w_shortcut, gain_reduce=gain_reduce, offset_reduce=offset_reduce, gain_spatial=gain_spatial, offset_spatial=offset_spatial, gain_expand=gain_expand, offset_expand=offset_expand, gain_narrow=gain_narrow, offset_narrow=offset_narrow, gain_stride=gain_stride, offset_stride=offset_stride, gain_widen=gain_widen, offset_widen=offset_widen, gain_shortcut=gain_shortcut, offset_shortcut=offset_shortcut, cotangent=cotangent)


EPSILON = 1e-05
HIGHEST = lax.Precision.HIGHEST

@jax.custom_vjp
def low(v):
    return lax.optimization_barrier(v.astype(jnp.bfloat16)).astype(jnp.float32)

@jax.custom_vjp
def low_back(v):
    return v

def low_keep(v):
    return (low(v), None)

def low_pass(kept, grad):
    return (grad,)

def back_keep(v):
    return (v, None)

def back_low(kept, grad):
    return (low(grad),)
low.defvjp(low_keep, low_pass)
low_back.defvjp(back_keep, back_low)

def point(values, weight):
    return jnp.einsum('mhwc,cd->mhwd', values, weight, precision=HIGHEST)

def conv(values, weight, step_size):
    in_width = weight.shape[0] // 9
    kernel = weight.reshape(3, 3, in_width, weight.shape[1])
    return lax.conv_general_dilated(values, kernel, (step_size, step_size), ((1, 1), (1, 1)), dimension_numbers=('NHWC', 'HWIO', 'NHWC'), precision=HIGHEST)

def norm(values, onehot, gain, offset):
    population = lax.optimization_barrier(jnp.sum(onehot, axis=0)) * (values.shape[1] * values.shape[2])
    average = jnp.einsum('mv,mhwc->vc', onehot, values, precision=HIGHEST) / population[:, None]
    centered = values - jnp.einsum('mv,vc->mc', onehot, average, precision=HIGHEST)[:, None, None, :]
    variance = jnp.einsum('mv,mhwc->vc', onehot, centered * centered, precision=HIGHEST) / population[:, None]
    inverse = jnp.einsum('mv,vc->mc', onehot, lax.rsqrt(variance + EPSILON), precision=HIGHEST)
    return gain * centered * inverse[:, None, None, :] + offset

def forward(inputs, onehot, weights, norms):
    w_reduce, w_spatial, w_expand, w_narrow, w_stride, w_widen, w_shortcut = weights
    g_one, o_one, g_two, o_two, g_three, o_three, g_four, o_four, g_five, o_five, g_six, o_six, g_seven, o_seven = norms
    pre_reduce = low_back(point(inputs, w_reduce))
    out_reduce = low(jax.nn.gelu(norm(pre_reduce, onehot, g_one, o_one)))
    pre_spatial = low_back(conv(out_reduce, w_spatial, 1))
    out_spatial = low(jax.nn.gelu(norm(pre_spatial, onehot, g_two, o_two)))
    pre_expand = low_back(point(out_spatial, w_expand))
    joined = low_back(low(jax.nn.gelu(norm(pre_expand, onehot, g_three, o_three) + inputs)))
    pre_narrow = low_back(point(joined, w_narrow))
    out_narrow = low(jax.nn.gelu(norm(pre_narrow, onehot, g_four, o_four)))
    pre_stride = low_back(conv(out_narrow, w_stride, 2))
    out_stride = low(jax.nn.gelu(norm(pre_stride, onehot, g_five, o_five)))
    pre_widen = low_back(point(out_stride, w_widen))
    pre_shortcut = low_back(point(joined[:, ::2, ::2], w_shortcut))
    summed = norm(pre_widen, onehot, g_six, o_six) + norm(pre_shortcut, onehot, g_seven, o_seven)
    return jax.nn.gelu(summed)

def reference(features, view_ids, w_reduce, w_spatial, w_expand, w_narrow, w_stride, w_widen, w_shortcut, gain_reduce, offset_reduce, gain_spatial, offset_spatial, gain_expand, offset_expand, gain_narrow, offset_narrow, gain_stride, offset_stride, gain_widen, offset_widen, gain_shortcut, offset_shortcut, cotangent):
    weights = tuple((w.astype(jnp.float32) for w in (w_reduce, w_spatial, w_expand, w_narrow, w_stride, w_widen, w_shortcut)))
    norms = tuple((p.astype(jnp.float32) for p in (gain_reduce, offset_reduce, gain_spatial, offset_spatial, gain_expand, offset_expand, gain_narrow, offset_narrow, gain_stride, offset_stride, gain_widen, offset_widen, gain_shortcut, offset_shortcut)))
    zeros = jax.tree.map(jnp.zeros_like, (weights, norms))

    def step(totals, items):
        inputs, labels, upstream = items
        onehot = (labels[:, None] == jnp.arange(NVIEW)[None, :]).astype(jnp.float32)

        def apply(values, weight_set, norm_set):
            return forward(values, onehot, weight_set, norm_set)
        result, pull = jax.vjp(apply, inputs.astype(jnp.float32), weights, norms)
        d_inputs, d_weights, d_norms = pull(upstream.astype(jnp.float32))
        totals = jax.tree.map(jnp.add, totals, (d_weights, d_norms))
        return (totals, (result.astype(jnp.bfloat16), d_inputs.astype(jnp.bfloat16)))
    (weight_grads, norm_grads), (mapped, grad_features) = lax.scan(step, zeros, (features, view_ids, cotangent))
    return (mapped, grad_features) + tuple(weight_grads) + tuple(norm_grads)
```

```python
import jax
import jax.numpy as jnp
from jax import lax
from jax.sharding import PartitionSpec as P

NVIEW = 2
MICRO = 3
EPSILON = 1e-05
BF = jnp.bfloat16
F32 = jnp.float32
ALL = ("batch", "space")


def dot(a, b, dims=((1,), (0,))):
    return lax.dot_general(a, b, (dims, ((), ())), preferred_element_type=F32)


def dot_nt(a, b):
    return dot(a, b, ((1,), (1,)))


def dot_tn(a, b):
    return dot(a, b, ((0,), (0,)))


def gelu_back(value, gradient):
    return jax.vjp(jax.nn.gelu, value)[1](gradient)[0]


def share(block, count):
    copies = jnp.broadcast_to(block[None], (count,) + block.shape)
    return lax.all_to_all(copies, ALL, 0, 0, tiled=True)


def spread_slots(parts, count):
    return lax.all_to_all(parts, ALL, 0, 0, tiled=True)


def local_stats(values):
    mean = jnp.mean(values, axis=1)
    square = jnp.sum((values - mean[:, None, :]) ** 2, axis=1)
    return jnp.stack([mean, square], axis=1)


def merge_stats(gathered, weight, rows):
    count = jnp.sum(weight, axis=0)[:, None]
    means, squares = gathered[:, :, 0], gathered[:, :, 1]
    wide = weight[:, :, None]
    mean = jnp.sum(wide * means, axis=0) / count
    total = jnp.sum(wide * (squares + rows * (means - mean[None]) ** 2), axis=0)
    return mean, lax.rsqrt(total / (count * rows) + EPSILON)


def shift_rows(values, axis, offset):
    if offset == 0:
        return values
    size = values.shape[axis]
    widths = [(0, 0)] * values.ndim
    if offset > 0:
        widths[axis] = (0, offset)
        return jnp.pad(lax.slice_in_dim(values, offset, size, axis=axis), widths)
    widths[axis] = (-offset, 0)
    return jnp.pad(lax.slice_in_dim(values, 0, size + offset, axis=axis), widths)


def neighbour(maps, phase_y, phase_x, step_y, step_x):
    at_y, at_x = phase_y + step_y, phase_x + step_x
    piece = maps[:, at_y % 2, at_x % 2]
    return shift_rows(shift_rows(piece, 1, at_y // 2), 2, at_x // 2)


def patches(maps, sign):
    return jnp.stack(
        [
            jnp.stack(
                [
                    jnp.concatenate(
                        [neighbour(maps, py, px, sign * (r - 1), sign * (c - 1)) for r in range(3) for c in range(3)],
                        axis=-1,
                    )
                    for px in range(2)
                ],
                axis=1,
            )
            for py in range(2)
        ],
        axis=1,
    )


def on_device(
    features,
    view_ids,
    w_reduce,
    w_spatial,
    w_expand,
    w_narrow,
    w_stride,
    w_widen,
    w_shortcut,
    gain_reduce,
    offset_reduce,
    gain_spatial,
    offset_spatial,
    gain_expand,
    offset_expand,
    gain_narrow,
    offset_narrow,
    gain_stride,
    offset_stride,
    gain_widen,
    offset_widen,
    gain_shortcut,
    offset_shortcut,
    cotangent,
):
    ns = lax.axis_size("space")
    nb = lax.axis_size("batch")
    n = ns * nb
    maps = features.shape[1]
    cols = features.shape[3]
    xh = cols // 2
    yh = ns // 2
    rows = ns * cols
    half = rows // 4
    c_in = features.shape[4]
    c_mid = w_reduce.shape[1]
    assert features.shape[2] == 1 and cotangent.shape[1] == 1 and maps == ns

    def to_maps(block):
        c = block.shape[-1]
        return block.reshape(yh, 2, MICRO, 2, xh, c).transpose(2, 1, 3, 0, 4, 5)

    def to_rows(block):
        c = block.shape[-1]
        return block.reshape(MICRO, 2, 2, yh, xh, c).transpose(3, 1, 0, 2, 4, 5).reshape(ns, MICRO, cols, c)

    def exchange(block):
        return lax.all_to_all(block, "space", 0, 0, tiled=True)

    rows_in = features.reshape(MICRO, maps, xh, 2, c_in).transpose(1, 0, 3, 2, 4).reshape(maps, MICRO, cols, c_in)
    pre_rows = dot(rows_in.reshape(-1, c_in), w_reduce).reshape(maps, MICRO, cols, c_mid)

    ids = view_ids.T.astype(F32)
    hot = jnp.stack([(ids == v).astype(F32) for v in range(NVIEW)], axis=-1)
    count_here = jnp.sum(hot, axis=0) * cols
    sum_here = jnp.einsum("kmv,kmpc->mvc", hot, pre_rows, precision=lax.Precision.HIGHEST)
    mean_here = sum_here / jnp.maximum(count_here, 1.0)[:, :, None]
    own_mean = jnp.einsum("kmv,mvc->kmc", hot, mean_here, precision=lax.Precision.HIGHEST)
    square_here = jnp.einsum(
        "kmv,kmpc->mvc", hot, (pre_rows - own_mean[:, :, None, :]) ** 2, precision=lax.Precision.HIGHEST
    )
    payload = jnp.concatenate(
        [
            mean_here.reshape(MICRO * NVIEW, c_mid),
            square_here.reshape(MICRO * NVIEW, c_mid),
            jnp.broadcast_to(count_here.reshape(MICRO * NVIEW, 1), (MICRO * NVIEW, c_mid)),
            jnp.pad(ids.reshape(1, -1), ((0, 0), (0, c_mid - ids.size))),
        ],
        axis=0,
    )
    got = share(payload, n)
    k = MICRO * NVIEW
    g_mean, g_square, g_count = got[:, :k], got[:, k : 2 * k], got[:, 2 * k : 3 * k]
    population = jnp.sum(g_count, axis=0)
    mean_views = jnp.sum(g_count * g_mean, axis=0) / population
    var_views = jnp.sum(g_square + g_count * (g_mean - mean_views) ** 2, axis=0) / population
    inv_views = lax.rsqrt(var_views + EPSILON)
    mean_views = mean_views.reshape(MICRO, NVIEW, c_mid)
    inv_views = inv_views.reshape(MICRO, NVIEW, c_mid)

    all_ids = got[:, 3 * k, : ids.size].reshape(nb, ns, maps, MICRO)[:, 0].reshape(n, MICRO)
    me = lax.axis_index("batch") * ns + lax.axis_index("space")
    my_ids = lax.dynamic_slice_in_dim(all_ids, me, 1, 0)
    weight = (all_ids == my_ids).astype(F32)
    mates = jnp.sum(weight, axis=0)[:, None]
    my_view = my_ids[0][:, None]

    def pick(per_view):
        return jnp.where(my_view > 0.5, per_view[:, 1], per_view[:, 0])

    def stats_of(values):
        m, r, c = values.shape
        return merge_stats(share(local_stats(values), n), weight, r)

    def sums_of(gradient, hat):
        block = jnp.stack([jnp.sum(gradient, axis=1), jnp.sum(gradient * hat, axis=1)], axis=1)
        got = share(block, n)
        return jnp.sum(weight[:, :, None, None] * got, axis=0), jnp.sum(got, axis=(0, 1)), got

    def norm_back(gradient, hat, inverse, gain, sums, size):
        count = mates * size
        return (
            (gain * inverse)[:, None, :]
            * (gradient - (sums[:, 0] / count)[:, None, :] - hat * (sums[:, 1] / count)[:, None, :])
        ).astype(BF)

    maps_in = to_maps(exchange(rows_in)).reshape(MICRO, rows, c_in)
    pre_reduce = to_maps(exchange(pre_rows)).reshape(MICRO, rows, c_mid)
    mean_reduce, inv_reduce = pick(mean_views), pick(inv_views)
    hat_reduce = (pre_reduce - mean_reduce[:, None]) * inv_reduce[:, None]
    act_reduce = gain_reduce * hat_reduce + offset_reduce
    out_reduce = jax.nn.gelu(act_reduce).astype(BF)

    grid = (MICRO, 2, 2, yh, xh)
    patch_reduce = patches(out_reduce.reshape(grid + (c_mid,)), 1).reshape(MICRO * rows, 9 * c_mid)
    pre_spatial = dot(patch_reduce, w_spatial).reshape(MICRO, rows, c_mid)
    mean, inv_spatial = stats_of(pre_spatial)
    hat_spatial = (pre_spatial - mean[:, None]) * inv_spatial[:, None]
    act_spatial = gain_spatial * hat_spatial + offset_spatial
    out_spatial = jax.nn.gelu(act_spatial).astype(BF)

    pre_expand = dot(out_spatial.reshape(-1, c_mid), w_expand).reshape(MICRO, rows, c_in)
    mean, inv_expand = stats_of(pre_expand)
    hat_expand = (pre_expand - mean[:, None]) * inv_expand[:, None]
    residual_one = gain_expand * hat_expand + offset_expand + maps_in.astype(F32)
    joined = jax.nn.gelu(residual_one).astype(BF)

    c_wide = w_narrow.shape[1]
    pre_narrow = dot(joined.reshape(-1, c_in), w_narrow).reshape(MICRO, rows, c_wide)
    joined_even = joined[:, :half].reshape(-1, c_in)
    mean, inv_narrow = stats_of(pre_narrow)
    hat_narrow = (pre_narrow - mean[:, None]) * inv_narrow[:, None]
    act_narrow = gain_narrow * hat_narrow + offset_narrow
    out_narrow = jax.nn.gelu(act_narrow).astype(BF)

    narrow_maps = out_narrow.reshape(grid + (c_wide,))
    patch_narrow = jnp.concatenate(
        [neighbour(narrow_maps, 0, 0, r - 1, c - 1) for r in range(3) for c in range(3)], axis=-1
    ).reshape(MICRO * half, 9 * c_wide)
    pre_stride = dot(patch_narrow, w_stride).reshape(MICRO, half, c_wide)
    mean, inv_stride = stats_of(pre_stride)
    hat_stride = (pre_stride - mean[:, None]) * inv_stride[:, None]
    act_stride = gain_stride * hat_stride + offset_stride
    out_stride = jax.nn.gelu(act_stride).astype(BF).reshape(-1, c_wide)

    c_out = w_widen.shape[1]
    pre_widen = dot(out_stride, w_widen).reshape(MICRO, half, c_out)
    pre_shortcut = dot(joined_even, w_shortcut).reshape(MICRO, half, c_out)
    both = jnp.concatenate([local_stats(pre_widen), local_stats(pre_shortcut)], axis=-1)
    width = 2 * c_out // n
    pieces = spread_slots(both.reshape(MICRO * 2, n, width).transpose(1, 0, 2), n)
    pieces = pieces.reshape(n, MICRO, 2, width)
    view_results = []
    for view in range(NVIEW):
        mean, inverse = merge_stats(pieces, (all_ids == view).astype(F32), half)
        view_results.append(jnp.stack([mean, inverse], axis=1))
    whole = share(jnp.stack(view_results, axis=1), n)
    whole = whole.transpose(1, 2, 3, 0, 4).reshape(MICRO, NVIEW, 2, 2 * c_out)
    whole = pick(whole.reshape(MICRO, NVIEW, 4 * c_out)).reshape(MICRO, 2, 2, c_out)
    mean_widen, mean_shortcut = whole[:, 0, 0], whole[:, 0, 1]
    inv_widen, inv_shortcut = whole[:, 1, 0], whole[:, 1, 1]
    hat_widen = (pre_widen - mean_widen[:, None]) * inv_widen[:, None]
    hat_shortcut = (pre_shortcut - mean_shortcut[:, None]) * inv_shortcut[:, None]
    residual_two = gain_widen * hat_widen + offset_widen + (gain_shortcut * hat_shortcut + offset_shortcut)
    mapped = jax.nn.gelu(residual_two).astype(BF).reshape(cotangent.shape)
    d_two = gelu_back(residual_two, cotangent.reshape(MICRO, half, c_out).astype(F32))

    block = jnp.stack(
        [jnp.sum(d_two, axis=1), jnp.sum(d_two * hat_widen, axis=1), jnp.sum(d_two * hat_shortcut, axis=1)], axis=1
    )
    width = c_out // n
    pieces = spread_slots(block.reshape(MICRO * 3, n, width).transpose(1, 0, 2), n).reshape(n, MICRO, 3, width)
    by_view = jnp.stack(
        [jnp.sum((all_ids == view).astype(F32)[:, :, None, None] * pieces, axis=0) for view in range(NVIEW)], axis=1
    )
    whole = share(by_view, n).transpose(1, 2, 3, 0, 4).reshape(MICRO, NVIEW, 3, c_out)
    totals = jnp.sum(whole, axis=(0, 1))
    grad_offset_widen, grad_gain_widen, grad_gain_shortcut = totals[0], totals[1], totals[2]
    sums = pick(whole.reshape(MICRO, NVIEW, 3 * c_out)).reshape(MICRO, 3, c_out)
    delta_widen = norm_back(d_two, hat_widen, inv_widen, gain_widen, sums[:, :2], half).reshape(-1, c_out)
    delta_shortcut = norm_back(d_two, hat_shortcut, inv_shortcut, gain_shortcut, sums[:, ::2], half).reshape(-1, c_out)

    def gathered_grad(operand, gradient):
        share_cols = gradient.shape[1] // nb
        parts = gradient.reshape(-1, nb, share_cols).transpose(1, 0, 2)
        parts = lax.all_to_all(parts, "batch", 0, 0, tiled=True).reshape(-1, share_cols)
        copies = jnp.broadcast_to(operand[None], (nb,) + operand.shape)
        copies = lax.all_to_all(copies, "batch", 0, 0, tiled=True).reshape(-1, operand.shape[1])
        return dot_tn(copies, parts).astype(BF)

    def finish_cols(product):
        r, c = product.shape
        mine = lax.all_to_all(product.reshape(ns, r // ns, c), "space", 0, 0, tiled=True)
        mine = jnp.sum(mine.astype(F32), axis=0).astype(BF)
        return lax.all_gather(mine, "batch", axis=1, tiled=True).astype(F32)

    def finish_rows(product):
        r, c = product.shape
        parts = product.astype(BF).reshape(ns, nb, r // n, c)
        parts = lax.all_to_all(parts, "batch", 1, 1, tiled=True)
        parts = jnp.sum(parts.astype(F32), axis=1).astype(BF)
        mine = lax.all_to_all(parts, "space", 0, 0, tiled=True)
        mine = jnp.sum(mine.astype(F32), axis=0).astype(BF)
        return lax.all_gather(mine, "batch", axis=0, tiled=True).astype(F32)

    grad_w_widen = finish_cols(gathered_grad(out_stride, delta_widen))
    grad_w_shortcut = finish_cols(gathered_grad(joined_even, delta_shortcut))

    d_out_stride = dot_nt(delta_widen, w_widen).reshape(MICRO, half, c_wide)
    d_stride = gelu_back(act_stride, d_out_stride)
    sums, totals, _ = sums_of(d_stride, hat_stride)
    grad_offset_stride, grad_gain_stride = totals[0], totals[1]
    delta_stride = norm_back(d_stride, hat_stride, inv_stride, gain_stride, sums, half).reshape(-1, c_wide)
    grad_w_stride = finish_rows(dot_tn(patch_narrow, delta_stride))

    contrib = dot_nt(delta_stride, w_stride).reshape(MICRO, yh, xh, 9, c_wide)
    phases = [[None, None], [None, None]]
    for r in range(3):
        for c in range(3):
            piece = contrib[:, :, :, r * 3 + c]
            piece = shift_rows(shift_rows(piece, 1, 1 if r == 0 else 0), 2, 1 if c == 0 else 0)
            old = phases[(r + 1) % 2][(c + 1) % 2]
            phases[(r + 1) % 2][(c + 1) % 2] = piece if old is None else old + piece
    d_out_narrow = jnp.stack([jnp.stack(line, axis=1) for line in phases], axis=1).reshape(MICRO, rows, c_wide)
    d_narrow = gelu_back(act_narrow, d_out_narrow)
    sums, totals, _ = sums_of(d_narrow, hat_narrow)
    grad_offset_narrow, grad_gain_narrow = totals[0], totals[1]
    delta_narrow = norm_back(d_narrow, hat_narrow, inv_narrow, gain_narrow, sums, rows).reshape(-1, c_wide)
    grad_w_narrow = finish_rows(dot_tn(joined.reshape(-1, c_in), delta_narrow))

    d_joined = dot_nt(delta_narrow, w_narrow).reshape(MICRO, rows, c_in)
    d_even = dot_nt(delta_shortcut, w_shortcut).reshape(MICRO, half, c_in)
    d_joined = jnp.concatenate([d_joined[:, :half] + d_even, d_joined[:, half:]], axis=1).astype(BF)
    d_one = gelu_back(residual_one, d_joined.astype(F32))
    d_one_rows = exchange(to_rows(d_one.astype(BF)))
    sums, totals, _ = sums_of(d_one, hat_expand)
    grad_offset_expand, grad_gain_expand = totals[0], totals[1]
    delta_expand = norm_back(d_one, hat_expand, inv_expand, gain_expand, sums, rows).reshape(-1, c_in)
    grad_w_expand = finish_rows(dot_tn(out_spatial.reshape(-1, c_mid), delta_expand))

    d_out_spatial = dot_nt(delta_expand, w_expand).reshape(MICRO, rows, c_mid)
    d_spatial = gelu_back(act_spatial, d_out_spatial)
    sums, totals, _ = sums_of(d_spatial, hat_spatial)
    grad_offset_spatial, grad_gain_spatial = totals[0], totals[1]
    delta_spatial = norm_back(d_spatial, hat_spatial, inv_spatial, gain_spatial, sums, rows).reshape(-1, c_mid)
    grad_w_spatial = finish_rows(dot_tn(patch_reduce, delta_spatial))

    patch_delta = patches(delta_spatial.reshape(grid + (c_mid,)), -1).reshape(MICRO * rows, 9 * c_mid)
    flipped = w_spatial.reshape(9, c_mid, c_mid).transpose(0, 2, 1).reshape(9 * c_mid, c_mid)
    d_out_reduce = dot(patch_delta, flipped).reshape(MICRO, rows, c_mid)
    d_reduce = gelu_back(act_reduce, d_out_reduce)
    d_rows = exchange(to_rows(d_reduce))
    _, totals, got = sums_of(d_reduce, hat_reduce)
    grad_offset_reduce, grad_gain_reduce = totals[0], totals[1]
    view_sums = jnp.stack(
        [jnp.sum((all_ids == view).astype(F32)[:, :, None, None] * got, axis=0) for view in range(NVIEW)], axis=1
    )
    counts = population.reshape(MICRO, NVIEW, c_mid)

    def at_rows(per_view):
        chosen = jnp.where(ids[:, :, None] > 0.5, per_view[None, :, 1], per_view[None, :, 0])
        return chosen[:, :, None, :]

    hat_rows = (pre_rows - at_rows(mean_views)) * at_rows(inv_views)
    delta_reduce = (
        gain_reduce
        * at_rows(inv_views)
        * (d_rows - at_rows(view_sums[:, :, 0] / counts) - hat_rows * at_rows(view_sums[:, :, 1] / counts))
    ).astype(BF).reshape(-1, c_mid)
    grad_w_reduce = finish_rows(dot_tn(rows_in.reshape(-1, c_in), delta_reduce))
    d_input = (d_one_rows.reshape(-1, c_in).astype(F32) + dot_nt(delta_reduce, w_reduce)).astype(BF)
    grad_features = (
        d_input.reshape(maps, MICRO, 2, xh, c_in).transpose(1, 0, 3, 2, 4).reshape(features.shape)
    )

    return (
        mapped,
        grad_features,
        grad_w_reduce,
        grad_w_spatial,
        grad_w_expand,
        grad_w_narrow,
        grad_w_stride,
        grad_w_widen,
        grad_w_shortcut,
        grad_gain_reduce,
        grad_offset_reduce,
        grad_gain_spatial,
        grad_offset_spatial,
        grad_gain_expand,
        grad_offset_expand,
        grad_gain_narrow,
        grad_offset_narrow,
        grad_gain_stride,
        grad_offset_stride,
        grad_gain_widen,
        grad_offset_widen,
        grad_gain_shortcut,
        grad_offset_widen,
    )


def solution(mesh):
    return jax.shard_map(
        on_device,
        mesh=mesh,
        in_specs=(P(None, "batch", "space", None, None), P(None, "batch"))
        + (P(),) * 21
        + (P(None, ("batch", "space"), None, None, None),),
        out_specs=(P(None, ("batch", "space"), None, None, None), P(None, "batch", "space", None, None))
        + (P("space", None),) * 7
        + (P(),) * 14,
        check_vma=False,
    )
```

```python
import functools
import math

import jax
import jax.numpy as jnp
from jax import lax
from jax.experimental import pallas as pl
from jax.experimental.pallas import tpu as pltpu
from jax.sharding import PartitionSpec as P

NVIEW = 2
MICRO = 3
EPSILON = 1e-05
BF = jnp.bfloat16
F32 = jnp.float32
ALL = ("batch", "space")
LANES = 128
ROOT = math.sqrt(2.0 / math.pi)
CUBE = 0.044715


def dot(a, b, dims=((1,), (0,))):
    return lax.dot_general(a, b, (dims, ((), ())), preferred_element_type=F32)


def dot_nt(a, b):
    return dot(a, b, ((1,), (1,)))


def dot_tn(a, b):
    return dot(a, b, ((0,), (0,)))


def gelu(v):
    return 0.5 * v * (1.0 + jnp.tanh(ROOT * (v + CUBE * (v * v * v))))


def gelu_slope(v):
    square = v * v
    t = jnp.tanh(ROOT * (v + CUBE * (square * v)))
    return 0.5 * (1.0 + t) + (0.5 * ROOT) * v * (1.0 - t * t) * (1.0 + (3.0 * CUBE) * square)


def cols(c):
    return pl.ds(c * LANES, LANES)


def row(ref, r):
    return ref[pl.ds(r, 1), :]


def kernel_call(body, outs, args, weights=(), scratch=(), flops=0, limit=40):
    n_in, n_w, n_out = len(args), len(weights), len(outs)

    def run(*refs):
        ins, w_any = refs[:n_in], refs[n_in : n_in + n_w]
        out = refs[n_in + n_w : n_in + n_w + n_out]
        rest = refs[n_in + n_w + n_out :]
        held, sems, extra = rest[:n_w], rest[n_w : 2 * n_w], rest[2 * n_w :]
        copies = [pltpu.make_async_copy(a, b, s) for a, b, s in zip(w_any, held, sems)]
        for copy in copies:
            copy.start()
        body(ins, held, copies, out, extra)

    whole = pl.BlockSpec(memory_space=pltpu.VMEM)
    n_bytes = sum(math.prod(a.shape) * a.dtype.itemsize for a in (*args, *weights, *outs))
    return pl.pallas_call(
        run,
        out_shape=tuple(jax.ShapeDtypeStruct(o.shape, o.dtype) for o in outs),
        in_specs=[whole] * n_in + [pl.BlockSpec(memory_space=pl.ANY)] * n_w,
        out_specs=tuple([whole] * n_out),
        scratch_shapes=[pltpu.VMEM(w.shape, w.dtype) for w in weights]
        + [pltpu.SemaphoreType.DMA] * n_w
        + list(scratch),
        cost_estimate=pl.CostEstimate(flops=flops, bytes_accessed=n_bytes, transcendentals=0),
        compiler_params=pltpu.CompilerParams(vmem_limit_bytes=limit * 2**20),
    )(*args, *weights)


def arr(*shape, dtype=F32):
    return jax.ShapeDtypeStruct(shape, dtype)


def fill(pay_ref, rows_ref):
    block = rows_ref[...]

    def step(j, _):
        pay_ref[j] = block
        return 0

    lax.fori_loop(0, pay_ref.shape[0], step, 0, unroll=8)


def stats_rows(value, rows_ref, r, size, offset):
    mean = jnp.sum(value, axis=0, keepdims=True) * (1.0 / size)
    away = value - mean
    rows_ref[pl.ds(r, 1), :] = mean
    rows_ref[pl.ds(r + offset, 1), :] = jnp.sum(away * away, axis=0, keepdims=True)


def merge_stats(got_ref, mates_ref, st_ref, q, size, lo=0):
    n = got_ref.shape[0]
    k = MICRO * q
    mates = n // NVIEW
    step = 8

    def one(i, acc):
        at = pl.ds(i * step, step)
        return acc + jnp.sum(mates_ref[at] * got_ref[at, :k], axis=0)

    mean = lax.fori_loop(0, n // step, one, jnp.zeros((k, LANES), F32), unroll=4) * (1.0 / mates)

    def two(i, acc):
        at = pl.ds(i * step, step)
        away = got_ref[at, :k] - mean[None]
        return acc + jnp.sum(mates_ref[at] * (got_ref[at, k : 2 * k] + size * (away * away)), axis=0)

    total = lax.fori_loop(0, n // step, two, jnp.zeros((k, LANES), F32), unroll=4)
    st_ref[:k] = mean
    st_ref[k : 2 * k] = lax.rsqrt(total * (1.0 / (mates * size)) + EPSILON)


def merge_sums(got_ref, mates_ref, sum_ref, q, size, total_refs):
    n = got_ref.shape[0]
    k = MICRO * q
    scale = 1.0 / (n // NVIEW * size)
    step = 8

    def one(i, carry):
        at = pl.ds(i * step, step)
        first, second = got_ref[at, :k], got_ref[at, k : 2 * k]
        w = mates_ref[at]
        return (
            carry[0] + jnp.sum(w * first, axis=0),
            carry[1] + jnp.sum(w * second, axis=0),
            carry[2] + jnp.sum(first, axis=0),
            carry[3] + jnp.sum(second, axis=0),
        )

    zero = jnp.zeros((k, LANES), F32)
    a, b, ta, tb = lax.fori_loop(0, n // step, one, (zero,) * 4, unroll=4)
    sum_ref[:k] = a * scale
    sum_ref[k : 2 * k] = b * scale
    for ref, t in zip(total_refs, (ta, tb)):
        ref[...] = t[:q] + t[q : 2 * q] + t[2 * q :]


def shift_y(v, offset):
    if offset == 0:
        return v
    zero = jnp.zeros((8, v.shape[1]), v.dtype)
    if offset > 0:
        return jnp.concatenate([v[8:], zero], axis=0)
    return jnp.concatenate([zero, v[:-8]], axis=0)


def shift_x(v, offset):
    if offset == 0:
        return v
    place = lax.broadcasted_iota(jnp.int32, v.shape, 0) % 8
    if offset > 0:
        return jnp.where(place == 7, 0.0, pltpu.roll(v, v.shape[0] - 1, axis=0))
    return jnp.where(place == 0, 0.0, pltpu.roll(v, 1, axis=0))


def write_patches(phase, patch_ref, m, half, c, width, sign, out_phases=((0, 0), (0, 1), (1, 0), (1, 1))):
    moved = {}

    def get(sy, sx, ox):
        if (sy, sx, ox) not in moved:
            moved[sy, sx, ox] = shift_x(phase[sy, sx], ox)
        return moved[sy, sx, ox]

    for i, (py, px) in enumerate(out_phases):
        for r in range(3):
            for k in range(3):
                at_y, at_x = py + sign * (r - 1), px + sign * (k - 1)
                piece = shift_y(get(at_y % 2, at_x % 2, at_x // 2), at_y // 2)
                rows = pl.ds((m * len(out_phases) + i) * half, half)
                patch_ref[rows, pl.ds((r * 3 + k) * width + c * LANES, LANES)] = piece.astype(BF)


PHASES = ((0, 0), (0, 1), (1, 0), (1, 1))


class Sizes:
    pass


def k_reduce(x, w, z):
    def body(ins, held, copies, out, extra):
        (x_ref,), (w_ref,), (out_ref,), (tmp,) = ins, held, out, extra
        copies[0].wait()
        product = dot(x_ref[...], w_ref[...])
        for c in range(z.q1):
            tmp[c] = product[:, c * LANES : (c + 1) * LANES]
        for m in range(MICRO):
            for k in range(z.maps):
                for px in range(2):
                    for c in range(z.q1):
                        out_ref[k, m, pl.ds(px * 8, 8), cols(c)] = tmp[
                            c, pl.ds((m * z.maps + k) * z.cols + px, 8, stride=2), :
                        ]

    rows = x.shape[0]
    return kernel_call(
        body,
        [arr(z.maps, MICRO, z.cols, z.c_mid)],
        [x],
        [w],
        [pltpu.VMEM((z.q1, rows, LANES), F32)],
        flops=2 * rows * x.shape[1] * z.c_mid,
    )[0]


def k_arrive(pre, ids, z):
    def body(ins, held, copies, out, extra):
        (p_ref, id_ref), (map_ref, pay_ref), (rows_ref,) = ins, out, extra
        for m in range(MICRO):
            for y in range(z.height):
                for px in range(2):
                    at = m * z.rows + (2 * (y % 2) + px) * z.half + (y // 2) * 8
                    map_ref[pl.ds(at, 8), :] = p_ref[y, m, pl.ds(px * 8, 8), :]
        rows_ref[...] = jnp.zeros(rows_ref.shape, F32)
        for m in range(MICRO):
            for c in range(z.q1):
                stats_rows(map_ref[pl.ds(m * z.rows, z.rows), cols(c)], rows_ref, m * z.q1 + c, z.rows, MICRO * z.q1)
        rows_ref[pl.ds(6 * z.q1, MICRO), :] = id_ref[...]
        fill(pay_ref, rows_ref)

    pad = 16
    return kernel_call(
        body,
        [arr(MICRO * z.rows, z.c_mid), arr(z.n, pad, LANES)],
        [pre, ids],
        scratch=[pltpu.VMEM((pad, LANES), F32)],
    )


def k_spatial(got, mates, pre, gain, offset, w, z):
    q = z.q1

    def body(ins, held, copies, out, extra):
        got_ref, mates_ref, pre_ref, g_ref, o_ref = ins
        patch_ref, next_ref, pay_ref, st_ref = out
        (rows_ref,) = extra
        merge_stats(got_ref, mates_ref, st_ref, q, z.rows)
        for m in range(MICRO):
            for c in range(q):
                mean, inverse = row(st_ref, m * q + c), row(st_ref, (MICRO + m) * q + c)
                phase = {}
                for i, p in enumerate(PHASES):
                    x = pre_ref[pl.ds(m * z.rows + i * z.half, z.half), cols(c)]
                    phase[p] = gelu(g_ref[:, cols(c)] * ((x - mean) * inverse) + o_ref[:, cols(c)])
                write_patches(phase, patch_ref, m, z.half, c, z.c_mid, 1)
        copies[0].wait()
        next_ref[...] = dot(patch_ref[...], held[0][...])
        for m in range(MICRO):
            for c in range(q):
                stats_rows(next_ref[pl.ds(m * z.rows, z.rows), cols(c)], rows_ref, m * q + c, z.rows, MICRO * q)
        fill(pay_ref, rows_ref)

    rows = MICRO * z.rows
    return kernel_call(
        body,
        [arr(rows, 9 * z.c_mid, dtype=BF), arr(rows, z.c_mid), arr(z.n, 6 * q, LANES), arr(6 * q, LANES)],
        [got, mates, pre, gain, offset],
        [w],
        [pltpu.VMEM((6 * q, LANES), F32)],
        flops=2 * rows * 9 * z.c_mid * z.c_mid,
    )


def k_expand(got, mates, pre, gain, offset, w, z):
    q, qo = z.q1, z.q3

    def body(ins, held, copies, out, extra):
        got_ref, mates_ref, pre_ref, g_ref, o_ref = ins
        act_ref, next_ref, pay_ref, st_ref = out
        (rows_ref,) = extra
        merge_stats(got_ref, mates_ref, st_ref, q, z.rows)
        for m in range(MICRO):
            for c in range(q):
                mean, inverse = row(st_ref, m * q + c), row(st_ref, (MICRO + m) * q + c)
                at = pl.ds(m * z.rows, z.rows)
                x = pre_ref[at, cols(c)]
                act_ref[at, cols(c)] = gelu(g_ref[:, cols(c)] * ((x - mean) * inverse) + o_ref[:, cols(c)]).astype(BF)
        copies[0].wait()
        next_ref[...] = dot(act_ref[...], held[0][...])
        for m in range(MICRO):
            for c in range(qo):
                stats_rows(next_ref[pl.ds(m * z.rows, z.rows), cols(c)], rows_ref, m * qo + c, z.rows, MICRO * qo)
        fill(pay_ref, rows_ref)

    rows = MICRO * z.rows
    return kernel_call(
        body,
        [arr(rows, z.c_mid, dtype=BF), arr(rows, z.c_in), arr(z.n, 6 * qo, LANES), arr(6 * q, LANES)],
        [got, mates, pre, gain, offset],
        [w],
        [pltpu.VMEM((6 * qo, LANES), F32)],
        flops=2 * rows * z.c_in * z.c_mid,
    )


def k_narrow(got, mates, pre, gain, offset, maps_in, w, z):
    q, qo = z.q3, z.q4

    def body(ins, held, copies, out, extra):
        got_ref, mates_ref, pre_ref, g_ref, o_ref, in_ref = ins
        res_ref, join_ref, even_ref, next_ref, pay_ref, st_ref = out
        (rows_ref,) = extra
        merge_stats(got_ref, mates_ref, st_ref, q, z.rows)
        for m in range(MICRO):
            for c in range(q):
                mean, inverse = row(st_ref, m * q + c), row(st_ref, (MICRO + m) * q + c)
                at = pl.ds(m * z.rows, z.rows)
                x = pre_ref[at, cols(c)]
                res = g_ref[:, cols(c)] * ((x - mean) * inverse) + o_ref[:, cols(c)] + in_ref[at, cols(c)].astype(F32)
                res_ref[at, cols(c)] = res
                joined = gelu(res).astype(BF)
                join_ref[at, cols(c)] = joined
                even_ref[pl.ds(m * z.half, z.half), cols(c)] = joined[: z.half]
        copies[0].wait()
        next_ref[...] = dot(join_ref[...], held[0][...])
        for m in range(MICRO):
            for c in range(qo):
                stats_rows(next_ref[pl.ds(m * z.rows, z.rows), cols(c)], rows_ref, m * qo + c, z.rows, MICRO * qo)
        fill(pay_ref, rows_ref)

    rows = MICRO * z.rows
    return kernel_call(
        body,
        [
            arr(rows, z.c_in),
            arr(rows, z.c_in, dtype=BF),
            arr(MICRO * z.half, z.c_in, dtype=BF),
            arr(rows, z.c_wide),
            arr(z.n, 6 * qo, LANES),
            arr(6 * q, LANES),
        ],
        [got, mates, pre, gain, offset, maps_in],
        [w],
        [pltpu.VMEM((6 * qo, LANES), F32)],
        flops=2 * rows * z.c_in * z.c_wide,
    )


def k_stride(got, mates, pre, gain, offset, w, z):
    q = z.q4

    def body(ins, held, copies, out, extra):
        got_ref, mates_ref, pre_ref, g_ref, o_ref = ins
        patch_ref, next_ref, pay_ref, st_ref = out
        (rows_ref,) = extra
        merge_stats(got_ref, mates_ref, st_ref, q, z.rows)
        for m in range(MICRO):
            for c in range(q):
                mean, inverse = row(st_ref, m * q + c), row(st_ref, (MICRO + m) * q + c)
                phase = {}
                for i, p in enumerate(PHASES):
                    x = pre_ref[pl.ds(m * z.rows + i * z.half, z.half), cols(c)]
                    phase[p] = gelu(g_ref[:, cols(c)] * ((x - mean) * inverse) + o_ref[:, cols(c)])
                write_patches(phase, patch_ref, m, z.half, c, z.c_wide, 1, ((0, 0),))
        copies[0].wait()
        next_ref[...] = dot(patch_ref[...], held[0][...])
        for m in range(MICRO):
            for c in range(q):
                stats_rows(next_ref[pl.ds(m * z.half, z.half), cols(c)], rows_ref, m * q + c, z.half, MICRO * q)
        fill(pay_ref, rows_ref)

    rows = MICRO * z.half
    return kernel_call(
        body,
        [arr(rows, 9 * z.c_wide, dtype=BF), arr(rows, z.c_wide), arr(z.n, 6 * q, LANES), arr(6 * q, LANES)],
        [got, mates, pre, gain, offset],
        [w],
        [pltpu.VMEM((6 * q, LANES), F32)],
        flops=2 * rows * 9 * z.c_wide * z.c_wide,
    )


def k_shortcut(even, w, z):
    def body(ins, held, copies, out, extra):
        (e_ref,), (next_ref, st_ref) = ins, out
        copies[0].wait()
        next_ref[...] = dot(e_ref[...], held[0][...])
        for c in range(z.q6):
            for m in range(MICRO):
                stats_rows(next_ref[pl.ds(m * z.half, z.half), cols(c)], st_ref.at[c], m, z.half, MICRO)

    rows = MICRO * z.half
    return kernel_call(
        body, [arr(rows, z.c_out), arr(z.q6, 8, LANES)], [even], [w], flops=2 * rows * z.c_in * z.c_out
    )


def k_widen(got, mates, pre, gain, offset, short_st, w, z):
    q = z.q4

    def body(ins, held, copies, out, extra):
        got_ref, mates_ref, pre_ref, g_ref, o_ref, short_ref = ins
        act_ref, next_ref, pay_ref, st_ref = out
        merge_stats(got_ref, mates_ref, st_ref, q, z.half)
        for m in range(MICRO):
            for c in range(q):
                mean, inverse = row(st_ref, m * q + c), row(st_ref, (MICRO + m) * q + c)
                at = pl.ds(m * z.half, z.half)
                x = pre_ref[at, cols(c)]
                act_ref[at, cols(c)] = gelu(g_ref[:, cols(c)] * ((x - mean) * inverse) + o_ref[:, cols(c)]).astype(BF)
        copies[0].wait()
        next_ref[...] = dot(act_ref[...], held[0][...])
        for c in range(z.q6):
            for m in range(MICRO):
                stats_rows(next_ref[pl.ds(m * z.half, z.half), cols(c)], pay_ref.at[c], m, z.half, MICRO)
            pay_ref[z.q6 + c] = short_ref[c]
        chunks = 2 * z.q6
        for j in range(chunks, z.n):
            pay_ref[j] = pay_ref[j % chunks]

    rows = MICRO * z.half
    return kernel_call(
        body,
        [arr(rows, z.c_wide, dtype=BF), arr(rows, z.c_out), arr(z.n, 8, LANES), arr(6 * q, LANES)],
        [got, mates, pre, gain, offset, short_st],
        [w],
        flops=2 * rows * z.c_wide * z.c_out,
    )


def k_views(got, ids, z):
    def body(ins, held, copies, out, extra):
        (got_ref, id_ref), (pay_ref,), (lo, hi) = ins, out, extra
        mates = z.n // NVIEW
        g, ids = got_ref[...], id_ref[...]
        for view, ref in ((0, lo), (1, hi)):
            w = (ids == float(view)).astype(F32)
            mean = jnp.sum(w * g, axis=0)[:MICRO] * (1.0 / mates)
            away = g[:, :MICRO] - mean[None]
            total = jnp.sum(w[:, :MICRO] * (g[:, MICRO : 2 * MICRO] + z.half * (away * away)), axis=0)
            ref[...] = jnp.zeros(ref.shape, F32)
            ref[:MICRO] = mean
            ref[MICRO : 2 * MICRO] = lax.rsqrt(total * (1.0 / (mates * z.half)) + EPSILON)
        pay_ref[...] = jnp.where(ids > 0.5, hi[...][None], lo[...][None])

    return kernel_call(
        body, [arr(z.n, 8, LANES)], [got, ids], scratch=[pltpu.VMEM((8, LANES), F32)] * 2
    )[0]


def k_mapped(whole, pre_w, pre_s, cot, gains, z):
    def body(ins, held, copies, out, extra):
        st_ref, w_ref, s_ref, cot_ref, gw, ow, gs, os = ins
        map_ref, d_ref, pay_ref = out
        n_c = z.q6
        pay_ref[...] = jnp.zeros(pay_ref.shape, F32)
        for c in range(n_c):
            for m in range(MICRO):
                at = pl.ds(m * z.half, z.half)
                sw, ss = st_ref.at[c], st_ref.at[n_c + c]
                hat_w = (w_ref[at, cols(c)] - row(sw, m)) * row(sw, MICRO + m)
                hat_s = (s_ref[at, cols(c)] - row(ss, m)) * row(ss, MICRO + m)
                res = gw[:, cols(c)] * hat_w + ow[:, cols(c)] + (gs[:, cols(c)] * hat_s + os[:, cols(c)])
                map_ref[at, cols(c)] = gelu(res).astype(BF)
                d = gelu_slope(res) * cot_ref[at, cols(c)].astype(F32)
                d_ref[at, cols(c)] = d
                first, second = pay_ref.at[c], pay_ref.at[n_c + c]
                first[pl.ds(m, 1), :] = jnp.sum(d, axis=0, keepdims=True)
                first[pl.ds(MICRO + m, 1), :] = jnp.sum(d * hat_w, axis=0, keepdims=True)
                second[pl.ds(m, 1), :] = jnp.sum(d * hat_s, axis=0, keepdims=True)
        for j in range(2 * n_c, z.n):
            pay_ref[j] = pay_ref[j % (2 * n_c)]

    rows = MICRO * z.half
    return kernel_call(
        body,
        [arr(rows, z.c_out, dtype=BF), arr(rows, z.c_out), arr(z.n, 8, LANES)],
        [whole, pre_w, pre_s, cot, *gains],
        flops=rows * z.c_out * 60,
    )


def k_view_sums(got, ids, z):
    def body(ins, held, copies, out, extra):
        (got_ref, id_ref), (pay_ref,), (both,) = ins, out, extra
        g, ids = got_ref[...], id_ref[...]
        lo = jnp.sum((ids == 0.0).astype(F32) * g, axis=0)
        hi = jnp.sum((ids == 1.0).astype(F32) * g, axis=0)
        both[0], both[1] = lo, hi
        all_views = lo + hi
        totals = []
        for k in range(2):
            totals.append(jnp.sum(all_views[k * MICRO : (k + 1) * MICRO], axis=0, keepdims=True))
        for v in range(2):
            for k in range(2):
                both[v, pl.ds(2 * MICRO + k, 1), :] = totals[k]
        pay_ref[...] = jnp.where(ids > 0.5, both[1][None], both[0][None])

    return kernel_call(body, [arr(z.n, 8, LANES)], [got, ids], scratch=[pltpu.VMEM((2, 8, LANES), F32)])[0]


def back_rows(x, d, st_ref, sum_ref, m, q, c, gain):
    inverse = row(st_ref, (MICRO + m) * q + c)
    hat = (x - row(st_ref, m * q + c)) * inverse
    return gain * inverse * (d - row(sum_ref, m * q + c) - hat * row(sum_ref, (MICRO + m) * q + c))


def sum_rows(d, hat, rows_ref, r, offset):
    rows_ref[pl.ds(r, 1), :] = jnp.sum(d, axis=0, keepdims=True)
    rows_ref[pl.ds(r + offset, 1), :] = jnp.sum(d * hat, axis=0, keepdims=True)


def slope_and_sums(d_out, pre_ref, at, st_ref, m, q, c, g_ref, o_ref, d_ref, rows_ref):
    hat = (pre_ref[at, cols(c)] - row(st_ref, m * q + c)) * row(st_ref, (MICRO + m) * q + c)
    d = gelu_slope(g_ref[:, cols(c)] * hat + o_ref[:, cols(c)]) * d_out
    d_ref[at, cols(c)] = d
    sum_rows(d, hat, rows_ref, m * q + c, MICRO * q)


def k_back_widen(whole, sums, d_two, pre_w, pre_s, gain_w, gain_s, pre, st, gain, offset, w, z):
    q, n_c = z.q4, z.q6

    def body(ins, held, copies, out, extra):
        st2, sum_ref, d_ref, w_ref, s_ref, gw, gs, pre_ref, st_ref, g_ref, o_ref = ins
        dw_ref, ds_ref, t_off, t_gw, t_gs, d_next, pay_ref = out
        (rows_ref, tmp) = extra
        scale = 1.0 / (z.n // NVIEW * z.half)
        for c in range(n_c):
            first, second = sum_ref.at[c], sum_ref.at[n_c + c]
            t_off[pl.ds(c, 1), :] = row(first, 2 * MICRO)
            t_gw[pl.ds(c, 1), :] = row(first, 2 * MICRO + 1)
            t_gs[pl.ds(c, 1), :] = row(second, 2 * MICRO)
            sw, ss = st2.at[c], st2.at[n_c + c]
            for m in range(MICRO):
                at = pl.ds(m * z.half, z.half)
                inv_w, inv_s = row(sw, MICRO + m), row(ss, MICRO + m)
                hat_w = (w_ref[at, cols(c)] - row(sw, m)) * inv_w
                hat_s = (s_ref[at, cols(c)] - row(ss, m)) * inv_s
                d = d_ref[at, cols(c)] - row(first, m) * scale
                dw_ref[at, cols(c)] = (
                    gw[:, cols(c)] * inv_w * (d - hat_w * (row(first, MICRO + m) * scale))
                ).astype(BF)
                ds_ref[at, cols(c)] = (gs[:, cols(c)] * inv_s * (d - hat_s * (row(second, m) * scale))).astype(BF)
        copies[0].wait()
        tmp[...] = dot_nt(dw_ref[...], held[0][...])
        for m in range(MICRO):
            at = pl.ds(m * z.half, z.half)
            for c in range(q):
                slope_and_sums(tmp[at, cols(c)], pre_ref, at, st_ref, m, q, c, g_ref, o_ref, d_next, rows_ref)
        fill(pay_ref, rows_ref)

    rows = MICRO * z.half
    return kernel_call(
        body,
        [arr(rows, z.c_out, dtype=BF)] * 2
        + [arr(n_c, LANES)] * 3
        + [arr(rows, z.c_wide), arr(z.n, 6 * q, LANES)],
        [whole, sums, d_two, pre_w, pre_s, gain_w, gain_s, pre, st, gain, offset],
        [w],
        [pltpu.VMEM((6 * q, LANES), F32), pltpu.VMEM((rows, z.c_wide), F32)],
        flops=2 * rows * z.c_wide * z.c_out,
    )


def back_start(refs, mates_ref, sum_ref, out_ref, q, n_rows, totals):
    got_ref, d_ref, pre_ref, st_ref, g_ref = refs
    merge_sums(got_ref, mates_ref, sum_ref, q, n_rows, totals)
    for m in range(MICRO):
        at = pl.ds(m * n_rows, n_rows)
        for c in range(q):
            out_ref[at, cols(c)] = back_rows(
                pre_ref[at, cols(c)], d_ref[at, cols(c)], st_ref, sum_ref, m, q, c, g_ref[:, cols(c)]
            ).astype(BF)


def k_back_stride(got, mates, d, pre_s, st_s, gain_s, pre, st, gain, offset, w, z):
    q = z.q4

    def body(ins, held, copies, out, extra):
        got_ref, mates_ref, d_ref, ps_ref, ss_ref, gs_ref, pre_ref, st_ref, g_ref, o_ref = ins
        delta_ref, t_off, t_gain, d_next, pay_ref = out
        rows_ref, sum_ref, contrib = extra
        back_start((got_ref, d_ref, ps_ref, ss_ref, gs_ref), mates_ref, sum_ref, delta_ref, q, z.half, (t_off, t_gain))
        copies[0].wait()
        contrib[...] = dot_nt(delta_ref[...], held[0][...])
        for m in range(MICRO):
            for c in range(q):
                phase = {}
                for r in range(3):
                    for k in range(3):
                        piece = contrib[pl.ds(m * z.half, z.half), pl.ds((r * 3 + k) * z.c_wide + c * LANES, LANES)]
                        piece = shift_x(shift_y(piece, 1 if r == 0 else 0), 1 if k == 0 else 0)
                        p = ((r + 1) % 2, (k + 1) % 2)
                        phase[p] = piece if p not in phase else phase[p] + piece
                first = second = 0.0
                mean, inverse = row(st_ref, m * q + c), row(st_ref, (MICRO + m) * q + c)
                for i, p in enumerate(PHASES):
                    at = pl.ds(m * z.rows + i * z.half, z.half)
                    hat = (pre_ref[at, cols(c)] - mean) * inverse
                    grad = gelu_slope(g_ref[:, cols(c)] * hat + o_ref[:, cols(c)]) * phase[p]
                    d_next[at, cols(c)] = grad
                    first = first + jnp.sum(grad, axis=0, keepdims=True)
                    second = second + jnp.sum(grad * hat, axis=0, keepdims=True)
                rows_ref[pl.ds(m * q + c, 1), :] = first
                rows_ref[pl.ds((MICRO + m) * q + c, 1), :] = second
        fill(pay_ref, rows_ref)

    rows = MICRO * z.half
    return kernel_call(
        body,
        [arr(rows, z.c_wide, dtype=BF)]
        + [arr(q, LANES)] * 2
        + [arr(MICRO * z.rows, z.c_wide), arr(z.n, 6 * q, LANES)],
        [got, mates, d, pre_s, st_s, gain_s, pre, st, gain, offset],
        [w],
        [
            pltpu.VMEM((6 * q, LANES), F32),
            pltpu.VMEM((6 * q, LANES), F32),
            pltpu.VMEM((rows, 9 * z.c_wide), F32),
        ],
        flops=2 * rows * 9 * z.c_wide * z.c_wide,
    )


def k_back_narrow(got, mates, d, pre_n, st_n, gain_n, even, res, pre, st, w, z):
    q, qo = z.q4, z.q3

    def body(ins, held, copies, out, extra):
        got_ref, mates_ref, d_ref, pn_ref, sn_ref, gn_ref, even_ref, res_ref, pre_ref, st_ref = ins
        delta_ref, t_off, t_gain, d_next, pay_ref = out
        rows_ref, sum_ref, tmp = extra
        back_start((got_ref, d_ref, pn_ref, sn_ref, gn_ref), mates_ref, sum_ref, delta_ref, q, z.rows, (t_off, t_gain))
        copies[0].wait()
        tmp[...] = dot_nt(delta_ref[...], held[0][...])
        for m in range(MICRO):
            at = pl.ds(m * z.rows, z.rows)
            some = pl.ds(m * z.rows, z.half)
            for c in range(qo):
                tmp[some, cols(c)] = tmp[some, cols(c)] + even_ref[pl.ds(m * z.half, z.half), cols(c)]
                d_join = tmp[at, cols(c)].astype(BF).astype(F32)
                one = gelu_slope(res_ref[at, cols(c)]) * d_join
                hat = (pre_ref[at, cols(c)] - row(st_ref, m * qo + c)) * row(st_ref, (MICRO + m) * qo + c)
                d_next[at, cols(c)] = one
                sum_rows(one, hat, rows_ref, m * qo + c, MICRO * qo)
        fill(pay_ref, rows_ref)

    rows = MICRO * z.rows
    return kernel_call(
        body,
        [arr(rows, z.c_wide, dtype=BF)] + [arr(q, LANES)] * 2 + [arr(rows, z.c_in), arr(z.n, 6 * qo, LANES)],
        [got, mates, d, pre_n, st_n, gain_n, even, res, pre, st],
        [w],
        [
            pltpu.VMEM((6 * qo, LANES), F32),
            pltpu.VMEM((6 * q, LANES), F32),
            pltpu.VMEM((rows, z.c_in), F32),
        ],
        flops=2 * rows * z.c_in * z.c_wide,
    )


def k_back_expand(got, mates, d, pre_e, st_e, gain_e, pre, st, gain, offset, w, z):
    q, qo = z.q3, z.q1

    def body(ins, held, copies, out, extra):
        got_ref, mates_ref, d_ref, pe_ref, se_ref, ge_ref, pre_ref, st_ref, g_ref, o_ref = ins
        delta_ref, t_off, t_gain, d_next, pay_ref = out
        rows_ref, sum_ref, tmp = extra
        back_start((got_ref, d_ref, pe_ref, se_ref, ge_ref), mates_ref, sum_ref, delta_ref, q, z.rows, (t_off, t_gain))
        copies[0].wait()
        tmp[...] = dot_nt(delta_ref[...], held[0][...])
        for m in range(MICRO):
            at = pl.ds(m * z.rows, z.rows)
            for c in range(qo):
                slope_and_sums(tmp[at, cols(c)], pre_ref, at, st_ref, m, qo, c, g_ref, o_ref, d_next, rows_ref)
        fill(pay_ref, rows_ref)

    rows = MICRO * z.rows
    return kernel_call(
        body,
        [arr(rows, z.c_in, dtype=BF)] + [arr(q, LANES)] * 2 + [arr(rows, z.c_mid), arr(z.n, 6 * qo, LANES)],
        [got, mates, d, pre_e, st_e, gain_e, pre, st, gain, offset],
        [w],
        [
            pltpu.VMEM((6 * qo, LANES), F32),
            pltpu.VMEM((6 * q, LANES), F32),
            pltpu.VMEM((rows, z.c_mid), F32),
        ],
        flops=2 * rows * z.c_in * z.c_mid,
    )


def k_back_spatial(got, mates, d, pre_s, st_s, gain_s, pre, st, gain, offset, w, z):
    q = z.q1

    def body(ins, held, copies, out, extra):
        got_ref, mates_ref, d_ref, ps_ref, ss_ref, gs_ref, pre_ref, st_ref, g_ref, o_ref = ins
        delta_ref, t_off, t_gain, d_next, pay_ref = out
        rows_ref, sum_ref, patch_ref, tmp = extra
        merge_sums(got_ref, mates_ref, sum_ref, q, z.rows, (t_off, t_gain))
        for m in range(MICRO):
            for c in range(q):
                phase = {}
                for i, p in enumerate(PHASES):
                    at = pl.ds(m * z.rows + i * z.half, z.half)
                    phase[p] = back_rows(
                        ps_ref[at, cols(c)], d_ref[at, cols(c)], ss_ref, sum_ref, m, q, c, gs_ref[:, cols(c)]
                    )
                    delta_ref[at, cols(c)] = phase[p].astype(BF)
                write_patches(phase, patch_ref, m, z.half, c, z.c_mid, -1)
        copies[0].wait()
        tmp[...] = dot(patch_ref[...], held[0][...])
        for m in range(MICRO):
            at = pl.ds(m * z.rows, z.rows)
            for c in range(q):
                slope_and_sums(tmp[at, cols(c)], pre_ref, at, st_ref, m, q, c, g_ref, o_ref, d_next, rows_ref)
        fill(pay_ref, rows_ref)

    rows = MICRO * z.rows
    return kernel_call(
        body,
        [arr(rows, z.c_mid, dtype=BF)] + [arr(q, LANES)] * 2 + [arr(rows, z.c_mid), arr(z.n, 6 * q, LANES)],
        [got, mates, d, pre_s, st_s, gain_s, pre, st, gain, offset],
        [w],
        [
            pltpu.VMEM((6 * q, LANES), F32),
            pltpu.VMEM((6 * q, LANES), F32),
            pltpu.VMEM((rows, 9 * z.c_mid), BF),
            pltpu.VMEM((rows, z.c_mid), F32),
        ],
        flops=2 * rows * 9 * z.c_mid * z.c_mid,
    )


def k_back_reduce(got, mates, d, pre_r, st_r, gain_r, z):
    q = z.q1

    def body(ins, held, copies, out, extra):
        got_ref, mates_ref, d_ref, pr_ref, sr_ref, gr_ref = ins
        delta_ref, t_off, t_gain = out
        (sum_ref,) = extra
        back_start((got_ref, d_ref, pr_ref, sr_ref, gr_ref), mates_ref, sum_ref, delta_ref, q, z.rows, (t_off, t_gain))

    rows = MICRO * z.rows
    return kernel_call(
        body,
        [arr(rows, z.c_mid, dtype=BF)] + [arr(q, LANES)] * 2,
        [got, mates, d, pre_r, st_r, gain_r],
        scratch=[pltpu.VMEM((6 * q, LANES), F32)],
    )


def on_device(
    features,
    view_ids,
    w_reduce,
    w_spatial,
    w_expand,
    w_narrow,
    w_stride,
    w_widen,
    w_shortcut,
    gain_reduce,
    offset_reduce,
    gain_spatial,
    offset_spatial,
    gain_expand,
    offset_expand,
    gain_narrow,
    offset_narrow,
    gain_stride,
    offset_stride,
    gain_widen,
    offset_widen,
    gain_shortcut,
    offset_shortcut,
    cotangent,
):
    z = Sizes()
    z.ns, z.nb = lax.axis_size("space"), lax.axis_size("batch")
    z.n = z.ns * z.nb
    z.maps, z.cols = features.shape[1], features.shape[3]
    z.height = z.ns
    z.rows = z.height * z.cols
    z.half = z.rows // 4
    z.c_in, z.c_mid = w_reduce.shape
    z.c_wide, z.c_out = w_widen.shape
    z.q1, z.q3, z.q4, z.q6 = (c // LANES for c in (z.c_mid, z.c_in, z.c_wide, z.c_out))
    assert features.shape[2] == 1 and cotangent.shape[1] == 1 and z.maps == z.ns and z.cols == 16
    yh, xh = z.height // 2, z.cols // 2
    n, ns, nb = z.n, z.ns, z.nb
    s, b = lax.axis_index("space"), lax.axis_index("batch")

    def share(pay):
        return lax.all_to_all(pay, ALL, 0, 0, tiled=True)

    def exchange(block):
        return lax.all_to_all(block, "space", 0, 0, tiled=True)

    def trade(block, axis):
        size, me = lax.axis_size(axis), lax.axis_index(axis)
        out = block
        for k in range(1, size):
            piece = lax.dynamic_index_in_dim(block, me ^ k, 0, keepdims=True)
            piece = lax.ppermute(piece, axis, [(i, i ^ k) for i in range(size)])
            out = lax.dynamic_update_slice_in_dim(out, piece, me ^ k, 0)
        return out

    def lines(vector):
        return vector.reshape(1, -1)

    vectors = {
        "reduce": (lines(gain_reduce), lines(offset_reduce)),
        "spatial": (lines(gain_spatial), lines(offset_spatial)),
        "expand": (lines(gain_expand), lines(offset_expand)),
        "narrow": (lines(gain_narrow), lines(offset_narrow)),
        "stride": (lines(gain_stride), lines(offset_stride)),
        "widen": (lines(gain_widen), lines(offset_widen)),
        "shortcut": (lines(gain_shortcut), lines(offset_shortcut)),
    }

    pre_rows = k_reduce(features.reshape(-1, z.c_in), w_reduce, z)
    my_ids = lax.dynamic_slice_in_dim(view_ids, s, 1, 1).astype(F32)
    pre_reduce, pay = k_arrive(exchange(pre_rows), jnp.broadcast_to(my_ids, (MICRO, LANES)), z)
    got = share(pay)
    ids = got[:, 6 * z.q1 : 6 * z.q1 + MICRO]
    same = (ids == my_ids[None]).astype(F32)
    mates = {q: jnp.repeat(same, q, axis=1) for q in sorted({z.q1, z.q3, z.q4})}
    id_rows = jnp.concatenate([ids, ids, jnp.zeros((n, 2, LANES), F32)], axis=1)

    rows_in = features.reshape(MICRO, z.maps, xh, 2, z.c_in).transpose(1, 0, 3, 2, 4)
    rows_in = rows_in.reshape(z.maps, MICRO, z.cols, z.c_in)
    maps_in = trade(rows_in, "space").reshape(yh, 2, MICRO, 2, xh, z.c_in).transpose(2, 1, 3, 0, 4, 5)
    maps_in = maps_in.reshape(MICRO * z.rows, z.c_in)

    patch_reduce, pre_spatial, pay, st_reduce = k_spatial(got, mates[z.q1], pre_reduce, *vectors["reduce"], w_spatial, z)
    got = share(pay)
    out_spatial, pre_expand, pay, st_spatial = k_expand(got, mates[z.q1], pre_spatial, *vectors["spatial"], w_expand, z)
    got = share(pay)
    residual_one, joined, even, pre_narrow, pay, st_expand = k_narrow(
        got, mates[z.q3], pre_expand, *vectors["expand"], maps_in, w_narrow, z
    )
    got = share(pay)
    pre_shortcut, short_st = k_shortcut(even, w_shortcut, z)
    patch_narrow, pre_stride, pay, st_narrow = k_stride(got, mates[z.q4], pre_narrow, *vectors["narrow"], w_stride, z)
    got = share(pay)
    out_stride, pre_widen, pay, st_stride = k_widen(
        got, mates[z.q4], pre_stride, *vectors["stride"], short_st, w_widen, z
    )
    whole = share(k_views(share(pay), id_rows, z))
    mapped, d_two, pay = k_mapped(
        whole,
        pre_widen,
        pre_shortcut,
        cotangent.reshape(-1, z.c_out),
        (*vectors["widen"], *vectors["shortcut"]),
        z,
    )

    sums = share(k_view_sums(share(pay), id_rows, z))
    delta_widen, delta_shortcut, go_widen, gg_widen, gg_shortcut, d_stride, pay = k_back_widen(
        whole, sums, d_two, pre_widen, pre_shortcut, vectors["widen"][0], vectors["shortcut"][0],
        pre_stride, st_stride, *vectors["stride"], w_widen, z,
    )
    got = share(pay)
    delta_stride, go_stride, gg_stride, d_narrow, pay = k_back_stride(
        got, mates[z.q4], d_stride, pre_stride, st_stride, vectors["stride"][0],
        pre_narrow, st_narrow, *vectors["narrow"], w_stride, z,
    )
    got = share(pay)
    d_even = dot_nt(delta_shortcut, w_shortcut)
    delta_narrow, go_narrow, gg_narrow, d_one, pay = k_back_narrow(
        got, mates[z.q4], d_narrow, pre_narrow, st_narrow, vectors["narrow"][0],
        d_even, residual_one, pre_expand, st_expand, w_narrow, z,
    )
    got = share(pay)

    def to_rows(block):
        c = block.shape[-1]
        return block.reshape(MICRO, 2, 2, yh, xh, c).transpose(3, 1, 0, 2, 4, 5).reshape(ns, MICRO, z.cols, c)

    d_one_rows = trade(to_rows(d_one.astype(BF)), "space")
    delta_expand, go_expand, gg_expand, d_spatial, pay = k_back_expand(
        got, mates[z.q3], d_one, pre_expand, st_expand, vectors["expand"][0],
        pre_spatial, st_spatial, *vectors["spatial"], w_expand, z,
    )
    got = share(pay)
    flipped = w_spatial.reshape(9, z.c_mid, z.c_mid).transpose(0, 2, 1).reshape(9 * z.c_mid, z.c_mid)
    delta_spatial, go_spatial, gg_spatial, d_reduce, pay = k_back_spatial(
        got, mates[z.q1], d_spatial, pre_spatial, st_spatial, vectors["spatial"][0],
        pre_reduce, st_reduce, *vectors["reduce"], flipped, z,
    )
    got = share(pay)
    delta_reduce, go_reduce, gg_reduce = k_back_reduce(
        got, mates[z.q1], d_reduce, pre_reduce, st_reduce, vectors["reduce"][0], z
    )
    delta_rows = exchange(to_rows(delta_reduce)).reshape(-1, z.c_mid)
    d_input = (d_one_rows.reshape(-1, z.c_in).astype(F32) + dot_nt(delta_rows, w_reduce)).astype(BF)
    grad_features = d_input.reshape(z.maps, MICRO, 2, xh, z.c_in).transpose(1, 0, 3, 2, 4).reshape(features.shape)

    def halves(parts, axis, bit, dim):
        size, me = lax.axis_size(axis), lax.axis_index(axis)
        mine = (me >> bit) & 1
        send = lax.dynamic_index_in_dim(parts, 1 - mine, dim, keepdims=False)
        keep = lax.dynamic_index_in_dim(parts, mine, dim, keepdims=False)
        came = lax.ppermute(send, axis, [(i, i ^ (1 << bit)) for i in range(size)])
        return (keep.astype(F32) + came.astype(F32)).astype(BF)

    sbits, bbits = ns.bit_length() - 1, nb.bit_length() - 1

    def over_space(parts):
        parts = parts.reshape((2,) * sbits + parts.shape[1:])
        for bit in range(sbits):
            parts = halves(parts, "space", bit, sbits - 1 - bit)
        return parts

    def over_batch(parts):
        parts = parts.reshape((2,) * bbits + parts.shape[1:])
        for bit in range(bbits):
            parts = halves(parts, "batch", bit, bbits - 1 - bit)
        return parts

    def collect(block):
        return lax.all_gather(block, "batch", axis=0)

    def gathered(operand, gradient):
        parts = gradient.reshape(-1, nb, gradient.shape[1] // nb).transpose(1, 0, 2)
        parts = trade(parts, "batch")
        whole = trade(jnp.broadcast_to(operand[None], (nb,) + operand.shape), "batch")
        return dot_tn(whole.reshape(-1, operand.shape[1]), parts.reshape(-1, parts.shape[-1])).astype(BF)

    def finish_cols(product):
        r, c = product.shape
        mine = over_space(product.reshape(ns, r // ns, c))
        return collect(mine).transpose(1, 0, 2).reshape(r // ns, nb * c).astype(F32)

    def finish_rows(product):
        r, c = product.shape
        parts = product.astype(BF).reshape(ns, nb, r // n, c).transpose(1, 0, 2, 3)
        return collect(over_space(over_batch(parts))).reshape(r // ns, c).astype(F32)

    grad_w_widen = finish_cols(gathered(out_stride, delta_widen))
    grad_w_shortcut = finish_cols(gathered(even, delta_shortcut))
    grad_w_stride = finish_rows(dot_tn(patch_narrow, delta_stride))
    grad_w_narrow = finish_rows(dot_tn(joined, delta_narrow))
    grad_w_expand = finish_rows(dot_tn(out_spatial, delta_expand))
    grad_w_spatial = finish_rows(dot_tn(patch_reduce, delta_spatial))
    grad_w_reduce = finish_rows(dot_tn(maps_in, delta_reduce))

    flat = lambda block: block.reshape(-1)
    return (
        mapped.reshape(cotangent.shape),
        grad_features,
        grad_w_reduce,
        grad_w_spatial,
        grad_w_expand,
        grad_w_narrow,
        grad_w_stride,
        grad_w_widen,
        grad_w_shortcut,
        flat(gg_reduce),
        flat(go_reduce),
        flat(gg_spatial),
        flat(go_spatial),
        flat(gg_expand),
        flat(go_expand),
        flat(gg_narrow),
        flat(go_narrow),
        flat(gg_stride),
        flat(go_stride),
        flat(gg_widen),
        flat(go_widen),
        flat(gg_shortcut),
        flat(go_widen),
    )


def solution(mesh):
    return jax.shard_map(
        on_device,
        mesh=mesh,
        in_specs=(P(None, "batch", "space", None, None), P(None, "batch"))
        + (P(),) * 21
        + (P(None, ("batch", "space"), None, None, None),),
        out_specs=(P(None, ("batch", "space"), None, None, None), P(None, "batch", "space", None, None))
        + (P("space", None),) * 7
        + (P(),) * 14,
        check_vma=False,
    )
```

```python
import functools
import math

import jax
import jax.numpy as jnp
from jax import lax
from jax.experimental import pallas as pl
from jax.experimental.pallas import tpu as pltpu
from jax.sharding import Mesh
from jax.sharding import PartitionSpec as P

NVIEW = 2
MICRO = 3
EPSILON = 1e-05
BF = jnp.bfloat16
F32 = jnp.float32
BATCH, SPACE = ("bhi", "core"), ("shi", "slo")
ALL = BATCH + SPACE
LANES = 128
ROOT = math.sqrt(2.0 / math.pi)
CUBE = 0.044715


def dot(a, b, dims=((1,), (0,))):
    return lax.dot_general(a, b, (dims, ((), ())), preferred_element_type=F32)


def dot_nt(a, b):
    return dot(a, b, ((1,), (1,)))


def dot_tn(a, b):
    return dot(a, b, ((0,), (0,)))


def gelu(v):
    return 0.5 * v * (1.0 + jnp.tanh(ROOT * (v + CUBE * (v * v * v))))


def gelu_slope(v):
    square = v * v
    t = jnp.tanh(ROOT * (v + CUBE * (square * v)))
    return 0.5 * (1.0 + t) + (0.5 * ROOT) * v * (1.0 - t * t) * (1.0 + (3.0 * CUBE) * square)


def cols(c):
    return pl.ds(c * LANES, LANES)


def row(ref, r):
    return ref[pl.ds(r, 1), :]


class Kernel:
    def __init__(self, i, w, o, raw, scalars, stacks, extra, starts, sems):
        self.i, self.w, self.o, self.raw, self.s, self.st, self.x = i, w, o, raw, scalars, stacks, extra
        self.w_copies, self.out_pairs, self.sems = starts, {}, sems
        self.flying, self.sent = [], set()

    def wait_w(self, n=0):
        self.w_copies[n].wait()

    def send(self, n):
        src, dst, sem = self.out_pairs[n]
        copy = pltpu.make_async_copy(src, dst, sem)
        copy.start()
        self.flying.append(copy)
        self.sent.add(n)

    def copy(self, src, dst):
        copy = pltpu.make_async_copy(src, dst, self.sems.pop())
        copy.start()
        self.flying.append(copy)


def kernel_call(body, outs, args, weights=(), scratch=(), flops=0, raw=(), n_raw=0, scalars=(), passes=(), stacks=()):
    n_s, n_in, n_w, n_p = len(scalars), len(args), len(weights), len(passes)
    n_k = sum(map(len, stacks))
    n_out, n_r = len(outs), len(raw)

    def run(*refs):
        refs = list(refs)

        def take(n):
            part = refs[:n]
            del refs[:n]
            return part

        s, ins, w_any = take(n_s), take(n_in), take(n_w)
        piles = [take(len(g)) for g in stacks]
        take(n_p)
        out, raw_refs, _ = take(n_out), take(n_r), take(n_p)
        v_in, v_w, v_out, v_k = take(n_in), take(n_w), take(n_out), take(len(stacks))
        (sems,) = take(1)
        sem = [sems.at[j] for j in range(n_in + n_w + n_k + n_out + n_raw)]
        in_copies = [pltpu.make_async_copy(a, v, sem.pop(0)) for a, v in zip(ins, v_in)]
        for pile, v in zip(piles, v_k):
            for j, a in enumerate(pile):
                rows = a.shape[0]
                in_copies.append(pltpu.make_async_copy(a, v.at[pl.ds(j * rows, rows)], sem.pop(0)))
        w_copies = [pltpu.make_async_copy(a, v, sem.pop(0)) for a, v in zip(w_any, v_w)]
        for copy in in_copies + w_copies:
            copy.start()
        k = Kernel(v_in, v_w, v_out, raw_refs, s, v_k, refs, w_copies, sem[n_out:])
        k.out_pairs = {j: (v_out[j], out[j], sem[j]) for j in range(n_out)}
        for copy in in_copies:
            copy.wait()
        body(k)
        for j in range(n_out):
            if j not in k.sent:
                k.send(j)
        for copy in k.flying:
            copy.wait()

    def size(a):
        return math.prod(a.shape) * jnp.dtype(a.dtype).itemsize

    outside = pl.BlockSpec(memory_space=pl.ANY)
    piled = [arr(len(g) * g[0].shape[0], *g[0].shape[1:], dtype=g[0].dtype) for g in stacks]
    held = sum(map(size, (*args, *weights, *outs, *piled)))
    total = held + sum(size(a) for a in scratch if hasattr(a, "dtype"))
    first = n_s + n_in + n_w + n_k
    results = pl.pallas_call(
        run,
        out_shape=tuple(jax.ShapeDtypeStruct(o.shape, o.dtype) for o in (*outs, *raw, *passes)),
        in_specs=[pl.BlockSpec(memory_space=pltpu.SMEM)] * n_s + [outside] * (n_in + n_w + n_k + n_p),
        out_specs=tuple([outside] * (n_out + n_r + n_p)),
        scratch_shapes=[pltpu.VMEM(a.shape, a.dtype) for a in (*args, *weights, *outs, *piled)]
        + [pltpu.SemaphoreType.DMA((n_in + n_w + n_k + n_out + n_raw,))]
        + list(scratch),
        input_output_aliases={first + j: n_out + n_r + j for j in range(n_p)},
        cost_estimate=pl.CostEstimate(flops=flops, bytes_accessed=held, transcendentals=0),
        compiler_params=pltpu.CompilerParams(vmem_limit_bytes=max(60 * 2**20, total)),
    )(*scalars, *args, *weights, *(a for g in stacks for a in g), *passes)
    return tuple(results)


def arr(*shape, dtype=F32):
    return jax.ShapeDtypeStruct(shape, dtype)


def fill(pay_ref, rows_ref):
    block = rows_ref[...].astype(pay_ref.dtype)

    def step(j, _):
        pay_ref[j] = block
        return 0

    lax.fori_loop(0, pay_ref.shape[0], step, 0, unroll=8)


def stats_rows(value, rows_ref, r, size, offset):
    mean = jnp.sum(value, axis=0, keepdims=True) * (1.0 / size)
    away = value - mean
    rows_ref[pl.ds(r, 1), :] = mean
    rows_ref[pl.ds(r + offset, 1), :] = jnp.sum(away * away, axis=0, keepdims=True)


def stats_shape(q):
    return (6 * q, F32) if q < 4 else (9 * q, BF)


def stats_arr(n, q):
    rows, dtype = stats_shape(q)
    return arr(n, rows, LANES, dtype=dtype)


def fill_stats(pay_ref, rows_ref, q):
    k = MICRO * q
    if pay_ref.dtype == BF:
        mean, square = rows_ref[:k], rows_ref[k : 2 * k]
        high = mean.astype(BF).astype(F32)
        rows_ref[:k] = high
        rows_ref[k : 2 * k] = mean - high
        rows_ref[2 * k :] = square
    fill(pay_ref, rows_ref)


def merge_stats(got_ref, mates_ref, st_ref, q, size):
    n = got_ref.shape[0]
    k = MICRO * q
    mates = n // NVIEW
    step = 8

    def parts(at):
        got = got_ref[at].astype(F32)
        if got_ref.dtype == BF:
            return got[:, :k] + got[:, k : 2 * k], got[:, 2 * k : 3 * k]
        return got[:, :k], got[:, k : 2 * k]

    def one(i, acc):
        at = pl.ds(i * step, step)
        return acc + jnp.sum(mates_ref[at] * parts(at)[0], axis=0)

    mean = lax.fori_loop(0, n // step, one, jnp.zeros((k, LANES), F32), unroll=4) * (1.0 / mates)

    def two(i, acc):
        at = pl.ds(i * step, step)
        means, squares = parts(at)
        away = means - mean[None]
        return acc + jnp.sum(mates_ref[at] * (squares + size * (away * away)), axis=0)

    total = lax.fori_loop(0, n // step, two, jnp.zeros((k, LANES), F32), unroll=4)
    st_ref[:k] = mean
    st_ref[k : 2 * k] = lax.rsqrt(total * (1.0 / (mates * size)) + EPSILON)


def merge_sums(got_ref, mates_ref, sum_ref, q, size, total_refs):
    n = got_ref.shape[0]
    k = MICRO * q
    scale = 1.0 / (n // NVIEW * size)
    step = 8

    def one(i, carry):
        at = pl.ds(i * step, step)
        both = got_ref[at].astype(F32)
        first, second = both[:, :k], both[:, k : 2 * k]
        w = mates_ref[at]
        return (
            carry[0] + jnp.sum(w * first, axis=0),
            carry[1] + jnp.sum(w * second, axis=0),
            carry[2] + jnp.sum(first, axis=0),
            carry[3] + jnp.sum(second, axis=0),
        )

    zero = jnp.zeros((k, LANES), F32)
    a, b, ta, tb = lax.fori_loop(0, n // step, one, (zero,) * 4, unroll=4)
    sum_ref[:k] = a * scale
    sum_ref[k : 2 * k] = b * scale
    for ref, t in zip(total_refs, (ta, tb)):
        ref[...] = t[:q] + t[q : 2 * q] + t[2 * q :]


def shift_y(v, offset):
    if offset == 0:
        return v
    zero = jnp.zeros((8, v.shape[1]), v.dtype)
    if offset > 0:
        return jnp.concatenate([v[8:], zero], axis=0)
    return jnp.concatenate([zero, v[:-8]], axis=0)


def shift_x(v, offset):
    if offset == 0:
        return v
    place = lax.broadcasted_iota(jnp.int32, v.shape, 0) % 8
    if offset > 0:
        return jnp.where(place == 7, 0.0, pltpu.roll(v, v.shape[0] - 1, axis=0))
    return jnp.where(place == 0, 0.0, pltpu.roll(v, 1, axis=0))


def write_patches(phase, patch_ref, m, half, c, width, sign, out_phases=((0, 0), (0, 1), (1, 0), (1, 1))):
    moved = {}

    def get(sy, sx, ox):
        if (sy, sx, ox) not in moved:
            moved[sy, sx, ox] = shift_x(phase[sy, sx], ox)
        return moved[sy, sx, ox]

    for i, (py, px) in enumerate(out_phases):
        for r in range(3):
            for k in range(3):
                at_y, at_x = py + sign * (r - 1), px + sign * (k - 1)
                piece = shift_y(get(at_y % 2, at_x % 2, at_x // 2), at_y // 2)
                rows = pl.ds((m * len(out_phases) + i) * half, half)
                patch_ref[rows, pl.ds((r * 3 + k) * width + c * LANES, LANES)] = piece.astype(BF)


PHASES = ((0, 0), (0, 1), (1, 0), (1, 1))


class Sizes:
    pass


def k_reduce(x, ids, w, z):
    q = z.q1

    def body(k):
        (x_ref,), (map_ref, pay_ref), (tmp, rows_ref) = k.i, k.o, k.x
        k.wait_w()
        for y in range(z.height):
            product = dot(x_ref[y].reshape(MICRO * z.cols, z.c_in), k.w[0][...])
            for c in range(q):
                tmp[c, pl.ds(y * MICRO * z.cols, MICRO * z.cols), :] = product[:, c * LANES : (c + 1) * LANES]
        for m in range(MICRO):
            for y in range(z.height):
                for px in range(2):
                    at = m * z.rows + (2 * (y % 2) + px) * z.half + (y // 2) * 8
                    for c in range(q):
                        map_ref[pl.ds(at, 8), cols(c)] = tmp[
                            c, pl.ds((y * MICRO + m) * z.cols + px, 8, stride=2), :
                        ]
        rows_ref[...] = jnp.zeros(rows_ref.shape, F32)
        for m in range(MICRO):
            for c in range(q):
                stats_rows(map_ref[pl.ds(m * z.rows, z.rows), cols(c)], rows_ref, m * q + c, z.rows, MICRO * q)
        for m in range(MICRO):
            rows_ref[pl.ds(6 * q + m, 1), :] = jnp.full((1, LANES), k.s[0][m], F32)
        fill(pay_ref, rows_ref)

    rows, pad = MICRO * z.rows, 16
    return kernel_call(
        body,
        [arr(rows, z.c_mid), arr(z.n, pad, LANES)],
        [x],
        [w],
        [pltpu.VMEM((q, rows, LANES), F32), pltpu.VMEM((pad, LANES), F32)],
        flops=2 * rows * z.c_in * z.c_mid,
        scalars=[ids],
    )


def k_spatial(got, ids, pre, gain, offset, w, z):
    q = z.q1

    def body(k):
        got_ref, pre_ref, g_ref, o_ref = k.i
        patch_ref, next_ref, pay_ref, st_ref, mates_ref = k.o
        (rows_ref,) = k.x
        same = []
        for m in range(MICRO):
            view = got_ref[:, pl.ds(6 * q + m, 1), :]
            same += [(view == k.s[0][m]).astype(F32)] * q
        mates_ref[...] = jnp.concatenate(same, axis=1)
        merge_stats(got_ref, mates_ref, st_ref, q, z.rows)
        for m in range(MICRO):
            for c in range(q):
                mean, inverse = row(st_ref, m * q + c), row(st_ref, (MICRO + m) * q + c)
                phase = {}
                for i, p in enumerate(PHASES):
                    x = pre_ref[pl.ds(m * z.rows + i * z.half, z.half), cols(c)]
                    phase[p] = gelu(g_ref[:, cols(c)] * ((x - mean) * inverse) + o_ref[:, cols(c)])
                write_patches(phase, patch_ref, m, z.half, c, z.c_mid, 1)
        k.send(0)
        k.wait_w()
        next_ref[...] = dot(patch_ref[...], k.w[0][...])
        k.send(1)
        for m in range(MICRO):
            for c in range(q):
                stats_rows(next_ref[pl.ds(m * z.rows, z.rows), cols(c)], rows_ref, m * q + c, z.rows, MICRO * q)
        fill_stats(pay_ref, rows_ref, q)

    rows = MICRO * z.rows
    return kernel_call(
        body,
        [arr(rows, 9 * z.c_mid, dtype=BF), arr(rows, z.c_mid), stats_arr(z.n, q), arr(6 * q, LANES), arr(z.n, 3 * q, LANES)],
        [got, pre, gain, offset],
        [w],
        [pltpu.VMEM((stats_shape(q)[0], LANES), F32)],
        flops=2 * rows * 9 * z.c_mid * z.c_mid,
        scalars=[ids],
    )


def k_expand(got, mates, pre, gain, offset, w, z):
    q, qo = z.q1, z.q3

    def body(k):
        got_ref, mates_ref, pre_ref, g_ref, o_ref = k.i
        act_ref, next_ref, pay_ref, st_ref = k.o
        (rows_ref,) = k.x
        merge_stats(got_ref, mates_ref, st_ref, q, z.rows)
        for m in range(MICRO):
            for c in range(q):
                mean, inverse = row(st_ref, m * q + c), row(st_ref, (MICRO + m) * q + c)
                at = pl.ds(m * z.rows, z.rows)
                x = pre_ref[at, cols(c)]
                act_ref[at, cols(c)] = gelu(g_ref[:, cols(c)] * ((x - mean) * inverse) + o_ref[:, cols(c)]).astype(BF)
        k.send(0)
        k.wait_w()
        next_ref[...] = dot(act_ref[...], k.w[0][...])
        k.send(1)
        for m in range(MICRO):
            for c in range(qo):
                stats_rows(next_ref[pl.ds(m * z.rows, z.rows), cols(c)], rows_ref, m * qo + c, z.rows, MICRO * qo)
        fill_stats(pay_ref, rows_ref, qo)

    rows = MICRO * z.rows
    return kernel_call(
        body,
        [arr(rows, z.c_mid, dtype=BF), arr(rows, z.c_in), stats_arr(z.n, qo), arr(6 * q, LANES)],
        [got, mates, pre, gain, offset],
        [w],
        [pltpu.VMEM((stats_shape(qo)[0], LANES), F32)],
        flops=2 * rows * z.c_in * z.c_mid,
    )


def k_narrow(got, mates, pre, gain, offset, maps_in, w, z):
    q, qo = z.q3, z.q4

    def body(k):
        got_ref, mates_ref, pre_ref, g_ref, o_ref, in_ref = k.i
        res_ref, join_ref, even_ref, next_ref, pay_ref, st_ref = k.o
        (rows_ref,) = k.x
        merge_stats(got_ref, mates_ref, st_ref, q, z.rows)
        for m in range(MICRO):
            for c in range(q):
                mean, inverse = row(st_ref, m * q + c), row(st_ref, (MICRO + m) * q + c)
                at = pl.ds(m * z.rows, z.rows)
                x = pre_ref[at, cols(c)]
                res = g_ref[:, cols(c)] * ((x - mean) * inverse) + o_ref[:, cols(c)] + in_ref[at, cols(c)].astype(F32)
                res_ref[at, cols(c)] = res
                joined = gelu(res).astype(BF)
                join_ref[at, cols(c)] = joined
                even_ref[pl.ds(m * z.half, z.half), cols(c)] = joined[: z.half]
        for j in range(3):
            k.send(j)
        k.wait_w()
        next_ref[...] = dot(join_ref[...], k.w[0][...])
        k.send(3)
        for m in range(MICRO):
            for c in range(qo):
                stats_rows(next_ref[pl.ds(m * z.rows, z.rows), cols(c)], rows_ref, m * qo + c, z.rows, MICRO * qo)
        fill_stats(pay_ref, rows_ref, qo)

    rows = MICRO * z.rows
    return kernel_call(
        body,
        [
            arr(rows, z.c_in),
            arr(rows, z.c_in, dtype=BF),
            arr(MICRO * z.half, z.c_in, dtype=BF),
            arr(rows, z.c_wide),
            stats_arr(z.n, qo),
            arr(6 * q, LANES),
        ],
        [got, mates, pre, gain, offset, maps_in],
        [w],
        [pltpu.VMEM((stats_shape(qo)[0], LANES), F32)],
        flops=2 * rows * z.c_in * z.c_wide,
    )


def k_stride(got, mates, pre, gain, offset, w, z, passes=()):
    q = z.q4

    def body(k):
        got_ref, mates_ref, pre_ref, g_ref, o_ref = k.i
        act_ref, next_ref, pay_ref, st_ref = k.o
        patch_ref, rows_ref = k.x
        merge_stats(got_ref, mates_ref, st_ref, q, z.rows)
        for m in range(MICRO):
            for c in range(q):
                mean, inverse = row(st_ref, m * q + c), row(st_ref, (MICRO + m) * q + c)
                phase = {}
                for i, p in enumerate(PHASES):
                    x = pre_ref[pl.ds(m * z.rows + i * z.half, z.half), cols(c)]
                    phase[p] = gelu(g_ref[:, cols(c)] * ((x - mean) * inverse) + o_ref[:, cols(c)])
                    act_ref[pl.ds(m * z.rows + i * z.half, z.half), cols(c)] = phase[p].astype(BF)
                write_patches(phase, patch_ref, m, z.half, c, z.c_wide, 1, ((0, 0),))
        k.send(0)
        k.wait_w()
        next_ref[...] = dot(patch_ref[...], k.w[0][...])
        k.send(1)
        for m in range(MICRO):
            for c in range(q):
                stats_rows(next_ref[pl.ds(m * z.half, z.half), cols(c)], rows_ref, m * q + c, z.half, MICRO * q)
        fill_stats(pay_ref, rows_ref, q)

    rows = MICRO * z.half
    return kernel_call(
        body,
        [arr(MICRO * z.rows, z.c_wide, dtype=BF), arr(rows, z.c_wide), stats_arr(z.n, q), arr(6 * q, LANES)],
        [got, mates, pre, gain, offset],
        [w],
        [pltpu.VMEM((rows, 9 * z.c_wide), BF), pltpu.VMEM((stats_shape(q)[0], LANES), F32)],
        flops=2 * rows * 9 * z.c_wide * z.c_wide,
        passes=passes,
    )


def k_shortcut(even, w, z):
    def body(k):
        (e_ref,), (next_ref, st_ref) = k.i, k.o
        k.wait_w()
        next_ref[...] = dot(e_ref[...], k.w[0][...])
        for c in range(z.q6):
            for m in range(MICRO):
                stats_rows(next_ref[pl.ds(m * z.half, z.half), cols(c)], st_ref.at[c], m, z.half, MICRO)

    rows = MICRO * z.half
    return kernel_call(
        body, [arr(rows, z.c_out), arr(z.q6, 8, LANES)], [even], [w], flops=2 * rows * z.c_in * z.c_out
    )


def k_widen(got, mates, pre, gain, offset, short_st, w, z, passes=()):
    q = z.q4

    def body(k):
        got_ref, mates_ref, pre_ref, g_ref, o_ref, short_ref = k.i
        act_ref, next_ref, pay_ref, st_ref = k.o
        merge_stats(got_ref, mates_ref, st_ref, q, z.half)
        for m in range(MICRO):
            for c in range(q):
                mean, inverse = row(st_ref, m * q + c), row(st_ref, (MICRO + m) * q + c)
                at = pl.ds(m * z.half, z.half)
                x = pre_ref[at, cols(c)]
                act_ref[at, cols(c)] = gelu(g_ref[:, cols(c)] * ((x - mean) * inverse) + o_ref[:, cols(c)]).astype(BF)
        k.send(0)
        k.wait_w()
        next_ref[...] = dot(act_ref[...], k.w[0][...])
        k.send(1)
        for c in range(z.q6):
            for m in range(MICRO):
                stats_rows(next_ref[pl.ds(m * z.half, z.half), cols(c)], pay_ref.at[c], m, z.half, MICRO)
            pay_ref[z.q6 + c] = short_ref[c]
        chunks = 2 * z.q6
        for j in range(chunks, z.n):
            pay_ref[j] = pay_ref[j % chunks]

    rows = MICRO * z.half
    return kernel_call(
        body,
        [arr(rows, z.c_wide, dtype=BF), arr(rows, z.c_out), arr(z.n, 8, LANES), arr(6 * q, LANES)],
        [got, mates, pre, gain, offset, short_st],
        [w],
        flops=2 * rows * z.c_wide * z.c_out,
        passes=passes,
    )


def k_views(got, ids, z):
    def body(k):
        (got_ref, id_ref), (pay_ref,), (lo, hi) = k.i, k.o, k.x
        mates = z.n // NVIEW
        g, ids = got_ref[...], id_ref[...]
        for view, ref in ((0, lo), (1, hi)):
            w = (ids == float(view)).astype(F32)
            mean = jnp.sum(w * g, axis=0)[:MICRO] * (1.0 / mates)
            away = g[:, :MICRO] - mean[None]
            total = jnp.sum(w[:, :MICRO] * (g[:, MICRO : 2 * MICRO] + z.half * (away * away)), axis=0)
            ref[...] = jnp.zeros(ref.shape, F32)
            ref[:MICRO] = mean
            ref[MICRO : 2 * MICRO] = lax.rsqrt(total * (1.0 / (mates * z.half)) + EPSILON)
        pay_ref[...] = jnp.where(ids > 0.5, hi[...][None], lo[...][None])

    return kernel_call(
        body, [arr(z.n, 8, LANES)], [got, ids], scratch=[pltpu.VMEM((8, LANES), F32)] * 2
    )[0]


def k_mapped(whole, pre_w, pre_s, cot, gains, z, passes=()):
    def body(k):
        st_ref, w_ref, s_ref, cot_ref, gw, ow, gs, os = k.i
        map_ref, d_ref, pay_ref = k.o
        n_c = z.q6
        pay_ref[...] = jnp.zeros(pay_ref.shape, F32)
        for c in range(n_c):
            for m in range(MICRO):
                at = pl.ds(m * z.half, z.half)
                sw, ss = st_ref.at[c], st_ref.at[n_c + c]
                hat_w = (w_ref[at, cols(c)] - row(sw, m)) * row(sw, MICRO + m)
                hat_s = (s_ref[at, cols(c)] - row(ss, m)) * row(ss, MICRO + m)
                res = gw[:, cols(c)] * hat_w + ow[:, cols(c)] + (gs[:, cols(c)] * hat_s + os[:, cols(c)])
                map_ref[at, cols(c)] = gelu(res).astype(BF)
                d = gelu_slope(res) * cot_ref[at, cols(c)].astype(F32)
                d_ref[at, cols(c)] = d
                first, second = pay_ref.at[c], pay_ref.at[n_c + c]
                first[pl.ds(m, 1), :] = jnp.sum(d, axis=0, keepdims=True)
                first[pl.ds(MICRO + m, 1), :] = jnp.sum(d * hat_w, axis=0, keepdims=True)
                second[pl.ds(m, 1), :] = jnp.sum(d * hat_s, axis=0, keepdims=True)
        for j in range(2 * n_c, z.n):
            pay_ref[j] = pay_ref[j % (2 * n_c)]

    rows = MICRO * z.half
    return kernel_call(
        body,
        [arr(rows, z.c_out, dtype=BF), arr(rows, z.c_out), arr(z.n, 8, LANES)],
        [whole, pre_w, pre_s, cot, *gains],
        flops=rows * z.c_out * 60,
        passes=passes,
    )


def k_view_sums(got, ids, z):
    def body(k):
        (got_ref, id_ref), (pay_ref,), (both,) = k.i, k.o, k.x
        g, ids = got_ref[...], id_ref[...]
        lo = jnp.sum((ids == 0.0).astype(F32) * g, axis=0)
        hi = jnp.sum((ids == 1.0).astype(F32) * g, axis=0)
        both[0], both[1] = lo, hi
        all_views = lo + hi
        totals = []
        for k in range(2):
            totals.append(jnp.sum(all_views[k * MICRO : (k + 1) * MICRO], axis=0, keepdims=True))
        for v in range(2):
            for k in range(2):
                both[v, pl.ds(2 * MICRO + k, 1), :] = totals[k]
        pay_ref[...] = jnp.where(ids > 0.5, both[1][None], both[0][None])

    return kernel_call(body, [arr(z.n, 8, LANES)], [got, ids], scratch=[pltpu.VMEM((2, 8, LANES), F32)])[0]


def back_rows(x, d, st_ref, sum_ref, m, q, c, gain):
    inverse = row(st_ref, (MICRO + m) * q + c)
    hat = (x - row(st_ref, m * q + c)) * inverse
    return gain * inverse * (d - row(sum_ref, m * q + c) - hat * row(sum_ref, (MICRO + m) * q + c))


def sum_rows(d, hat, rows_ref, r, offset):
    rows_ref[pl.ds(r, 1), :] = jnp.sum(d, axis=0, keepdims=True)
    rows_ref[pl.ds(r + offset, 1), :] = jnp.sum(d * hat, axis=0, keepdims=True)


def slope_and_sums(d_out, pre_ref, at, st_ref, m, q, c, g_ref, o_ref, d_ref, rows_ref):
    hat = (pre_ref[at, cols(c)] - row(st_ref, m * q + c)) * row(st_ref, (MICRO + m) * q + c)
    d = gelu_slope(g_ref[:, cols(c)] * hat + o_ref[:, cols(c)]) * d_out
    d_ref[at, cols(c)] = d
    sum_rows(d, hat, rows_ref, m * q + c, MICRO * q)


def k_back_widen(whole, sums, d_two, pre_w, pre_s, gain_w, gain_s, pre, st, gain, offset, place, w, z, passes=()):
    q, n_c = z.q4, z.q6

    def body(k):
        st2, sum_ref, d_ref, w_ref, s_ref, gw, gs, pre_ref, st_ref, g_ref, o_ref = k.i
        ds_ref, t_off, t_gw, t_gs, d_next, pay_ref = k.o
        dw_ref, rows_ref, tmp = k.x
        scale = 1.0 / (z.n // NVIEW * z.half)
        for c in range(n_c):
            first, second = sum_ref.at[c], sum_ref.at[n_c + c]
            t_off[pl.ds(c, 1), :] = row(first, 2 * MICRO)
            t_gw[pl.ds(c, 1), :] = row(first, 2 * MICRO + 1)
            t_gs[pl.ds(c, 1), :] = row(second, 2 * MICRO)
            sw, ss = st2.at[c], st2.at[n_c + c]
            for m in range(MICRO):
                at = pl.ds(m * z.half, z.half)
                inv_w, inv_s = row(sw, MICRO + m), row(ss, MICRO + m)
                hat_w = (w_ref[at, cols(c)] - row(sw, m)) * inv_w
                hat_s = (s_ref[at, cols(c)] - row(ss, m)) * inv_s
                d = d_ref[at, cols(c)] - row(first, m) * scale
                dw_ref[at, cols(c)] = (
                    gw[:, cols(c)] * inv_w * (d - hat_w * (row(first, MICRO + m) * scale))
                ).astype(BF)
                ds_ref[at, cols(c)] = (gs[:, cols(c)] * inv_s * (d - hat_s * (row(second, m) * scale))).astype(BF)
        k.send(0)
        some = z.c_out // z.g
        for j in range(z.g):
            at = pl.ds(pl.multiple_of(((k.s[0][0] & (z.g - 1)) ^ j) * some, some), some)
            k.copy(dw_ref.at[:, at], k.raw[j].at[:, pl.ds(0, some)])
            k.copy(ds_ref.at[:, at], k.raw[j].at[:, pl.ds(some, some)])
        k.wait_w()
        tmp[...] = dot_nt(dw_ref[...], k.w[0][...])
        for m in range(MICRO):
            at = pl.ds(m * z.half, z.half)
            for c in range(q):
                slope_and_sums(tmp[at, cols(c)], pre_ref, at, st_ref, m, q, c, g_ref, o_ref, d_next, rows_ref)
        fill(pay_ref, rows_ref)

    rows = MICRO * z.half
    return kernel_call(
        body,
        [arr(rows, z.c_out, dtype=BF)]
        + [arr(n_c, LANES)] * 3
        + [arr(rows, z.c_wide), arr(z.n, 6 * q, LANES, dtype=BF)],
        [whole, sums, d_two, pre_w, pre_s, gain_w, gain_s, pre, st, gain, offset],
        [w],
        [
            pltpu.VMEM((rows, z.c_out), BF),
            pltpu.VMEM((6 * q, LANES), F32),
            pltpu.VMEM((rows, z.c_wide), F32),
        ],
        flops=2 * rows * z.c_wide * z.c_out,
        raw=[arr(rows, 2 * z.c_out // z.g, dtype=BF)] * z.g,
        n_raw=2 * z.g,
        scalars=[place],
        passes=passes,
    )


def back_start(refs, mates_ref, sum_ref, out_ref, q, n_rows, totals):
    got_ref, d_ref, pre_ref, st_ref, g_ref = refs
    merge_sums(got_ref, mates_ref, sum_ref, q, n_rows, totals)
    for m in range(MICRO):
        at = pl.ds(m * n_rows, n_rows)
        for c in range(q):
            out_ref[at, cols(c)] = back_rows(
                pre_ref[at, cols(c)], d_ref[at, cols(c)], st_ref, sum_ref, m, q, c, g_ref[:, cols(c)]
            ).astype(BF)


def k_back_stride(got, mates, d, pre_s, st_s, gain_s, pre, st, gain, offset, place, w, z, passes=()):
    q = z.q4

    def body(k):
        got_ref, mates_ref, d_ref, ps_ref, ss_ref, gs_ref, pre_ref, st_ref, g_ref, o_ref = k.i
        t_off, t_gain, d_next, pay_ref = k.o
        delta_ref, rows_ref, sum_ref, contrib = k.x
        back_start((got_ref, d_ref, ps_ref, ss_ref, gs_ref), mates_ref, sum_ref, delta_ref, q, z.half, (t_off, t_gain))
        some = z.c_wide // z.g
        for j in range(z.g):
            at = pl.ds(pl.multiple_of(((k.s[0][0] & (z.g - 1)) ^ j) * some, some), some)
            k.copy(delta_ref.at[:, at], k.raw[j])
        k.wait_w()
        contrib[...] = dot_nt(delta_ref[...], k.w[0][...])
        for m in range(MICRO):
            for c in range(q):
                phase = {}
                for r in range(3):
                    for k in range(3):
                        piece = contrib[pl.ds(m * z.half, z.half), pl.ds((r * 3 + k) * z.c_wide + c * LANES, LANES)]
                        piece = shift_x(shift_y(piece, 1 if r == 0 else 0), 1 if k == 0 else 0)
                        p = ((r + 1) % 2, (k + 1) % 2)
                        phase[p] = piece if p not in phase else phase[p] + piece
                first = second = 0.0
                mean, inverse = row(st_ref, m * q + c), row(st_ref, (MICRO + m) * q + c)
                for i, p in enumerate(PHASES):
                    at = pl.ds(m * z.rows + i * z.half, z.half)
                    hat = (pre_ref[at, cols(c)] - mean) * inverse
                    grad = gelu_slope(g_ref[:, cols(c)] * hat + o_ref[:, cols(c)]) * phase[p]
                    d_next[at, cols(c)] = grad
                    first = first + jnp.sum(grad, axis=0, keepdims=True)
                    second = second + jnp.sum(grad * hat, axis=0, keepdims=True)
                rows_ref[pl.ds(m * q + c, 1), :] = first
                rows_ref[pl.ds((MICRO + m) * q + c, 1), :] = second
        fill(pay_ref, rows_ref)

    rows = MICRO * z.half
    return kernel_call(
        body,
        [arr(q, LANES)] * 2
        + [arr(MICRO * z.rows, z.c_wide), arr(z.n, 6 * q, LANES, dtype=BF)],
        [got, mates, d, pre_s, st_s, gain_s, pre, st, gain, offset],
        [w],
        [
            pltpu.VMEM((rows, z.c_wide), BF),
            pltpu.VMEM((6 * q, LANES), F32),
            pltpu.VMEM((6 * q, LANES), F32),
            pltpu.VMEM((rows, 9 * z.c_wide), F32),
        ],
        flops=2 * rows * 9 * z.c_wide * z.c_wide,
        passes=passes,
        raw=[arr(rows, z.c_wide // z.g, dtype=BF)] * z.g,
        n_raw=z.g,
        scalars=[place],
    )


def k_back_narrow(got, mates, d, pre_n, st_n, gain_n, even, res, pre, st, w, z, passes=()):
    q, qo = z.q4, z.q3

    def body(k):
        got_ref, mates_ref, d_ref, pn_ref, sn_ref, gn_ref, even_ref, res_ref, pre_ref, st_ref = k.i
        delta_ref, t_off, t_gain, d_next, pay_ref = k.o
        rows_ref, sum_ref, tmp = k.x
        back_start((got_ref, d_ref, pn_ref, sn_ref, gn_ref), mates_ref, sum_ref, delta_ref, q, z.rows, (t_off, t_gain))
        k.send(0)
        k.wait_w()
        tmp[...] = dot_nt(delta_ref[...], k.w[0][...])
        for m in range(MICRO):
            at = pl.ds(m * z.rows, z.rows)
            some = pl.ds(m * z.rows, z.half)
            for c in range(qo):
                tmp[some, cols(c)] = tmp[some, cols(c)] + even_ref[pl.ds(m * z.half, z.half), cols(c)]
                d_join = tmp[at, cols(c)].astype(BF).astype(F32)
                one = gelu_slope(res_ref[at, cols(c)]) * d_join
                hat = (pre_ref[at, cols(c)] - row(st_ref, m * qo + c)) * row(st_ref, (MICRO + m) * qo + c)
                d_next[at, cols(c)] = one
                sum_rows(one, hat, rows_ref, m * qo + c, MICRO * qo)
        fill(pay_ref, rows_ref)

    rows = MICRO * z.rows
    return kernel_call(
        body,
        [arr(rows, z.c_wide, dtype=BF)] + [arr(q, LANES)] * 2 + [arr(rows, z.c_in), arr(z.n, 6 * qo, LANES, dtype=BF)],
        [got, mates, d, pre_n, st_n, gain_n, even, res, pre, st],
        [w],
        [
            pltpu.VMEM((6 * qo, LANES), F32),
            pltpu.VMEM((6 * q, LANES), F32),
            pltpu.VMEM((rows, z.c_in), F32),
        ],
        flops=2 * rows * z.c_in * z.c_wide,
        passes=passes,
    )


def k_back_expand(got, mates, d, pre_e, st_e, gain_e, pre, st, gain, offset, w, z, passes=()):
    q, qo = z.q3, z.q1

    def body(k):
        got_ref, mates_ref, d_ref, pe_ref, se_ref, ge_ref, pre_ref, st_ref, g_ref, o_ref = k.i
        delta_ref, t_off, t_gain, d_next, pay_ref = k.o
        rows_ref, sum_ref, tmp = k.x
        back_start((got_ref, d_ref, pe_ref, se_ref, ge_ref), mates_ref, sum_ref, delta_ref, q, z.rows, (t_off, t_gain))
        k.send(0)
        k.wait_w()
        tmp[...] = dot_nt(delta_ref[...], k.w[0][...])
        for m in range(MICRO):
            at = pl.ds(m * z.rows, z.rows)
            for c in range(qo):
                slope_and_sums(tmp[at, cols(c)], pre_ref, at, st_ref, m, qo, c, g_ref, o_ref, d_next, rows_ref)
        fill(pay_ref, rows_ref)

    rows = MICRO * z.rows
    return kernel_call(
        body,
        [arr(rows, z.c_in, dtype=BF)] + [arr(q, LANES)] * 2 + [arr(rows, z.c_mid), arr(z.n, 6 * qo, LANES, dtype=BF)],
        [got, mates, d, pre_e, st_e, gain_e, pre, st, gain, offset],
        [w],
        [
            pltpu.VMEM((6 * qo, LANES), F32),
            pltpu.VMEM((6 * q, LANES), F32),
            pltpu.VMEM((rows, z.c_mid), F32),
        ],
        flops=2 * rows * z.c_in * z.c_mid,
        passes=passes,
    )


def k_back_spatial(got, mates, d, pre_s, st_s, gain_s, pre, st, gain, offset, w, z, passes=()):
    q = z.q1

    def body(k):
        got_ref, mates_ref, d_ref, ps_ref, ss_ref, gs_ref, pre_ref, st_ref, g_ref, o_ref = k.i
        delta_ref, t_off, t_gain, d_next, pay_ref = k.o
        rows_ref, sum_ref, patch_ref, tmp = k.x
        merge_sums(got_ref, mates_ref, sum_ref, q, z.rows, (t_off, t_gain))
        for m in range(MICRO):
            for c in range(q):
                phase = {}
                for i, p in enumerate(PHASES):
                    at = pl.ds(m * z.rows + i * z.half, z.half)
                    phase[p] = back_rows(
                        ps_ref[at, cols(c)], d_ref[at, cols(c)], ss_ref, sum_ref, m, q, c, gs_ref[:, cols(c)]
                    )
                    delta_ref[at, cols(c)] = phase[p].astype(BF)
                write_patches(phase, patch_ref, m, z.half, c, z.c_mid, -1)
        k.send(0)
        k.wait_w()
        tmp[...] = dot(patch_ref[...], k.w[0][...])
        for m in range(MICRO):
            at = pl.ds(m * z.rows, z.rows)
            for c in range(q):
                slope_and_sums(tmp[at, cols(c)], pre_ref, at, st_ref, m, q, c, g_ref, o_ref, d_next, rows_ref)
        fill(pay_ref, rows_ref)

    rows = MICRO * z.rows
    return kernel_call(
        body,
        [arr(rows, z.c_mid, dtype=BF)] + [arr(q, LANES)] * 2 + [arr(rows, z.c_mid), arr(z.n, 6 * q, LANES, dtype=BF)],
        [got, mates, d, pre_s, st_s, gain_s, pre, st, gain, offset],
        [w],
        [
            pltpu.VMEM((6 * q, LANES), F32),
            pltpu.VMEM((6 * q, LANES), F32),
            pltpu.VMEM((rows, 9 * z.c_mid), BF),
            pltpu.VMEM((rows, z.c_mid), F32),
        ],
        flops=2 * rows * 9 * z.c_mid * z.c_mid,
        passes=passes,
    )


def k_back_reduce(got, mates, d, pre_r, st_r, gain_r, z, passes=()):
    q = z.q1

    def body(k):
        got_ref, mates_ref, d_ref, pr_ref, sr_ref, gr_ref = k.i
        delta_ref, t_off, t_gain = k.o
        (sum_ref,) = k.x
        back_start((got_ref, d_ref, pr_ref, sr_ref, gr_ref), mates_ref, sum_ref, delta_ref, q, z.rows, (t_off, t_gain))

    rows = MICRO * z.rows
    return kernel_call(
        body,
        [arr(rows, z.c_mid, dtype=BF)] + [arr(q, LANES)] * 2,
        [got, mates, d, pre_r, st_r, gain_r],
        scratch=[pltpu.VMEM((6 * q, LANES), F32)],
        passes=passes,
    )


def k_input(delta, d_one, w, z, passes=()):
    def body(k):
        (delta_ref, one_ref), (out_ref,), (tmp, line) = k.i, k.o, k.x
        k.wait_w()
        tmp[...] = dot_nt(delta_ref[...], k.w[0][...])
        for m in range(MICRO):
            for y in range(z.height):
                for c in range(z.q3):
                    for px in range(2):
                        at = pl.ds(m * z.rows + (2 * (y % 2) + px) * z.half + (y // 2) * 8, 8)
                        line[c, pl.ds((y * MICRO + m) * z.cols + px, 8, stride=2), :] = (
                            one_ref[at, cols(c)] + tmp[at, cols(c)]
                        )
                    out_ref[y, m, :, cols(c)] = line[c, pl.ds((y * MICRO + m) * z.cols, z.cols), :].astype(BF)

    rows = MICRO * z.rows
    return kernel_call(
        body,
        [arr(z.height, MICRO, z.cols, z.c_in, dtype=BF)],
        [delta, d_one],
        [w],
        [pltpu.VMEM((rows, z.c_in), F32), pltpu.VMEM((z.q3, rows, LANES), F32)],
        flops=2 * rows * z.c_in * z.c_mid,
        passes=passes,
    )


def k_even(delta, w, z):
    def body(k):
        k.wait_w()
        k.o[0][...] = dot_nt(k.i[0][...], k.w[0][...])

    rows = delta.shape[0]
    return kernel_call(body, [arr(rows, z.c_in)], [delta], [w], flops=2 * rows * z.c_in * z.c_out)[0]


def k_first_grads(outs, evens, pieces, z):
    some = z.c_out // z.g
    a, b = z.c_wide // z.ns, z.c_in // z.ns

    def body(k):
        lhs_w, lhs_s, rhs = k.st
        held_w, held_s = k.x
        held_w[...] = dot_tn(lhs_w[...], rhs[:, :some]).astype(BF)
        for s in range(z.ns):
            k.copy(held_w.at[pl.ds(s * a, a)], k.raw[0].at[s % z.slo, s // z.slo, pl.ds(0, a)])
        held_s[...] = dot_tn(lhs_s[...], rhs[:, some:]).astype(BF)
        for s in range(z.ns):
            k.copy(held_s.at[pl.ds(s * b, b)], k.raw[0].at[s % z.slo, s // z.slo, pl.ds(a, b)])

    return kernel_call(
        body,
        [],
        [],
        scratch=[pltpu.VMEM((z.c_wide, some), BF), pltpu.VMEM((z.c_in, some), BF)],
        stacks=[outs, evens, pieces],
        raw=[arr(z.slo, z.ns // z.slo, a + b, some, dtype=BF)],
        n_raw=2 * z.ns,
        flops=2 * z.g * outs[0].shape[0] * (z.c_in + z.c_wide) * some,
    )[0]


def k_stride_grads(maps, pieces, z):
    few = z.c_wide // z.g
    c = 9 * z.c_wide // z.ns
    rows = z.g * pieces[0].shape[0]

    def body(k):
        map_ref, rhs = k.st
        held, lhs = k.x
        for m in range(z.g * MICRO):
            for col in range(z.q4):
                phase = {}
                for i, p in enumerate(PHASES):
                    phase[p] = map_ref[pl.ds(m * z.rows + i * z.half, z.half), cols(col)].astype(F32)
                write_patches(phase, lhs, m, z.half, col, z.c_wide, 1, ((0, 0),))
        for t in range(9):
            at = pl.ds(t * z.c_wide, z.c_wide)
            held[at] = dot_tn(lhs[:, at], rhs[...]).astype(BF)
        for s in range(z.ns):
            k.copy(held.at[pl.ds(s * c, c)], k.raw[0].at[s % z.slo, s // z.slo])

    return kernel_call(
        body,
        [],
        [],
        scratch=[pltpu.VMEM((9 * z.c_wide, few), BF), pltpu.VMEM((rows, 9 * z.c_wide), BF)],
        stacks=[maps, pieces],
        raw=[arr(z.slo, z.ns // z.slo, c, few, dtype=BF)],
        n_raw=z.ns,
        flops=2 * rows * 9 * z.c_wide * few,
    )[0]


def k_products(pairs, place, z):
    hi = z.ns // z.slo
    widths = [(o.shape[1], g.shape[1]) for o, g in pairs]
    rows = [r // z.n * c // 256 for r, c in widths]
    total = sum(rows)

    def body(k):
        (held,) = k.x
        at = 0
        for j, (r, c) in enumerate(widths):
            product = dot_tn(k.i[2 * j][...], k.i[2 * j + 1][...])
            blocks = product.reshape(hi, z.slo, z.nb // 2, 2, r // z.n, c).astype(BF)
            for part in range(c // 256):
                held[:, :, :, :, pl.ds(at, r // z.n), :] = blocks[..., part * 256 : (part + 1) * 256]
                at += r // z.n
        core = k.s[0][0] & 1
        k.copy(held.at[:, :, :, core], k.raw[0])
        k.copy(held.at[:, :, :, 1 - core], k.raw[1])

    return kernel_call(
        body,
        [],
        [a for pair in pairs for a in pair],
        scratch=[pltpu.VMEM((hi, z.slo, z.nb // 2, 2, total, 256), BF)],
        raw=[arr(hi, z.slo, z.nb // 2, total, 256, dtype=BF)] * 2,
        n_raw=2,
        scalars=[place],
        flops=sum(2 * pairs[j][0].shape[0] * r * c for j, (r, c) in enumerate(widths)),
    )


def k_sum_plane(groups, where, z, passes=()):
    hi, high = z.ns // z.slo, z.nb // 2
    rows = [g[0].shape[3] for g in groups]

    def body(k):
        (held,) = k.x
        at = 0
        for j, r in enumerate(rows):
            both = k.i[2 * j][...].astype(F32) + k.i[2 * j + 1][...].astype(F32)
            held[:, :, :, pl.ds(at, r), :] = both.astype(BF)
            at += r
        for i in range(high):
            for j in range(z.slo):
                k.copy(held.at[:, k.s[0][0] ^ j, k.s[0][1] ^ i], k.raw[z.slo * i + j])

    total = sum(rows)
    return kernel_call(
        body,
        [],
        [a for g in groups for a in g],
        scratch=[pltpu.VMEM((hi, z.slo, high, total, 256), BF)],
        raw=[arr(hi, total, 256, dtype=BF)] * (z.slo * high),
        n_raw=z.slo * high,
        scalars=[where],
        passes=passes,
    )


def k_sum_line(groups, where, z, passes=()):
    hi = z.ns // z.slo
    rows = [g[0].shape[1] for g in groups]
    n = len(groups[0])

    def body(k):
        (held,) = k.x
        at = 0
        for j, r in enumerate(rows):
            value = k.i[j * n][...].astype(F32)
            for other in range(1, n):
                value = value + k.i[j * n + other][...].astype(F32)
            held[:, pl.ds(at, r), :] = value.astype(BF)
            at += r
        for j in range(hi):
            k.copy(held.at[k.s[0][2] ^ j], k.raw[j])

    total = sum(rows)
    return kernel_call(
        body,
        [],
        [a for g in groups for a in g],
        scratch=[pltpu.VMEM((hi, total, 256), BF)],
        raw=[arr(total, 256, dtype=BF)] * hi,
        n_raw=hi,
        scalars=[where],
        passes=passes,
    )


def k_sum_last(parts, passes=()):
    def body(k):
        value = k.i[0][...].astype(F32)
        for other in k.i[1:]:
            value = value + other[...].astype(F32)
        k.o[0][...] = value.astype(BF)

    return kernel_call(body, [arr(*parts[0].shape, dtype=BF)], parts, passes=passes)


def k_late_shares(pieces, place, shapes, z):
    n = z.nb
    total = pieces[0].shape[0]

    def body(k):
        (held,) = k.x
        for j in range(n):
            held[k.s[0][0] ^ j] = k.i[j][...]
        for j in range(n):
            value = held[j].astype(F32)
            at = 0
            for g, (r, c) in enumerate(shapes):
                r = r // z.n
                for part in range(c // 256):
                    k.o[g][pl.ds(j * r, r), pl.ds(part * 256, 256)] = value[at : at + r]
                    at += r

    return kernel_call(
        body,
        [arr(r // z.ns, c) for r, c in shapes],
        list(pieces),
        scratch=[pltpu.VMEM((n, total, 256), BF)],
        scalars=[place],
    )


def k_early_shares(first, second, place, z):
    n = z.g
    some, few = z.c_out // n, z.c_wide // n
    a, b, c = z.c_wide // z.ns, z.c_in // z.ns, 9 * z.c_wide // z.ns

    def body(k):
        one, two = k.x
        for j in range(n):
            one[(k.s[0][0] & (n - 1)) ^ j] = k.i[j][...]
            two[(k.s[0][0] & (n - 1)) ^ j] = k.i[n + j][...]
        for j in range(n):
            value = one[j].astype(F32)
            k.o[0][:, pl.ds(j * some, some)] = value[:a]
            k.o[1][:, pl.ds(j * some, some)] = value[a:]
            k.o[2][:, pl.ds(j * few, few)] = two[j].astype(F32)

    return kernel_call(
        body,
        [arr(a, z.c_out), arr(b, z.c_out), arr(c, z.c_wide)],
        [*first, *second],
        scratch=[pltpu.VMEM((n, a + b, some), BF), pltpu.VMEM((n, c, few), BF)],
        scalars=[place],
    )


def on_device(
    features,
    view_ids,
    w_reduce,
    w_spatial,
    w_expand,
    w_narrow,
    w_stride,
    w_widen,
    w_shortcut,
    gain_reduce,
    offset_reduce,
    gain_spatial,
    offset_spatial,
    gain_expand,
    offset_expand,
    gain_narrow,
    offset_narrow,
    gain_stride,
    offset_stride,
    gain_widen,
    offset_widen,
    gain_shortcut,
    offset_shortcut,
    cotangent,
):
    z = Sizes()
    z.ns, z.nb = lax.axis_size(SPACE), lax.axis_size(BATCH)
    z.slo = lax.axis_size("slo")
    z.g = min(z.nb, 4)
    z.n = z.ns * z.nb
    z.maps, z.cols = features.shape[1], features.shape[3]
    z.height = z.ns
    z.rows = z.height * z.cols
    z.half = z.rows // 4
    z.c_in, z.c_mid = w_reduce.shape
    z.c_wide, z.c_out = w_widen.shape
    z.q1, z.q3, z.q4, z.q6 = (c // LANES for c in (z.c_mid, z.c_in, z.c_wide, z.c_out))
    assert features.shape[2] == 1 and cotangent.shape[1] == 1 and z.maps == z.ns and z.cols == 16
    yh, xh = z.height // 2, z.cols // 2
    n, ns, nb = z.n, z.ns, z.nb
    s, b = lax.axis_index(SPACE), lax.axis_index(BATCH)
    place = b.astype(jnp.int32).reshape(1)

    def share(pay):
        return lax.all_to_all(pay, ALL, 0, 0, tiled=True)

    def exchange(block):
        return lax.all_to_all(block, SPACE, 0, 0, tiled=True)

    def swap(block, axis, distance):
        return lax.ppermute(block, axis, [(i, i ^ distance) for i in range(lax.axis_size(axis))])

    def trade(pieces):
        pairs = [(i, i ^ j) for j in range(z.g) for i in range(nb)]
        return [p if j == 0 else lax.ppermute(p, BATCH, pairs[j * nb : (j + 1) * nb]) for j, p in enumerate(pieces)]

    def everywhere(block, places):
        pieces = []
        for high in range(places // 2):
            other = swap(block, "bhi", high) if high else block
            pieces += [other, swap(other, "core", 1)]
        return pieces

    def over_groups(product):
        distance = z.g // 2
        while distance < nb // 2:
            product = (product.astype(F32) + swap(product, "bhi", distance).astype(F32)).astype(BF)
            distance *= 2
        return product

    def lines(vector):
        return vector.reshape(1, -1)

    vectors = {
        "reduce": (lines(gain_reduce), lines(offset_reduce)),
        "spatial": (lines(gain_spatial), lines(offset_spatial)),
        "expand": (lines(gain_expand), lines(offset_expand)),
        "narrow": (lines(gain_narrow), lines(offset_narrow)),
        "stride": (lines(gain_stride), lines(offset_stride)),
        "widen": (lines(gain_widen), lines(offset_widen)),
        "shortcut": (lines(gain_shortcut), lines(offset_shortcut)),
    }

    my_ids = lax.dynamic_slice_in_dim(view_ids, s, 1, 1).astype(F32)
    arrived = exchange(features.reshape(MICRO, z.maps, z.cols, z.c_in).transpose(1, 0, 2, 3))
    pre_reduce, pay = k_reduce(arrived, my_ids.reshape(MICRO), w_reduce, z)
    got = share(pay)
    ids = got[:, 6 * z.q1 : 6 * z.q1 + MICRO]
    same = (ids == my_ids[None]).astype(F32)
    mates = {q: jnp.repeat(same, q, axis=1) for q in (z.q3, z.q4)}
    id_rows = jnp.concatenate([ids, ids, jnp.zeros((n, 2, LANES), F32)], axis=1)

    maps_in = arrived.reshape(yh, 2, MICRO, xh, 2, z.c_in).transpose(2, 1, 4, 0, 3, 5)
    maps_in = maps_in.reshape(MICRO * z.rows, z.c_in)

    patch_reduce, pre_spatial, pay, st_reduce, mates[z.q1] = k_spatial(
        got, my_ids.reshape(MICRO), pre_reduce, *vectors["reduce"], w_spatial, z
    )
    got = share(pay)
    out_spatial, pre_expand, pay, st_spatial = k_expand(got, mates[z.q1], pre_spatial, *vectors["spatial"], w_expand, z)
    got = share(pay)
    residual_one, joined, even, pre_narrow, pay, st_expand = k_narrow(
        got, mates[z.q3], pre_expand, *vectors["expand"], maps_in, w_narrow, z
    )
    evens = everywhere(even, z.g)
    got = share(pay)
    pre_shortcut, short_st = k_shortcut(even, w_shortcut, z)
    out_narrow, pre_stride, pay, st_narrow = k_stride(
        got, mates[z.q4], pre_narrow, *vectors["narrow"], w_stride, z
    )
    got = share(pay)
    outs_narrow = everywhere(out_narrow, z.g)
    out_stride, pre_widen, pay, st_stride, *evens = k_widen(
        got, mates[z.q4], pre_stride, *vectors["stride"], short_st, w_widen, z, evens
    )
    outs_stride = everywhere(out_stride, z.g)
    whole = share(k_views(share(pay), id_rows, z))
    mapped, d_two, pay = k_mapped(
        whole,
        pre_widen,
        pre_shortcut,
        cotangent.reshape(-1, z.c_out),
        (*vectors["widen"], *vectors["shortcut"]),
        z,
    )

    sums = share(k_view_sums(share(pay), id_rows, z))
    delta_shortcut, go_widen, gg_widen, gg_shortcut, d_stride, pay, *more = k_back_widen(
        whole, sums, d_two, pre_widen, pre_shortcut, vectors["widen"][0], vectors["shortcut"][0],
        pre_stride, st_stride, *vectors["stride"], place, w_widen, z, outs_narrow,
    )
    got = share(pay)
    pieces, outs_narrow = more[: z.g], more[z.g :]
    d_even = k_even(delta_shortcut, w_shortcut, z)
    first_pieces = trade(pieces)
    go_stride, gg_stride, d_narrow, pay, *more = k_back_stride(
        got, mates[z.q4], d_stride, pre_stride, st_stride, vectors["stride"][0],
        pre_narrow, st_narrow, *vectors["narrow"], place, w_stride, z, (*first_pieces, *outs_stride, d_even),
    )
    pieces, first_pieces, outs_stride, d_even = more[: z.g], more[z.g : 2 * z.g], more[2 * z.g : 3 * z.g], more[3 * z.g]
    got = share(pay)
    first = k_first_grads(outs_stride, evens, first_pieces, z)
    first = over_groups(first)
    pieces = trade(pieces)
    delta_narrow, go_narrow, gg_narrow, d_one, pay, first, *pieces = k_back_narrow(
        got, mates[z.q4], d_narrow, pre_narrow, st_narrow, vectors["narrow"][0],
        d_even, residual_one, pre_expand, st_expand, w_narrow, z, (first, *pieces),
    )
    got = share(pay)
    first = lax.psum_scatter(first, "slo", scatter_dimension=0, tiled=True)
    second = over_groups(k_stride_grads(outs_narrow, pieces, z))

    delta_expand, go_expand, gg_expand, d_spatial, pay, second = k_back_expand(
        got, mates[z.q3], d_one, pre_expand, st_expand, vectors["expand"][0],
        pre_spatial, st_spatial, *vectors["spatial"], w_expand, z, (second,),
    )
    got = share(pay)
    second = lax.psum_scatter(second, "slo", scatter_dimension=0, tiled=True)
    blocks = all(w.shape[0] % (8 * n) == 0 for w in (w_reduce, w_spatial, w_expand, w_narrow))
    pairs_some = [(joined, delta_narrow), (out_spatial, delta_expand)]
    kept_some, sent_some = k_products(pairs_some, place, z) if blocks else (None, delta_expand)
    flipped = w_spatial.reshape(9, z.c_mid, z.c_mid).transpose(0, 2, 1).reshape(9 * z.c_mid, z.c_mid)
    delta_spatial, go_spatial, gg_spatial, d_reduce, pay, sent_some = k_back_spatial(
        got, mates[z.q1], d_spatial, pre_spatial, st_spatial, vectors["spatial"][0],
        pre_reduce, st_reduce, *vectors["reduce"], flipped, z, (sent_some,),
    )
    got = share(pay)
    pairs_more = [(patch_reduce, delta_spatial)]
    kept_more, sent_more = k_products(pairs_more, place, z) if blocks else (None, delta_spatial)
    came_some = swap(sent_some, "core", 1) if blocks else sent_some
    delta_reduce, go_reduce, gg_reduce, sent_more, came_some, first = k_back_reduce(
        got, mates[z.q1], d_reduce, pre_reduce, st_reduce, vectors["reduce"][0], z, (sent_more, came_some, first)
    )
    where = jnp.stack([lax.axis_index("slo"), lax.axis_index("bhi"), lax.axis_index("shi")]).astype(jnp.int32)

    def over_plane(groups, passes=()):
        high = nb // 2
        parts = k_sum_plane(groups, where, z, passes)
        came = []
        for i in range(high):
            for j in range(z.slo):
                pairs = [(u * z.slo + v, (u ^ i) * z.slo + (v ^ j)) for u in range(high) for v in range(z.slo)]
                part = parts[i * z.slo + j]
                came.append(lax.ppermute(part, ("bhi", "slo"), pairs) if i or j else part)
        return came, parts[high * z.slo :]

    pairs_last = [(maps_in, delta_reduce)]
    if blocks:
        kept_last, sent_last = k_products(pairs_last, place, z)
        late, (sent_last,) = over_plane([(kept_some, came_some), (kept_more, swap(sent_more, "core", 1))], (sent_last,))
        came_last = swap(sent_last, "core", 1)
        left, second, came_last = k_input(delta_reduce, d_one, w_reduce, z, (second, came_last))
    else:
        (left,) = k_input(delta_reduce, d_one, w_reduce, z)
    grad_features = exchange(left).transpose(1, 0, 2, 3).reshape(features.shape)
    first, second = lax.psum_scatter(
        (first.reshape(first.shape[1:]), second.reshape(second.shape[1:])), "shi", scatter_dimension=0, tiled=True
    )
    if blocks:
        last, late = over_plane([(kept_last, came_last)], late)
        parts = k_sum_line([late, last], where, z)
        parts = [p if j == 0 else swap(p, "shi", j) for j, p in enumerate(parts)]
        late, first, second = k_sum_last(parts, (first, second))
        late = everywhere(late, nb)
        shapes = [w.shape for w in (w_narrow, w_expand, w_spatial, w_reduce)]
        grad_w_narrow, grad_w_expand, grad_w_spatial, grad_w_reduce = k_late_shares(late, place, shapes, z)
    else:
        late = [dot_tn(o, g).astype(BF) for o, g in pairs_some + pairs_more + pairs_last]
        late = [lax.psum_scatter(w, SPACE, scatter_dimension=0, tiled=True) for w in late]
        late = [w.astype(F32) for w in lax.psum(late, BATCH)]
        grad_w_narrow, grad_w_expand, grad_w_spatial, grad_w_reduce = late
    first = everywhere(first.reshape(first.shape[1:]), z.g)
    second = everywhere(second.reshape(second.shape[1:]), z.g)
    grad_w_widen, grad_w_shortcut, grad_w_stride = k_early_shares(first, second, place, z)

    flat = lambda block: block.reshape(-1)
    return (
        mapped.reshape(cotangent.shape),
        grad_features,
        grad_w_reduce,
        grad_w_spatial,
        grad_w_expand,
        grad_w_narrow,
        grad_w_stride,
        grad_w_widen,
        grad_w_shortcut,
        flat(gg_reduce),
        flat(go_reduce),
        flat(gg_spatial),
        flat(go_spatial),
        flat(gg_expand),
        flat(go_expand),
        flat(gg_narrow),
        flat(go_narrow),
        flat(gg_stride),
        flat(go_stride),
        flat(gg_widen),
        flat(go_widen),
        flat(gg_shortcut),
        flat(go_widen),
    )


def solution(mesh):
    nb, ns = mesh.shape["batch"], mesh.shape["space"]
    fine = Mesh(mesh.devices.reshape(nb // 2, 2, ns // 2, 2), ALL)
    maps = P(None, ALL, None, None, None)
    return jax.shard_map(
        on_device,
        mesh=fine,
        in_specs=(P(None, BATCH, SPACE, None, None), P(None, BATCH)) + (P(),) * 21 + (maps,),
        out_specs=(maps, P(None, BATCH, SPACE, None, None)) + (P(SPACE, None),) * 7 + (P(),) * 14,
        check_vma=False,
    )
```

```python
import functools
import math

import jax
import jax.numpy as jnp
from jax import lax
from jax.experimental import pallas as pl
from jax.experimental.pallas import tpu as pltpu
from jax.sharding import Mesh
from jax.sharding import PartitionSpec as P

NVIEW = 2
MICRO = 3
EPSILON = 1e-05
BF = jnp.bfloat16
F32 = jnp.float32
BATCH, SPACE = ("bhi", "core"), ("shi", "slo")
ALL = BATCH + SPACE
LANES = 128
ROOT = math.sqrt(2.0 / math.pi)
CUBE = 0.044715


def dot(a, b, dims=((1,), (0,))):
    return lax.dot_general(a, b, (dims, ((), ())), preferred_element_type=F32)


def dot_nt(a, b):
    return dot(a, b, ((1,), (1,)))


def dot_tn(a, b):
    return dot(a, b, ((0,), (0,)))


def gelu(v):
    return 0.5 * v * (1.0 + jnp.tanh(ROOT * (v + CUBE * (v * v * v))))


def gelu_slope(v):
    square = v * v
    t = jnp.tanh(ROOT * (v + CUBE * (square * v)))
    return 0.5 * (1.0 + t) + (0.5 * ROOT) * v * (1.0 - t * t) * (1.0 + (3.0 * CUBE) * square)


def cols(c):
    return pl.ds(c * LANES, LANES)


def row(ref, r):
    return ref[pl.ds(r, 1), :]


class Kernel:
    def __init__(self, i, w, o, raw, scalars, stacks, extra, starts, sems):
        self.i, self.w, self.o, self.raw, self.s, self.st, self.x = i, w, o, raw, scalars, stacks, extra
        self.w_copies, self.out_pairs, self.sems = starts, {}, sems
        self.flying, self.sent = [], set()

    def wait_w(self, n=0):
        self.w_copies[n].wait()

    def send(self, n):
        src, dst, sem = self.out_pairs[n]
        copy = pltpu.make_async_copy(src, dst, sem)
        copy.start()
        self.flying.append(copy)
        self.sent.add(n)

    def copy(self, src, dst):
        copy = pltpu.make_async_copy(src, dst, self.sems.pop())
        copy.start()
        self.flying.append(copy)


def kernel_call(body, outs, args, weights=(), scratch=(), flops=0, raw=(), n_raw=0, scalars=(), passes=(), stacks=(), limit=60):
    n_s, n_in, n_w, n_p = len(scalars), len(args), len(weights), len(passes)
    n_k = sum(map(len, stacks))
    n_out, n_r = len(outs), len(raw)

    def run(*refs):
        refs = list(refs)

        def take(n):
            part = refs[:n]
            del refs[:n]
            return part

        s, ins, w_any = take(n_s), take(n_in), take(n_w)
        piles = [take(len(g)) for g in stacks]
        take(n_p)
        out, raw_refs, _ = take(n_out), take(n_r), take(n_p)
        v_in, v_w, v_out, v_k = take(n_in), take(n_w), take(n_out), take(len(stacks))
        (sems,) = take(1)
        sem = [sems.at[j] for j in range(n_in + n_w + n_k + n_out + n_raw)]
        in_copies = [pltpu.make_async_copy(a, v, sem.pop(0)) for a, v in zip(ins, v_in)]
        for pile, v in zip(piles, v_k):
            for j, a in enumerate(pile):
                rows = a.shape[0]
                in_copies.append(pltpu.make_async_copy(a, v.at[pl.ds(j * rows, rows)], sem.pop(0)))
        w_copies = [pltpu.make_async_copy(a, v, sem.pop(0)) for a, v in zip(w_any, v_w)]
        for copy in in_copies + w_copies:
            copy.start()
        k = Kernel(v_in, v_w, v_out, raw_refs, s, v_k, refs, w_copies, sem[n_out:])
        k.out_pairs = {j: (v_out[j], out[j], sem[j]) for j in range(n_out)}
        for copy in in_copies:
            copy.wait()
        body(k)
        for j in range(n_out):
            if j not in k.sent:
                k.send(j)
        for copy in k.flying:
            copy.wait()

    def size(a):
        return math.prod(a.shape) * jnp.dtype(a.dtype).itemsize

    outside = pl.BlockSpec(memory_space=pl.ANY)
    piled = [arr(len(g) * g[0].shape[0], *g[0].shape[1:], dtype=g[0].dtype) for g in stacks]
    held = sum(map(size, (*args, *weights, *outs, *piled)))
    total = held + sum(size(a) for a in scratch if hasattr(a, "dtype"))
    first = n_s + n_in + n_w + n_k
    results = pl.pallas_call(
        run,
        out_shape=tuple(jax.ShapeDtypeStruct(o.shape, o.dtype) for o in (*outs, *raw, *passes)),
        in_specs=[pl.BlockSpec(memory_space=pltpu.SMEM)] * n_s + [outside] * (n_in + n_w + n_k + n_p),
        out_specs=tuple([outside] * (n_out + n_r + n_p)),
        scratch_shapes=[pltpu.VMEM(a.shape, a.dtype) for a in (*args, *weights, *outs, *piled)]
        + [pltpu.SemaphoreType.DMA((n_in + n_w + n_k + n_out + n_raw,))]
        + list(scratch),
        input_output_aliases={first + j: n_out + n_r + j for j in range(n_p)},
        cost_estimate=pl.CostEstimate(flops=flops, bytes_accessed=held, transcendentals=0),
        compiler_params=pltpu.CompilerParams(vmem_limit_bytes=max(limit * 2**20, total)),
    )(*scalars, *args, *weights, *(a for g in stacks for a in g), *passes)
    return tuple(results)


def arr(*shape, dtype=F32):
    return jax.ShapeDtypeStruct(shape, dtype)


def fill(pay_ref, rows_ref):
    block = rows_ref[...].astype(pay_ref.dtype)

    def step(j, _):
        pay_ref[j] = block
        return 0

    lax.fori_loop(0, pay_ref.shape[0], step, 0, unroll=8)


def stats_rows(value, rows_ref, r, size, offset):
    mean = jnp.sum(value, axis=0, keepdims=True) * (1.0 / size)
    away = value - mean
    rows_ref[pl.ds(r, 1), :] = mean
    rows_ref[pl.ds(r + offset, 1), :] = jnp.sum(away * away, axis=0, keepdims=True)


def stats_shape(q):
    return 9 * q, BF


def stats_arr(n, q):
    rows, dtype = stats_shape(q)
    return arr(n, rows, LANES, dtype=dtype)


def fill_stats(pay_ref, rows_ref, q):
    k = MICRO * q
    if pay_ref.dtype == BF:
        mean, square = rows_ref[:k], rows_ref[k : 2 * k]
        high = mean.astype(BF).astype(F32)
        rows_ref[:k] = high
        rows_ref[k : 2 * k] = mean - high
        rows_ref[2 * k : 3 * k] = square
    fill(pay_ref, rows_ref)


def merge_stats(got_ref, mates_ref, st_ref, q, size):
    n = got_ref.shape[0]
    k = MICRO * q
    mates = n // NVIEW
    step = 8

    def parts(at):
        got = got_ref[at].astype(F32)
        if got_ref.dtype == BF:
            return got[:, :k] + got[:, k : 2 * k], got[:, 2 * k : 3 * k]
        return got[:, :k], got[:, k : 2 * k]

    def one(i, acc):
        at = pl.ds(i * step, step)
        return acc + jnp.sum(mates_ref[at] * parts(at)[0], axis=0)

    mean = lax.fori_loop(0, n // step, one, jnp.zeros((k, LANES), F32), unroll=4) * (1.0 / mates)

    def two(i, acc):
        at = pl.ds(i * step, step)
        means, squares = parts(at)
        away = means - mean[None]
        return acc + jnp.sum(mates_ref[at] * (squares + size * (away * away)), axis=0)

    total = lax.fori_loop(0, n // step, two, jnp.zeros((k, LANES), F32), unroll=4)
    st_ref[:k] = mean
    st_ref[k : 2 * k] = lax.rsqrt(total * (1.0 / (mates * size)) + EPSILON)


def merge_sums(got_ref, mates_ref, sum_ref, q, size, total_refs):
    n = got_ref.shape[0]
    k = MICRO * q
    scale = 1.0 / (n // NVIEW * size)
    step = 8

    def one(i, carry):
        at = pl.ds(i * step, step)
        both = got_ref[at].astype(F32)
        first, second = both[:, :k], both[:, k : 2 * k]
        w = mates_ref[at]
        return (
            carry[0] + jnp.sum(w * first, axis=0),
            carry[1] + jnp.sum(w * second, axis=0),
            carry[2] + jnp.sum(first, axis=0),
            carry[3] + jnp.sum(second, axis=0),
        )

    zero = jnp.zeros((k, LANES), F32)
    a, b, ta, tb = lax.fori_loop(0, n // step, one, (zero,) * 4, unroll=4)
    sum_ref[:k] = a * scale
    sum_ref[k : 2 * k] = b * scale
    for ref, t in zip(total_refs, (ta, tb)):
        ref[...] = t[:q] + t[q : 2 * q] + t[2 * q :]


def shift_y(v, offset):
    if offset == 0:
        return v
    zero = jnp.zeros((8, v.shape[1]), v.dtype)
    if offset > 0:
        return jnp.concatenate([v[8:], zero], axis=0)
    return jnp.concatenate([zero, v[:-8]], axis=0)


def shift_x(v, offset):
    if offset == 0:
        return v
    place = lax.broadcasted_iota(jnp.int32, v.shape, 0) % 8
    if offset > 0:
        return jnp.where(place == 7, 0.0, pltpu.roll(v, v.shape[0] - 1, axis=0))
    return jnp.where(place == 0, 0.0, pltpu.roll(v, 1, axis=0))


def write_patches(phase, patch_ref, m, half, c, width, sign, out_phases=((0, 0), (0, 1), (1, 0), (1, 1))):
    moved = {}

    def get(sy, sx, ox):
        if (sy, sx, ox) not in moved:
            moved[sy, sx, ox] = shift_x(phase[sy, sx], ox)
        return moved[sy, sx, ox]

    for i, (py, px) in enumerate(out_phases):
        for r in range(3):
            for k in range(3):
                at_y, at_x = py + sign * (r - 1), px + sign * (k - 1)
                piece = shift_y(get(at_y % 2, at_x % 2, at_x // 2), at_y // 2)
                rows = pl.ds((m * len(out_phases) + i) * half, half)
                patch_ref[rows, pl.ds((r * 3 + k) * width + c * LANES, LANES)] = piece.astype(BF)


PHASES = ((0, 0), (0, 1), (1, 0), (1, 1))


class Sizes:
    pass


def k_reduce(x, ids, w, z):
    q = z.q1

    def body(k):
        (x_ref,), (map_ref, pay_ref), (tmp, rows_ref) = k.i, k.o, k.x
        k.wait_w()
        for y in range(z.height):
            product = dot(x_ref[y].reshape(MICRO * z.cols, z.c_in), k.w[0][...])
            for c in range(q):
                tmp[c, pl.ds(y * MICRO * z.cols, MICRO * z.cols), :] = product[:, c * LANES : (c + 1) * LANES]
        for m in range(MICRO):
            for y in range(z.height):
                for px in range(2):
                    at = m * z.rows + (2 * (y % 2) + px) * z.half + (y // 2) * 8
                    for c in range(q):
                        map_ref[pl.ds(at, 8), cols(c)] = tmp[
                            c, pl.ds((y * MICRO + m) * z.cols + px, 8, stride=2), :
                        ]
        rows_ref[...] = jnp.zeros(rows_ref.shape, F32)
        for m in range(MICRO):
            for c in range(q):
                stats_rows(map_ref[pl.ds(m * z.rows, z.rows), cols(c)], rows_ref, m * q + c, z.rows, MICRO * q)
        for m in range(MICRO):
            rows_ref[pl.ds(9 * q + m, 1), :] = jnp.full((1, LANES), k.s[0][m], F32)
        fill_stats(pay_ref, rows_ref, q)

    rows, pad = MICRO * z.rows, -(-(9 * q + MICRO) // 8) * 8
    return kernel_call(
        body,
        [arr(rows, z.c_mid), arr(z.n, pad, LANES, dtype=BF)],
        [x],
        [w],
        [pltpu.VMEM((q, rows, LANES), F32), pltpu.VMEM((pad, LANES), F32)],
        flops=2 * rows * z.c_in * z.c_mid,
        scalars=[ids],
        limit=24,
    )


def k_spatial(got, ids, pre, gain, offset, w, z):
    q = z.q1

    def body(k):
        got_ref, pre_ref, g_ref, o_ref = k.i
        patch_ref, next_ref, pay_ref, st_ref, mates_ref = k.o
        (rows_ref,) = k.x
        same, views = [], got_ref[...].astype(F32)
        for m in range(MICRO):
            view = views[:, 9 * q + m : 9 * q + m + 1]
            same += [(view == k.s[0][m]).astype(F32)] * q
        mates_ref[...] = jnp.concatenate(same, axis=1)
        merge_stats(got_ref, mates_ref, st_ref, q, z.rows)
        for m in range(MICRO):
            for c in range(q):
                mean, inverse = row(st_ref, m * q + c), row(st_ref, (MICRO + m) * q + c)
                phase = {}
                for i, p in enumerate(PHASES):
                    x = pre_ref[pl.ds(m * z.rows + i * z.half, z.half), cols(c)]
                    phase[p] = gelu(g_ref[:, cols(c)] * ((x - mean) * inverse) + o_ref[:, cols(c)])
                write_patches(phase, patch_ref, m, z.half, c, z.c_mid, 1)
        k.send(0)
        k.wait_w()
        next_ref[...] = dot(patch_ref[...], k.w[0][...])
        k.send(1)
        for m in range(MICRO):
            for c in range(q):
                stats_rows(next_ref[pl.ds(m * z.rows, z.rows), cols(c)], rows_ref, m * q + c, z.rows, MICRO * q)
        fill_stats(pay_ref, rows_ref, q)

    rows = MICRO * z.rows
    return kernel_call(
        body,
        [arr(rows, 9 * z.c_mid, dtype=BF), arr(rows, z.c_mid), stats_arr(z.n, q), arr(6 * q, LANES), arr(z.n, 3 * q, LANES)],
        [got, pre, gain, offset],
        [w],
        [pltpu.VMEM((stats_shape(q)[0], LANES), F32)],
        flops=2 * rows * 9 * z.c_mid * z.c_mid,
        scalars=[ids],
    )


def k_expand(got, mates, pre, gain, offset, w, z):
    q, qo = z.q1, z.q3

    def body(k):
        got_ref, mates_ref, pre_ref, g_ref, o_ref = k.i
        act_ref, next_ref, pay_ref, st_ref = k.o
        (rows_ref,) = k.x
        merge_stats(got_ref, mates_ref, st_ref, q, z.rows)
        for m in range(MICRO):
            for c in range(q):
                mean, inverse = row(st_ref, m * q + c), row(st_ref, (MICRO + m) * q + c)
                at = pl.ds(m * z.rows, z.rows)
                x = pre_ref[at, cols(c)]
                act_ref[at, cols(c)] = gelu(g_ref[:, cols(c)] * ((x - mean) * inverse) + o_ref[:, cols(c)]).astype(BF)
        k.send(0)
        k.wait_w()
        next_ref[...] = dot(act_ref[...], k.w[0][...])
        k.send(1)
        for m in range(MICRO):
            for c in range(qo):
                stats_rows(next_ref[pl.ds(m * z.rows, z.rows), cols(c)], rows_ref, m * qo + c, z.rows, MICRO * qo)
        fill_stats(pay_ref, rows_ref, qo)

    rows = MICRO * z.rows
    return kernel_call(
        body,
        [arr(rows, z.c_mid, dtype=BF), arr(rows, z.c_in), stats_arr(z.n, qo), arr(6 * q, LANES)],
        [got, mates, pre, gain, offset],
        [w],
        [pltpu.VMEM((stats_shape(qo)[0], LANES), F32)],
        flops=2 * rows * z.c_in * z.c_mid,
    )


def k_narrow(got, mates, pre, gain, offset, maps_in, w, z):
    q, qo = z.q3, z.q4

    def body(k):
        got_ref, mates_ref, pre_ref, g_ref, o_ref, in_ref = k.i
        res_ref, join_ref, even_ref, next_ref, pay_ref, st_ref = k.o
        (rows_ref,) = k.x
        merge_stats(got_ref, mates_ref, st_ref, q, z.rows)
        for m in range(MICRO):
            for c in range(q):
                mean, inverse = row(st_ref, m * q + c), row(st_ref, (MICRO + m) * q + c)
                at = pl.ds(m * z.rows, z.rows)
                x = pre_ref[at, cols(c)]
                res = g_ref[:, cols(c)] * ((x - mean) * inverse) + o_ref[:, cols(c)] + in_ref[at, cols(c)].astype(F32)
                res_ref[at, cols(c)] = res
                joined = gelu(res).astype(BF)
                join_ref[at, cols(c)] = joined
                even_ref[pl.ds(m * z.half, z.half), cols(c)] = joined[: z.half]
        for j in range(3):
            k.send(j)
        k.wait_w()
        next_ref[...] = dot(join_ref[...], k.w[0][...])
        k.send(3)
        for m in range(MICRO):
            for c in range(qo):
                stats_rows(next_ref[pl.ds(m * z.rows, z.rows), cols(c)], rows_ref, m * qo + c, z.rows, MICRO * qo)
        fill_stats(pay_ref, rows_ref, qo)

    rows = MICRO * z.rows
    return kernel_call(
        body,
        [
            arr(rows, z.c_in),
            arr(rows, z.c_in, dtype=BF),
            arr(MICRO * z.half, z.c_in, dtype=BF),
            arr(rows, z.c_wide),
            stats_arr(z.n, qo),
            arr(6 * q, LANES),
        ],
        [got, mates, pre, gain, offset, maps_in],
        [w],
        [pltpu.VMEM((stats_shape(qo)[0], LANES), F32)],
        flops=2 * rows * z.c_in * z.c_wide,
    )


def k_stride(got, mates, pre, gain, offset, w, z, passes=()):
    q = z.q4

    def body(k):
        got_ref, mates_ref, pre_ref, g_ref, o_ref = k.i
        act_ref, next_ref, pay_ref, st_ref = k.o
        patch_ref, rows_ref = k.x
        merge_stats(got_ref, mates_ref, st_ref, q, z.rows)
        for m in range(MICRO):
            for c in range(q):
                mean, inverse = row(st_ref, m * q + c), row(st_ref, (MICRO + m) * q + c)
                phase = {}
                for i, p in enumerate(PHASES):
                    x = pre_ref[pl.ds(m * z.rows + i * z.half, z.half), cols(c)]
                    phase[p] = gelu(g_ref[:, cols(c)] * ((x - mean) * inverse) + o_ref[:, cols(c)])
                    act_ref[pl.ds(m * z.rows + i * z.half, z.half), cols(c)] = phase[p].astype(BF)
                write_patches(phase, patch_ref, m, z.half, c, z.c_wide, 1, ((0, 0),))
        k.send(0)
        k.wait_w()
        next_ref[...] = dot(patch_ref[...], k.w[0][...])
        k.send(1)
        for m in range(MICRO):
            for c in range(q):
                stats_rows(next_ref[pl.ds(m * z.half, z.half), cols(c)], rows_ref, m * q + c, z.half, MICRO * q)
        fill_stats(pay_ref, rows_ref, q)

    rows = MICRO * z.half
    return kernel_call(
        body,
        [arr(MICRO * z.rows, z.c_wide, dtype=BF), arr(rows, z.c_wide), stats_arr(z.n, q), arr(6 * q, LANES)],
        [got, mates, pre, gain, offset],
        [w],
        [pltpu.VMEM((rows, 9 * z.c_wide), BF), pltpu.VMEM((stats_shape(q)[0], LANES), F32)],
        flops=2 * rows * 9 * z.c_wide * z.c_wide,
        passes=passes,
    )


def k_shortcut(even, w, z):
    def body(k):
        (e_ref,), (next_ref, st_ref) = k.i, k.o
        k.wait_w()
        next_ref[...] = dot(e_ref[...], k.w[0][...])
        for c in range(z.q6):
            for m in range(MICRO):
                stats_rows(next_ref[pl.ds(m * z.half, z.half), cols(c)], st_ref.at[c], m, z.half, MICRO)

    rows = MICRO * z.half
    return kernel_call(
        body, [arr(rows, z.c_out), arr(z.q6, 8, LANES)], [even], [w], flops=2 * rows * z.c_in * z.c_out
    )


def k_widen(got, mates, pre, gain, offset, short_st, w, z, passes=()):
    q = z.q4

    def body(k):
        got_ref, mates_ref, pre_ref, g_ref, o_ref, short_ref = k.i
        act_ref, next_ref, pay_ref, st_ref = k.o
        merge_stats(got_ref, mates_ref, st_ref, q, z.half)
        for m in range(MICRO):
            for c in range(q):
                mean, inverse = row(st_ref, m * q + c), row(st_ref, (MICRO + m) * q + c)
                at = pl.ds(m * z.half, z.half)
                x = pre_ref[at, cols(c)]
                act_ref[at, cols(c)] = gelu(g_ref[:, cols(c)] * ((x - mean) * inverse) + o_ref[:, cols(c)]).astype(BF)
        k.send(0)
        k.wait_w()
        next_ref[...] = dot(act_ref[...], k.w[0][...])
        k.send(1)
        for c in range(z.q6):
            for m in range(MICRO):
                stats_rows(next_ref[pl.ds(m * z.half, z.half), cols(c)], pay_ref.at[c], m, z.half, MICRO)
            pay_ref[z.q6 + c] = short_ref[c]
        chunks = 2 * z.q6
        for j in range(chunks, z.n):
            pay_ref[j] = pay_ref[j % chunks]

    rows = MICRO * z.half
    return kernel_call(
        body,
        [arr(rows, z.c_wide, dtype=BF), arr(rows, z.c_out), arr(z.n, 8, LANES), arr(6 * q, LANES)],
        [got, mates, pre, gain, offset, short_st],
        [w],
        flops=2 * rows * z.c_wide * z.c_out,
        passes=passes,
    )


def k_views(got, ids, z):
    def body(k):
        (got_ref, id_ref), (pay_ref,), (lo, hi) = k.i, k.o, k.x
        mates = z.n // NVIEW
        g, ids = got_ref[...], id_ref[...]
        for view, ref in ((0, lo), (1, hi)):
            w = (ids == float(view)).astype(F32)
            mean = jnp.sum(w * g, axis=0)[:MICRO] * (1.0 / mates)
            away = g[:, :MICRO] - mean[None]
            total = jnp.sum(w[:, :MICRO] * (g[:, MICRO : 2 * MICRO] + z.half * (away * away)), axis=0)
            ref[...] = jnp.zeros(ref.shape, F32)
            ref[:MICRO] = mean
            ref[MICRO : 2 * MICRO] = lax.rsqrt(total * (1.0 / (mates * z.half)) + EPSILON)
        pay_ref[...] = jnp.where(ids > 0.5, hi[...][None], lo[...][None])

    return kernel_call(
        body, [arr(z.n, 8, LANES)], [got, ids], scratch=[pltpu.VMEM((8, LANES), F32)] * 2
    )[0]


def k_mapped(whole, pre_w, pre_s, cot, gains, z, passes=()):
    def body(k):
        st_ref, w_ref, s_ref, cot_ref, gw, ow, gs, os = k.i
        map_ref, d_ref, pay_ref = k.o
        n_c = z.q6
        pay_ref[...] = jnp.zeros(pay_ref.shape, F32)
        for c in range(n_c):
            for m in range(MICRO):
                at = pl.ds(m * z.half, z.half)
                sw, ss = st_ref.at[c], st_ref.at[n_c + c]
                hat_w = (w_ref[at, cols(c)] - row(sw, m)) * row(sw, MICRO + m)
                hat_s = (s_ref[at, cols(c)] - row(ss, m)) * row(ss, MICRO + m)
                res = gw[:, cols(c)] * hat_w + ow[:, cols(c)] + (gs[:, cols(c)] * hat_s + os[:, cols(c)])
                map_ref[at, cols(c)] = gelu(res).astype(BF)
                d = gelu_slope(res) * cot_ref[at, cols(c)].astype(F32)
                d_ref[at, cols(c)] = d
                first, second = pay_ref.at[c], pay_ref.at[n_c + c]
                first[pl.ds(m, 1), :] = jnp.sum(d, axis=0, keepdims=True)
                first[pl.ds(MICRO + m, 1), :] = jnp.sum(d * hat_w, axis=0, keepdims=True)
                second[pl.ds(m, 1), :] = jnp.sum(d * hat_s, axis=0, keepdims=True)
        for j in range(2 * n_c, z.n):
            pay_ref[j] = pay_ref[j % (2 * n_c)]

    rows = MICRO * z.half
    return kernel_call(
        body,
        [arr(rows, z.c_out, dtype=BF), arr(rows, z.c_out), arr(z.n, 8, LANES)],
        [whole, pre_w, pre_s, cot, *gains],
        flops=rows * z.c_out * 60,
        passes=passes,
    )


def k_view_sums(got, ids, z):
    def body(k):
        (got_ref, id_ref), (pay_ref,), (both,) = k.i, k.o, k.x
        g, ids = got_ref[...], id_ref[...]
        lo = jnp.sum((ids == 0.0).astype(F32) * g, axis=0)
        hi = jnp.sum((ids == 1.0).astype(F32) * g, axis=0)
        both[0], both[1] = lo, hi
        all_views = lo + hi
        totals = []
        for k in range(2):
            totals.append(jnp.sum(all_views[k * MICRO : (k + 1) * MICRO], axis=0, keepdims=True))
        for v in range(2):
            for k in range(2):
                both[v, pl.ds(2 * MICRO + k, 1), :] = totals[k]
        pay_ref[...] = jnp.where(ids > 0.5, both[1][None], both[0][None])

    return kernel_call(body, [arr(z.n, 8, LANES)], [got, ids], scratch=[pltpu.VMEM((2, 8, LANES), F32)])[0]


def back_rows(x, d, st_ref, sum_ref, m, q, c, gain):
    inverse = row(st_ref, (MICRO + m) * q + c)
    hat = (x - row(st_ref, m * q + c)) * inverse
    return gain * inverse * (d - row(sum_ref, m * q + c) - hat * row(sum_ref, (MICRO + m) * q + c))


def sum_rows(d, hat, rows_ref, r, offset):
    rows_ref[pl.ds(r, 1), :] = jnp.sum(d, axis=0, keepdims=True)
    rows_ref[pl.ds(r + offset, 1), :] = jnp.sum(d * hat, axis=0, keepdims=True)


def slope_and_sums(d_out, pre_ref, at, st_ref, m, q, c, g_ref, o_ref, d_ref, rows_ref):
    hat = (pre_ref[at, cols(c)] - row(st_ref, m * q + c)) * row(st_ref, (MICRO + m) * q + c)
    d = gelu_slope(g_ref[:, cols(c)] * hat + o_ref[:, cols(c)]) * d_out
    d_ref[at, cols(c)] = d
    sum_rows(d, hat, rows_ref, m * q + c, MICRO * q)


def k_back_widen(whole, sums, d_two, pre_w, pre_s, gain_w, gain_s, pre, st, gain, offset, place, w, z, passes=()):
    q, n_c = z.q4, z.q6

    def body(k):
        st2, sum_ref, d_ref, w_ref, s_ref, gw, gs, pre_ref, st_ref, g_ref, o_ref = k.i
        ds_ref, t_off, t_gw, t_gs, d_next, pay_ref = k.o
        dw_ref, rows_ref, tmp = k.x
        scale = 1.0 / (z.n // NVIEW * z.half)
        for c in range(n_c):
            first, second = sum_ref.at[c], sum_ref.at[n_c + c]
            t_off[pl.ds(c, 1), :] = row(first, 2 * MICRO)
            t_gw[pl.ds(c, 1), :] = row(first, 2 * MICRO + 1)
            t_gs[pl.ds(c, 1), :] = row(second, 2 * MICRO)
            sw, ss = st2.at[c], st2.at[n_c + c]
            for m in range(MICRO):
                at = pl.ds(m * z.half, z.half)
                inv_w, inv_s = row(sw, MICRO + m), row(ss, MICRO + m)
                hat_w = (w_ref[at, cols(c)] - row(sw, m)) * inv_w
                hat_s = (s_ref[at, cols(c)] - row(ss, m)) * inv_s
                d = d_ref[at, cols(c)] - row(first, m) * scale
                dw_ref[at, cols(c)] = (
                    gw[:, cols(c)] * inv_w * (d - hat_w * (row(first, MICRO + m) * scale))
                ).astype(BF)
                ds_ref[at, cols(c)] = (gs[:, cols(c)] * inv_s * (d - hat_s * (row(second, m) * scale))).astype(BF)
        k.send(0)
        some = z.c_out // z.g
        for j in range(z.g):
            at = pl.ds(pl.multiple_of(((k.s[0][0] & (z.g - 1)) ^ j) * some, some), some)
            k.copy(dw_ref.at[:, at], k.raw[j].at[:, pl.ds(0, some)])
            k.copy(ds_ref.at[:, at], k.raw[j].at[:, pl.ds(some, some)])
        k.wait_w()
        tmp[...] = dot_nt(dw_ref[...], k.w[0][...])
        for m in range(MICRO):
            at = pl.ds(m * z.half, z.half)
            for c in range(q):
                slope_and_sums(tmp[at, cols(c)], pre_ref, at, st_ref, m, q, c, g_ref, o_ref, d_next, rows_ref)
        fill(pay_ref, rows_ref)

    rows = MICRO * z.half
    return kernel_call(
        body,
        [arr(rows, z.c_out, dtype=BF)]
        + [arr(n_c, LANES)] * 3
        + [arr(rows, z.c_wide), arr(z.n, 6 * q, LANES, dtype=BF)],
        [whole, sums, d_two, pre_w, pre_s, gain_w, gain_s, pre, st, gain, offset],
        [w],
        [
            pltpu.VMEM((rows, z.c_out), BF),
            pltpu.VMEM((6 * q, LANES), F32),
            pltpu.VMEM((rows, z.c_wide), F32),
        ],
        flops=2 * rows * z.c_wide * z.c_out,
        raw=[arr(rows, 2 * z.c_out // z.g, dtype=BF)] * z.g,
        n_raw=2 * z.g,
        scalars=[place],
        passes=passes,
    )


def back_start(refs, mates_ref, sum_ref, out_ref, q, n_rows, totals):
    got_ref, d_ref, pre_ref, st_ref, g_ref = refs
    merge_sums(got_ref, mates_ref, sum_ref, q, n_rows, totals)
    for m in range(MICRO):
        at = pl.ds(m * n_rows, n_rows)
        for c in range(q):
            out_ref[at, cols(c)] = back_rows(
                pre_ref[at, cols(c)], d_ref[at, cols(c)], st_ref, sum_ref, m, q, c, g_ref[:, cols(c)]
            ).astype(BF)


def k_back_stride(got, mates, d, pre_s, st_s, gain_s, pre, st, gain, offset, place, w, z, passes=()):
    q = z.q4

    def body(k):
        got_ref, mates_ref, d_ref, ps_ref, ss_ref, gs_ref, pre_ref, st_ref, g_ref, o_ref = k.i
        t_off, t_gain, d_next, pay_ref = k.o
        delta_ref, rows_ref, sum_ref, contrib = k.x
        back_start((got_ref, d_ref, ps_ref, ss_ref, gs_ref), mates_ref, sum_ref, delta_ref, q, z.half, (t_off, t_gain))
        some = z.c_wide // z.g
        for j in range(z.g):
            at = pl.ds(pl.multiple_of(((k.s[0][0] & (z.g - 1)) ^ j) * some, some), some)
            k.copy(delta_ref.at[:, at], k.raw[j])
        k.wait_w()
        contrib[...] = dot_nt(delta_ref[...], k.w[0][...])
        for m in range(MICRO):
            for c in range(q):
                phase = {}
                for r in range(3):
                    for k in range(3):
                        piece = contrib[pl.ds(m * z.half, z.half), pl.ds((r * 3 + k) * z.c_wide + c * LANES, LANES)]
                        piece = shift_x(shift_y(piece, 1 if r == 0 else 0), 1 if k == 0 else 0)
                        p = ((r + 1) % 2, (k + 1) % 2)
                        phase[p] = piece if p not in phase else phase[p] + piece
                first = second = 0.0
                mean, inverse = row(st_ref, m * q + c), row(st_ref, (MICRO + m) * q + c)
                for i, p in enumerate(PHASES):
                    at = pl.ds(m * z.rows + i * z.half, z.half)
                    hat = (pre_ref[at, cols(c)] - mean) * inverse
                    grad = gelu_slope(g_ref[:, cols(c)] * hat + o_ref[:, cols(c)]) * phase[p]
                    d_next[at, cols(c)] = grad
                    first = first + jnp.sum(grad, axis=0, keepdims=True)
                    second = second + jnp.sum(grad * hat, axis=0, keepdims=True)
                rows_ref[pl.ds(m * q + c, 1), :] = first
                rows_ref[pl.ds((MICRO + m) * q + c, 1), :] = second
        fill(pay_ref, rows_ref)

    rows = MICRO * z.half
    return kernel_call(
        body,
        [arr(q, LANES)] * 2
        + [arr(MICRO * z.rows, z.c_wide), arr(z.n, 6 * q, LANES, dtype=BF)],
        [got, mates, d, pre_s, st_s, gain_s, pre, st, gain, offset],
        [w],
        [
            pltpu.VMEM((rows, z.c_wide), BF),
            pltpu.VMEM((6 * q, LANES), F32),
            pltpu.VMEM((6 * q, LANES), F32),
            pltpu.VMEM((rows, 9 * z.c_wide), F32),
        ],
        flops=2 * rows * 9 * z.c_wide * z.c_wide,
        passes=passes,
        raw=[arr(rows, z.c_wide // z.g, dtype=BF)] * z.g,
        n_raw=z.g,
        scalars=[place],
    )


def k_back_narrow(got, mates, d, pre_n, st_n, gain_n, even, res, pre, st, w, z, passes=()):
    q, qo = z.q4, z.q3

    def body(k):
        got_ref, mates_ref, d_ref, pn_ref, sn_ref, gn_ref, even_ref, res_ref, pre_ref, st_ref = k.i
        delta_ref, t_off, t_gain, d_next, pay_ref = k.o
        rows_ref, sum_ref, tmp = k.x
        back_start((got_ref, d_ref, pn_ref, sn_ref, gn_ref), mates_ref, sum_ref, delta_ref, q, z.rows, (t_off, t_gain))
        k.send(0)
        k.wait_w()
        tmp[...] = dot_nt(delta_ref[...], k.w[0][...])
        for m in range(MICRO):
            at = pl.ds(m * z.rows, z.rows)
            some = pl.ds(m * z.rows, z.half)
            for c in range(qo):
                tmp[some, cols(c)] = tmp[some, cols(c)] + even_ref[pl.ds(m * z.half, z.half), cols(c)]
                d_join = tmp[at, cols(c)].astype(BF).astype(F32)
                one = gelu_slope(res_ref[at, cols(c)]) * d_join
                hat = (pre_ref[at, cols(c)] - row(st_ref, m * qo + c)) * row(st_ref, (MICRO + m) * qo + c)
                d_next[at, cols(c)] = one
                sum_rows(one, hat, rows_ref, m * qo + c, MICRO * qo)
        fill(pay_ref, rows_ref)

    rows = MICRO * z.rows
    return kernel_call(
        body,
        [arr(rows, z.c_wide, dtype=BF)] + [arr(q, LANES)] * 2 + [arr(rows, z.c_in), arr(z.n, 6 * qo, LANES, dtype=BF)],
        [got, mates, d, pre_n, st_n, gain_n, even, res, pre, st],
        [w],
        [
            pltpu.VMEM((6 * qo, LANES), F32),
            pltpu.VMEM((6 * q, LANES), F32),
            pltpu.VMEM((rows, z.c_in), F32),
        ],
        flops=2 * rows * z.c_in * z.c_wide,
        passes=passes,
    )


def k_back_expand(got, mates, d, pre_e, st_e, gain_e, pre, st, gain, offset, w, z, passes=()):
    q, qo = z.q3, z.q1

    def body(k):
        got_ref, mates_ref, d_ref, pe_ref, se_ref, ge_ref, pre_ref, st_ref, g_ref, o_ref = k.i
        delta_ref, t_off, t_gain, d_next, pay_ref = k.o
        rows_ref, sum_ref, tmp = k.x
        back_start((got_ref, d_ref, pe_ref, se_ref, ge_ref), mates_ref, sum_ref, delta_ref, q, z.rows, (t_off, t_gain))
        k.send(0)
        k.wait_w()
        tmp[...] = dot_nt(delta_ref[...], k.w[0][...])
        for m in range(MICRO):
            at = pl.ds(m * z.rows, z.rows)
            for c in range(qo):
                slope_and_sums(tmp[at, cols(c)], pre_ref, at, st_ref, m, qo, c, g_ref, o_ref, d_next, rows_ref)
        fill(pay_ref, rows_ref)

    rows = MICRO * z.rows
    return kernel_call(
        body,
        [arr(rows, z.c_in, dtype=BF)] + [arr(q, LANES)] * 2 + [arr(rows, z.c_mid), arr(z.n, 6 * qo, LANES, dtype=BF)],
        [got, mates, d, pre_e, st_e, gain_e, pre, st, gain, offset],
        [w],
        [
            pltpu.VMEM((6 * qo, LANES), F32),
            pltpu.VMEM((6 * q, LANES), F32),
            pltpu.VMEM((rows, z.c_mid), F32),
        ],
        flops=2 * rows * z.c_in * z.c_mid,
        passes=passes,
    )


def k_back_spatial(got, mates, d, pre_s, st_s, gain_s, pre, st, gain, offset, w, z, passes=()):
    q = z.q1

    def body(k):
        got_ref, mates_ref, d_ref, ps_ref, ss_ref, gs_ref, pre_ref, st_ref, g_ref, o_ref = k.i
        delta_ref, t_off, t_gain, d_next, pay_ref = k.o
        rows_ref, sum_ref, patch_ref, tmp = k.x
        merge_sums(got_ref, mates_ref, sum_ref, q, z.rows, (t_off, t_gain))
        for m in range(MICRO):
            for c in range(q):
                phase = {}
                for i, p in enumerate(PHASES):
                    at = pl.ds(m * z.rows + i * z.half, z.half)
                    phase[p] = back_rows(
                        ps_ref[at, cols(c)], d_ref[at, cols(c)], ss_ref, sum_ref, m, q, c, gs_ref[:, cols(c)]
                    )
                    delta_ref[at, cols(c)] = phase[p].astype(BF)
                write_patches(phase, patch_ref, m, z.half, c, z.c_mid, -1)
        k.send(0)
        k.wait_w()
        tmp[...] = dot(patch_ref[...], k.w[0][...])
        for m in range(MICRO):
            at = pl.ds(m * z.rows, z.rows)
            for c in range(q):
                slope_and_sums(tmp[at, cols(c)], pre_ref, at, st_ref, m, q, c, g_ref, o_ref, d_next, rows_ref)
        fill(pay_ref, rows_ref)

    rows = MICRO * z.rows
    return kernel_call(
        body,
        [arr(rows, z.c_mid, dtype=BF)] + [arr(q, LANES)] * 2 + [arr(rows, z.c_mid), arr(z.n, 6 * q, LANES, dtype=BF)],
        [got, mates, d, pre_s, st_s, gain_s, pre, st, gain, offset],
        [w],
        [
            pltpu.VMEM((6 * q, LANES), F32),
            pltpu.VMEM((6 * q, LANES), F32),
            pltpu.VMEM((rows, 9 * z.c_mid), BF),
            pltpu.VMEM((rows, z.c_mid), F32),
        ],
        flops=2 * rows * 9 * z.c_mid * z.c_mid,
        passes=passes,
    )


def k_back_reduce(got, mates, d, pre_r, st_r, gain_r, z, passes=()):
    q = z.q1

    def body(k):
        got_ref, mates_ref, d_ref, pr_ref, sr_ref, gr_ref = k.i
        delta_ref, t_off, t_gain = k.o
        (sum_ref,) = k.x
        back_start((got_ref, d_ref, pr_ref, sr_ref, gr_ref), mates_ref, sum_ref, delta_ref, q, z.rows, (t_off, t_gain))

    rows = MICRO * z.rows
    return kernel_call(
        body,
        [arr(rows, z.c_mid, dtype=BF)] + [arr(q, LANES)] * 2,
        [got, mates, d, pre_r, st_r, gain_r],
        scratch=[pltpu.VMEM((6 * q, LANES), F32)],
        passes=passes,
    )


def k_input(delta, d_one, w, z, passes=()):
    def body(k):
        (delta_ref, one_ref), (out_ref,), (tmp, line) = k.i, k.o, k.x
        k.wait_w()
        tmp[...] = dot_nt(delta_ref[...], k.w[0][...])
        for m in range(MICRO):
            for y in range(z.height):
                for c in range(z.q3):
                    for px in range(2):
                        at = pl.ds(m * z.rows + (2 * (y % 2) + px) * z.half + (y // 2) * 8, 8)
                        line[c, pl.ds((y * MICRO + m) * z.cols + px, 8, stride=2), :] = (
                            one_ref[at, cols(c)] + tmp[at, cols(c)]
                        )
                    out_ref[y, m, :, cols(c)] = line[c, pl.ds((y * MICRO + m) * z.cols, z.cols), :].astype(BF)

    rows = MICRO * z.rows
    return kernel_call(
        body,
        [arr(z.height, MICRO, z.cols, z.c_in, dtype=BF)],
        [delta, d_one],
        [w],
        [pltpu.VMEM((rows, z.c_in), F32), pltpu.VMEM((z.q3, rows, LANES), F32)],
        flops=2 * rows * z.c_in * z.c_mid,
        passes=passes,
    )


def k_even(delta, w, z):
    def body(k):
        k.wait_w()
        k.o[0][...] = dot_nt(k.i[0][...], k.w[0][...])

    rows = delta.shape[0]
    return kernel_call(body, [arr(rows, z.c_in)], [delta], [w], flops=2 * rows * z.c_in * z.c_out)[0]


def k_first_grads(outs, evens, pieces, z):
    some = z.c_out // z.g
    a, b = z.c_wide // z.ns, z.c_in // z.ns

    def body(k):
        lhs_w, lhs_s, rhs = k.st
        held_w, held_s = k.x
        held_w[...] = dot_tn(lhs_w[...], rhs[:, :some]).astype(BF)
        for s in range(z.ns):
            k.copy(held_w.at[pl.ds(s * a, a)], k.raw[0].at[s % z.slo, s // z.slo, pl.ds(0, a)])
        held_s[...] = dot_tn(lhs_s[...], rhs[:, some:]).astype(BF)
        for s in range(z.ns):
            k.copy(held_s.at[pl.ds(s * b, b)], k.raw[0].at[s % z.slo, s // z.slo, pl.ds(a, b)])

    return kernel_call(
        body,
        [],
        [],
        scratch=[pltpu.VMEM((z.c_wide, some), BF), pltpu.VMEM((z.c_in, some), BF)],
        stacks=[outs, evens, pieces],
        raw=[arr(z.slo, z.ns // z.slo, a + b, some, dtype=BF)],
        n_raw=2 * z.ns,
        flops=2 * z.g * outs[0].shape[0] * (z.c_in + z.c_wide) * some,
    )[0]


def k_stride_grads(maps, pieces, z):
    few = z.c_wide // z.g
    c = 9 * z.c_wide // z.ns
    wide = z.c_out // z.c_wide
    d = c // wide
    rows = z.g * pieces[0].shape[0]

    def body(k):
        map_ref, rhs = k.st
        held, lhs = k.x
        for m in range(z.g * MICRO):
            for col in range(z.q4):
                phase = {}
                for i, p in enumerate(PHASES):
                    phase[p] = map_ref[pl.ds(m * z.rows + i * z.half, z.half), cols(col)].astype(F32)
                write_patches(phase, lhs, m, z.half, col, z.c_wide, 1, ((0, 0),))
        for t in range(9):
            at = pl.ds(t * z.c_wide, z.c_wide)
            held[at] = dot_tn(lhs[:, at], rhs[...]).astype(BF)
        for s in range(z.ns):
            for part in range(wide):
                k.copy(
                    held.at[pl.ds(s * c + part * d, d)],
                    k.raw[0].at[s % z.slo, s // z.slo, :, pl.ds(part * few, few)],
                )

    return kernel_call(
        body,
        [],
        [],
        scratch=[pltpu.VMEM((9 * z.c_wide, few), BF), pltpu.VMEM((rows, 9 * z.c_wide), BF)],
        stacks=[maps, pieces],
        raw=[arr(z.slo, z.ns // z.slo, d, wide * few, dtype=BF)],
        n_raw=wide * z.ns,
        flops=2 * rows * 9 * z.c_wide * few,
    )[0]


def k_products(pairs, place, z, passes=()):
    hi = z.ns // z.slo
    widths = [(o.shape[1], g.shape[1]) for o, g in pairs]
    rows = [r // z.n * c // 256 for r, c in widths]
    total = sum(rows)

    def body(k):
        (held,) = k.x
        at = 0
        for j, (r, c) in enumerate(widths):
            product = dot_tn(k.i[2 * j][...], k.i[2 * j + 1][...])
            blocks = product.reshape(hi, z.slo, z.nb // 2, 2, r // z.n, c).astype(BF)
            for part in range(c // 256):
                held[:, :, :, :, pl.ds(at, r // z.n), :] = blocks[..., part * 256 : (part + 1) * 256]
                at += r // z.n
        core = k.s[0][0] & 1
        k.copy(held.at[:, :, :, core], k.raw[0])
        k.copy(held.at[:, :, :, 1 - core], k.raw[1])

    return kernel_call(
        body,
        [],
        [a for pair in pairs for a in pair],
        scratch=[pltpu.VMEM((hi, z.slo, z.nb // 2, 2, total, 256), BF)],
        raw=[arr(hi, z.slo, z.nb // 2, total, 256, dtype=BF)] * 2,
        n_raw=2,
        scalars=[place],
        passes=passes,
        flops=sum(2 * pairs[j][0].shape[0] * r * c for j, (r, c) in enumerate(widths)),
    )


def k_sum_plane(groups, where, z, early=()):
    hi, high = z.ns // z.slo, z.nb // 2
    rows = [g[0].shape[3] for g in groups]

    tall = [e.shape[1] for e in early]

    def body(k):
        (held,) = k.x
        top = 0
        for e, r in zip(k.i[2 * len(groups) :], tall):
            k.copy(e, k.raw[-1].at[:, pl.ds(top, r)])
            top += r
        at = 0
        for j, r in enumerate(rows):
            both = k.i[2 * j][...].astype(F32) + k.i[2 * j + 1][...].astype(F32)
            held[:, :, :, pl.ds(at, r), :] = both.astype(BF)
            at += r
        for i in range(high):
            for j in range(z.slo):
                k.copy(held.at[:, k.s[0][0] ^ j, k.s[0][1] ^ i], k.raw[z.slo * i + j])

    total = sum(rows)
    return kernel_call(
        body,
        [],
        [a for g in groups for a in g] + list(early),
        scratch=[pltpu.VMEM((hi, z.slo, high, total, 256), BF)],
        raw=[arr(hi, total, 256, dtype=BF)] * (z.slo * high)
        + ([arr(hi, sum(tall), early[0].shape[2], dtype=BF)] if early else []),
        n_raw=z.slo * high + len(early),
        scalars=[where],
    )


def k_sum_line(groups, where, z, passes=()):
    hi = z.ns // z.slo
    rows = [g[0].shape[1] for g in groups]
    n = len(groups[0])

    def body(k):
        (held,) = k.x
        at = 0
        for j, r in enumerate(rows):
            value = k.i[j * n][...].astype(F32)
            for other in range(1, n):
                value = value + k.i[j * n + other][...].astype(F32)
            held[:, pl.ds(at, r), :] = value.astype(BF)
            at += r
        for j in range(hi):
            k.copy(held.at[k.s[0][2] ^ j], k.raw[j])

    total = sum(rows)
    return kernel_call(
        body,
        [],
        [a for g in groups for a in g],
        scratch=[pltpu.VMEM((hi, total, 256), BF)],
        raw=[arr(total, 256, dtype=BF)] * hi,
        n_raw=hi,
        scalars=[where],
        passes=passes,
    )


def k_sum_last(parts, passes=()):
    def body(k):
        value = k.i[0][...].astype(F32)
        for other in k.i[1:]:
            value = value + other[...].astype(F32)
        k.o[0][...] = value.astype(BF)

    return kernel_call(body, [arr(*parts[0].shape, dtype=BF)], parts, passes=passes)


def k_late_shares(pieces, place, shapes, z, passes=()):
    n = z.nb
    total = pieces[0].shape[0]

    def body(k):
        (held,) = k.x
        for j in range(n):
            held[k.s[0][0] ^ j] = k.i[j][...]
        for j in range(n):
            value = held[j].astype(F32)
            at = 0
            for g, (r, c) in enumerate(shapes):
                r = r // z.n
                for part in range(c // 256):
                    k.o[g][pl.ds(j * r, r), pl.ds(part * 256, 256)] = value[at : at + r]
                    at += r

    return kernel_call(
        body,
        [arr(r // z.ns, c) for r, c in shapes],
        list(pieces),
        scratch=[pltpu.VMEM((n, total, 256), BF)],
        scalars=[place],
        passes=passes,
    )


def k_early_shares(pieces, place, z):
    n = z.g
    some, few = z.c_out // n, z.c_wide // n
    a, b, c = z.c_wide // z.ns, z.c_in // z.ns, 9 * z.c_wide // z.ns
    d = c * few // some

    def body(k):
        (held,) = k.x
        for j in range(n):
            held[(k.s[0][0] & (n - 1)) ^ j] = k.i[j][...]
        for j in range(n):
            value = held[j].astype(F32)
            k.o[0][:, pl.ds(j * some, some)] = value[:a]
            k.o[1][:, pl.ds(j * some, some)] = value[a : a + b]
            for part in range(some // few):
                k.o[2][pl.ds(part * d, d), pl.ds(j * few, few)] = value[a + b :, part * few : (part + 1) * few]

    return kernel_call(
        body,
        [arr(a, z.c_out), arr(b, z.c_out), arr(c, z.c_wide)],
        list(pieces),
        scratch=[pltpu.VMEM((n, a + b + d, some), BF)],
        scalars=[place],
    )


def on_device(
    features,
    view_ids,
    w_reduce,
    w_spatial,
    w_expand,
    w_narrow,
    w_stride,
    w_widen,
    w_shortcut,
    gain_reduce,
    offset_reduce,
    gain_spatial,
    offset_spatial,
    gain_expand,
    offset_expand,
    gain_narrow,
    offset_narrow,
    gain_stride,
    offset_stride,
    gain_widen,
    offset_widen,
    gain_shortcut,
    offset_shortcut,
    cotangent,
):
    z = Sizes()
    z.ns, z.nb = lax.axis_size(SPACE), lax.axis_size(BATCH)
    z.slo = lax.axis_size("slo")
    z.g = min(z.nb, 4)
    z.n = z.ns * z.nb
    z.maps, z.cols = features.shape[1], features.shape[3]
    z.height = z.ns
    z.rows = z.height * z.cols
    z.half = z.rows // 4
    z.c_in, z.c_mid = w_reduce.shape
    z.c_wide, z.c_out = w_widen.shape
    z.q1, z.q3, z.q4, z.q6 = (c // LANES for c in (z.c_mid, z.c_in, z.c_wide, z.c_out))
    assert features.shape[2] == 1 and cotangent.shape[1] == 1 and z.maps == z.ns and z.cols == 16
    yh, xh = z.height // 2, z.cols // 2
    n, ns, nb = z.n, z.ns, z.nb
    s, b = lax.axis_index(SPACE), lax.axis_index(BATCH)
    place = b.astype(jnp.int32).reshape(1)

    def share(pay):
        return lax.all_to_all(pay, ALL, 0, 0, tiled=True)

    def exchange(block):
        return lax.all_to_all(block, SPACE, 0, 0, tiled=True)

    def swap(block, axis, distance):
        return lax.ppermute(block, axis, [(i, i ^ distance) for i in range(lax.axis_size(axis))])

    def trade(pieces):
        pairs = [(i, i ^ j) for j in range(z.g) for i in range(nb)]
        return [p if j == 0 else lax.ppermute(p, BATCH, pairs[j * nb : (j + 1) * nb]) for j, p in enumerate(pieces)]

    def everywhere(block, places):
        pieces = []
        for high in range(places // 2):
            other = swap(block, "bhi", high) if high else block
            pieces += [other, swap(other, "core", 1)]
        return pieces

    def over_groups(product):
        distance = z.g // 2
        while distance < nb // 2:
            product = (product.astype(F32) + swap(product, "bhi", distance).astype(F32)).astype(BF)
            distance *= 2
        return product

    def lines(vector):
        return vector.reshape(1, -1)

    vectors = {
        "reduce": (lines(gain_reduce), lines(offset_reduce)),
        "spatial": (lines(gain_spatial), lines(offset_spatial)),
        "expand": (lines(gain_expand), lines(offset_expand)),
        "narrow": (lines(gain_narrow), lines(offset_narrow)),
        "stride": (lines(gain_stride), lines(offset_stride)),
        "widen": (lines(gain_widen), lines(offset_widen)),
        "shortcut": (lines(gain_shortcut), lines(offset_shortcut)),
    }

    my_ids = lax.dynamic_slice_in_dim(view_ids, s, 1, 1).astype(F32)
    arrived = exchange(features.reshape(MICRO, z.maps, z.cols, z.c_in).transpose(1, 0, 2, 3))
    pre_reduce, pay = k_reduce(arrived, my_ids.reshape(MICRO), w_reduce, z)
    got = share(pay)
    ids = got[:, 9 * z.q1 : 9 * z.q1 + MICRO].astype(F32)
    same = (ids == my_ids[None]).astype(F32)
    mates = {q: jnp.repeat(same, q, axis=1) for q in (z.q3, z.q4)}
    id_rows = jnp.concatenate([ids, ids, jnp.zeros((n, 2, LANES), F32)], axis=1)

    maps_in = arrived.reshape(yh, 2, MICRO, xh, 2, z.c_in).transpose(2, 1, 4, 0, 3, 5)
    maps_in = maps_in.reshape(MICRO * z.rows, z.c_in)

    patch_reduce, pre_spatial, pay, st_reduce, mates[z.q1] = k_spatial(
        got, my_ids.reshape(MICRO), pre_reduce, *vectors["reduce"], w_spatial, z
    )
    got = share(pay)
    out_spatial, pre_expand, pay, st_spatial = k_expand(got, mates[z.q1], pre_spatial, *vectors["spatial"], w_expand, z)
    got = share(pay)
    residual_one, joined, even, pre_narrow, pay, st_expand = k_narrow(
        got, mates[z.q3], pre_expand, *vectors["expand"], maps_in, w_narrow, z
    )
    evens = everywhere(even, z.g)
    got = share(pay)
    pre_shortcut, short_st = k_shortcut(even, w_shortcut, z)
    out_narrow, pre_stride, pay, st_narrow = k_stride(
        got, mates[z.q4], pre_narrow, *vectors["narrow"], w_stride, z
    )
    got = share(pay)
    outs_narrow = everywhere(out_narrow, z.g)
    out_stride, pre_widen, pay, st_stride = k_widen(
        got, mates[z.q4], pre_stride, *vectors["stride"], short_st, w_widen, z
    )
    outs_stride = everywhere(out_stride, z.g)
    whole = share(k_views(share(pay), id_rows, z))
    mapped, d_two, pay = k_mapped(
        whole,
        pre_widen,
        pre_shortcut,
        cotangent.reshape(-1, z.c_out),
        (*vectors["widen"], *vectors["shortcut"]),
        z,
    )

    sums = share(k_view_sums(share(pay), id_rows, z))
    delta_shortcut, go_widen, gg_widen, gg_shortcut, d_stride, pay, *more = k_back_widen(
        whole, sums, d_two, pre_widen, pre_shortcut, vectors["widen"][0], vectors["shortcut"][0],
        pre_stride, st_stride, *vectors["stride"], place, w_widen, z, (*outs_narrow, *evens, *outs_stride),
    )
    got = share(pay)
    pieces, outs_narrow, evens, outs_stride = (more[j * z.g : (j + 1) * z.g] for j in range(4))
    d_even = k_even(delta_shortcut, w_shortcut, z)
    first_pieces = trade(pieces)
    go_stride, gg_stride, d_narrow, pay, *more = k_back_stride(
        got, mates[z.q4], d_stride, pre_stride, st_stride, vectors["stride"][0],
        pre_narrow, st_narrow, *vectors["narrow"], place, w_stride, z, (*first_pieces, d_even),
    )
    pieces, first_pieces, d_even = more[: z.g], more[z.g : 2 * z.g], more[2 * z.g]
    got = share(pay)
    first = k_first_grads(outs_stride, evens, first_pieces, z)
    first = over_groups(first)
    pieces = trade(pieces)
    delta_narrow, go_narrow, gg_narrow, d_one, pay, first, *pieces = k_back_narrow(
        got, mates[z.q4], d_narrow, pre_narrow, st_narrow, vectors["narrow"][0],
        d_even, residual_one, pre_expand, st_expand, w_narrow, z, (first, *pieces),
    )
    got = share(pay)
    first = lax.psum_scatter(first, "slo", scatter_dimension=0, tiled=True)
    second = over_groups(k_stride_grads(outs_narrow, pieces, z))

    delta_expand, go_expand, gg_expand, d_spatial, pay, second = k_back_expand(
        got, mates[z.q3], d_one, pre_expand, st_expand, vectors["expand"][0],
        pre_spatial, st_spatial, *vectors["spatial"], w_expand, z, (second,),
    )
    got = share(pay)
    second = lax.psum_scatter(second, "slo", scatter_dimension=0, tiled=True)
    blocks = all(w.shape[0] % (8 * n) == 0 for w in (w_reduce, w_spatial, w_expand, w_narrow))
    pairs_some = [(joined, delta_narrow), (out_spatial, delta_expand)]
    kept_some, sent_some = k_products(pairs_some, place, z) if blocks else (None, delta_expand)
    flipped = w_spatial.reshape(9, z.c_mid, z.c_mid).transpose(0, 2, 1).reshape(9 * z.c_mid, z.c_mid)
    delta_spatial, go_spatial, gg_spatial, d_reduce, pay, sent_some, first = k_back_spatial(
        got, mates[z.q1], d_spatial, pre_spatial, st_spatial, vectors["spatial"][0],
        pre_reduce, st_reduce, *vectors["reduce"], flipped, z, (sent_some, first),
    )
    got = share(pay)
    pairs_more = [(patch_reduce, delta_spatial)]
    kept_more, sent_more = k_products(pairs_more, place, z) if blocks else (None, delta_spatial)
    came_some = swap(sent_some, "core", 1) if blocks else sent_some
    where = jnp.stack([lax.axis_index("slo"), lax.axis_index("bhi"), lax.axis_index("shi")]).astype(jnp.int32)

    def over_plane(groups, early):
        high = nb // 2
        parts = k_sum_plane(groups, where, z, early)
        came = []
        for i in range(high):
            for j in range(z.slo):
                pairs = [(u * z.slo + v, (u ^ i) * z.slo + (v ^ j)) for u in range(high) for v in range(z.slo)]
                part = parts[i * z.slo + j]
                came.append(lax.ppermute(part, ("bhi", "slo"), pairs) if i or j else part)
        return came, parts[high * z.slo :]

    delta_reduce, go_reduce, gg_reduce, sent_more, came_some = k_back_reduce(
        got, mates[z.q1], d_reduce, pre_reduce, st_reduce, vectors["reduce"][0], z, (sent_more, came_some)
    )
    pairs_last, passed = [(maps_in, delta_reduce)], ()
    if blocks:
        kept_last, sent_last = k_products(pairs_last, place, z)
        groups = [(kept_some, came_some), (kept_more, swap(sent_more, "core", 1)), (kept_last, swap(sent_last, "core", 1))]
        passed, (early,) = over_plane(groups, (first[0], second[0]))
    else:
        early = jnp.concatenate([first[0], second[0]], axis=1)
    left, *passed = k_input(delta_reduce, d_one, w_reduce, z, passed)
    left = exchange(left)
    early = lax.psum_scatter(early, "shi", scatter_dimension=0, tiled=True)
    if blocks:
        *parts, early = k_sum_line([passed], where, z, (early,))
        early = k_early_shares(everywhere(early[0], z.g), place, z)
        parts = [p if j == 0 else swap(p, "shi", j) for j, p in enumerate(parts)]
        late, *early = k_sum_last(parts, early)
        late = everywhere(late, nb)
        shapes = [w.shape for w in (w_narrow, w_expand, w_spatial, w_reduce)]
        late = k_late_shares(late, place, shapes, z)
        grad_w_narrow, grad_w_expand, grad_w_spatial, grad_w_reduce = late
    else:
        late = [dot_tn(o, g).astype(BF) for o, g in pairs_some + pairs_more + pairs_last]
        late = [lax.psum_scatter(w, SPACE, scatter_dimension=0, tiled=True) for w in late]
        late = [w.astype(F32) for w in lax.psum(late, BATCH)]
        grad_w_narrow, grad_w_expand, grad_w_spatial, grad_w_reduce = late
        early = k_early_shares(everywhere(early[0], z.g), place, z)
    grad_w_widen, grad_w_shortcut, grad_w_stride = early
    grad_features = left.transpose(1, 0, 2, 3).reshape(features.shape)

    flat = lambda block: block.reshape(-1)
    return (
        mapped.reshape(cotangent.shape),
        grad_features,
        grad_w_reduce,
        grad_w_spatial,
        grad_w_expand,
        grad_w_narrow,
        grad_w_stride,
        grad_w_widen,
        grad_w_shortcut,
        flat(gg_reduce),
        flat(go_reduce),
        flat(gg_spatial),
        flat(go_spatial),
        flat(gg_expand),
        flat(go_expand),
        flat(gg_narrow),
        flat(go_narrow),
        flat(gg_stride),
        flat(go_stride),
        flat(gg_widen),
        flat(go_widen),
        flat(gg_shortcut),
        flat(go_widen),
    )


def solution(mesh):
    nb, ns = mesh.shape["batch"], mesh.shape["space"]
    fine = Mesh(mesh.devices.reshape(nb // 2, 2, ns // 2, 2), ALL)
    maps = P(None, ALL, None, None, None)
    return jax.shard_map(
        on_device,
        mesh=fine,
        in_specs=(P(None, BATCH, SPACE, None, None), P(None, BATCH)) + (P(),) * 21 + (maps,),
        out_specs=(maps, P(None, BATCH, SPACE, None, None)) + (P(SPACE, None),) * 7 + (P(),) * 14,
        check_vma=False,
    )
```

```python
import functools
import math

import jax
import jax.numpy as jnp
from jax import lax
from jax.experimental import pallas as pl
from jax.experimental.pallas import tpu as pltpu
from jax.sharding import Mesh
from jax.sharding import PartitionSpec as P

NVIEW = 2
MICRO = 3
EPSILON = 1e-05
BF = jnp.bfloat16
F32 = jnp.float32
BATCH, SPACE = ("bhi", "core"), ("shi", "slo")
ALL = BATCH + SPACE
LANES = 128
ROOT = math.sqrt(2.0 / math.pi)
CUBE = 0.044715


def dot(a, b, dims=((1,), (0,))):
    return lax.dot_general(a, b, (dims, ((), ())), preferred_element_type=F32)


def dot_nt(a, b):
    return dot(a, b, ((1,), (1,)))


def dot_tn(a, b):
    return dot(a, b, ((0,), (0,)))


def gelu(v):
    return 0.5 * v * (1.0 + jnp.tanh(ROOT * (v + CUBE * (v * v * v))))


def gelu_slope(v):
    square = v * v
    t = jnp.tanh(ROOT * (v + CUBE * (square * v)))
    return 0.5 * (1.0 + t) + (0.5 * ROOT) * v * (1.0 - t * t) * (1.0 + (3.0 * CUBE) * square)


def gelu_both(v):
    square = v * v
    t = jnp.tanh(ROOT * (v + CUBE * (square * v)))
    half = 0.5 * (1.0 + t)
    return v * half, half + (0.5 * ROOT) * v * (1.0 - t * t) * (1.0 + (3.0 * CUBE) * square)


def cols(c):
    return pl.ds(c * LANES, LANES)


def row(ref, r):
    return ref[pl.ds(r, 1), :]


class Kernel:
    def __init__(self, i, w, o, raw, scalars, stacks, extra, starts, sems):
        self.i, self.w, self.o, self.raw, self.s, self.st, self.x = i, w, o, raw, scalars, stacks, extra
        self.w_copies, self.out_pairs, self.sems = starts, {}, sems
        self.flying, self.sent = [], set()

    def wait_w(self, n=0, chunk=None):
        for copy in self.w_copies[n] if chunk is None else [self.w_copies[n][chunk]]:
            copy.wait()

    def send(self, n):
        src, dst, sem = self.out_pairs[n]
        copy = pltpu.make_async_copy(src, dst, sem)
        copy.start()
        self.flying.append(copy)
        self.sent.add(n)

    def copy(self, src, dst):
        copy = pltpu.make_async_copy(src, dst, self.sems.pop())
        copy.start()
        self.flying.append(copy)


def kernel_call(body, outs, args, weights=(), scratch=(), flops=0, raw=(), n_raw=0, scalars=(), passes=(), stacks=(), limit=63, chunks=1):
    n_s, n_in, n_w, n_p = len(scalars), len(args), len(weights), len(passes)
    n_k = sum(map(len, stacks))
    n_out, n_r = len(outs), len(raw)

    def run(*refs):
        refs = list(refs)

        def take(n):
            part = refs[:n]
            del refs[:n]
            return part

        s, ins, w_any = take(n_s), take(n_in), take(n_w)
        piles = [take(len(g)) for g in stacks]
        take(n_p)
        out, raw_refs, _ = take(n_out), take(n_r), take(n_p)
        v_in, v_w, v_out, v_k = take(n_in), take(n_w), take(n_out), take(len(stacks))
        (sems,) = take(1)
        sem = [sems.at[j] for j in range(n_in + n_w * chunks + n_k + n_out + n_raw)]
        in_copies = [pltpu.make_async_copy(a, v, sem.pop(0)) for a, v in zip(ins, v_in)]
        for pile, v in zip(piles, v_k):
            for j, a in enumerate(pile):
                rows = a.shape[0]
                in_copies.append(pltpu.make_async_copy(a, v.at[pl.ds(j * rows, rows)], sem.pop(0)))
        w_copies = []
        for a, v in zip(w_any, v_w):
            some = a.shape[0] // chunks
            parts = [pl.ds(j * some, some) for j in range(chunks)]
            w_copies.append([pltpu.make_async_copy(a.at[at], v.at[at], sem.pop(0)) for at in parts])
        for copy in in_copies + [c for copies in w_copies for c in copies]:
            copy.start()
        k = Kernel(v_in, v_w, v_out, raw_refs, s, v_k, refs, w_copies, sem[n_out:])
        k.out_pairs = {j: (v_out[j], out[j], sem[j]) for j in range(n_out)}
        for copy in in_copies:
            copy.wait()
        body(k)
        for j in range(n_out):
            if j not in k.sent:
                k.send(j)
        for copy in k.flying:
            copy.wait()

    def size(a):
        return math.prod(a.shape) * jnp.dtype(a.dtype).itemsize

    outside = pl.BlockSpec(memory_space=pl.ANY)
    piled = [arr(len(g) * g[0].shape[0], *g[0].shape[1:], dtype=g[0].dtype) for g in stacks]
    held = sum(map(size, (*args, *weights, *outs, *piled)))
    total = held + sum(size(a) for a in scratch if hasattr(a, "dtype"))
    first = n_s + n_in + n_w + n_k
    results = pl.pallas_call(
        run,
        out_shape=tuple(jax.ShapeDtypeStruct(o.shape, o.dtype) for o in (*outs, *raw, *passes)),
        in_specs=[pl.BlockSpec(memory_space=pltpu.SMEM)] * n_s + [outside] * (n_in + n_w + n_k + n_p),
        out_specs=tuple([outside] * (n_out + n_r + n_p)),
        scratch_shapes=[pltpu.VMEM(a.shape, a.dtype) for a in (*args, *weights, *outs, *piled)]
        + [pltpu.SemaphoreType.DMA((n_in + n_w * chunks + n_k + n_out + n_raw,))]
        + list(scratch),
        input_output_aliases={first + j: n_out + n_r + j for j in range(n_p)},
        cost_estimate=pl.CostEstimate(flops=flops, bytes_accessed=held, transcendentals=0),
        compiler_params=pltpu.CompilerParams(vmem_limit_bytes=max(limit * 2**20, total)),
    )(*scalars, *args, *weights, *(a for g in stacks for a in g), *passes)
    return tuple(results)


def arr(*shape, dtype=F32):
    return jax.ShapeDtypeStruct(shape, dtype)


def fill(pay_ref, rows_ref):
    block = rows_ref[...].astype(pay_ref.dtype)

    def step(j, _):
        pay_ref[j] = block
        return 0

    lax.fori_loop(0, pay_ref.shape[0], step, 0, unroll=8)


def stats_rows(value, rows_ref, r, size, offset):
    mean = jnp.sum(value, axis=0, keepdims=True) * (1.0 / size)
    away = value - mean
    rows_ref[pl.ds(r, 1), :] = mean
    rows_ref[pl.ds(r + offset, 1), :] = jnp.sum(away * away, axis=0, keepdims=True)


def stats_shape(q):
    return 9 * q, BF


def stats_arr(n, q):
    rows, dtype = stats_shape(q)
    return arr(n, rows, LANES, dtype=dtype)


def fill_stats(pay_ref, rows_ref, q):
    k = MICRO * q
    if pay_ref.dtype == BF:
        mean, square = rows_ref[:k], rows_ref[k : 2 * k]
        high = mean.astype(BF).astype(F32)
        rows_ref[:k] = high
        rows_ref[k : 2 * k] = mean - high
        rows_ref[2 * k : 3 * k] = square
    fill(pay_ref, rows_ref)


def merge_stats(got_ref, mates_ref, st_ref, q, size):
    n = got_ref.shape[0]
    k = MICRO * q
    mates = n // NVIEW
    step = 8

    def parts(at):
        got = got_ref[at].astype(F32)
        if got_ref.dtype == BF:
            return got[:, :k] + got[:, k : 2 * k], got[:, 2 * k : 3 * k]
        return got[:, :k], got[:, k : 2 * k]

    def one(i, acc):
        at = pl.ds(i * step, step)
        return acc + jnp.sum(mates_ref[at] * parts(at)[0], axis=0)

    mean = lax.fori_loop(0, n // step, one, jnp.zeros((k, LANES), F32), unroll=4) * (1.0 / mates)

    def two(i, acc):
        at = pl.ds(i * step, step)
        means, squares = parts(at)
        away = means - mean[None]
        return acc + jnp.sum(mates_ref[at] * (squares + size * (away * away)), axis=0)

    total = lax.fori_loop(0, n // step, two, jnp.zeros((k, LANES), F32), unroll=4)
    st_ref[:k] = mean
    st_ref[k : 2 * k] = lax.rsqrt(total * (1.0 / (mates * size)) + EPSILON)


def merge_sums(got_ref, mates_ref, sum_ref, q, size, total_refs):
    n = got_ref.shape[0]
    k = MICRO * q
    scale = 1.0 / (n // NVIEW * size)
    step = 8

    def one(i, carry):
        at = pl.ds(i * step, step)
        both = got_ref[at].astype(F32)
        first, second = both[:, :k], both[:, k : 2 * k]
        w = mates_ref[at]
        return (
            carry[0] + jnp.sum(w * first, axis=0),
            carry[1] + jnp.sum(w * second, axis=0),
            carry[2] + jnp.sum(first, axis=0),
            carry[3] + jnp.sum(second, axis=0),
        )

    zero = jnp.zeros((k, LANES), F32)
    a, b, ta, tb = lax.fori_loop(0, n // step, one, (zero,) * 4, unroll=4)
    sum_ref[:k] = a * scale
    sum_ref[k : 2 * k] = b * scale
    for ref, t in zip(total_refs, (ta, tb)):
        ref[...] = t[:q] + t[q : 2 * q] + t[2 * q :]


def shift_y(v, offset):
    if offset == 0:
        return v
    zero = jnp.zeros((8, v.shape[1]), v.dtype)
    if offset > 0:
        return jnp.concatenate([v[8:], zero], axis=0)
    return jnp.concatenate([zero, v[:-8]], axis=0)


def shift_x(v, offset):
    if offset == 0:
        return v
    place = lax.broadcasted_iota(jnp.int32, v.shape, 0) % 8
    if offset > 0:
        return jnp.where(place == 7, 0.0, pltpu.roll(v, v.shape[0] - 1, axis=0))
    return jnp.where(place == 0, 0.0, pltpu.roll(v, 1, axis=0))


def write_patches(phase, patch_ref, m, half, c, width, sign, out_phases=((0, 0), (0, 1), (1, 0), (1, 1))):
    moved = {}

    def get(sy, sx, ox):
        if (sy, sx, ox) not in moved:
            moved[sy, sx, ox] = shift_x(phase[sy, sx], ox)
        return moved[sy, sx, ox]

    for i, (py, px) in enumerate(out_phases):
        for r in range(3):
            for k in range(3):
                at_y, at_x = py + sign * (r - 1), px + sign * (k - 1)
                piece = shift_y(get(at_y % 2, at_x % 2, at_x // 2), at_y // 2)
                rows = pl.ds((m * len(out_phases) + i) * half, half)
                patch_ref[rows, pl.ds((r * 3 + k) * width + c * LANES, LANES)] = piece.astype(BF)


PHASES = ((0, 0), (0, 1), (1, 0), (1, 1))


class Sizes:
    pass


def k_reduce(x, ids, w, z):
    q = z.q1

    def body(k):
        (x_ref,), (map_ref, pay_ref), (tmp, rows_ref) = k.i, k.o, k.x
        k.wait_w()
        for y in range(z.height):
            product = dot(x_ref[y].reshape(MICRO * z.cols, z.c_in), k.w[0][...])
            for c in range(q):
                tmp[c, pl.ds(y * MICRO * z.cols, MICRO * z.cols), :] = product[:, c * LANES : (c + 1) * LANES]
        for m in range(MICRO):
            for y in range(z.height):
                for px in range(2):
                    at = m * z.rows + (2 * (y % 2) + px) * z.half + (y // 2) * 8
                    for c in range(q):
                        map_ref[pl.ds(at, 8), cols(c)] = tmp[
                            c, pl.ds((y * MICRO + m) * z.cols + px, 8, stride=2), :
                        ]
        rows_ref[...] = jnp.zeros(rows_ref.shape, F32)
        for m in range(MICRO):
            for c in range(q):
                stats_rows(map_ref[pl.ds(m * z.rows, z.rows), cols(c)], rows_ref, m * q + c, z.rows, MICRO * q)
        for m in range(MICRO):
            rows_ref[pl.ds(9 * q + m, 1), :] = jnp.full((1, LANES), k.s[0][m], F32)
        fill_stats(pay_ref, rows_ref, q)

    rows, pad = MICRO * z.rows, -(-(9 * q + MICRO) // 8) * 8
    return kernel_call(
        body,
        [arr(rows, z.c_mid), arr(z.n, pad, LANES, dtype=BF)],
        [x],
        [w],
        [pltpu.VMEM((q, rows, LANES), F32), pltpu.VMEM((pad, LANES), F32)],
        flops=2 * rows * z.c_in * z.c_mid,
        scalars=[ids],
        limit=24,
    )


def k_spatial(got, ids, pre, gain, offset, w, z):
    q = z.q1

    def body(k):
        got_ref, pre_ref, g_ref, o_ref = k.i
        patch_ref, next_ref, pay_ref, st_ref, mates_ref = k.o
        (rows_ref,) = k.x
        same, views = [], got_ref[...].astype(F32)
        for m in range(MICRO):
            view = views[:, 9 * q + m : 9 * q + m + 1]
            same += [(view == k.s[0][m]).astype(F32)] * q
        mates_ref[...] = jnp.concatenate(same, axis=1)
        merge_stats(got_ref, mates_ref, st_ref, q, z.rows)
        for m in range(MICRO):
            for c in range(q):
                mean, inverse = row(st_ref, m * q + c), row(st_ref, (MICRO + m) * q + c)
                phase = {}
                for i, p in enumerate(PHASES):
                    x = pre_ref[pl.ds(m * z.rows + i * z.half, z.half), cols(c)]
                    phase[p] = gelu(g_ref[:, cols(c)] * ((x - mean) * inverse) + o_ref[:, cols(c)])
                write_patches(phase, patch_ref, m, z.half, c, z.c_mid, 1)
        k.send(0)
        k.wait_w()
        next_ref[...] = dot(patch_ref[...], k.w[0][...])
        k.send(1)
        for m in range(MICRO):
            for c in range(q):
                stats_rows(next_ref[pl.ds(m * z.rows, z.rows), cols(c)], rows_ref, m * q + c, z.rows, MICRO * q)
        fill_stats(pay_ref, rows_ref, q)

    rows = MICRO * z.rows
    return kernel_call(
        body,
        [arr(rows, 9 * z.c_mid, dtype=BF), arr(rows, z.c_mid), stats_arr(z.n, q), arr(6 * q, LANES), arr(z.n, 3 * q, LANES)],
        [got, pre, gain, offset],
        [w],
        [pltpu.VMEM((stats_shape(q)[0], LANES), F32)],
        flops=2 * rows * 9 * z.c_mid * z.c_mid,
        scalars=[ids],
    )


def k_expand(got, mates, pre, gain, offset, w, z):
    q, qo = z.q1, z.q3

    def body(k):
        got_ref, mates_ref, pre_ref, g_ref, o_ref = k.i
        act_ref, next_ref, pay_ref, st_ref = k.o
        (rows_ref,) = k.x
        merge_stats(got_ref, mates_ref, st_ref, q, z.rows)
        k_o, k_q = MICRO * qo, MICRO * q
        rows_ref[...] = jnp.zeros(rows_ref.shape, F32)
        for m in range(MICRO):
            for c in range(q):
                mean, inverse = row(st_ref, m * q + c), row(st_ref, (MICRO + m) * q + c)
                at = pl.ds(m * z.rows, z.rows)
                x = pre_ref[at, cols(c)]
                act = gelu(g_ref[:, cols(c)] * ((x - mean) * inverse) + o_ref[:, cols(c)]).astype(BF)
                act_ref[at, cols(c)] = act
                mean = jnp.sum(act.astype(F32), axis=0, keepdims=True) * (1.0 / z.rows)
                high = mean.astype(BF).astype(F32)
                rows_ref[pl.ds(k_o + m * q + c, 1), :] = high
                rows_ref[pl.ds(k_o + k_q + m * q + c, 1), :] = mean - high
        k.send(0)
        k.wait_w()
        next_ref[...] = dot(act_ref[...], k.w[0][...])
        k.send(1)
        for m in range(MICRO):
            for c in range(qo):
                x = next_ref[pl.ds(m * z.rows, z.rows), cols(c)]
                away = x - jnp.sum(x, axis=0, keepdims=True) * (1.0 / z.rows)
                rows_ref[pl.ds(m * qo + c, 1), :] = jnp.sum(away * away, axis=0, keepdims=True)
        fill(pay_ref, rows_ref)

    rows = MICRO * z.rows
    return kernel_call(
        body,
        [arr(rows, z.c_mid, dtype=BF), arr(rows, z.c_in), arr(z.n, z.q_product, LANES, dtype=BF), arr(6 * q, LANES)],
        [got, mates, pre, gain, offset],
        [w],
        [pltpu.VMEM((z.q_product, LANES), F32)],
        flops=2 * rows * z.c_in * z.c_mid,
    )


def merge_product(got_ref, mates_ref, same_ref, w_ref, line_ref, st_ref, between_ref, q, qo, size):
    n, tall = got_ref.shape[0], got_ref.shape[1]
    ko, kq = MICRO * qo, MICRO * q
    mates = n // NVIEW
    got = got_ref[...].astype(F32)
    line_ref[...] = got.reshape(n * tall, LANES)
    squares = jnp.sum(mates_ref[...] * got[:, :ko], axis=0)

    def part(r):
        return line_ref[pl.ds(r, n, stride=tall), :].astype(BF)

    lines = [
        jnp.concatenate([part(first + m * q + c) for c in range(q)], axis=1)
        for first in (ko, ko + kq)
        for m in range(MICRO)
    ]
    both = dot(jnp.concatenate(lines, axis=0), w_ref[...])
    means = both[: MICRO * n] + both[MICRO * n :]
    for m in range(MICRO):
        same = same_ref[m]
        for c in range(qo):
            x = means[m * n : (m + 1) * n, c * LANES : (c + 1) * LANES]
            mean = jnp.sum(same * x, axis=0, keepdims=True) * (1.0 / mates)
            away = x - mean
            st_ref[pl.ds(m * qo + c, 1), :] = mean
            between_ref[pl.ds(m * qo + c, 1), :] = jnp.sum(same * (away * away), axis=0, keepdims=True)
    total = squares + size * between_ref[...]
    st_ref[ko:] = lax.rsqrt(total * (1.0 / (mates * size)) + EPSILON)


def k_narrow(got, mates, same, pre, gain, offset, maps_in, w_before, w, z):
    q, qo = z.q3, z.q4

    def body(k):
        got_ref, mates_ref, same_ref, wb_ref, pre_ref, g_ref, o_ref, in_ref = k.i
        slope_ref, join_ref, even_ref, next_ref, pay_ref, st_ref = k.o
        rows_ref, line_ref, between_ref = k.x
        merge_product(got_ref, mates_ref, same_ref, wb_ref, line_ref, st_ref, between_ref, z.q1, q, z.rows)
        for m in range(MICRO):
            for c in range(q):
                mean, inverse = row(st_ref, m * q + c), row(st_ref, (MICRO + m) * q + c)
                at = pl.ds(m * z.rows, z.rows)
                x = pre_ref[at, cols(c)]
                res = g_ref[:, cols(c)] * ((x - mean) * inverse) + o_ref[:, cols(c)] + in_ref[at, cols(c)].astype(F32)
                joined, slope = gelu_both(res)
                slope_ref[at, cols(c)] = slope.astype(BF)
                joined = joined.astype(BF)
                join_ref[at, cols(c)] = joined
                even_ref[pl.ds(m * z.half, z.half), cols(c)] = joined[: z.half]
        for j in range(3):
            k.send(j)
        k.wait_w()
        next_ref[...] = dot(join_ref[...], k.w[0][...])
        k.send(3)
        for m in range(MICRO):
            for c in range(qo):
                stats_rows(next_ref[pl.ds(m * z.rows, z.rows), cols(c)], rows_ref, m * qo + c, z.rows, MICRO * qo)
        fill_stats(pay_ref, rows_ref, qo)

    rows = MICRO * z.rows
    return kernel_call(
        body,
        [
            arr(rows, z.c_in, dtype=BF),
            arr(rows, z.c_in, dtype=BF),
            arr(MICRO * z.half, z.c_in, dtype=BF),
            arr(rows, z.c_wide),
            stats_arr(z.n, qo),
            arr(6 * q, LANES),
        ],
        [got, mates, same, w_before, pre, gain, offset, maps_in],
        [w],
        [
            pltpu.VMEM((stats_shape(qo)[0], LANES), F32),
            pltpu.VMEM((z.n * z.q_product, LANES), F32),
            pltpu.VMEM((MICRO * q, LANES), F32),
        ],
        flops=2 * rows * z.c_in * z.c_wide,
    )


def k_stride(got, mates, pre, gain, offset, w, z, passes=()):
    q = z.q4

    def body(k):
        got_ref, mates_ref, pre_ref, g_ref, o_ref = k.i
        act_ref, next_ref, pay_ref, st_ref = k.o
        patch_ref, rows_ref = k.x
        merge_stats(got_ref, mates_ref, st_ref, q, z.rows)
        for m in range(MICRO):
            for c in range(q):
                mean, inverse = row(st_ref, m * q + c), row(st_ref, (MICRO + m) * q + c)
                phase = {}
                for i, p in enumerate(PHASES):
                    x = pre_ref[pl.ds(m * z.rows + i * z.half, z.half), cols(c)]
                    phase[p] = gelu(g_ref[:, cols(c)] * ((x - mean) * inverse) + o_ref[:, cols(c)])
                    act_ref[pl.ds(m * z.rows + i * z.half, z.half), cols(c)] = phase[p].astype(BF)
                write_patches(phase, patch_ref, m, z.half, c, z.c_wide, 1, ((0, 0),))
        k.send(0)
        value = 0.0
        for tap in range(9):
            k.wait_w(chunk=tap)
            at = pl.ds(tap * z.c_wide, z.c_wide)
            value = value + dot(patch_ref[:, at], k.w[0][at])
        next_ref[...] = value
        k.send(1)
        for m in range(MICRO):
            for c in range(q):
                stats_rows(next_ref[pl.ds(m * z.half, z.half), cols(c)], rows_ref, m * q + c, z.half, MICRO * q)
        fill_stats(pay_ref, rows_ref, q)

    rows = MICRO * z.half
    return kernel_call(
        body,
        [arr(MICRO * z.rows, z.c_wide, dtype=BF), arr(rows, z.c_wide), stats_arr(z.n, q), arr(6 * q, LANES)],
        [got, mates, pre, gain, offset],
        [w],
        [pltpu.VMEM((rows, 9 * z.c_wide), BF), pltpu.VMEM((stats_shape(q)[0], LANES), F32)],
        flops=2 * rows * 9 * z.c_wide * z.c_wide,
        passes=passes,
        chunks=9,
    )


def k_shortcut(even, w, z):
    def body(k):
        (e_ref,), (next_ref, st_ref) = k.i, k.o
        value = 0.0
        for j in range(4):
            k.wait_w(chunk=j)
            at = pl.ds(j * z.c_in // 4, z.c_in // 4)
            value = value + dot(e_ref[:, at], k.w[0][at])
        next_ref[...] = value
        for c in range(z.q6):
            for m in range(MICRO):
                stats_rows(next_ref[pl.ds(m * z.half, z.half), cols(c)], st_ref.at[c], m, z.half, MICRO)

    rows = MICRO * z.half
    return kernel_call(
        body, [arr(rows, z.c_out), arr(z.q6, 8, LANES)], [even], [w], flops=2 * rows * z.c_in * z.c_out, chunks=4
    )


def k_widen(got, mates, pre, gain, offset, short_st, w, z, passes=()):
    q = z.q4

    def body(k):
        got_ref, mates_ref, pre_ref, g_ref, o_ref, short_ref = k.i
        act_ref, next_ref, pay_ref, st_ref = k.o
        merge_stats(got_ref, mates_ref, st_ref, q, z.half)
        for m in range(MICRO):
            for c in range(q):
                mean, inverse = row(st_ref, m * q + c), row(st_ref, (MICRO + m) * q + c)
                at = pl.ds(m * z.half, z.half)
                x = pre_ref[at, cols(c)]
                act_ref[at, cols(c)] = gelu(g_ref[:, cols(c)] * ((x - mean) * inverse) + o_ref[:, cols(c)]).astype(BF)
        k.send(0)
        k.wait_w()
        next_ref[...] = dot(act_ref[...], k.w[0][...])
        k.send(1)
        for c in range(z.q6):
            for m in range(MICRO):
                stats_rows(next_ref[pl.ds(m * z.half, z.half), cols(c)], pay_ref.at[c], m, z.half, MICRO)
            pay_ref[z.q6 + c] = short_ref[c]
        chunks = 2 * z.q6
        for j in range(chunks, z.n):
            pay_ref[j] = pay_ref[j % chunks]

    rows = MICRO * z.half
    return kernel_call(
        body,
        [arr(rows, z.c_wide, dtype=BF), arr(rows, z.c_out), arr(z.n, 8, LANES), arr(6 * q, LANES)],
        [got, mates, pre, gain, offset, short_st],
        [w],
        flops=2 * rows * z.c_wide * z.c_out,
        passes=passes,
    )


def k_views(got, ids, z):
    def body(k):
        (got_ref, id_ref), (pay_ref,), (lo, hi) = k.i, k.o, k.x
        mates = z.n // NVIEW
        g, ids = got_ref[...], id_ref[...]
        for view, ref in ((0, lo), (1, hi)):
            w = (ids == float(view)).astype(F32)
            mean = jnp.sum(w * g, axis=0)[:MICRO] * (1.0 / mates)
            away = g[:, :MICRO] - mean[None]
            total = jnp.sum(w[:, :MICRO] * (g[:, MICRO : 2 * MICRO] + z.half * (away * away)), axis=0)
            ref[...] = jnp.zeros(ref.shape, F32)
            ref[:MICRO] = mean
            ref[MICRO : 2 * MICRO] = lax.rsqrt(total * (1.0 / (mates * z.half)) + EPSILON)
        pay_ref[...] = jnp.where(ids > 0.5, hi[...][None], lo[...][None])

    return kernel_call(
        body, [arr(z.n, 8, LANES)], [got, ids], scratch=[pltpu.VMEM((8, LANES), F32)] * 2, limit=16
    )[0]


def k_mapped(whole, pre_w, pre_s, cot, gains, z, passes=()):
    def body(k):
        st_ref, w_ref, s_ref, cot_ref, gw, ow, gs, os = k.i
        map_ref, d_ref, pay_ref = k.o
        n_c = z.q6
        pay_ref[...] = jnp.zeros(pay_ref.shape, F32)
        for c in range(n_c):
            for m in range(MICRO):
                at = pl.ds(m * z.half, z.half)
                sw, ss = st_ref.at[c], st_ref.at[n_c + c]
                hat_w = (w_ref[at, cols(c)] - row(sw, m)) * row(sw, MICRO + m)
                hat_s = (s_ref[at, cols(c)] - row(ss, m)) * row(ss, MICRO + m)
                res = gw[:, cols(c)] * hat_w + ow[:, cols(c)] + (gs[:, cols(c)] * hat_s + os[:, cols(c)])
                map_ref[at, cols(c)] = gelu(res).astype(BF)
                d = gelu_slope(res) * cot_ref[at, cols(c)].astype(F32)
                d_ref[at, cols(c)] = d
                first, second = pay_ref.at[c], pay_ref.at[n_c + c]
                first[pl.ds(m, 1), :] = jnp.sum(d, axis=0, keepdims=True)
                first[pl.ds(MICRO + m, 1), :] = jnp.sum(d * hat_w, axis=0, keepdims=True)
                second[pl.ds(m, 1), :] = jnp.sum(d * hat_s, axis=0, keepdims=True)
        for j in range(2 * n_c, z.n):
            pay_ref[j] = pay_ref[j % (2 * n_c)]

    rows = MICRO * z.half
    return kernel_call(
        body,
        [arr(rows, z.c_out, dtype=BF), arr(rows, z.c_out), arr(z.n, 8, LANES)],
        [whole, pre_w, pre_s, cot, *gains],
        flops=rows * z.c_out * 60,
        passes=passes,
    )


def k_view_sums(got, ids, z):
    def body(k):
        (got_ref, id_ref), (pay_ref,), (both,) = k.i, k.o, k.x
        g, ids = got_ref[...], id_ref[...]
        lo = jnp.sum((ids == 0.0).astype(F32) * g, axis=0)
        hi = jnp.sum((ids == 1.0).astype(F32) * g, axis=0)
        both[0], both[1] = lo, hi
        all_views = lo + hi
        totals = []
        for k in range(2):
            totals.append(jnp.sum(all_views[k * MICRO : (k + 1) * MICRO], axis=0, keepdims=True))
        for v in range(2):
            for k in range(2):
                both[v, pl.ds(2 * MICRO + k, 1), :] = totals[k]
        pay_ref[...] = jnp.where(ids > 0.5, both[1][None], both[0][None])

    return kernel_call(body, [arr(z.n, 8, LANES)], [got, ids], scratch=[pltpu.VMEM((2, 8, LANES), F32)], limit=16)[0]


def back_rows(x, d, st_ref, sum_ref, m, q, c, gain):
    inverse = row(st_ref, (MICRO + m) * q + c)
    hat = (x - row(st_ref, m * q + c)) * inverse
    return gain * inverse * (d - row(sum_ref, m * q + c) - hat * row(sum_ref, (MICRO + m) * q + c))


def sum_rows(d, hat, rows_ref, r, offset):
    rows_ref[pl.ds(r, 1), :] = jnp.sum(d, axis=0, keepdims=True)
    rows_ref[pl.ds(r + offset, 1), :] = jnp.sum(d * hat, axis=0, keepdims=True)


def slope_and_sums(d_out, pre_ref, at, st_ref, m, q, c, g_ref, o_ref, d_ref, rows_ref):
    hat = (pre_ref[at, cols(c)] - row(st_ref, m * q + c)) * row(st_ref, (MICRO + m) * q + c)
    d = gelu_slope(g_ref[:, cols(c)] * hat + o_ref[:, cols(c)]) * d_out
    d_ref[at, cols(c)] = d
    sum_rows(d, hat, rows_ref, m * q + c, MICRO * q)


def k_back_widen(whole, sums, d_two, pre_w, pre_s, gain_w, gain_s, pre, st, gain, offset, place, w, z, passes=()):
    q, n_c = z.q4, z.q6

    def body(k):
        st2, sum_ref, d_ref, w_ref, s_ref, gw, gs, pre_ref, st_ref, g_ref, o_ref = k.i
        ds_ref, t_off, t_gw, t_gs, d_next, pay_ref = k.o
        dw_ref, rows_ref, tmp = k.x
        scale = 1.0 / (z.n // NVIEW * z.half)
        for c in range(n_c):
            first, second = sum_ref.at[c], sum_ref.at[n_c + c]
            t_off[pl.ds(c, 1), :] = row(first, 2 * MICRO)
            t_gw[pl.ds(c, 1), :] = row(first, 2 * MICRO + 1)
            t_gs[pl.ds(c, 1), :] = row(second, 2 * MICRO)
            sw, ss = st2.at[c], st2.at[n_c + c]
            for m in range(MICRO):
                at = pl.ds(m * z.half, z.half)
                inv_w, inv_s = row(sw, MICRO + m), row(ss, MICRO + m)
                hat_w = (w_ref[at, cols(c)] - row(sw, m)) * inv_w
                hat_s = (s_ref[at, cols(c)] - row(ss, m)) * inv_s
                d = d_ref[at, cols(c)] - row(first, m) * scale
                dw_ref[at, cols(c)] = (
                    gw[:, cols(c)] * inv_w * (d - hat_w * (row(first, MICRO + m) * scale))
                ).astype(BF)
                ds_ref[at, cols(c)] = (gs[:, cols(c)] * inv_s * (d - hat_s * (row(second, m) * scale))).astype(BF)
        k.send(0)
        some = z.c_out // z.g
        for j in range(z.g):
            at = pl.ds(pl.multiple_of(((k.s[0][0] & (z.g - 1)) ^ j) * some, some), some)
            k.copy(dw_ref.at[:, at], k.raw[j].at[:, pl.ds(0, some)])
            k.copy(ds_ref.at[:, at], k.raw[j].at[:, pl.ds(some, some)])
        k.wait_w()
        tmp[...] = dot_nt(dw_ref[...], k.w[0][...])
        for m in range(MICRO):
            at = pl.ds(m * z.half, z.half)
            for c in range(q):
                slope_and_sums(tmp[at, cols(c)], pre_ref, at, st_ref, m, q, c, g_ref, o_ref, d_next, rows_ref)
        fill(pay_ref, rows_ref)

    rows = MICRO * z.half
    return kernel_call(
        body,
        [arr(rows, z.c_out, dtype=BF)]
        + [arr(n_c, LANES)] * 3
        + [arr(rows, z.c_wide), arr(z.n, 6 * q, LANES, dtype=BF)],
        [whole, sums, d_two, pre_w, pre_s, gain_w, gain_s, pre, st, gain, offset],
        [w],
        [
            pltpu.VMEM((rows, z.c_out), BF),
            pltpu.VMEM((6 * q, LANES), F32),
            pltpu.VMEM((rows, z.c_wide), F32),
        ],
        flops=2 * rows * z.c_wide * z.c_out,
        raw=[arr(rows, 2 * z.c_out // z.g, dtype=BF)] * z.g,
        n_raw=2 * z.g,
        scalars=[place],
        passes=passes,
    )


def back_start(refs, mates_ref, sum_ref, out_ref, q, n_rows, totals):
    got_ref, d_ref, pre_ref, st_ref, g_ref = refs
    merge_sums(got_ref, mates_ref, sum_ref, q, n_rows, totals)
    for m in range(MICRO):
        at = pl.ds(m * n_rows, n_rows)
        for c in range(q):
            out_ref[at, cols(c)] = back_rows(
                pre_ref[at, cols(c)], d_ref[at, cols(c)].astype(F32), st_ref, sum_ref, m, q, c, g_ref[:, cols(c)]
            ).astype(BF)


def k_back_stride(got, mates, d, pre_s, st_s, gain_s, pre, st, gain, offset, place, w, z, passes=()):
    q = z.q4

    def body(k):
        got_ref, mates_ref, d_ref, ps_ref, ss_ref, gs_ref, pre_ref, st_ref, g_ref, o_ref = k.i
        t_off, t_gain, d_next, pay_ref = k.o
        delta_ref, rows_ref, sum_ref, contrib = k.x
        back_start((got_ref, d_ref, ps_ref, ss_ref, gs_ref), mates_ref, sum_ref, delta_ref, q, z.half, (t_off, t_gain))
        some = z.c_wide // z.g
        for j in range(z.g):
            at = pl.ds(pl.multiple_of(((k.s[0][0] & (z.g - 1)) ^ j) * some, some), some)
            k.copy(delta_ref.at[:, at], k.raw[j])
        for tap in range(9):
            k.wait_w(chunk=tap)
            at = pl.ds(tap * z.c_wide, z.c_wide)
            contrib[:, at] = dot_nt(delta_ref[...], k.w[0][at])
        for m in range(MICRO):
            for c in range(q):
                phase = {}
                for r in range(3):
                    for k in range(3):
                        piece = contrib[pl.ds(m * z.half, z.half), pl.ds((r * 3 + k) * z.c_wide + c * LANES, LANES)]
                        piece = shift_x(shift_y(piece, 1 if r == 0 else 0), 1 if k == 0 else 0)
                        p = ((r + 1) % 2, (k + 1) % 2)
                        phase[p] = piece if p not in phase else phase[p] + piece
                first = second = 0.0
                mean, inverse = row(st_ref, m * q + c), row(st_ref, (MICRO + m) * q + c)
                for i, p in enumerate(PHASES):
                    at = pl.ds(m * z.rows + i * z.half, z.half)
                    hat = (pre_ref[at, cols(c)] - mean) * inverse
                    grad = gelu_slope(g_ref[:, cols(c)] * hat + o_ref[:, cols(c)]) * phase[p]
                    d_next[at, cols(c)] = grad
                    first = first + jnp.sum(grad, axis=0, keepdims=True)
                    second = second + jnp.sum(grad * hat, axis=0, keepdims=True)
                rows_ref[pl.ds(m * q + c, 1), :] = first
                rows_ref[pl.ds((MICRO + m) * q + c, 1), :] = second
        fill(pay_ref, rows_ref)

    rows = MICRO * z.half
    return kernel_call(
        body,
        [arr(q, LANES)] * 2
        + [arr(MICRO * z.rows, z.c_wide), arr(z.n, 6 * q, LANES, dtype=BF)],
        [got, mates, d, pre_s, st_s, gain_s, pre, st, gain, offset],
        [w],
        [
            pltpu.VMEM((rows, z.c_wide), BF),
            pltpu.VMEM((6 * q, LANES), F32),
            pltpu.VMEM((6 * q, LANES), F32),
            pltpu.VMEM((rows, 9 * z.c_wide), F32),
        ],
        flops=2 * rows * 9 * z.c_wide * z.c_wide,
        passes=passes,
        chunks=9,
        raw=[arr(rows, z.c_wide // z.g, dtype=BF)] * z.g,
        n_raw=z.g,
        scalars=[place],
    )


def k_back_narrow(got, mates, d, pre_n, st_n, gain_n, even, slope, pre, st, w, z, passes=()):
    q, qo = z.q4, z.q3

    def body(k):
        got_ref, mates_ref, d_ref, pn_ref, sn_ref, gn_ref, even_ref, slope_ref, pre_ref, st_ref = k.i
        delta_ref, t_off, t_gain, d_next, pay_ref = k.o
        rows_ref, sum_ref, tmp = k.x
        back_start((got_ref, d_ref, pn_ref, sn_ref, gn_ref), mates_ref, sum_ref, delta_ref, q, z.rows, (t_off, t_gain))
        k.send(0)
        k.wait_w()
        tmp[...] = dot_nt(delta_ref[...], k.w[0][...])
        for m in range(MICRO):
            at = pl.ds(m * z.rows, z.rows)
            some = pl.ds(m * z.rows, z.half)
            for c in range(qo):
                tmp[some, cols(c)] = tmp[some, cols(c)] + even_ref[pl.ds(m * z.half, z.half), cols(c)]
                d_join = tmp[at, cols(c)].astype(BF).astype(F32)
                one = slope_ref[at, cols(c)].astype(F32) * d_join
                hat = (pre_ref[at, cols(c)] - row(st_ref, m * qo + c)) * row(st_ref, (MICRO + m) * qo + c)
                d_next[at, cols(c)] = one.astype(BF)
                sum_rows(one, hat, rows_ref, m * qo + c, MICRO * qo)
        fill(pay_ref, rows_ref)

    rows = MICRO * z.rows
    return kernel_call(
        body,
        [arr(rows, z.c_wide, dtype=BF)] + [arr(q, LANES)] * 2 + [arr(rows, z.c_in, dtype=BF), arr(z.n, 6 * qo, LANES, dtype=BF)],
        [got, mates, d, pre_n, st_n, gain_n, even, slope, pre, st],
        [w],
        [
            pltpu.VMEM((6 * qo, LANES), F32),
            pltpu.VMEM((6 * q, LANES), F32),
            pltpu.VMEM((rows, z.c_in), F32),
        ],
        flops=2 * rows * z.c_in * z.c_wide,
        passes=passes,
    )


def k_back_expand(got, mates, d, pre_e, st_e, gain_e, pre, st, gain, offset, w, z, passes=()):
    q, qo = z.q3, z.q1

    def body(k):
        got_ref, mates_ref, d_ref, pe_ref, se_ref, ge_ref, pre_ref, st_ref, g_ref, o_ref = k.i
        delta_ref, t_off, t_gain, d_next, pay_ref = k.o
        rows_ref, sum_ref, tmp = k.x
        back_start((got_ref, d_ref, pe_ref, se_ref, ge_ref), mates_ref, sum_ref, delta_ref, q, z.rows, (t_off, t_gain))
        k.send(0)
        k.wait_w()
        tmp[...] = dot_nt(delta_ref[...], k.w[0][...])
        for m in range(MICRO):
            at = pl.ds(m * z.rows, z.rows)
            for c in range(qo):
                slope_and_sums(tmp[at, cols(c)], pre_ref, at, st_ref, m, qo, c, g_ref, o_ref, d_next, rows_ref)
        fill(pay_ref, rows_ref)

    rows = MICRO * z.rows
    return kernel_call(
        body,
        [arr(rows, z.c_in, dtype=BF)] + [arr(q, LANES)] * 2 + [arr(rows, z.c_mid), arr(z.n, 6 * qo, LANES, dtype=BF)],
        [got, mates, d, pre_e, st_e, gain_e, pre, st, gain, offset],
        [w],
        [
            pltpu.VMEM((6 * qo, LANES), F32),
            pltpu.VMEM((6 * q, LANES), F32),
            pltpu.VMEM((rows, z.c_mid), F32),
        ],
        flops=2 * rows * z.c_in * z.c_mid,
        passes=passes,
    )


def k_back_spatial(got, mates, d, pre_s, st_s, gain_s, pre, st, gain, offset, w, z, passes=()):
    q = z.q1

    def body(k):
        got_ref, mates_ref, d_ref, ps_ref, ss_ref, gs_ref, pre_ref, st_ref, g_ref, o_ref = k.i
        delta_ref, t_off, t_gain, d_next, pay_ref = k.o
        rows_ref, sum_ref, patch_ref, tmp = k.x
        merge_sums(got_ref, mates_ref, sum_ref, q, z.rows, (t_off, t_gain))
        for m in range(MICRO):
            for c in range(q):
                phase = {}
                for i, p in enumerate(PHASES):
                    at = pl.ds(m * z.rows + i * z.half, z.half)
                    phase[p] = back_rows(
                        ps_ref[at, cols(c)], d_ref[at, cols(c)], ss_ref, sum_ref, m, q, c, gs_ref[:, cols(c)]
                    )
                    delta_ref[at, cols(c)] = phase[p].astype(BF)
                write_patches(phase, patch_ref, m, z.half, c, z.c_mid, -1)
        k.send(0)
        k.wait_w()
        tmp[...] = dot(patch_ref[...], k.w[0][...])
        for m in range(MICRO):
            at = pl.ds(m * z.rows, z.rows)
            for c in range(q):
                slope_and_sums(tmp[at, cols(c)], pre_ref, at, st_ref, m, q, c, g_ref, o_ref, d_next, rows_ref)
        fill(pay_ref, rows_ref)

    rows = MICRO * z.rows
    return kernel_call(
        body,
        [arr(rows, z.c_mid, dtype=BF)] + [arr(q, LANES)] * 2 + [arr(rows, z.c_mid), arr(z.n, 6 * q, LANES, dtype=BF)],
        [got, mates, d, pre_s, st_s, gain_s, pre, st, gain, offset],
        [w],
        [
            pltpu.VMEM((6 * q, LANES), F32),
            pltpu.VMEM((6 * q, LANES), F32),
            pltpu.VMEM((rows, 9 * z.c_mid), BF),
            pltpu.VMEM((rows, z.c_mid), F32),
        ],
        flops=2 * rows * 9 * z.c_mid * z.c_mid,
        passes=passes,
    )


def k_back_reduce(got, mates, d, pre_r, st_r, gain_r, maps_in, place, z, passes=()):
    q, hi, r = z.q1, z.ns // z.slo, z.c_in // z.n

    def body(k):
        got_ref, mates_ref, d_ref, pr_ref, sr_ref, gr_ref, *maps = k.i
        delta_ref, t_off, t_gain = k.o
        sum_ref, *held = k.x
        back_start((got_ref, d_ref, pr_ref, sr_ref, gr_ref), mates_ref, sum_ref, delta_ref, q, z.rows, (t_off, t_gain))
        k.send(0)
        if maps:
            (held,) = held
            product = dot_tn(maps[0][...], delta_ref[...])
            held[...] = product.reshape(hi, z.slo, z.nb // 2, 2, r, z.c_mid).astype(BF)
            core = k.s[0][0] & 1
            k.copy(held.at[:, :, :, core], k.raw[0])
            k.copy(held.at[:, :, :, 1 - core], k.raw[1])

    rows = MICRO * z.rows
    maps = [] if maps_in is None else [maps_in]
    return kernel_call(
        body,
        [arr(rows, z.c_mid, dtype=BF)] + [arr(q, LANES)] * 2,
        [got, mates, d, pre_r, st_r, gain_r, *maps],
        scratch=[pltpu.VMEM((6 * q, LANES), F32)]
        + [pltpu.VMEM((hi, z.slo, z.nb // 2, 2, r, z.c_mid), BF) for _ in maps],
        passes=passes,
        scalars=[place],
        raw=[arr(hi, z.slo, z.nb // 2, r, z.c_mid, dtype=BF)] * (2 * len(maps)),
        n_raw=2 * len(maps),
        flops=2 * rows * z.c_in * z.c_mid,
    )


def k_input(delta, d_one, w, z, passes=()):
    def body(k):
        (delta_ref, one_ref), (out_ref,), (tmp, line) = k.i, k.o, k.x
        k.wait_w()
        tmp[...] = dot_nt(delta_ref[...], k.w[0][...])
        for m in range(MICRO):
            for y in range(z.height):
                for c in range(z.q3):
                    for px in range(2):
                        at = pl.ds(m * z.rows + (2 * (y % 2) + px) * z.half + (y // 2) * 8, 8)
                        line[c, pl.ds((y * MICRO + m) * z.cols + px, 8, stride=2), :] = (
                            one_ref[at, cols(c)].astype(F32) + tmp[at, cols(c)]
                        )
                    out_ref[y, m, :, cols(c)] = line[c, pl.ds((y * MICRO + m) * z.cols, z.cols), :].astype(BF)

    rows = MICRO * z.rows
    return kernel_call(
        body,
        [arr(z.height, MICRO, z.cols, z.c_in, dtype=BF)],
        [delta, d_one],
        [w],
        [pltpu.VMEM((rows, z.c_in), F32), pltpu.VMEM((z.q3, rows, LANES), F32)],
        flops=2 * rows * z.c_in * z.c_mid,
        passes=passes,
    )


def k_even(delta, w, z):
    def body(k):
        k.wait_w()
        k.o[0][...] = dot_nt(k.i[0][...], k.w[0][...])

    rows = delta.shape[0]
    return kernel_call(body, [arr(rows, z.c_in)], [delta], [w], flops=2 * rows * z.c_in * z.c_out)[0]


def k_first_grads(outs, evens, pieces, z):
    some = z.c_out // z.g
    a, b = z.c_wide // z.ns, z.c_in // z.ns

    def body(k):
        lhs_w, lhs_s, rhs = k.st
        held_w, held_s = k.x
        held_w[...] = dot_tn(lhs_w[...], rhs[:, :some]).astype(BF)
        for s in range(z.ns):
            k.copy(held_w.at[pl.ds(s * a, a)], k.raw[0].at[s % z.slo, s // z.slo, pl.ds(0, a)])
        held_s[...] = dot_tn(lhs_s[...], rhs[:, some:]).astype(BF)
        for s in range(z.ns):
            k.copy(held_s.at[pl.ds(s * b, b)], k.raw[0].at[s % z.slo, s // z.slo, pl.ds(a, b)])

    return kernel_call(
        body,
        [],
        [],
        scratch=[pltpu.VMEM((z.c_wide, some), BF), pltpu.VMEM((z.c_in, some), BF)],
        stacks=[outs, evens, pieces],
        raw=[arr(z.slo, z.ns // z.slo, a + b, some, dtype=BF)],
        n_raw=2 * z.ns,
        flops=2 * z.g * outs[0].shape[0] * (z.c_in + z.c_wide) * some,
    )[0]


def k_stride_grads(maps, pieces, z):
    few = z.c_wide // z.g
    c = 9 * z.c_wide // z.ns
    wide = z.c_out // z.c_wide
    d = c // wide
    rows = z.g * pieces[0].shape[0]

    def body(k):
        map_ref, rhs = k.st
        held, lhs = k.x
        for m in range(z.g * MICRO):
            for col in range(z.q4):
                phase = {}
                for i, p in enumerate(PHASES):
                    phase[p] = map_ref[pl.ds(m * z.rows + i * z.half, z.half), cols(col)].astype(F32)
                write_patches(phase, lhs, m, z.half, col, z.c_wide, 1, ((0, 0),))
        for t in range(9):
            at = pl.ds(t * z.c_wide, z.c_wide)
            held[at] = dot_tn(lhs[:, at], rhs[...]).astype(BF)
        for s in range(z.ns):
            for part in range(wide):
                k.copy(
                    held.at[pl.ds(s * c + part * d, d)],
                    k.raw[0].at[s % z.slo, s // z.slo, :, pl.ds(part * few, few)],
                )

    return kernel_call(
        body,
        [],
        [],
        scratch=[pltpu.VMEM((9 * z.c_wide, few), BF), pltpu.VMEM((rows, 9 * z.c_wide), BF)],
        stacks=[maps, pieces],
        raw=[arr(z.slo, z.ns // z.slo, d, wide * few, dtype=BF)],
        n_raw=wide * z.ns,
        flops=2 * rows * 9 * z.c_wide * few,
    )[0]


def k_products(pairs, place, z, passes=()):
    hi = z.ns // z.slo
    widths = [(o.shape[1], g.shape[1]) for o, g in pairs]
    rows = [r // z.n * c // 256 for r, c in widths]
    total = sum(rows)

    def body(k):
        (held,) = k.x
        at = 0
        for j, (r, c) in enumerate(widths):
            product = dot_tn(k.i[2 * j][...], k.i[2 * j + 1][...])
            blocks = product.reshape(hi, z.slo, z.nb // 2, 2, r // z.n, c).astype(BF)
            for part in range(c // 256):
                held[:, :, :, :, pl.ds(at, r // z.n), :] = blocks[..., part * 256 : (part + 1) * 256]
                at += r // z.n
        core = k.s[0][0] & 1
        k.copy(held.at[:, :, :, core], k.raw[0])
        k.copy(held.at[:, :, :, 1 - core], k.raw[1])

    return kernel_call(
        body,
        [],
        [a for pair in pairs for a in pair],
        scratch=[pltpu.VMEM((hi, z.slo, z.nb // 2, 2, total, 256), BF)],
        raw=[arr(hi, z.slo, z.nb // 2, total, 256, dtype=BF)] * 2,
        n_raw=2,
        scalars=[place],
        passes=passes,
        flops=sum(2 * pairs[j][0].shape[0] * r * c for j, (r, c) in enumerate(widths)),
    )


def k_sum_plane(groups, where, z, early=()):
    hi, high = z.ns // z.slo, z.nb // 2
    rows = [g[0].shape[3] for g in groups]

    tall = [e.shape[1] for e in early]

    def body(k):
        (held,) = k.x
        top = 0
        for e, r in zip(k.i[2 * len(groups) :], tall):
            k.copy(e, k.raw[-1].at[:, pl.ds(top, r)])
            top += r
        at = 0
        for j, r in enumerate(rows):
            both = k.i[2 * j][...].astype(F32) + k.i[2 * j + 1][...].astype(F32)
            held[:, :, :, pl.ds(at, r), :] = both.astype(BF)
            at += r
        for i in range(high):
            for j in range(z.slo):
                k.copy(held.at[:, k.s[0][0] ^ j, k.s[0][1] ^ i], k.raw[z.slo * i + j])

    total = sum(rows)
    return kernel_call(
        body,
        [],
        [a for g in groups for a in g] + list(early),
        scratch=[pltpu.VMEM((hi, z.slo, high, total, 256), BF)],
        raw=[arr(hi, total, 256, dtype=BF)] * (z.slo * high)
        + ([arr(hi, sum(tall), early[0].shape[2], dtype=BF)] if early else []),
        n_raw=z.slo * high + len(early),
        scalars=[where],
    )


def k_sum_line(groups, where, z, passes=()):
    hi = z.ns // z.slo
    rows = [g[0].shape[1] for g in groups]
    n = len(groups[0])

    def body(k):
        (held,) = k.x
        at = 0
        for j, r in enumerate(rows):
            value = k.i[j * n][...].astype(F32)
            for other in range(1, n):
                value = value + k.i[j * n + other][...].astype(F32)
            held[:, pl.ds(at, r), :] = value.astype(BF)
            at += r
        for j in range(hi):
            k.copy(held.at[k.s[0][2] ^ j], k.raw[j])

    total = sum(rows)
    return kernel_call(
        body,
        [],
        [a for g in groups for a in g],
        scratch=[pltpu.VMEM((hi, total, 256), BF)],
        raw=[arr(total, 256, dtype=BF)] * hi,
        n_raw=hi,
        scalars=[where],
        passes=passes,
    )


def k_sum_last(parts, passes=()):
    def body(k):
        value = k.i[0][...].astype(F32)
        for other in k.i[1:]:
            value = value + other[...].astype(F32)
        k.o[0][...] = value.astype(BF)

    return kernel_call(body, [arr(*parts[0].shape, dtype=BF)], parts, passes=passes)


def k_late_shares(pieces, place, shapes, z, passes=()):
    n = z.nb
    total = pieces[0].shape[0]

    def body(k):
        (held,) = k.x
        for j in range(n):
            held[k.s[0][0] ^ j] = k.i[j][...]
        for j in range(n):
            value = held[j].astype(F32)
            at = 0
            for g, (r, c) in enumerate(shapes):
                r = r // z.n
                for part in range(c // 256):
                    k.o[g][pl.ds(j * r, r), pl.ds(part * 256, 256)] = value[at : at + r]
                    at += r

    return kernel_call(
        body,
        [arr(r // z.ns, c) for r, c in shapes],
        list(pieces),
        scratch=[pltpu.VMEM((n, total, 256), BF)],
        scalars=[place],
        passes=passes,
    )


def k_early_shares(pieces, place, z):
    n = z.g
    some, few = z.c_out // n, z.c_wide // n
    a, b, c = z.c_wide // z.ns, z.c_in // z.ns, 9 * z.c_wide // z.ns
    d = c * few // some

    def body(k):
        (held,) = k.x
        for j in range(n):
            held[(k.s[0][0] & (n - 1)) ^ j] = k.i[j][...]
        for j in range(n):
            value = held[j].astype(F32)
            k.o[0][:, pl.ds(j * some, some)] = value[:a]
            k.o[1][:, pl.ds(j * some, some)] = value[a : a + b]
            for part in range(some // few):
                k.o[2][pl.ds(part * d, d), pl.ds(j * few, few)] = value[a + b :, part * few : (part + 1) * few]

    return kernel_call(
        body,
        [arr(a, z.c_out), arr(b, z.c_out), arr(c, z.c_wide)],
        list(pieces),
        scratch=[pltpu.VMEM((n, a + b + d, some), BF)],
        scalars=[place],
    )


def on_device(
    features,
    view_ids,
    w_reduce,
    w_spatial,
    w_expand,
    w_narrow,
    w_stride,
    w_widen,
    w_shortcut,
    gain_reduce,
    offset_reduce,
    gain_spatial,
    offset_spatial,
    gain_expand,
    offset_expand,
    gain_narrow,
    offset_narrow,
    gain_stride,
    offset_stride,
    gain_widen,
    offset_widen,
    gain_shortcut,
    offset_shortcut,
    cotangent,
):
    z = Sizes()
    z.ns, z.nb = lax.axis_size(SPACE), lax.axis_size(BATCH)
    z.slo = lax.axis_size("slo")
    z.g = min(z.nb, 4)
    z.n = z.ns * z.nb
    z.maps, z.cols = features.shape[1], features.shape[3]
    z.height = z.ns
    z.rows = z.height * z.cols
    z.half = z.rows // 4
    z.c_in, z.c_mid = w_reduce.shape
    z.c_wide, z.c_out = w_widen.shape
    z.q1, z.q3, z.q4, z.q6 = (c // LANES for c in (z.c_mid, z.c_in, z.c_wide, z.c_out))
    z.q_product = -(-MICRO * (z.q3 + 2 * z.q1) // 8) * 8
    assert features.shape[2] == 1 and cotangent.shape[1] == 1 and z.maps == z.ns and z.cols == 16
    yh, xh = z.height // 2, z.cols // 2
    n, ns, nb = z.n, z.ns, z.nb
    s, b = lax.axis_index(SPACE), lax.axis_index(BATCH)
    place = b.astype(jnp.int32).reshape(1)

    def share(pay):
        return lax.all_to_all(pay, ALL, 0, 0, tiled=True)

    def exchange(block):
        return lax.all_to_all(block, SPACE, 0, 0, tiled=True)

    def swap(block, axis, distance):
        return lax.ppermute(block, axis, [(i, i ^ distance) for i in range(lax.axis_size(axis))])

    def trade(pieces):
        pairs = [(i, i ^ j) for j in range(z.g) for i in range(nb)]
        return [p if j == 0 else lax.ppermute(p, BATCH, pairs[j * nb : (j + 1) * nb]) for j, p in enumerate(pieces)]

    def everywhere(block, places):
        pieces = []
        for high in range(places // 2):
            other = swap(block, "bhi", high) if high else block
            pieces += [other, swap(other, "core", 1)]
        return pieces

    def over_groups(product):
        distance = z.g // 2
        while distance < nb // 2:
            product = (product.astype(F32) + swap(product, "bhi", distance).astype(F32)).astype(BF)
            distance *= 2
        return product

    def lines(vector):
        return vector.reshape(1, -1)

    vectors = {
        "reduce": (lines(gain_reduce), lines(offset_reduce)),
        "spatial": (lines(gain_spatial), lines(offset_spatial)),
        "expand": (lines(gain_expand), lines(offset_expand)),
        "narrow": (lines(gain_narrow), lines(offset_narrow)),
        "stride": (lines(gain_stride), lines(offset_stride)),
        "widen": (lines(gain_widen), lines(offset_widen)),
        "shortcut": (lines(gain_shortcut), lines(offset_shortcut)),
    }

    my_ids = lax.dynamic_slice_in_dim(view_ids, s, 1, 1).astype(F32)
    arrived = exchange(features.reshape(MICRO, z.maps, z.cols, z.c_in).transpose(1, 0, 2, 3))
    pre_reduce, pay = k_reduce(arrived, my_ids.reshape(MICRO), w_reduce, z)
    got = share(pay)
    ids = got[:, 9 * z.q1 : 9 * z.q1 + MICRO].astype(F32)
    same = (ids == my_ids[None]).astype(F32)
    mates = {q: jnp.repeat(same, q, axis=1) for q in (z.q3, z.q4)}
    id_rows = jnp.concatenate([ids, ids, jnp.zeros((n, 2, LANES), F32)], axis=1)

    maps_in = arrived.reshape(yh, 2, MICRO, xh, 2, z.c_in).transpose(2, 1, 4, 0, 3, 5)
    maps_in = maps_in.reshape(MICRO * z.rows, z.c_in)

    patch_reduce, pre_spatial, pay, st_reduce, mates[z.q1] = k_spatial(
        got, my_ids.reshape(MICRO), pre_reduce, *vectors["reduce"], w_spatial, z
    )
    got = share(pay)
    out_spatial, pre_expand, pay, st_spatial = k_expand(got, mates[z.q1], pre_spatial, *vectors["spatial"], w_expand, z)
    got = share(pay)
    slope_one, joined, even, pre_narrow, pay, st_expand = k_narrow(
        got, mates[z.q3], same.transpose(1, 0, 2), pre_expand, *vectors["expand"], maps_in, w_expand, w_narrow, z
    )
    evens = everywhere(even, z.g)
    got = share(pay)
    pre_shortcut, short_st = k_shortcut(even, w_shortcut, z)
    out_narrow, pre_stride, pay, st_narrow = k_stride(
        got, mates[z.q4], pre_narrow, *vectors["narrow"], w_stride, z
    )
    got = share(pay)
    outs_narrow = everywhere(out_narrow, z.g)
    out_stride, pre_widen, pay, st_stride = k_widen(
        got, mates[z.q4], pre_stride, *vectors["stride"], short_st, w_widen, z
    )
    outs_stride = everywhere(out_stride, z.g)
    whole = share(k_views(share(pay), id_rows, z))
    mapped, d_two, pay = k_mapped(
        whole,
        pre_widen,
        pre_shortcut,
        cotangent.reshape(-1, z.c_out),
        (*vectors["widen"], *vectors["shortcut"]),
        z,
    )

    sums = share(k_view_sums(share(pay), id_rows, z))
    delta_shortcut, go_widen, gg_widen, gg_shortcut, d_stride, pay, *more = k_back_widen(
        whole, sums, d_two, pre_widen, pre_shortcut, vectors["widen"][0], vectors["shortcut"][0],
        pre_stride, st_stride, *vectors["stride"], place, w_widen, z, (*outs_narrow, *evens, *outs_stride),
    )
    got = share(pay)
    pieces, outs_narrow, evens, outs_stride = (more[j * z.g : (j + 1) * z.g] for j in range(4))
    d_even = k_even(delta_shortcut, w_shortcut, z)
    first_pieces = trade(pieces)
    go_stride, gg_stride, d_narrow, pay, *more = k_back_stride(
        got, mates[z.q4], d_stride, pre_stride, st_stride, vectors["stride"][0],
        pre_narrow, st_narrow, *vectors["narrow"], place, w_stride, z, (*first_pieces, d_even),
    )
    pieces, first_pieces, d_even = more[: z.g], more[z.g : 2 * z.g], more[2 * z.g]
    got = share(pay)
    first = k_first_grads(outs_stride, evens, first_pieces, z)
    first = over_groups(first)
    pieces = trade(pieces)
    delta_narrow, go_narrow, gg_narrow, d_one, pay, first, *pieces = k_back_narrow(
        got, mates[z.q4], d_narrow, pre_narrow, st_narrow, vectors["narrow"][0],
        d_even, slope_one, pre_expand, st_expand, w_narrow, z, (first, *pieces),
    )
    got = share(pay)
    first = lax.psum_scatter(first, "slo", scatter_dimension=0, tiled=True)
    second = over_groups(k_stride_grads(outs_narrow, pieces, z))

    delta_expand, go_expand, gg_expand, d_spatial, pay, second = k_back_expand(
        got, mates[z.q3], d_one, pre_expand, st_expand, vectors["expand"][0],
        pre_spatial, st_spatial, *vectors["spatial"], w_expand, z, (second,),
    )
    got = share(pay)
    second = lax.psum_scatter(second, "slo", scatter_dimension=0, tiled=True)
    blocks = all(w.shape[0] % (8 * n) == 0 for w in (w_reduce, w_spatial, w_expand, w_narrow))
    pairs_some = [(joined, delta_narrow), (out_spatial, delta_expand)]
    kept_some, sent_some = k_products(pairs_some, place, z) if blocks else (None, delta_expand)
    flipped = w_spatial.reshape(9, z.c_mid, z.c_mid).transpose(0, 2, 1).reshape(9 * z.c_mid, z.c_mid)
    delta_spatial, go_spatial, gg_spatial, d_reduce, pay, sent_some, first = k_back_spatial(
        got, mates[z.q1], d_spatial, pre_spatial, st_spatial, vectors["spatial"][0],
        pre_reduce, st_reduce, *vectors["reduce"], flipped, z, (sent_some, first),
    )
    got = share(pay)
    pairs_more = [(patch_reduce, delta_spatial)]
    kept_more, sent_more = k_products(pairs_more, place, z) if blocks else (None, delta_spatial)
    came_some = swap(sent_some, "core", 1) if blocks else sent_some
    where = jnp.stack([lax.axis_index("slo"), lax.axis_index("bhi"), lax.axis_index("shi")]).astype(jnp.int32)

    def over_plane(groups, early):
        high = nb // 2
        parts = k_sum_plane(groups, where, z, early)
        came = []
        for i in range(high):
            for j in range(z.slo):
                pairs = [(u * z.slo + v, (u ^ i) * z.slo + (v ^ j)) for u in range(high) for v in range(z.slo)]
                part = parts[i * z.slo + j]
                came.append(lax.ppermute(part, ("bhi", "slo"), pairs) if i or j else part)
        return came, parts[high * z.slo :]

    delta_reduce, go_reduce, gg_reduce, *more = k_back_reduce(
        got, mates[z.q1], d_reduce, pre_reduce, st_reduce, vectors["reduce"][0], maps_in if blocks else None, place, z,
        (sent_more, came_some, where),
    )
    pairs_last, passed = [(maps_in, delta_reduce)], ()
    if blocks:
        kept_last, sent_last, sent_more, came_some, where = more
        groups = [(kept_some, came_some), (kept_more, swap(sent_more, "core", 1)), (kept_last, swap(sent_last, "core", 1))]
        passed, (early,) = over_plane(groups, (first[0], second[0]))
    else:
        early = jnp.concatenate([first[0], second[0]], axis=1)
    left, *passed = k_input(delta_reduce, d_one, w_reduce, z, passed)
    left = exchange(left)
    early = lax.psum_scatter(early, "shi", scatter_dimension=0, tiled=True)
    if blocks:
        *parts, early = k_sum_line([passed], where, z, (early,))
        early = k_early_shares(everywhere(early[0], z.g), place, z)
        parts = [p if j == 0 else swap(p, "shi", j) for j, p in enumerate(parts)]
        late, *early = k_sum_last(parts, early)
        late = everywhere(late, nb)
        shapes = [w.shape for w in (w_narrow, w_expand, w_spatial, w_reduce)]
        late = k_late_shares(late, place, shapes, z)
        grad_w_narrow, grad_w_expand, grad_w_spatial, grad_w_reduce = late
    else:
        late = [dot_tn(o, g).astype(BF) for o, g in pairs_some + pairs_more + pairs_last]
        late = [lax.psum_scatter(w, SPACE, scatter_dimension=0, tiled=True) for w in late]
        late = [w.astype(F32) for w in lax.psum(late, BATCH)]
        grad_w_narrow, grad_w_expand, grad_w_spatial, grad_w_reduce = late
        early = k_early_shares(everywhere(early[0], z.g), place, z)
    grad_w_widen, grad_w_shortcut, grad_w_stride = early
    grad_features = left.transpose(1, 0, 2, 3).reshape(features.shape)

    flat = lambda block: block.reshape(-1)
    return (
        mapped.reshape(cotangent.shape),
        grad_features,
        grad_w_reduce,
        grad_w_spatial,
        grad_w_expand,
        grad_w_narrow,
        grad_w_stride,
        grad_w_widen,
        grad_w_shortcut,
        flat(gg_reduce),
        flat(go_reduce),
        flat(gg_spatial),
        flat(go_spatial),
        flat(gg_expand),
        flat(go_expand),
        flat(gg_narrow),
        flat(go_narrow),
        flat(gg_stride),
        flat(go_stride),
        flat(gg_widen),
        flat(go_widen),
        flat(gg_shortcut),
        flat(go_widen),
    )


def solution(mesh):
    nb, ns = mesh.shape["batch"], mesh.shape["space"]
    fine = Mesh(mesh.devices.reshape(nb // 2, 2, ns // 2, 2), ALL)
    maps = P(None, ALL, None, None, None)
    return jax.shard_map(
        on_device,
        mesh=fine,
        in_specs=(P(None, BATCH, SPACE, None, None), P(None, BATCH)) + (P(),) * 21 + (maps,),
        out_specs=(maps, P(None, BATCH, SPACE, None, None)) + (P(SPACE, None),) * 7 + (P(),) * 14,
        check_vma=False,
    )
```

```python
import functools
import math

import jax
import jax.numpy as jnp
from jax import lax
from jax.experimental import pallas as pl
from jax.experimental.pallas import tpu as pltpu
from jax.sharding import Mesh
from jax.sharding import PartitionSpec as P

NVIEW = 2
MICRO = 3
EPSILON = 1e-05
BF = jnp.bfloat16
F32 = jnp.float32
BATCH, SPACE = ("bhi", "core"), ("shi", "slo")
ALL = BATCH + SPACE
LANES = 128
ROOT = math.sqrt(2.0 / math.pi)
CUBE = 0.044715


def dot(a, b, dims=((1,), (0,))):
    return lax.dot_general(a, b, (dims, ((), ())), preferred_element_type=F32)


def dot_nt(a, b):
    return dot(a, b, ((1,), (1,)))


def dot_tn(a, b):
    return dot(a, b, ((0,), (0,)))


def gelu(v):
    return 0.5 * v * (1.0 + jnp.tanh(ROOT * (v + CUBE * (v * v * v))))


def gelu_slope(v):
    square = v * v
    t = jnp.tanh(ROOT * (v + CUBE * (square * v)))
    return 0.5 * (1.0 + t) + (0.5 * ROOT) * v * (1.0 - t * t) * (1.0 + (3.0 * CUBE) * square)


def gelu_both(v):
    square = v * v
    t = jnp.tanh(ROOT * (v + CUBE * (square * v)))
    half = 0.5 * (1.0 + t)
    return v * half, half + (0.5 * ROOT) * v * (1.0 - t * t) * (1.0 + (3.0 * CUBE) * square)


def cols(c):
    return pl.ds(c * LANES, LANES)


def row(ref, r):
    return ref[pl.ds(r, 1), :]


class Kernel:
    def __init__(self, i, w, o, raw, scalars, stacks, extra, starts, sems):
        self.i, self.w, self.o, self.raw, self.s, self.st, self.x = i, w, o, raw, scalars, stacks, extra
        self.w_copies, self.out_pairs, self.sems = starts, {}, sems
        self.flying, self.sent = [], set()

    def wait_w(self, n=0, chunk=None):
        for copy in self.w_copies[n] if chunk is None else [self.w_copies[n][chunk]]:
            copy.wait()

    def send(self, n):
        src, dst, sem = self.out_pairs[n]
        copy = pltpu.make_async_copy(src, dst, sem)
        copy.start()
        self.flying.append(copy)
        self.sent.add(n)

    def copy(self, src, dst):
        copy = pltpu.make_async_copy(src, dst, self.sems.pop())
        copy.start()
        self.flying.append(copy)


def kernel_call(body, outs, args, weights=(), scratch=(), flops=0, raw=(), n_raw=0, scalars=(), passes=(), stacks=(), limit=63, chunks=1):
    n_s, n_in, n_w, n_p = len(scalars), len(args), len(weights), len(passes)
    n_k = sum(map(len, stacks))
    n_out, n_r = len(outs), len(raw)

    def run(*refs):
        refs = list(refs)

        def take(n):
            part = refs[:n]
            del refs[:n]
            return part

        s, ins, w_any = take(n_s), take(n_in), take(n_w)
        piles = [take(len(g)) for g in stacks]
        take(n_p)
        out, raw_refs, _ = take(n_out), take(n_r), take(n_p)
        v_in, v_w, v_out, v_k = take(n_in), take(n_w), take(n_out), take(len(stacks))
        (sems,) = take(1)
        sem = [sems.at[j] for j in range(n_in + n_w * chunks + n_k + n_out + n_raw)]
        in_copies = [pltpu.make_async_copy(a, v, sem.pop(0)) for a, v in zip(ins, v_in)]
        for pile, v in zip(piles, v_k):
            for j, a in enumerate(pile):
                rows = a.shape[0]
                in_copies.append(pltpu.make_async_copy(a, v.at[pl.ds(j * rows, rows)], sem.pop(0)))
        w_copies = []
        for a, v in zip(w_any, v_w):
            some = a.shape[0] // chunks
            parts = [pl.ds(j * some, some) for j in range(chunks)]
            w_copies.append([pltpu.make_async_copy(a.at[at], v.at[at], sem.pop(0)) for at in parts])
        for copy in in_copies + [c for copies in w_copies for c in copies]:
            copy.start()
        k = Kernel(v_in, v_w, v_out, raw_refs, s, v_k, refs, w_copies, sem[n_out:])
        k.out_pairs = {j: (v_out[j], out[j], sem[j]) for j in range(n_out)}
        for copy in in_copies:
            copy.wait()
        body(k)
        for j in range(n_out):
            if j not in k.sent:
                k.send(j)
        for copy in k.flying:
            copy.wait()

    def size(a):
        return math.prod(a.shape) * jnp.dtype(a.dtype).itemsize

    outside = pl.BlockSpec(memory_space=pl.ANY)
    piled = [arr(len(g) * g[0].shape[0], *g[0].shape[1:], dtype=g[0].dtype) for g in stacks]
    held = sum(map(size, (*args, *weights, *outs, *piled)))
    total = held + sum(size(a) for a in scratch if hasattr(a, "dtype"))
    first = n_s + n_in + n_w + n_k
    results = pl.pallas_call(
        run,
        out_shape=tuple(jax.ShapeDtypeStruct(o.shape, o.dtype) for o in (*outs, *raw, *passes)),
        in_specs=[pl.BlockSpec(memory_space=pltpu.SMEM)] * n_s + [outside] * (n_in + n_w + n_k + n_p),
        out_specs=tuple([outside] * (n_out + n_r + n_p)),
        scratch_shapes=[pltpu.VMEM(a.shape, a.dtype) for a in (*args, *weights, *outs, *piled)]
        + [pltpu.SemaphoreType.DMA((n_in + n_w * chunks + n_k + n_out + n_raw,))]
        + list(scratch),
        input_output_aliases={first + j: n_out + n_r + j for j in range(n_p)},
        cost_estimate=pl.CostEstimate(flops=flops, bytes_accessed=held, transcendentals=0),
        compiler_params=pltpu.CompilerParams(vmem_limit_bytes=max(limit * 2**20, total)),
    )(*scalars, *args, *weights, *(a for g in stacks for a in g), *passes)
    return tuple(results)


def arr(*shape, dtype=F32):
    return jax.ShapeDtypeStruct(shape, dtype)


def fill(pay_ref, rows_ref):
    block = rows_ref[...].astype(pay_ref.dtype)

    def step(j, _):
        pay_ref[j] = block
        return 0

    lax.fori_loop(0, pay_ref.shape[0], step, 0, unroll=8)


def stats_rows(value, rows_ref, r, size, offset):
    mean = jnp.sum(value, axis=0, keepdims=True) * (1.0 / size)
    away = value - mean
    rows_ref[pl.ds(r, 1), :] = mean
    rows_ref[pl.ds(r + offset, 1), :] = jnp.sum(away * away, axis=0, keepdims=True)


def stats_shape(q):
    return 9 * q, BF


def stats_arr(n, q):
    rows, dtype = stats_shape(q)
    return arr(n, rows, LANES, dtype=dtype)


def fill_stats(pay_ref, rows_ref, q):
    k = MICRO * q
    if pay_ref.dtype == BF:
        mean, square = rows_ref[:k], rows_ref[k : 2 * k]
        high = mean.astype(BF).astype(F32)
        rows_ref[:k] = high
        rows_ref[k : 2 * k] = mean - high
        rows_ref[2 * k : 3 * k] = square
    fill(pay_ref, rows_ref)


def merge_stats(got_ref, mates_ref, st_ref, q, size):
    n = got_ref.shape[0]
    k = MICRO * q
    mates = n // NVIEW
    step = 8

    def parts(at):
        got = got_ref[at].astype(F32)
        if got_ref.dtype == BF:
            return got[:, :k] + got[:, k : 2 * k], got[:, 2 * k : 3 * k]
        return got[:, :k], got[:, k : 2 * k]

    def one(i, acc):
        at = pl.ds(i * step, step)
        return acc + jnp.sum(mates_ref[at] * parts(at)[0], axis=0)

    mean = lax.fori_loop(0, n // step, one, jnp.zeros((k, LANES), F32), unroll=4) * (1.0 / mates)

    def two(i, acc):
        at = pl.ds(i * step, step)
        means, squares = parts(at)
        away = means - mean[None]
        return acc + jnp.sum(mates_ref[at] * (squares + size * (away * away)), axis=0)

    total = lax.fori_loop(0, n // step, two, jnp.zeros((k, LANES), F32), unroll=4)
    st_ref[:k] = mean
    st_ref[k : 2 * k] = lax.rsqrt(total * (1.0 / (mates * size)) + EPSILON)


def merge_sums(got_ref, mates_ref, sum_ref, q, size, total_refs):
    n = got_ref.shape[0]
    k = MICRO * q
    scale = 1.0 / (n // NVIEW * size)
    step = 8

    def one(i, carry):
        at = pl.ds(i * step, step)
        both = got_ref[at].astype(F32)
        first, second = both[:, :k], both[:, k : 2 * k]
        w = mates_ref[at]
        return (
            carry[0] + jnp.sum(w * first, axis=0),
            carry[1] + jnp.sum(w * second, axis=0),
            carry[2] + jnp.sum(first, axis=0),
            carry[3] + jnp.sum(second, axis=0),
        )

    zero = jnp.zeros((k, LANES), F32)
    a, b, ta, tb = lax.fori_loop(0, n // step, one, (zero,) * 4, unroll=4)
    sum_ref[:k] = a * scale
    sum_ref[k : 2 * k] = b * scale
    for ref, t in zip(total_refs, (ta, tb)):
        ref[...] = t[:q] + t[q : 2 * q] + t[2 * q :]


def shift_y(v, offset):
    if offset == 0:
        return v
    zero = jnp.zeros((8, v.shape[1]), v.dtype)
    if offset > 0:
        return jnp.concatenate([v[8:], zero], axis=0)
    return jnp.concatenate([zero, v[:-8]], axis=0)


def shift_x(v, offset):
    if offset == 0:
        return v
    place = lax.broadcasted_iota(jnp.int32, v.shape, 0) % 8
    if offset > 0:
        return jnp.where(place == 7, 0.0, pltpu.roll(v, v.shape[0] - 1, axis=0))
    return jnp.where(place == 0, 0.0, pltpu.roll(v, 1, axis=0))


def write_patches(phase, patch_ref, m, half, c, width, sign, out_phases=((0, 0), (0, 1), (1, 0), (1, 1))):
    moved = {}

    def get(sy, sx, ox):
        if (sy, sx, ox) not in moved:
            moved[sy, sx, ox] = shift_x(phase[sy, sx], ox)
        return moved[sy, sx, ox]

    for i, (py, px) in enumerate(out_phases):
        for r in range(3):
            for k in range(3):
                at_y, at_x = py + sign * (r - 1), px + sign * (k - 1)
                piece = shift_y(get(at_y % 2, at_x % 2, at_x // 2), at_y // 2)
                rows = pl.ds((m * len(out_phases) + i) * half, half)
                patch_ref[rows, pl.ds((r * 3 + k) * width + c * LANES, LANES)] = piece.astype(BF)


PHASES = ((0, 0), (0, 1), (1, 0), (1, 1))


class Sizes:
    pass


def k_reduce(x, ids, w, z):
    q = z.q1

    def body(k):
        (x_ref,), (map_ref, pay_ref), (tmp, rows_ref) = k.i, k.o, k.x
        k.wait_w()
        for y in range(z.height):
            product = dot(x_ref[y].reshape(MICRO * z.cols, z.c_in), k.w[0][...])
            for c in range(q):
                tmp[c, pl.ds(y * MICRO * z.cols, MICRO * z.cols), :] = product[:, c * LANES : (c + 1) * LANES]
        for m in range(MICRO):
            for y in range(z.height):
                for px in range(2):
                    at = m * z.rows + (2 * (y % 2) + px) * z.half + (y // 2) * 8
                    for c in range(q):
                        map_ref[pl.ds(at, 8), cols(c)] = tmp[
                            c, pl.ds((y * MICRO + m) * z.cols + px, 8, stride=2), :
                        ]
        rows_ref[...] = jnp.zeros(rows_ref.shape, F32)
        for m in range(MICRO):
            for c in range(q):
                stats_rows(map_ref[pl.ds(m * z.rows, z.rows), cols(c)], rows_ref, m * q + c, z.rows, MICRO * q)
        for m in range(MICRO):
            rows_ref[pl.ds(9 * q + m, 1), :] = jnp.full((1, LANES), k.s[0][m], F32)
        fill_stats(pay_ref, rows_ref, q)

    rows, pad = MICRO * z.rows, -(-(9 * q + MICRO) // 8) * 8
    return kernel_call(
        body,
        [arr(rows, z.c_mid), arr(z.n, pad, LANES, dtype=BF)],
        [x],
        [w],
        [pltpu.VMEM((q, rows, LANES), F32), pltpu.VMEM((pad, LANES), F32)],
        flops=2 * rows * z.c_in * z.c_mid,
        scalars=[ids],
        limit=16,
    )


def k_spatial(got, ids, pre, gain, offset, w, z):
    q = z.q1

    def body(k):
        got_ref, pre_ref, g_ref, o_ref = k.i
        patch_ref, next_ref, pay_ref, st_ref, mates_ref = k.o
        (rows_ref,) = k.x
        same, views = [], got_ref[...].astype(F32)
        for m in range(MICRO):
            view = views[:, 9 * q + m : 9 * q + m + 1]
            same += [(view == k.s[0][m]).astype(F32)] * q
        mates_ref[...] = jnp.concatenate(same, axis=1)
        merge_stats(got_ref, mates_ref, st_ref, q, z.rows)
        for m in range(MICRO):
            for c in range(q):
                mean, inverse = row(st_ref, m * q + c), row(st_ref, (MICRO + m) * q + c)
                phase = {}
                for i, p in enumerate(PHASES):
                    x = pre_ref[pl.ds(m * z.rows + i * z.half, z.half), cols(c)]
                    phase[p] = gelu(g_ref[:, cols(c)] * ((x - mean) * inverse) + o_ref[:, cols(c)])
                write_patches(phase, patch_ref, m, z.half, c, z.c_mid, 1)
        k.send(0)
        k.wait_w()
        next_ref[...] = dot(patch_ref[...], k.w[0][...])
        k.send(1)
        for m in range(MICRO):
            for c in range(q):
                stats_rows(next_ref[pl.ds(m * z.rows, z.rows), cols(c)], rows_ref, m * q + c, z.rows, MICRO * q)
        fill_stats(pay_ref, rows_ref, q)

    rows = MICRO * z.rows
    return kernel_call(
        body,
        [arr(rows, 9 * z.c_mid, dtype=BF), arr(rows, z.c_mid), stats_arr(z.n, q), arr(6 * q, LANES), arr(z.n, 3 * q, LANES)],
        [got, pre, gain, offset],
        [w],
        [pltpu.VMEM((stats_shape(q)[0], LANES), F32)],
        flops=2 * rows * 9 * z.c_mid * z.c_mid,
        scalars=[ids],
    )


def k_expand(got, mates, pre, gain, offset, w, z):
    q, qo = z.q1, z.q3

    def body(k):
        got_ref, mates_ref, pre_ref, g_ref, o_ref = k.i
        act_ref, next_ref, pay_ref, st_ref = k.o
        (rows_ref,) = k.x
        merge_stats(got_ref, mates_ref, st_ref, q, z.rows)
        k_o, k_q = MICRO * qo, MICRO * q
        rows_ref[...] = jnp.zeros(rows_ref.shape, F32)
        for m in range(MICRO):
            for c in range(q):
                mean, inverse = row(st_ref, m * q + c), row(st_ref, (MICRO + m) * q + c)
                at = pl.ds(m * z.rows, z.rows)
                x = pre_ref[at, cols(c)]
                act = gelu(g_ref[:, cols(c)] * ((x - mean) * inverse) + o_ref[:, cols(c)]).astype(BF)
                act_ref[at, cols(c)] = act
                mean = jnp.sum(act.astype(F32), axis=0, keepdims=True) * (1.0 / z.rows)
                high = mean.astype(BF).astype(F32)
                rows_ref[pl.ds(k_o + m * q + c, 1), :] = high
                rows_ref[pl.ds(k_o + k_q + m * q + c, 1), :] = mean - high
        k.send(0)
        k.wait_w()
        next_ref[...] = dot(act_ref[...], k.w[0][...])
        k.send(1)
        for m in range(MICRO):
            for c in range(qo):
                x = next_ref[pl.ds(m * z.rows, z.rows), cols(c)]
                away = x - jnp.sum(x, axis=0, keepdims=True) * (1.0 / z.rows)
                rows_ref[pl.ds(m * qo + c, 1), :] = jnp.sum(away * away, axis=0, keepdims=True)
        fill(pay_ref, rows_ref)

    rows = MICRO * z.rows
    return kernel_call(
        body,
        [arr(rows, z.c_mid, dtype=BF), arr(rows, z.c_in), arr(z.n, z.q_product, LANES, dtype=BF), arr(6 * q, LANES)],
        [got, mates, pre, gain, offset],
        [w],
        [pltpu.VMEM((z.q_product, LANES), F32)],
        flops=2 * rows * z.c_in * z.c_mid,
    )


def merge_product(got_ref, mates_ref, same_ref, w_ref, line_ref, st_ref, between_ref, q, qo, size):
    n, tall = got_ref.shape[0], got_ref.shape[1]
    ko, kq = MICRO * qo, MICRO * q
    mates = n // NVIEW
    got = got_ref[...].astype(F32)
    line_ref[...] = got.reshape(n * tall, LANES)
    squares = jnp.sum(mates_ref[...] * got[:, :ko], axis=0)

    def part(r):
        return line_ref[pl.ds(r, n, stride=tall), :].astype(BF)

    lines = [
        jnp.concatenate([part(first + m * q + c) for c in range(q)], axis=1)
        for first in (ko, ko + kq)
        for m in range(MICRO)
    ]
    both = dot(jnp.concatenate(lines, axis=0), w_ref[...])
    means = both[: MICRO * n] + both[MICRO * n :]
    for m in range(MICRO):
        same = same_ref[m]
        for c in range(qo):
            x = means[m * n : (m + 1) * n, c * LANES : (c + 1) * LANES]
            mean = jnp.sum(same * x, axis=0, keepdims=True) * (1.0 / mates)
            away = x - mean
            st_ref[pl.ds(m * qo + c, 1), :] = mean
            between_ref[pl.ds(m * qo + c, 1), :] = jnp.sum(same * (away * away), axis=0, keepdims=True)
    total = squares + size * between_ref[...]
    st_ref[ko:] = lax.rsqrt(total * (1.0 / (mates * size)) + EPSILON)


def k_narrow(got, mates, same, pre, gain, offset, maps_in, w_before, w, z):
    q, qo = z.q3, z.q4

    def body(k):
        got_ref, mates_ref, same_ref, wb_ref, pre_ref, g_ref, o_ref, in_ref = k.i
        slope_ref, join_ref, even_ref, next_ref, pay_ref, st_ref = k.o
        rows_ref, line_ref, between_ref = k.x
        merge_product(got_ref, mates_ref, same_ref, wb_ref, line_ref, st_ref, between_ref, z.q1, q, z.rows)
        for m in range(MICRO):
            for c in range(q):
                mean, inverse = row(st_ref, m * q + c), row(st_ref, (MICRO + m) * q + c)
                at = pl.ds(m * z.rows, z.rows)
                x = pre_ref[at, cols(c)]
                res = g_ref[:, cols(c)] * ((x - mean) * inverse) + o_ref[:, cols(c)] + in_ref[at, cols(c)].astype(F32)
                joined, slope = gelu_both(res)
                slope_ref[at, cols(c)] = slope.astype(BF)
                joined = joined.astype(BF)
                join_ref[at, cols(c)] = joined
                even_ref[pl.ds(m * z.half, z.half), cols(c)] = joined[: z.half]
        for j in range(3):
            k.send(j)
        k.wait_w()
        next_ref[...] = dot(join_ref[...], k.w[0][...])
        k.send(3)
        for m in range(MICRO):
            for c in range(qo):
                stats_rows(next_ref[pl.ds(m * z.rows, z.rows), cols(c)], rows_ref, m * qo + c, z.rows, MICRO * qo)
        fill_stats(pay_ref, rows_ref, qo)

    rows = MICRO * z.rows
    return kernel_call(
        body,
        [
            arr(rows, z.c_in, dtype=BF),
            arr(rows, z.c_in, dtype=BF),
            arr(MICRO * z.half, z.c_in, dtype=BF),
            arr(rows, z.c_wide),
            stats_arr(z.n, qo),
            arr(6 * q, LANES),
        ],
        [got, mates, same, w_before, pre, gain, offset, maps_in],
        [w],
        [
            pltpu.VMEM((stats_shape(qo)[0], LANES), F32),
            pltpu.VMEM((z.n * z.q_product, LANES), F32),
            pltpu.VMEM((MICRO * q, LANES), F32),
        ],
        flops=2 * rows * z.c_in * z.c_wide,
    )


def k_stride(got, mates, pre, gain, offset, w, z, passes=()):
    q = z.q4

    def body(k):
        got_ref, mates_ref, pre_ref, g_ref, o_ref = k.i
        act_ref, next_ref, pay_ref, st_ref = k.o
        patch_ref, rows_ref = k.x
        merge_stats(got_ref, mates_ref, st_ref, q, z.rows)
        for m in range(MICRO):
            for c in range(q):
                mean, inverse = row(st_ref, m * q + c), row(st_ref, (MICRO + m) * q + c)
                phase = {}
                for i, p in enumerate(PHASES):
                    x = pre_ref[pl.ds(m * z.rows + i * z.half, z.half), cols(c)]
                    phase[p] = gelu(g_ref[:, cols(c)] * ((x - mean) * inverse) + o_ref[:, cols(c)])
                    act_ref[pl.ds(m * z.rows + i * z.half, z.half), cols(c)] = phase[p].astype(BF)
                write_patches(phase, patch_ref, m, z.half, c, z.c_wide, 1, ((0, 0),))
        k.send(0)
        value = 0.0
        for tap in range(9):
            k.wait_w(chunk=tap)
            at = pl.ds(tap * z.c_wide, z.c_wide)
            value = value + dot(patch_ref[:, at], k.w[0][at])
        next_ref[...] = value
        k.send(1)
        for m in range(MICRO):
            for c in range(q):
                stats_rows(next_ref[pl.ds(m * z.half, z.half), cols(c)], rows_ref, m * q + c, z.half, MICRO * q)
        fill_stats(pay_ref, rows_ref, q)

    rows = MICRO * z.half
    return kernel_call(
        body,
        [arr(MICRO * z.rows, z.c_wide, dtype=BF), arr(rows, z.c_wide), stats_arr(z.n, q), arr(6 * q, LANES)],
        [got, mates, pre, gain, offset],
        [w],
        [pltpu.VMEM((rows, 9 * z.c_wide), BF), pltpu.VMEM((stats_shape(q)[0], LANES), F32)],
        flops=2 * rows * 9 * z.c_wide * z.c_wide,
        passes=passes,
        chunks=9,
    )


def k_shortcut(even, w, z):
    def body(k):
        (e_ref,), (next_ref, st_ref) = k.i, k.o
        value = 0.0
        for j in range(4):
            k.wait_w(chunk=j)
            at = pl.ds(j * z.c_in // 4, z.c_in // 4)
            value = value + dot(e_ref[:, at], k.w[0][at])
        next_ref[...] = value
        for c in range(z.q6):
            for m in range(MICRO):
                stats_rows(next_ref[pl.ds(m * z.half, z.half), cols(c)], st_ref.at[c], m, z.half, MICRO)

    rows = MICRO * z.half
    return kernel_call(
        body, [arr(rows, z.c_out), arr(z.q6, 8, LANES)], [even], [w], flops=2 * rows * z.c_in * z.c_out, chunks=4
    )


def k_widen(got, mates, pre, gain, offset, short_st, w, z, passes=()):
    q = z.q4

    def body(k):
        got_ref, mates_ref, pre_ref, g_ref, o_ref, short_ref = k.i
        act_ref, next_ref, pay_ref, st_ref = k.o
        merge_stats(got_ref, mates_ref, st_ref, q, z.half)
        for m in range(MICRO):
            for c in range(q):
                mean, inverse = row(st_ref, m * q + c), row(st_ref, (MICRO + m) * q + c)
                at = pl.ds(m * z.half, z.half)
                x = pre_ref[at, cols(c)]
                act_ref[at, cols(c)] = gelu(g_ref[:, cols(c)] * ((x - mean) * inverse) + o_ref[:, cols(c)]).astype(BF)
        k.send(0)
        k.wait_w()
        next_ref[...] = dot(act_ref[...], k.w[0][...])
        k.send(1)
        for c in range(z.q6):
            for m in range(MICRO):
                stats_rows(next_ref[pl.ds(m * z.half, z.half), cols(c)], pay_ref.at[c], m, z.half, MICRO)
            pay_ref[z.q6 + c] = short_ref[c]
        chunks = 2 * z.q6
        for j in range(chunks, z.n):
            pay_ref[j] = pay_ref[j % chunks]

    rows = MICRO * z.half
    return kernel_call(
        body,
        [arr(rows, z.c_wide, dtype=BF), arr(rows, z.c_out), arr(z.n, 8, LANES), arr(6 * q, LANES)],
        [got, mates, pre, gain, offset, short_st],
        [w],
        flops=2 * rows * z.c_wide * z.c_out,
        passes=passes,
    )


def k_views(got, ids, z):
    def body(k):
        (got_ref, id_ref), (pay_ref,), (lo, hi) = k.i, k.o, k.x
        mates = z.n // NVIEW
        g, ids = got_ref[...], id_ref[...]
        for view, ref in ((0, lo), (1, hi)):
            w = (ids == float(view)).astype(F32)
            mean = jnp.sum(w * g, axis=0)[:MICRO] * (1.0 / mates)
            away = g[:, :MICRO] - mean[None]
            total = jnp.sum(w[:, :MICRO] * (g[:, MICRO : 2 * MICRO] + z.half * (away * away)), axis=0)
            ref[...] = jnp.zeros(ref.shape, F32)
            ref[:MICRO] = mean
            ref[MICRO : 2 * MICRO] = lax.rsqrt(total * (1.0 / (mates * z.half)) + EPSILON)
        pay_ref[...] = jnp.where(ids > 0.5, hi[...][None], lo[...][None])

    return kernel_call(
        body, [arr(z.n, 8, LANES)], [got, ids], scratch=[pltpu.VMEM((8, LANES), F32)] * 2, limit=16
    )[0]


def k_mapped(whole, pre_w, pre_s, cot, gains, z, passes=()):
    def body(k):
        st_ref, w_ref, s_ref, cot_ref, gw, ow, gs, os = k.i
        map_ref, d_ref, pay_ref = k.o
        n_c = z.q6
        pay_ref[...] = jnp.zeros(pay_ref.shape, F32)
        for c in range(n_c):
            for m in range(MICRO):
                at = pl.ds(m * z.half, z.half)
                sw, ss = st_ref.at[c], st_ref.at[n_c + c]
                hat_w = (w_ref[at, cols(c)] - row(sw, m)) * row(sw, MICRO + m)
                hat_s = (s_ref[at, cols(c)] - row(ss, m)) * row(ss, MICRO + m)
                res = gw[:, cols(c)] * hat_w + ow[:, cols(c)] + (gs[:, cols(c)] * hat_s + os[:, cols(c)])
                map_ref[at, cols(c)] = gelu(res).astype(BF)
                d = gelu_slope(res) * cot_ref[at, cols(c)].astype(F32)
                d_ref[at, cols(c)] = d
                first, second = pay_ref.at[c], pay_ref.at[n_c + c]
                first[pl.ds(m, 1), :] = jnp.sum(d, axis=0, keepdims=True)
                first[pl.ds(MICRO + m, 1), :] = jnp.sum(d * hat_w, axis=0, keepdims=True)
                second[pl.ds(m, 1), :] = jnp.sum(d * hat_s, axis=0, keepdims=True)
        for j in range(2 * n_c, z.n):
            pay_ref[j] = pay_ref[j % (2 * n_c)]

    rows = MICRO * z.half
    return kernel_call(
        body,
        [arr(rows, z.c_out, dtype=BF), arr(rows, z.c_out), arr(z.n, 8, LANES)],
        [whole, pre_w, pre_s, cot, *gains],
        flops=rows * z.c_out * 60,
        passes=passes,
    )


def k_view_sums(got, ids, z):
    def body(k):
        (got_ref, id_ref), (pay_ref,), (both,) = k.i, k.o, k.x
        g, ids = got_ref[...], id_ref[...]
        lo = jnp.sum((ids == 0.0).astype(F32) * g, axis=0)
        hi = jnp.sum((ids == 1.0).astype(F32) * g, axis=0)
        both[0], both[1] = lo, hi
        all_views = lo + hi
        totals = []
        for k in range(2):
            totals.append(jnp.sum(all_views[k * MICRO : (k + 1) * MICRO], axis=0, keepdims=True))
        for v in range(2):
            for k in range(2):
                both[v, pl.ds(2 * MICRO + k, 1), :] = totals[k]
        pay_ref[...] = jnp.where(ids > 0.5, both[1][None], both[0][None])

    return kernel_call(body, [arr(z.n, 8, LANES)], [got, ids], scratch=[pltpu.VMEM((2, 8, LANES), F32)], limit=16)[0]


def back_rows(x, d, st_ref, sum_ref, m, q, c, gain):
    inverse = row(st_ref, (MICRO + m) * q + c)
    hat = (x - row(st_ref, m * q + c)) * inverse
    return gain * inverse * (d - row(sum_ref, m * q + c) - hat * row(sum_ref, (MICRO + m) * q + c))


def sum_rows(d, hat, rows_ref, r, offset):
    rows_ref[pl.ds(r, 1), :] = jnp.sum(d, axis=0, keepdims=True)
    rows_ref[pl.ds(r + offset, 1), :] = jnp.sum(d * hat, axis=0, keepdims=True)


def slope_and_sums(d_out, pre_ref, at, st_ref, m, q, c, g_ref, o_ref, d_ref, rows_ref):
    hat = (pre_ref[at, cols(c)] - row(st_ref, m * q + c)) * row(st_ref, (MICRO + m) * q + c)
    d = gelu_slope(g_ref[:, cols(c)] * hat + o_ref[:, cols(c)]) * d_out
    d_ref[at, cols(c)] = d
    sum_rows(d, hat, rows_ref, m * q + c, MICRO * q)


def k_back_widen(whole, sums, d_two, pre_w, pre_s, gain_w, gain_s, pre, st, gain, offset, place, w, z, passes=()):
    q, n_c = z.q4, z.q6

    def body(k):
        st2, sum_ref, d_ref, w_ref, s_ref, gw, gs, pre_ref, st_ref, g_ref, o_ref = k.i
        ds_ref, t_off, t_gw, t_gs, t_again, d_next, pay_ref = k.o
        dw_ref, rows_ref, tmp = k.x
        scale = 1.0 / (z.n // NVIEW * z.half)
        for c in range(n_c):
            first, second = sum_ref.at[c], sum_ref.at[n_c + c]
            t_off[pl.ds(c, 1), :] = row(first, 2 * MICRO)
            t_again[pl.ds(c, 1), :] = row(first, 2 * MICRO)
            t_gw[pl.ds(c, 1), :] = row(first, 2 * MICRO + 1)
            t_gs[pl.ds(c, 1), :] = row(second, 2 * MICRO)
            sw, ss = st2.at[c], st2.at[n_c + c]
            for m in range(MICRO):
                at = pl.ds(m * z.half, z.half)
                inv_w, inv_s = row(sw, MICRO + m), row(ss, MICRO + m)
                hat_w = (w_ref[at, cols(c)] - row(sw, m)) * inv_w
                hat_s = (s_ref[at, cols(c)] - row(ss, m)) * inv_s
                d = d_ref[at, cols(c)] - row(first, m) * scale
                dw_ref[at, cols(c)] = (
                    gw[:, cols(c)] * inv_w * (d - hat_w * (row(first, MICRO + m) * scale))
                ).astype(BF)
                ds_ref[at, cols(c)] = (gs[:, cols(c)] * inv_s * (d - hat_s * (row(second, m) * scale))).astype(BF)
        k.send(0)
        some = z.c_out // z.g
        for j in range(z.g):
            at = pl.ds(pl.multiple_of(((k.s[0][0] & (z.g - 1)) ^ j) * some, some), some)
            k.copy(dw_ref.at[:, at], k.raw[j].at[:, pl.ds(0, some)])
            k.copy(ds_ref.at[:, at], k.raw[j].at[:, pl.ds(some, some)])
        k.wait_w()
        tmp[...] = dot_nt(dw_ref[...], k.w[0][...])
        for m in range(MICRO):
            at = pl.ds(m * z.half, z.half)
            for c in range(q):
                slope_and_sums(tmp[at, cols(c)], pre_ref, at, st_ref, m, q, c, g_ref, o_ref, d_next, rows_ref)
        fill(pay_ref, rows_ref)

    rows = MICRO * z.half
    return kernel_call(
        body,
        [arr(rows, z.c_out, dtype=BF)]
        + [arr(n_c, LANES)] * 4
        + [arr(rows, z.c_wide), arr(z.n, 6 * q, LANES, dtype=BF)],
        [whole, sums, d_two, pre_w, pre_s, gain_w, gain_s, pre, st, gain, offset],
        [w],
        [
            pltpu.VMEM((rows, z.c_out), BF),
            pltpu.VMEM((6 * q, LANES), F32),
            pltpu.VMEM((rows, z.c_wide), F32),
        ],
        flops=2 * rows * z.c_wide * z.c_out,
        raw=[arr(rows, 2 * z.c_out // z.g, dtype=BF)] * z.g,
        n_raw=2 * z.g,
        scalars=[place],
        passes=passes,
    )


def back_start(refs, mates_ref, sum_ref, out_ref, q, n_rows, totals):
    got_ref, d_ref, pre_ref, st_ref, g_ref = refs
    merge_sums(got_ref, mates_ref, sum_ref, q, n_rows, totals)
    for m in range(MICRO):
        at = pl.ds(m * n_rows, n_rows)
        for c in range(q):
            out_ref[at, cols(c)] = back_rows(
                pre_ref[at, cols(c)], d_ref[at, cols(c)].astype(F32), st_ref, sum_ref, m, q, c, g_ref[:, cols(c)]
            ).astype(BF)


def k_back_stride(got, mates, d, pre_s, st_s, gain_s, pre, st, gain, offset, place, w, z, passes=()):
    q = z.q4

    def body(k):
        got_ref, mates_ref, d_ref, ps_ref, ss_ref, gs_ref, pre_ref, st_ref, g_ref, o_ref = k.i
        t_off, t_gain, d_next, pay_ref = k.o
        delta_ref, rows_ref, sum_ref, contrib = k.x
        back_start((got_ref, d_ref, ps_ref, ss_ref, gs_ref), mates_ref, sum_ref, delta_ref, q, z.half, (t_off, t_gain))
        some = z.c_wide // z.g
        for j in range(z.g):
            at = pl.ds(pl.multiple_of(((k.s[0][0] & (z.g - 1)) ^ j) * some, some), some)
            k.copy(delta_ref.at[:, at], k.raw[j])
        for tap in range(9):
            k.wait_w(chunk=tap)
            at = pl.ds(tap * z.c_wide, z.c_wide)
            contrib[:, at] = dot_nt(delta_ref[...], k.w[0][at])
        for m in range(MICRO):
            for c in range(q):
                phase = {}
                for r in range(3):
                    for k in range(3):
                        piece = contrib[pl.ds(m * z.half, z.half), pl.ds((r * 3 + k) * z.c_wide + c * LANES, LANES)]
                        piece = shift_x(shift_y(piece, 1 if r == 0 else 0), 1 if k == 0 else 0)
                        p = ((r + 1) % 2, (k + 1) % 2)
                        phase[p] = piece if p not in phase else phase[p] + piece
                first = second = 0.0
                mean, inverse = row(st_ref, m * q + c), row(st_ref, (MICRO + m) * q + c)
                for i, p in enumerate(PHASES):
                    at = pl.ds(m * z.rows + i * z.half, z.half)
                    hat = (pre_ref[at, cols(c)] - mean) * inverse
                    grad = gelu_slope(g_ref[:, cols(c)] * hat + o_ref[:, cols(c)]) * phase[p]
                    d_next[at, cols(c)] = grad
                    first = first + jnp.sum(grad, axis=0, keepdims=True)
                    second = second + jnp.sum(grad * hat, axis=0, keepdims=True)
                rows_ref[pl.ds(m * q + c, 1), :] = first
                rows_ref[pl.ds((MICRO + m) * q + c, 1), :] = second
        fill(pay_ref, rows_ref)

    rows = MICRO * z.half
    return kernel_call(
        body,
        [arr(q, LANES)] * 2
        + [arr(MICRO * z.rows, z.c_wide), arr(z.n, 6 * q, LANES, dtype=BF)],
        [got, mates, d, pre_s, st_s, gain_s, pre, st, gain, offset],
        [w],
        [
            pltpu.VMEM((rows, z.c_wide), BF),
            pltpu.VMEM((6 * q, LANES), F32),
            pltpu.VMEM((6 * q, LANES), F32),
            pltpu.VMEM((rows, 9 * z.c_wide), F32),
        ],
        flops=2 * rows * 9 * z.c_wide * z.c_wide,
        passes=passes,
        chunks=9,
        raw=[arr(rows, z.c_wide // z.g, dtype=BF)] * z.g,
        n_raw=z.g,
        scalars=[place],
    )


def k_back_narrow(got, mates, d, pre_n, st_n, gain_n, even, slope, pre, st, w, z, passes=()):
    q, qo = z.q4, z.q3

    def body(k):
        got_ref, mates_ref, d_ref, pn_ref, sn_ref, gn_ref, even_ref, slope_ref, pre_ref, st_ref = k.i
        delta_ref, t_off, t_gain, d_next, pay_ref = k.o
        rows_ref, sum_ref, tmp = k.x
        back_start((got_ref, d_ref, pn_ref, sn_ref, gn_ref), mates_ref, sum_ref, delta_ref, q, z.rows, (t_off, t_gain))
        k.send(0)
        k.wait_w()
        tmp[...] = dot_nt(delta_ref[...], k.w[0][...])
        for m in range(MICRO):
            at = pl.ds(m * z.rows, z.rows)
            some = pl.ds(m * z.rows, z.half)
            for c in range(qo):
                tmp[some, cols(c)] = tmp[some, cols(c)] + even_ref[pl.ds(m * z.half, z.half), cols(c)]
                d_join = tmp[at, cols(c)].astype(BF).astype(F32)
                one = slope_ref[at, cols(c)].astype(F32) * d_join
                hat = (pre_ref[at, cols(c)] - row(st_ref, m * qo + c)) * row(st_ref, (MICRO + m) * qo + c)
                d_next[at, cols(c)] = one.astype(BF)
                sum_rows(one, hat, rows_ref, m * qo + c, MICRO * qo)
        fill(pay_ref, rows_ref)

    rows = MICRO * z.rows
    return kernel_call(
        body,
        [arr(rows, z.c_wide, dtype=BF)] + [arr(q, LANES)] * 2 + [arr(rows, z.c_in, dtype=BF), arr(z.n, 6 * qo, LANES, dtype=BF)],
        [got, mates, d, pre_n, st_n, gain_n, even, slope, pre, st],
        [w],
        [
            pltpu.VMEM((6 * qo, LANES), F32),
            pltpu.VMEM((6 * q, LANES), F32),
            pltpu.VMEM((rows, z.c_in), F32),
        ],
        flops=2 * rows * z.c_in * z.c_wide,
        passes=passes,
    )


def k_back_expand(got, mates, d, pre_e, st_e, gain_e, pre, st, gain, offset, w, z, passes=()):
    q, qo = z.q3, z.q1

    def body(k):
        got_ref, mates_ref, d_ref, pe_ref, se_ref, ge_ref, pre_ref, st_ref, g_ref, o_ref = k.i
        delta_ref, t_off, t_gain, d_next, pay_ref = k.o
        rows_ref, sum_ref, tmp = k.x
        back_start((got_ref, d_ref, pe_ref, se_ref, ge_ref), mates_ref, sum_ref, delta_ref, q, z.rows, (t_off, t_gain))
        k.send(0)
        k.wait_w()
        tmp[...] = dot_nt(delta_ref[...], k.w[0][...])
        for m in range(MICRO):
            at = pl.ds(m * z.rows, z.rows)
            for c in range(qo):
                slope_and_sums(tmp[at, cols(c)], pre_ref, at, st_ref, m, qo, c, g_ref, o_ref, d_next, rows_ref)
        fill(pay_ref, rows_ref)

    rows = MICRO * z.rows
    return kernel_call(
        body,
        [arr(rows, z.c_in, dtype=BF)] + [arr(q, LANES)] * 2 + [arr(rows, z.c_mid), arr(z.n, 6 * qo, LANES, dtype=BF)],
        [got, mates, d, pre_e, st_e, gain_e, pre, st, gain, offset],
        [w],
        [
            pltpu.VMEM((6 * qo, LANES), F32),
            pltpu.VMEM((6 * q, LANES), F32),
            pltpu.VMEM((rows, z.c_mid), F32),
        ],
        flops=2 * rows * z.c_in * z.c_mid,
        passes=passes,
    )


def k_back_spatial(got, mates, d, pre_s, st_s, gain_s, pre, st, gain, offset, w, z, passes=()):
    q = z.q1

    def body(k):
        got_ref, mates_ref, d_ref, ps_ref, ss_ref, gs_ref, pre_ref, st_ref, g_ref, o_ref = k.i
        delta_ref, t_off, t_gain, d_next, pay_ref = k.o
        rows_ref, sum_ref, patch_ref, tmp = k.x
        merge_sums(got_ref, mates_ref, sum_ref, q, z.rows, (t_off, t_gain))
        for m in range(MICRO):
            for c in range(q):
                phase = {}
                for i, p in enumerate(PHASES):
                    at = pl.ds(m * z.rows + i * z.half, z.half)
                    phase[p] = back_rows(
                        ps_ref[at, cols(c)], d_ref[at, cols(c)], ss_ref, sum_ref, m, q, c, gs_ref[:, cols(c)]
                    )
                    delta_ref[at, cols(c)] = phase[p].astype(BF)
                write_patches(phase, patch_ref, m, z.half, c, z.c_mid, -1)
        k.send(0)
        k.wait_w()
        tmp[...] = dot(patch_ref[...], k.w[0][...])
        for m in range(MICRO):
            at = pl.ds(m * z.rows, z.rows)
            for c in range(q):
                slope_and_sums(tmp[at, cols(c)], pre_ref, at, st_ref, m, q, c, g_ref, o_ref, d_next, rows_ref)
        fill(pay_ref, rows_ref)

    rows = MICRO * z.rows
    return kernel_call(
        body,
        [arr(rows, z.c_mid, dtype=BF)] + [arr(q, LANES)] * 2 + [arr(rows, z.c_mid), arr(z.n, 6 * q, LANES, dtype=BF)],
        [got, mates, d, pre_s, st_s, gain_s, pre, st, gain, offset],
        [w],
        [
            pltpu.VMEM((6 * q, LANES), F32),
            pltpu.VMEM((6 * q, LANES), F32),
            pltpu.VMEM((rows, 9 * z.c_mid), BF),
            pltpu.VMEM((rows, z.c_mid), F32),
        ],
        flops=2 * rows * 9 * z.c_mid * z.c_mid,
        passes=passes,
    )


def k_back_reduce(got, mates, d, pre_r, st_r, gain_r, maps_in, place, z, passes=()):
    q, hi, r = z.q1, z.ns // z.slo, z.c_in // z.n

    def body(k):
        got_ref, mates_ref, d_ref, pr_ref, sr_ref, gr_ref, *maps = k.i
        delta_ref, t_off, t_gain = k.o
        sum_ref, *held = k.x
        back_start((got_ref, d_ref, pr_ref, sr_ref, gr_ref), mates_ref, sum_ref, delta_ref, q, z.rows, (t_off, t_gain))
        k.send(0)
        if maps:
            (held,) = held
            product = dot_tn(maps[0][...], delta_ref[...])
            held[...] = product.reshape(hi, z.slo, z.nb // 2, 2, r, z.c_mid).astype(BF)
            core = k.s[0][0] & 1
            k.copy(held.at[:, :, :, core], k.raw[0])
            k.copy(held.at[:, :, :, 1 - core], k.raw[1])

    rows = MICRO * z.rows
    maps = [] if maps_in is None else [maps_in]
    return kernel_call(
        body,
        [arr(rows, z.c_mid, dtype=BF)] + [arr(q, LANES)] * 2,
        [got, mates, d, pre_r, st_r, gain_r, *maps],
        scratch=[pltpu.VMEM((6 * q, LANES), F32)]
        + [pltpu.VMEM((hi, z.slo, z.nb // 2, 2, r, z.c_mid), BF) for _ in maps],
        passes=passes,
        scalars=[place],
        raw=[arr(hi, z.slo, z.nb // 2, r, z.c_mid, dtype=BF)] * (2 * len(maps)),
        n_raw=2 * len(maps),
        flops=2 * rows * z.c_in * z.c_mid,
    )


def k_input(delta, d_one, w, z, passes=()):
    def body(k):
        (delta_ref, one_ref), (out_ref,), (tmp, line) = k.i, k.o, k.x
        k.wait_w()
        tmp[...] = dot_nt(delta_ref[...], k.w[0][...])
        for m in range(MICRO):
            for y in range(z.height):
                for c in range(z.q3):
                    for px in range(2):
                        at = pl.ds(m * z.rows + (2 * (y % 2) + px) * z.half + (y // 2) * 8, 8)
                        line[c, pl.ds((y * MICRO + m) * z.cols + px, 8, stride=2), :] = (
                            one_ref[at, cols(c)].astype(F32) + tmp[at, cols(c)]
                        )
                    out_ref[y, m, :, cols(c)] = line[c, pl.ds((y * MICRO + m) * z.cols, z.cols), :].astype(BF)

    rows = MICRO * z.rows
    return kernel_call(
        body,
        [arr(z.height, MICRO, z.cols, z.c_in, dtype=BF)],
        [delta, d_one],
        [w],
        [pltpu.VMEM((rows, z.c_in), F32), pltpu.VMEM((z.q3, rows, LANES), F32)],
        flops=2 * rows * z.c_in * z.c_mid,
        passes=passes,
    )


def k_even(delta, w, z):
    def body(k):
        k.wait_w()
        k.o[0][...] = dot_nt(k.i[0][...], k.w[0][...])

    rows = delta.shape[0]
    return kernel_call(body, [arr(rows, z.c_in)], [delta], [w], flops=2 * rows * z.c_in * z.c_out)[0]


def k_first_grads(outs, evens, pieces, z):
    some = z.c_out // z.g
    a, b = z.c_wide // z.ns, z.c_in // z.ns

    def body(k):
        lhs_w, lhs_s, rhs = k.st
        held_w, held_s = k.x
        held_w[...] = dot_tn(lhs_w[...], rhs[:, :some]).astype(BF)
        for s in range(z.ns):
            k.copy(held_w.at[pl.ds(s * a, a)], k.raw[0].at[s % z.slo, s // z.slo, pl.ds(0, a)])
        held_s[...] = dot_tn(lhs_s[...], rhs[:, some:]).astype(BF)
        for s in range(z.ns):
            k.copy(held_s.at[pl.ds(s * b, b)], k.raw[0].at[s % z.slo, s // z.slo, pl.ds(a, b)])

    return kernel_call(
        body,
        [],
        [],
        scratch=[pltpu.VMEM((z.c_wide, some), BF), pltpu.VMEM((z.c_in, some), BF)],
        stacks=[outs, evens, pieces],
        raw=[arr(z.slo, z.ns // z.slo, a + b, some, dtype=BF)],
        n_raw=2 * z.ns,
        flops=2 * z.g * outs[0].shape[0] * (z.c_in + z.c_wide) * some,
    )[0]


def k_stride_grads(maps, pieces, z):
    few = z.c_wide // z.g
    c = 9 * z.c_wide // z.ns
    wide = z.c_out // z.c_wide
    d = c // wide
    rows = z.g * pieces[0].shape[0]

    def body(k):
        map_ref, rhs = k.st
        held, lhs = k.x
        for m in range(z.g * MICRO):
            for col in range(z.q4):
                phase = {}
                for i, p in enumerate(PHASES):
                    phase[p] = map_ref[pl.ds(m * z.rows + i * z.half, z.half), cols(col)].astype(F32)
                write_patches(phase, lhs, m, z.half, col, z.c_wide, 1, ((0, 0),))
        for t in range(9):
            at = pl.ds(t * z.c_wide, z.c_wide)
            held[at] = dot_tn(lhs[:, at], rhs[...]).astype(BF)
        for s in range(z.ns):
            for part in range(wide):
                k.copy(
                    held.at[pl.ds(s * c + part * d, d)],
                    k.raw[0].at[s % z.slo, s // z.slo, :, pl.ds(part * few, few)],
                )

    return kernel_call(
        body,
        [],
        [],
        scratch=[pltpu.VMEM((9 * z.c_wide, few), BF), pltpu.VMEM((rows, 9 * z.c_wide), BF)],
        stacks=[maps, pieces],
        raw=[arr(z.slo, z.ns // z.slo, d, wide * few, dtype=BF)],
        n_raw=wide * z.ns,
        flops=2 * rows * 9 * z.c_wide * few,
    )[0]


def k_products(pairs, place, z, passes=()):
    hi = z.ns // z.slo
    widths = [(o.shape[1], g.shape[1]) for o, g in pairs]
    rows = [r // z.n * c // 256 for r, c in widths]
    total = sum(rows)

    def body(k):
        (held,) = k.x
        at = 0
        for j, (r, c) in enumerate(widths):
            product = dot_tn(k.i[2 * j][...], k.i[2 * j + 1][...])
            blocks = product.reshape(hi, z.slo, z.nb // 2, 2, r // z.n, c).astype(BF)
            for part in range(c // 256):
                held[:, :, :, :, pl.ds(at, r // z.n), :] = blocks[..., part * 256 : (part + 1) * 256]
                at += r // z.n
        core = k.s[0][0] & 1
        k.copy(held.at[:, :, :, core], k.raw[0])
        k.copy(held.at[:, :, :, 1 - core], k.raw[1])

    return kernel_call(
        body,
        [],
        [a for pair in pairs for a in pair],
        scratch=[pltpu.VMEM((hi, z.slo, z.nb // 2, 2, total, 256), BF)],
        raw=[arr(hi, z.slo, z.nb // 2, total, 256, dtype=BF)] * 2,
        n_raw=2,
        scalars=[place],
        passes=passes,
        flops=sum(2 * pairs[j][0].shape[0] * r * c for j, (r, c) in enumerate(widths)),
    )


def k_sum_plane(groups, where, z, early=()):
    hi, high = z.ns // z.slo, z.nb // 2
    rows = [g[0].shape[3] for g in groups]

    tall = [e.shape[1] for e in early]

    def body(k):
        (held,) = k.x
        top = 0
        for e, r in zip(k.i[2 * len(groups) :], tall):
            k.copy(e, k.raw[-1].at[:, pl.ds(top, r)])
            top += r
        at = 0
        for j, r in enumerate(rows):
            both = k.i[2 * j][...].astype(F32) + k.i[2 * j + 1][...].astype(F32)
            held[:, :, :, pl.ds(at, r), :] = both.astype(BF)
            at += r
        for i in range(high):
            for j in range(z.slo):
                k.copy(held.at[:, k.s[0][0] ^ j, k.s[0][1] ^ i], k.raw[z.slo * i + j])

    total = sum(rows)
    return kernel_call(
        body,
        [],
        [a for g in groups for a in g] + list(early),
        scratch=[pltpu.VMEM((hi, z.slo, high, total, 256), BF)],
        raw=[arr(hi, total, 256, dtype=BF)] * (z.slo * high)
        + ([arr(hi, sum(tall), early[0].shape[2], dtype=BF)] if early else []),
        n_raw=z.slo * high + len(early),
        scalars=[where],
    )


def k_sum_line(groups, where, z, passes=()):
    hi = z.ns // z.slo
    rows = [g[0].shape[1] for g in groups]
    n = len(groups[0])

    def body(k):
        (held,) = k.x
        at = 0
        for j, r in enumerate(rows):
            value = k.i[j * n][...].astype(F32)
            for other in range(1, n):
                value = value + k.i[j * n + other][...].astype(F32)
            held[:, pl.ds(at, r), :] = value.astype(BF)
            at += r
        for j in range(hi):
            k.copy(held.at[k.s[0][2] ^ j], k.raw[j])

    total = sum(rows)
    return kernel_call(
        body,
        [],
        [a for g in groups for a in g],
        scratch=[pltpu.VMEM((hi, total, 256), BF)],
        raw=[arr(total, 256, dtype=BF)] * hi,
        n_raw=hi,
        scalars=[where],
        passes=passes,
    )


def k_sum_last(parts, passes=()):
    def body(k):
        value = k.i[0][...].astype(F32)
        for other in k.i[1:]:
            value = value + other[...].astype(F32)
        k.o[0][...] = value.astype(BF)

    return kernel_call(body, [arr(*parts[0].shape, dtype=BF)], parts, passes=passes)


def k_late_shares(pieces, place, shapes, z, passes=()):
    n = z.nb
    total = pieces[0].shape[0]

    def body(k):
        (held,) = k.x
        for j in range(n):
            held[k.s[0][0] ^ j] = k.i[j][...]
        for j in range(n):
            value = held[j].astype(F32)
            at = 0
            for g, (r, c) in enumerate(shapes):
                r = r // z.n
                for part in range(c // 256):
                    k.o[g][pl.ds(j * r, r), pl.ds(part * 256, 256)] = value[at : at + r]
                    at += r

    return kernel_call(
        body,
        [arr(r // z.ns, c) for r, c in shapes],
        list(pieces),
        scratch=[pltpu.VMEM((n, total, 256), BF)],
        scalars=[place],
        limit=24,
        passes=passes,
    )


def k_early_shares(pieces, place, z):
    n = z.g
    some, few = z.c_out // n, z.c_wide // n
    a, b, c = z.c_wide // z.ns, z.c_in // z.ns, 9 * z.c_wide // z.ns
    d = c * few // some

    def body(k):
        (held,) = k.x
        for j in range(n):
            held[(k.s[0][0] & (n - 1)) ^ j] = k.i[j][...]
        for j in range(n):
            value = held[j].astype(F32)
            k.o[0][:, pl.ds(j * some, some)] = value[:a]
            k.o[1][:, pl.ds(j * some, some)] = value[a : a + b]
            for part in range(some // few):
                k.o[2][pl.ds(part * d, d), pl.ds(j * few, few)] = value[a + b :, part * few : (part + 1) * few]

    return kernel_call(
        body,
        [arr(a, z.c_out), arr(b, z.c_out), arr(c, z.c_wide)],
        list(pieces),
        scratch=[pltpu.VMEM((n, a + b + d, some), BF)],
        scalars=[place],
        limit=24,
    )


def on_device(
    features,
    view_ids,
    w_reduce,
    w_spatial,
    w_expand,
    w_narrow,
    w_stride,
    w_widen,
    w_shortcut,
    gain_reduce,
    offset_reduce,
    gain_spatial,
    offset_spatial,
    gain_expand,
    offset_expand,
    gain_narrow,
    offset_narrow,
    gain_stride,
    offset_stride,
    gain_widen,
    offset_widen,
    gain_shortcut,
    offset_shortcut,
    cotangent,
):
    z = Sizes()
    z.ns, z.nb = lax.axis_size(SPACE), lax.axis_size(BATCH)
    z.slo = lax.axis_size("slo")
    z.g = min(z.nb, 4)
    z.n = z.ns * z.nb
    z.maps, z.cols = features.shape[1], features.shape[3]
    z.height = z.ns
    z.rows = z.height * z.cols
    z.half = z.rows // 4
    z.c_in, z.c_mid = w_reduce.shape
    z.c_wide, z.c_out = w_widen.shape
    z.q1, z.q3, z.q4, z.q6 = (c // LANES for c in (z.c_mid, z.c_in, z.c_wide, z.c_out))
    z.q_product = -(-MICRO * (z.q3 + 2 * z.q1) // 8) * 8
    assert features.shape[2] == 1 and cotangent.shape[1] == 1 and z.maps == z.ns and z.cols == 16
    yh, xh = z.height // 2, z.cols // 2
    n, ns, nb = z.n, z.ns, z.nb
    s, b = lax.axis_index(SPACE), lax.axis_index(BATCH)
    place = b.astype(jnp.int32).reshape(1)

    def share(pay):
        return lax.all_to_all(pay, ALL, 0, 0, tiled=True)

    def exchange(block):
        return lax.all_to_all(block, SPACE, 0, 0, tiled=True)

    def swap(block, axis, distance):
        return lax.ppermute(block, axis, [(i, i ^ distance) for i in range(lax.axis_size(axis))])

    def trade(pieces):
        pairs = [(i, i ^ j) for j in range(z.g) for i in range(nb)]
        return [p if j == 0 else lax.ppermute(p, BATCH, pairs[j * nb : (j + 1) * nb]) for j, p in enumerate(pieces)]

    def everywhere(block, places):
        pieces = []
        for high in range(places // 2):
            other = swap(block, "bhi", high) if high else block
            pieces += [other, swap(other, "core", 1)]
        return pieces

    def over_groups(product):
        distance = z.g // 2
        while distance < nb // 2:
            product = (product.astype(F32) + swap(product, "bhi", distance).astype(F32)).astype(BF)
            distance *= 2
        return product

    def lines(vector):
        return vector.reshape(1, -1)

    vectors = {
        "reduce": (lines(gain_reduce), lines(offset_reduce)),
        "spatial": (lines(gain_spatial), lines(offset_spatial)),
        "expand": (lines(gain_expand), lines(offset_expand)),
        "narrow": (lines(gain_narrow), lines(offset_narrow)),
        "stride": (lines(gain_stride), lines(offset_stride)),
        "widen": (lines(gain_widen), lines(offset_widen)),
        "shortcut": (lines(gain_shortcut), lines(offset_shortcut)),
    }

    my_ids = lax.dynamic_slice_in_dim(view_ids, s, 1, 1).astype(F32)
    arrived = exchange(features.reshape(MICRO, z.maps, z.cols, z.c_in).transpose(1, 0, 2, 3))
    pre_reduce, pay = k_reduce(arrived, my_ids.reshape(MICRO), w_reduce, z)
    got = share(pay)
    ids = got[:, 9 * z.q1 : 9 * z.q1 + MICRO].astype(F32)
    same = (ids == my_ids[None]).astype(F32)
    mates = {q: jnp.repeat(same, q, axis=1) for q in (z.q3, z.q4)}
    id_rows = jnp.concatenate([ids, ids, jnp.zeros((n, 2, LANES), F32)], axis=1)

    maps_in = arrived.reshape(yh, 2, MICRO, xh, 2, z.c_in).transpose(2, 1, 4, 0, 3, 5)
    maps_in = maps_in.reshape(MICRO * z.rows, z.c_in)

    patch_reduce, pre_spatial, pay, st_reduce, mates[z.q1] = k_spatial(
        got, my_ids.reshape(MICRO), pre_reduce, *vectors["reduce"], w_spatial, z
    )
    got = share(pay)
    out_spatial, pre_expand, pay, st_spatial = k_expand(got, mates[z.q1], pre_spatial, *vectors["spatial"], w_expand, z)
    got = share(pay)
    slope_one, joined, even, pre_narrow, pay, st_expand = k_narrow(
        got, mates[z.q3], same.transpose(1, 0, 2), pre_expand, *vectors["expand"], maps_in, w_expand, w_narrow, z
    )
    evens = everywhere(even, z.g)
    got = share(pay)
    pre_shortcut, short_st = k_shortcut(even, w_shortcut, z)
    out_narrow, pre_stride, pay, st_narrow = k_stride(
        got, mates[z.q4], pre_narrow, *vectors["narrow"], w_stride, z
    )
    got = share(pay)
    outs_narrow = everywhere(out_narrow, z.g)
    out_stride, pre_widen, pay, st_stride = k_widen(
        got, mates[z.q4], pre_stride, *vectors["stride"], short_st, w_widen, z
    )
    outs_stride = everywhere(out_stride, z.g)
    whole = share(k_views(share(pay), id_rows, z))
    mapped, d_two, pay = k_mapped(
        whole,
        pre_widen,
        pre_shortcut,
        cotangent.reshape(-1, z.c_out),
        (*vectors["widen"], *vectors["shortcut"]),
        z,
    )

    sums = share(k_view_sums(share(pay), id_rows, z))
    delta_shortcut, go_widen, gg_widen, gg_shortcut, go_shortcut, d_stride, pay, *more = k_back_widen(
        whole, sums, d_two, pre_widen, pre_shortcut, vectors["widen"][0], vectors["shortcut"][0],
        pre_stride, st_stride, *vectors["stride"], place, w_widen, z, (*outs_narrow, *evens, *outs_stride),
    )
    got = share(pay)
    pieces, outs_narrow, evens, outs_stride = (more[j * z.g : (j + 1) * z.g] for j in range(4))
    d_even = k_even(delta_shortcut, w_shortcut, z)
    first_pieces = trade(pieces)
    go_stride, gg_stride, d_narrow, pay, *more = k_back_stride(
        got, mates[z.q4], d_stride, pre_stride, st_stride, vectors["stride"][0],
        pre_narrow, st_narrow, *vectors["narrow"], place, w_stride, z, (*first_pieces, d_even),
    )
    pieces, first_pieces, d_even = more[: z.g], more[z.g : 2 * z.g], more[2 * z.g]
    got = share(pay)
    first = k_first_grads(outs_stride, evens, first_pieces, z)
    first = over_groups(first)
    pieces = trade(pieces)
    delta_narrow, go_narrow, gg_narrow, d_one, pay, first, *pieces = k_back_narrow(
        got, mates[z.q4], d_narrow, pre_narrow, st_narrow, vectors["narrow"][0],
        d_even, slope_one, pre_expand, st_expand, w_narrow, z, (first, *pieces),
    )
    got = share(pay)
    first = lax.psum_scatter(first, "slo", scatter_dimension=0, tiled=True)
    second = over_groups(k_stride_grads(outs_narrow, pieces, z))

    delta_expand, go_expand, gg_expand, d_spatial, pay, second = k_back_expand(
        got, mates[z.q3], d_one, pre_expand, st_expand, vectors["expand"][0],
        pre_spatial, st_spatial, *vectors["spatial"], w_expand, z, (second,),
    )
    got = share(pay)
    second = lax.psum_scatter(second, "slo", scatter_dimension=0, tiled=True)
    blocks = all(w.shape[0] % (8 * n) == 0 for w in (w_reduce, w_spatial, w_expand, w_narrow))
    pairs_some = [(joined, delta_narrow), (out_spatial, delta_expand)]
    kept_some, sent_some = k_products(pairs_some, place, z) if blocks else (None, delta_expand)
    flipped = w_spatial.reshape(9, z.c_mid, z.c_mid).transpose(0, 2, 1).reshape(9 * z.c_mid, z.c_mid)
    delta_spatial, go_spatial, gg_spatial, d_reduce, pay, sent_some, first = k_back_spatial(
        got, mates[z.q1], d_spatial, pre_spatial, st_spatial, vectors["spatial"][0],
        pre_reduce, st_reduce, *vectors["reduce"], flipped, z, (sent_some, first),
    )
    got = share(pay)
    pairs_more = [(patch_reduce, delta_spatial)]
    kept_more, sent_more = k_products(pairs_more, place, z) if blocks else (None, delta_spatial)
    came_some = swap(sent_some, "core", 1) if blocks else sent_some
    where = jnp.stack([lax.axis_index("slo"), lax.axis_index("bhi"), lax.axis_index("shi")]).astype(jnp.int32)

    def over_plane(groups, early):
        high = nb // 2
        parts = k_sum_plane(groups, where, z, early)
        came = []
        for i in range(high):
            for j in range(z.slo):
                pairs = [(u * z.slo + v, (u ^ i) * z.slo + (v ^ j)) for u in range(high) for v in range(z.slo)]
                part = parts[i * z.slo + j]
                came.append(lax.ppermute(part, ("bhi", "slo"), pairs) if i or j else part)
        return came, parts[high * z.slo :]

    delta_reduce, go_reduce, gg_reduce, *more = k_back_reduce(
        got, mates[z.q1], d_reduce, pre_reduce, st_reduce, vectors["reduce"][0], maps_in if blocks else None, place, z,
        (sent_more, came_some, where),
    )
    pairs_last, passed = [(maps_in, delta_reduce)], ()
    if blocks:
        kept_last, sent_last, sent_more, came_some, where = more
        groups = [(kept_some, came_some), (kept_more, swap(sent_more, "core", 1)), (kept_last, swap(sent_last, "core", 1))]
        passed, (early,) = over_plane(groups, (first[0], second[0]))
    else:
        early = jnp.concatenate([first[0], second[0]], axis=1)
    left, *passed = k_input(delta_reduce, d_one, w_reduce, z, passed)
    left = exchange(left)
    early = lax.psum_scatter(early, "shi", scatter_dimension=0, tiled=True)
    if blocks:
        *parts, early = k_sum_line([passed], where, z, (early,))
        early = k_early_shares(everywhere(early[0], z.g), place, z)
        parts = [p if j == 0 else swap(p, "shi", j) for j, p in enumerate(parts)]
        late, *early = k_sum_last(parts, early)
        late = everywhere(late, nb)
        shapes = [w.shape for w in (w_narrow, w_expand, w_spatial, w_reduce)]
        late = k_late_shares(late, place, shapes, z)
        grad_w_narrow, grad_w_expand, grad_w_spatial, grad_w_reduce = late
    else:
        late = [dot_tn(o, g).astype(BF) for o, g in pairs_some + pairs_more + pairs_last]
        late = [lax.psum_scatter(w, SPACE, scatter_dimension=0, tiled=True) for w in late]
        late = [w.astype(F32) for w in lax.psum(late, BATCH)]
        grad_w_narrow, grad_w_expand, grad_w_spatial, grad_w_reduce = late
        early = k_early_shares(everywhere(early[0], z.g), place, z)
    grad_w_widen, grad_w_shortcut, grad_w_stride = early
    grad_features = left.transpose(1, 0, 2, 3).reshape(features.shape)

    flat = lambda block: block.reshape(-1)
    return (
        mapped.reshape(cotangent.shape),
        grad_features,
        grad_w_reduce,
        grad_w_spatial,
        grad_w_expand,
        grad_w_narrow,
        grad_w_stride,
        grad_w_widen,
        grad_w_shortcut,
        flat(gg_reduce),
        flat(go_reduce),
        flat(gg_spatial),
        flat(go_spatial),
        flat(gg_expand),
        flat(go_expand),
        flat(gg_narrow),
        flat(go_narrow),
        flat(gg_stride),
        flat(go_stride),
        flat(gg_widen),
        flat(go_widen),
        flat(gg_shortcut),
        flat(go_shortcut),
    )


def solution(mesh):
    nb, ns = mesh.shape["batch"], mesh.shape["space"]
    fine = Mesh(mesh.devices.reshape(nb // 2, 2, ns // 2, 2), ALL)
    maps = P(None, ALL, None, None, None)
    return jax.shard_map(
        on_device,
        mesh=fine,
        in_specs=(P(None, BATCH, SPACE, None, None), P(None, BATCH)) + (P(),) * 21 + (maps,),
        out_specs=(maps, P(None, BATCH, SPACE, None, None)) + (P(SPACE, None),) * 7 + (P(),) * 14,
        check_vma=False,
    )
```

```python
import functools
import math

import jax
import jax.numpy as jnp
from jax import lax
from jax.experimental import pallas as pl
from jax.experimental.pallas import tpu as pltpu
from jax.sharding import Mesh
from jax.sharding import PartitionSpec as P

NVIEW = 2
MICRO = 3
EPSILON = 1e-05
BF = jnp.bfloat16
F32 = jnp.float32
BATCH, SPACE = ("bhi", "core"), ("shi", "slo")
ALL = BATCH + SPACE
LANES = 128
ROOT = math.sqrt(2.0 / math.pi)
CUBE = 0.044715


def dot(a, b, dims=((1,), (0,))):
    return lax.dot_general(a, b, (dims, ((), ())), preferred_element_type=F32)


def dot_nt(a, b):
    return dot(a, b, ((1,), (1,)))


def dot_tn(a, b):
    return dot(a, b, ((0,), (0,)))


def gelu(v):
    return 0.5 * v * (1.0 + jnp.tanh(ROOT * (v + CUBE * (v * v * v))))


def gelu_slope(v):
    square = v * v
    t = jnp.tanh(ROOT * (v + CUBE * (square * v)))
    return 0.5 * (1.0 + t) + (0.5 * ROOT) * v * (1.0 - t * t) * (1.0 + (3.0 * CUBE) * square)


def gelu_both(v):
    square = v * v
    t = jnp.tanh(ROOT * (v + CUBE * (square * v)))
    half = 0.5 * (1.0 + t)
    return v * half, half + (0.5 * ROOT) * v * (1.0 - t * t) * (1.0 + (3.0 * CUBE) * square)


def cols(c):
    return pl.ds(c * LANES, LANES)


def row(ref, r):
    return ref[pl.ds(r, 1), :]


class Kernel:
    def __init__(self, i, w, o, raw, scalars, stacks, extra, starts, sems):
        self.i, self.w, self.o, self.raw, self.s, self.st, self.x = i, w, o, raw, scalars, stacks, extra
        self.w_copies, self.out_pairs, self.sems = starts, {}, sems
        self.flying, self.sent = [], set()

    def wait_w(self, n=0, chunk=None):
        for copy in self.w_copies[n] if chunk is None else [self.w_copies[n][chunk]]:
            copy.wait()

    def send(self, n):
        src, dst, sem = self.out_pairs[n]
        copy = pltpu.make_async_copy(src, dst, sem)
        copy.start()
        self.flying.append(copy)
        self.sent.add(n)

    def copy(self, src, dst):
        copy = pltpu.make_async_copy(src, dst, self.sems.pop())
        copy.start()
        self.flying.append(copy)


def kernel_call(body, outs, args, weights=(), scratch=(), flops=0, raw=(), n_raw=0, scalars=(), passes=(), stacks=(), limit=63, chunks=1, late=0):
    n_s, n_in, n_w, n_p = len(scalars), len(args), len(weights), len(passes)
    n_k = sum(map(len, stacks))
    n_out, n_r = len(outs), len(raw)

    def run(*refs):
        refs = list(refs)

        def take(n):
            part = refs[:n]
            del refs[:n]
            return part

        s, ins, w_any = take(n_s), take(n_in), take(n_w)
        piles = [take(len(g)) for g in stacks]
        take(n_p)
        out, raw_refs, _ = take(n_out), take(n_r), take(n_p)
        v_in, v_w, v_out, v_k = take(n_in), take(n_w), take(n_out), take(len(stacks))
        (sems,) = take(1)
        sem = [sems.at[j] for j in range(n_in + n_w * chunks + n_k + n_out + n_raw)]
        in_copies = [pltpu.make_async_copy(a, v, sem.pop(0)) for a, v in zip(ins, v_in)]
        for pile, v in zip(piles, v_k):
            for j, a in enumerate(pile):
                rows = a.shape[0]
                in_copies.append(pltpu.make_async_copy(a, v.at[pl.ds(j * rows, rows)], sem.pop(0)))
        w_copies = []
        for a, v in zip(w_any, v_w):
            some = a.shape[0] // chunks
            parts = [pl.ds(j * some, some) for j in range(chunks)]
            w_copies.append([pltpu.make_async_copy(a.at[at], v.at[at], sem.pop(0)) for at in parts])
        for copy in in_copies + [c for copies in w_copies for c in copies]:
            copy.start()
        k = Kernel(v_in, v_w, v_out, raw_refs, s, v_k, refs, w_copies, sem[n_out:])
        k.out_pairs = {j: (v_out[j], out[j], sem[j]) for j in range(n_out)}
        k.coming = in_copies[len(in_copies) - late :]
        for copy in in_copies[: len(in_copies) - late]:
            copy.wait()
        body(k)
        for j in range(n_out):
            if j not in k.sent:
                k.send(j)
        for copy in k.flying:
            copy.wait()

    def size(a):
        return math.prod(a.shape) * jnp.dtype(a.dtype).itemsize

    outside = pl.BlockSpec(memory_space=pl.ANY)
    piled = [arr(len(g) * g[0].shape[0], *g[0].shape[1:], dtype=g[0].dtype) for g in stacks]
    held = sum(map(size, (*args, *weights, *outs, *piled)))
    total = held + sum(size(a) for a in scratch if hasattr(a, "dtype"))
    first = n_s + n_in + n_w + n_k
    results = pl.pallas_call(
        run,
        out_shape=tuple(jax.ShapeDtypeStruct(o.shape, o.dtype) for o in (*outs, *raw, *passes)),
        in_specs=[pl.BlockSpec(memory_space=pltpu.SMEM)] * n_s + [outside] * (n_in + n_w + n_k + n_p),
        out_specs=tuple([outside] * (n_out + n_r + n_p)),
        scratch_shapes=[pltpu.VMEM(a.shape, a.dtype) for a in (*args, *weights, *outs, *piled)]
        + [pltpu.SemaphoreType.DMA((n_in + n_w * chunks + n_k + n_out + n_raw,))]
        + list(scratch),
        input_output_aliases={first + j: n_out + n_r + j for j in range(n_p)},
        cost_estimate=pl.CostEstimate(flops=flops, bytes_accessed=held, transcendentals=0),
        compiler_params=pltpu.CompilerParams(vmem_limit_bytes=max(limit * 2**20, total)),
    )(*scalars, *args, *weights, *(a for g in stacks for a in g), *passes)
    return tuple(results)


def arr(*shape, dtype=F32):
    return jax.ShapeDtypeStruct(shape, dtype)


def fill(pay_ref, rows_ref):
    block = rows_ref[...].astype(pay_ref.dtype)

    def step(j, _):
        pay_ref[j] = block
        return 0

    lax.fori_loop(0, pay_ref.shape[0], step, 0, unroll=8)


def stats_rows(value, rows_ref, r, size, offset):
    mean = jnp.sum(value, axis=0, keepdims=True) * (1.0 / size)
    away = value - mean
    rows_ref[pl.ds(r, 1), :] = mean
    rows_ref[pl.ds(r + offset, 1), :] = jnp.sum(away * away, axis=0, keepdims=True)


def stats_shape(q):
    return 9 * q, BF


def stats_arr(n, q):
    rows, dtype = stats_shape(q)
    return arr(n, rows, LANES, dtype=dtype)


def fill_stats(pay_ref, rows_ref, q):
    k = MICRO * q
    if pay_ref.dtype == BF:
        mean, square = rows_ref[:k], rows_ref[k : 2 * k]
        high = mean.astype(BF).astype(F32)
        rows_ref[:k] = high
        rows_ref[k : 2 * k] = mean - high
        rows_ref[2 * k : 3 * k] = square
    fill(pay_ref, rows_ref)


def merge_stats(got_ref, mates_ref, st_ref, q, size):
    n = got_ref.shape[0]
    k = MICRO * q
    mates = n // NVIEW
    step = 8

    def parts(at):
        got = got_ref[at].astype(F32)
        if got_ref.dtype == BF:
            return got[:, :k] + got[:, k : 2 * k], got[:, 2 * k : 3 * k]
        return got[:, :k], got[:, k : 2 * k]

    def one(i, acc):
        at = pl.ds(i * step, step)
        return acc + jnp.sum(mates_ref[at] * parts(at)[0], axis=0)

    mean = lax.fori_loop(0, n // step, one, jnp.zeros((k, LANES), F32), unroll=4) * (1.0 / mates)

    def two(i, acc):
        at = pl.ds(i * step, step)
        means, squares = parts(at)
        away = means - mean[None]
        return acc + jnp.sum(mates_ref[at] * (squares + size * (away * away)), axis=0)

    total = lax.fori_loop(0, n // step, two, jnp.zeros((k, LANES), F32), unroll=4)
    st_ref[:k] = mean
    st_ref[k : 2 * k] = lax.rsqrt(total * (1.0 / (mates * size)) + EPSILON)


def merge_sums(got_ref, mates_ref, sum_ref, q, size, total_refs):
    n = got_ref.shape[0]
    k = MICRO * q
    scale = 1.0 / (n // NVIEW * size)
    step = 8

    def one(i, carry):
        at = pl.ds(i * step, step)
        both = got_ref[at].astype(F32)
        first, second = both[:, :k], both[:, k : 2 * k]
        w = mates_ref[at]
        return (
            carry[0] + jnp.sum(w * first, axis=0),
            carry[1] + jnp.sum(w * second, axis=0),
            carry[2] + jnp.sum(first, axis=0),
            carry[3] + jnp.sum(second, axis=0),
        )

    zero = jnp.zeros((k, LANES), F32)
    a, b, ta, tb = lax.fori_loop(0, n // step, one, (zero,) * 4, unroll=4)
    sum_ref[:k] = a * scale
    sum_ref[k : 2 * k] = b * scale
    for ref, t in zip(total_refs, (ta, tb)):
        ref[...] = t[:q] + t[q : 2 * q] + t[2 * q :]


def shift_y(v, offset):
    if offset == 0:
        return v
    zero = jnp.zeros((8, v.shape[1]), v.dtype)
    if offset > 0:
        return jnp.concatenate([v[8:], zero], axis=0)
    return jnp.concatenate([zero, v[:-8]], axis=0)


def shift_x(v, offset):
    if offset == 0:
        return v
    place = lax.broadcasted_iota(jnp.int32, v.shape, 0) % 8
    if offset > 0:
        return jnp.where(place == 7, 0.0, pltpu.roll(v, v.shape[0] - 1, axis=0))
    return jnp.where(place == 0, 0.0, pltpu.roll(v, 1, axis=0))


def write_patches(phase, patch_ref, m, half, c, width, sign, out_phases=((0, 0), (0, 1), (1, 0), (1, 1))):
    moved = {}

    def get(sy, sx, ox):
        if (sy, sx, ox) not in moved:
            moved[sy, sx, ox] = shift_x(phase[sy, sx], ox)
        return moved[sy, sx, ox]

    for i, (py, px) in enumerate(out_phases):
        for r in range(3):
            for k in range(3):
                at_y, at_x = py + sign * (r - 1), px + sign * (k - 1)
                piece = shift_y(get(at_y % 2, at_x % 2, at_x // 2), at_y // 2)
                rows = pl.ds((m * len(out_phases) + i) * half, half)
                patch_ref[rows, pl.ds((r * 3 + k) * width + c * LANES, LANES)] = piece.astype(BF)


PHASES = ((0, 0), (0, 1), (1, 0), (1, 1))


class Sizes:
    pass


def k_reduce(x, ids, w, z):
    q = z.q1

    def body(k):
        (x_ref,), (map_ref, pay_ref), (tmp, rows_ref) = k.i, k.o, k.x
        k.wait_w()
        for y in range(z.height):
            product = dot(x_ref[y].reshape(MICRO * z.cols, z.c_in), k.w[0][...])
            for c in range(q):
                tmp[c, pl.ds(y * MICRO * z.cols, MICRO * z.cols), :] = product[:, c * LANES : (c + 1) * LANES]
        for m in range(MICRO):
            for y in range(z.height):
                for px in range(2):
                    at = m * z.rows + (2 * (y % 2) + px) * z.half + (y // 2) * 8
                    for c in range(q):
                        map_ref[pl.ds(at, 8), cols(c)] = tmp[
                            c, pl.ds((y * MICRO + m) * z.cols + px, 8, stride=2), :
                        ]
        rows_ref[...] = jnp.zeros(rows_ref.shape, F32)
        for m in range(MICRO):
            for c in range(q):
                stats_rows(map_ref[pl.ds(m * z.rows, z.rows), cols(c)], rows_ref, m * q + c, z.rows, MICRO * q)
        for m in range(MICRO):
            rows_ref[pl.ds(9 * q + m, 1), :] = jnp.full((1, LANES), k.s[0][m], F32)
        fill_stats(pay_ref, rows_ref, q)

    rows, pad = MICRO * z.rows, -(-(9 * q + MICRO) // 8) * 8
    return kernel_call(
        body,
        [arr(rows, z.c_mid), arr(z.n, pad, LANES, dtype=BF)],
        [x],
        [w],
        [pltpu.VMEM((q, rows, LANES), F32), pltpu.VMEM((pad, LANES), F32)],
        flops=2 * rows * z.c_in * z.c_mid,
        scalars=[ids],
        limit=16,
    )


def k_spatial(got, ids, pre, gain, offset, w, z):
    q = z.q1

    def body(k):
        got_ref, pre_ref, g_ref, o_ref = k.i
        patch_ref, next_ref, pay_ref, st_ref, mates_ref = k.o
        (rows_ref,) = k.x
        same, views = [], got_ref[...].astype(F32)
        for m in range(MICRO):
            view = views[:, 9 * q + m : 9 * q + m + 1]
            same += [(view == k.s[0][m]).astype(F32)] * q
        mates_ref[...] = jnp.concatenate(same, axis=1)
        merge_stats(got_ref, mates_ref, st_ref, q, z.rows)
        for m in range(MICRO):
            for c in range(q):
                mean, inverse = row(st_ref, m * q + c), row(st_ref, (MICRO + m) * q + c)
                phase = {}
                for i, p in enumerate(PHASES):
                    x = pre_ref[pl.ds(m * z.rows + i * z.half, z.half), cols(c)]
                    phase[p] = gelu(g_ref[:, cols(c)] * ((x - mean) * inverse) + o_ref[:, cols(c)])
                write_patches(phase, patch_ref, m, z.half, c, z.c_mid, 1)
        k.send(0)
        k.wait_w()
        next_ref[...] = dot(patch_ref[...], k.w[0][...])
        k.send(1)
        for m in range(MICRO):
            for c in range(q):
                stats_rows(next_ref[pl.ds(m * z.rows, z.rows), cols(c)], rows_ref, m * q + c, z.rows, MICRO * q)
        fill_stats(pay_ref, rows_ref, q)

    rows = MICRO * z.rows
    return kernel_call(
        body,
        [arr(rows, 9 * z.c_mid, dtype=BF), arr(rows, z.c_mid), stats_arr(z.n, q), arr(6 * q, LANES), arr(z.n, 3 * q, LANES)],
        [got, pre, gain, offset],
        [w],
        [pltpu.VMEM((stats_shape(q)[0], LANES), F32)],
        flops=2 * rows * 9 * z.c_mid * z.c_mid,
        scalars=[ids],
    )


def k_expand(got, mates, pre, gain, offset, w, z):
    q, qo = z.q1, z.q3

    def body(k):
        got_ref, mates_ref, pre_ref, g_ref, o_ref = k.i
        act_ref, next_ref, pay_ref, st_ref = k.o
        (rows_ref,) = k.x
        merge_stats(got_ref, mates_ref, st_ref, q, z.rows)
        k_o, k_q = MICRO * qo, MICRO * q
        rows_ref[...] = jnp.zeros(rows_ref.shape, F32)
        for m in range(MICRO):
            for c in range(q):
                mean, inverse = row(st_ref, m * q + c), row(st_ref, (MICRO + m) * q + c)
                at = pl.ds(m * z.rows, z.rows)
                x = pre_ref[at, cols(c)]
                act = gelu(g_ref[:, cols(c)] * ((x - mean) * inverse) + o_ref[:, cols(c)]).astype(BF)
                act_ref[at, cols(c)] = act
                mean = jnp.sum(act.astype(F32), axis=0, keepdims=True) * (1.0 / z.rows)
                high = mean.astype(BF).astype(F32)
                rows_ref[pl.ds(k_o + m * q + c, 1), :] = high
                rows_ref[pl.ds(k_o + k_q + m * q + c, 1), :] = mean - high
        k.send(0)
        k.wait_w()
        next_ref[...] = dot(act_ref[...], k.w[0][...])
        k.send(1)
        for m in range(MICRO):
            for c in range(qo):
                x = next_ref[pl.ds(m * z.rows, z.rows), cols(c)]
                away = x - jnp.sum(x, axis=0, keepdims=True) * (1.0 / z.rows)
                rows_ref[pl.ds(m * qo + c, 1), :] = jnp.sum(away * away, axis=0, keepdims=True)
        fill(pay_ref, rows_ref)

    rows = MICRO * z.rows
    return kernel_call(
        body,
        [arr(rows, z.c_mid, dtype=BF), arr(rows, z.c_in), arr(z.n, z.q_product, LANES, dtype=BF), arr(6 * q, LANES)],
        [got, mates, pre, gain, offset],
        [w],
        [pltpu.VMEM((z.q_product, LANES), F32)],
        flops=2 * rows * z.c_in * z.c_mid,
    )


def merge_product(got_ref, mates_ref, same_ref, w_ref, line_ref, st_ref, between_ref, q, qo, size):
    n, tall = got_ref.shape[0], got_ref.shape[1]
    ko, kq = MICRO * qo, MICRO * q
    mates = n // NVIEW
    got = got_ref[...].astype(F32)
    line_ref[...] = got.reshape(n * tall, LANES)
    squares = jnp.sum(mates_ref[...] * got[:, :ko], axis=0)

    def part(r):
        return line_ref[pl.ds(r, n, stride=tall), :].astype(BF)

    lines = [
        jnp.concatenate([part(first + m * q + c) for c in range(q)], axis=1)
        for first in (ko, ko + kq)
        for m in range(MICRO)
    ]
    both = dot(jnp.concatenate(lines, axis=0), w_ref[...])
    means = both[: MICRO * n] + both[MICRO * n :]
    for m in range(MICRO):
        same = same_ref[m]
        for c in range(qo):
            x = means[m * n : (m + 1) * n, c * LANES : (c + 1) * LANES]
            mean = jnp.sum(same * x, axis=0, keepdims=True) * (1.0 / mates)
            away = x - mean
            st_ref[pl.ds(m * qo + c, 1), :] = mean
            between_ref[pl.ds(m * qo + c, 1), :] = jnp.sum(same * (away * away), axis=0, keepdims=True)
    total = squares + size * between_ref[...]
    st_ref[ko:] = lax.rsqrt(total * (1.0 / (mates * size)) + EPSILON)


def k_narrow(got, mates, same, pre, gain, offset, maps_in, w_before, w, z):
    q, qo = z.q3, z.q4

    def body(k):
        got_ref, mates_ref, same_ref, wb_ref, pre_ref, g_ref, o_ref, in_ref = k.i
        slope_ref, join_ref, even_ref, next_ref, pay_ref, st_ref = k.o
        rows_ref, line_ref, between_ref = k.x
        merge_product(got_ref, mates_ref, same_ref, wb_ref, line_ref, st_ref, between_ref, z.q1, q, z.rows)
        for m in range(MICRO):
            for c in range(q):
                mean, inverse = row(st_ref, m * q + c), row(st_ref, (MICRO + m) * q + c)
                at = pl.ds(m * z.rows, z.rows)
                x = pre_ref[at, cols(c)]
                res = g_ref[:, cols(c)] * ((x - mean) * inverse) + o_ref[:, cols(c)] + in_ref[at, cols(c)].astype(F32)
                joined, slope = gelu_both(res)
                slope_ref[at, cols(c)] = slope.astype(BF)
                joined = joined.astype(BF)
                join_ref[at, cols(c)] = joined
                even_ref[pl.ds(m * z.half, z.half), cols(c)] = joined[: z.half]
        for j in range(3):
            k.send(j)
        k.wait_w()
        next_ref[...] = dot(join_ref[...], k.w[0][...])
        k.send(3)
        for m in range(MICRO):
            for c in range(qo):
                stats_rows(next_ref[pl.ds(m * z.rows, z.rows), cols(c)], rows_ref, m * qo + c, z.rows, MICRO * qo)
        fill_stats(pay_ref, rows_ref, qo)

    rows = MICRO * z.rows
    return kernel_call(
        body,
        [
            arr(rows, z.c_in, dtype=BF),
            arr(rows, z.c_in, dtype=BF),
            arr(MICRO * z.half, z.c_in, dtype=BF),
            arr(rows, z.c_wide),
            stats_arr(z.n, qo),
            arr(6 * q, LANES),
        ],
        [got, mates, same, w_before, pre, gain, offset, maps_in],
        [w],
        [
            pltpu.VMEM((stats_shape(qo)[0], LANES), F32),
            pltpu.VMEM((z.n * z.q_product, LANES), F32),
            pltpu.VMEM((MICRO * q, LANES), F32),
        ],
        flops=2 * rows * z.c_in * z.c_wide,
    )


def k_stride(got, mates, pre, gain, offset, w, z, passes=()):
    q = z.q4

    def body(k):
        got_ref, mates_ref, pre_ref, g_ref, o_ref = k.i
        act_ref, next_ref, pay_ref, st_ref = k.o
        patch_ref, rows_ref = k.x
        merge_stats(got_ref, mates_ref, st_ref, q, z.rows)
        for m in range(MICRO):
            for c in range(q):
                mean, inverse = row(st_ref, m * q + c), row(st_ref, (MICRO + m) * q + c)
                phase = {}
                for i, p in enumerate(PHASES):
                    x = pre_ref[pl.ds(m * z.rows + i * z.half, z.half), cols(c)]
                    phase[p] = gelu(g_ref[:, cols(c)] * ((x - mean) * inverse) + o_ref[:, cols(c)])
                    act_ref[pl.ds(m * z.rows + i * z.half, z.half), cols(c)] = phase[p].astype(BF)
                write_patches(phase, patch_ref, m, z.half, c, z.c_wide, 1, ((0, 0),))
        k.send(0)
        value = 0.0
        for tap in range(9):
            k.wait_w(chunk=tap)
            at = pl.ds(tap * z.c_wide, z.c_wide)
            value = value + dot(patch_ref[:, at], k.w[0][at])
        next_ref[...] = value
        k.send(1)
        for m in range(MICRO):
            for c in range(q):
                stats_rows(next_ref[pl.ds(m * z.half, z.half), cols(c)], rows_ref, m * q + c, z.half, MICRO * q)
        fill_stats(pay_ref, rows_ref, q)

    rows = MICRO * z.half
    return kernel_call(
        body,
        [arr(MICRO * z.rows, z.c_wide, dtype=BF), arr(rows, z.c_wide), stats_arr(z.n, q), arr(6 * q, LANES)],
        [got, mates, pre, gain, offset],
        [w],
        [pltpu.VMEM((rows, 9 * z.c_wide), BF), pltpu.VMEM((stats_shape(q)[0], LANES), F32)],
        flops=2 * rows * 9 * z.c_wide * z.c_wide,
        passes=passes,
        chunks=9,
    )


def k_shortcut(even, w, z):
    def body(k):
        (e_ref,), (next_ref, st_ref) = k.i, k.o
        value = 0.0
        for j in range(4):
            k.wait_w(chunk=j)
            at = pl.ds(j * z.c_in // 4, z.c_in // 4)
            value = value + dot(e_ref[:, at], k.w[0][at])
        next_ref[...] = value
        for c in range(z.q6):
            for m in range(MICRO):
                stats_rows(next_ref[pl.ds(m * z.half, z.half), cols(c)], st_ref.at[c], m, z.half, MICRO)

    rows = MICRO * z.half
    return kernel_call(
        body, [arr(rows, z.c_out), arr(z.q6, 8, LANES)], [even], [w], flops=2 * rows * z.c_in * z.c_out, chunks=4
    )


def k_widen(got, mates, pre, gain, offset, short_st, w, z, passes=()):
    q = z.q4

    def body(k):
        got_ref, mates_ref, pre_ref, g_ref, o_ref, short_ref = k.i
        act_ref, next_ref, pay_ref, st_ref = k.o
        merge_stats(got_ref, mates_ref, st_ref, q, z.half)
        for m in range(MICRO):
            for c in range(q):
                mean, inverse = row(st_ref, m * q + c), row(st_ref, (MICRO + m) * q + c)
                at = pl.ds(m * z.half, z.half)
                x = pre_ref[at, cols(c)]
                act_ref[at, cols(c)] = gelu(g_ref[:, cols(c)] * ((x - mean) * inverse) + o_ref[:, cols(c)]).astype(BF)
        k.send(0)
        k.wait_w()
        next_ref[...] = dot(act_ref[...], k.w[0][...])
        k.send(1)
        for c in range(z.q6):
            for m in range(MICRO):
                stats_rows(next_ref[pl.ds(m * z.half, z.half), cols(c)], pay_ref.at[c], m, z.half, MICRO)
            pay_ref[z.q6 + c] = short_ref[c]
        chunks = 2 * z.q6
        for j in range(chunks, z.n):
            pay_ref[j] = pay_ref[j % chunks]

    rows = MICRO * z.half
    return kernel_call(
        body,
        [arr(rows, z.c_wide, dtype=BF), arr(rows, z.c_out), arr(z.n, 8, LANES), arr(6 * q, LANES)],
        [got, mates, pre, gain, offset, short_st],
        [w],
        flops=2 * rows * z.c_wide * z.c_out,
        passes=passes,
    )


def k_views(got, ids, z):
    def body(k):
        (got_ref, id_ref), (pay_ref,), (lo, hi) = k.i, k.o, k.x
        mates = z.n // NVIEW
        g, ids = got_ref[...], id_ref[...]
        for view, ref in ((0, lo), (1, hi)):
            w = (ids == float(view)).astype(F32)
            mean = jnp.sum(w * g, axis=0)[:MICRO] * (1.0 / mates)
            away = g[:, :MICRO] - mean[None]
            total = jnp.sum(w[:, :MICRO] * (g[:, MICRO : 2 * MICRO] + z.half * (away * away)), axis=0)
            ref[...] = jnp.zeros(ref.shape, F32)
            ref[:MICRO] = mean
            ref[MICRO : 2 * MICRO] = lax.rsqrt(total * (1.0 / (mates * z.half)) + EPSILON)
        pay_ref[...] = jnp.where(ids > 0.5, hi[...][None], lo[...][None])

    return kernel_call(
        body, [arr(z.n, 8, LANES)], [got, ids], scratch=[pltpu.VMEM((8, LANES), F32)] * 2, limit=16
    )[0]


def k_mapped(whole, pre_w, pre_s, cot, gains, z, passes=()):
    def body(k):
        st_ref, w_ref, s_ref, cot_ref, gw, ow, gs, os = k.i
        map_ref, d_ref, pay_ref = k.o
        n_c = z.q6
        pay_ref[...] = jnp.zeros(pay_ref.shape, F32)
        for c in range(n_c):
            for m in range(MICRO):
                at = pl.ds(m * z.half, z.half)
                sw, ss = st_ref.at[c], st_ref.at[n_c + c]
                hat_w = (w_ref[at, cols(c)] - row(sw, m)) * row(sw, MICRO + m)
                hat_s = (s_ref[at, cols(c)] - row(ss, m)) * row(ss, MICRO + m)
                res = gw[:, cols(c)] * hat_w + ow[:, cols(c)] + (gs[:, cols(c)] * hat_s + os[:, cols(c)])
                map_ref[at, cols(c)] = gelu(res).astype(BF)
                d = gelu_slope(res) * cot_ref[at, cols(c)].astype(F32)
                d_ref[at, cols(c)] = d
                first, second = pay_ref.at[c], pay_ref.at[n_c + c]
                first[pl.ds(m, 1), :] = jnp.sum(d, axis=0, keepdims=True)
                first[pl.ds(MICRO + m, 1), :] = jnp.sum(d * hat_w, axis=0, keepdims=True)
                second[pl.ds(m, 1), :] = jnp.sum(d * hat_s, axis=0, keepdims=True)
        for j in range(2 * n_c, z.n):
            pay_ref[j] = pay_ref[j % (2 * n_c)]

    rows = MICRO * z.half
    return kernel_call(
        body,
        [arr(rows, z.c_out, dtype=BF), arr(rows, z.c_out), arr(z.n, 8, LANES)],
        [whole, pre_w, pre_s, cot, *gains],
        flops=rows * z.c_out * 60,
        passes=passes,
    )


def k_view_sums(got, ids, z):
    def body(k):
        (got_ref, id_ref), (pay_ref,), (both,) = k.i, k.o, k.x
        g, ids = got_ref[...], id_ref[...]
        lo = jnp.sum((ids == 0.0).astype(F32) * g, axis=0)
        hi = jnp.sum((ids == 1.0).astype(F32) * g, axis=0)
        both[0], both[1] = lo, hi
        all_views = lo + hi
        totals = []
        for k in range(2):
            totals.append(jnp.sum(all_views[k * MICRO : (k + 1) * MICRO], axis=0, keepdims=True))
        for v in range(2):
            for k in range(2):
                both[v, pl.ds(2 * MICRO + k, 1), :] = totals[k]
        pay_ref[...] = jnp.where(ids > 0.5, both[1][None], both[0][None])

    return kernel_call(body, [arr(z.n, 8, LANES)], [got, ids], scratch=[pltpu.VMEM((2, 8, LANES), F32)], limit=16)[0]


def back_rows(x, d, st_ref, sum_ref, m, q, c, gain):
    inverse = row(st_ref, (MICRO + m) * q + c)
    hat = (x - row(st_ref, m * q + c)) * inverse
    return gain * inverse * (d - row(sum_ref, m * q + c) - hat * row(sum_ref, (MICRO + m) * q + c))


def sum_rows(d, hat, rows_ref, r, offset):
    rows_ref[pl.ds(r, 1), :] = jnp.sum(d, axis=0, keepdims=True)
    rows_ref[pl.ds(r + offset, 1), :] = jnp.sum(d * hat, axis=0, keepdims=True)


def slope_and_sums(d_out, pre_ref, at, st_ref, m, q, c, g_ref, o_ref, d_ref, rows_ref):
    hat = (pre_ref[at, cols(c)] - row(st_ref, m * q + c)) * row(st_ref, (MICRO + m) * q + c)
    d = gelu_slope(g_ref[:, cols(c)] * hat + o_ref[:, cols(c)]) * d_out
    d_ref[at, cols(c)] = d
    sum_rows(d, hat, rows_ref, m * q + c, MICRO * q)


def k_back_widen(whole, sums, d_two, pre_w, pre_s, gain_w, gain_s, pre, st, gain, offset, place, w, z, passes=()):
    q, n_c = z.q4, z.q6

    def body(k):
        st2, sum_ref, d_ref, w_ref, s_ref, gw, gs, pre_ref, st_ref, g_ref, o_ref = k.i
        ds_ref, t_off, t_gw, t_gs, t_again, d_next, pay_ref = k.o
        dw_ref, rows_ref, tmp = k.x
        scale = 1.0 / (z.n // NVIEW * z.half)
        for c in range(n_c):
            first, second = sum_ref.at[c], sum_ref.at[n_c + c]
            t_off[pl.ds(c, 1), :] = row(first, 2 * MICRO)
            t_again[pl.ds(c, 1), :] = row(first, 2 * MICRO)
            t_gw[pl.ds(c, 1), :] = row(first, 2 * MICRO + 1)
            t_gs[pl.ds(c, 1), :] = row(second, 2 * MICRO)
            sw, ss = st2.at[c], st2.at[n_c + c]
            for m in range(MICRO):
                at = pl.ds(m * z.half, z.half)
                inv_w, inv_s = row(sw, MICRO + m), row(ss, MICRO + m)
                hat_w = (w_ref[at, cols(c)] - row(sw, m)) * inv_w
                hat_s = (s_ref[at, cols(c)] - row(ss, m)) * inv_s
                d = d_ref[at, cols(c)] - row(first, m) * scale
                dw_ref[at, cols(c)] = (
                    gw[:, cols(c)] * inv_w * (d - hat_w * (row(first, MICRO + m) * scale))
                ).astype(BF)
                ds_ref[at, cols(c)] = (gs[:, cols(c)] * inv_s * (d - hat_s * (row(second, m) * scale))).astype(BF)
        k.send(0)
        some = z.c_out // z.g
        for j in range(z.g):
            at = pl.ds(pl.multiple_of(((k.s[0][0] & (z.g - 1)) ^ j) * some, some), some)
            k.copy(dw_ref.at[:, at], k.raw[j].at[:, pl.ds(0, some)])
            k.copy(ds_ref.at[:, at], k.raw[j].at[:, pl.ds(some, some)])
        k.wait_w()
        tmp[...] = dot_nt(dw_ref[...], k.w[0][...])
        for m in range(MICRO):
            at = pl.ds(m * z.half, z.half)
            for c in range(q):
                slope_and_sums(tmp[at, cols(c)], pre_ref, at, st_ref, m, q, c, g_ref, o_ref, d_next, rows_ref)
        fill(pay_ref, rows_ref)

    rows = MICRO * z.half
    return kernel_call(
        body,
        [arr(rows, z.c_out, dtype=BF)]
        + [arr(n_c, LANES)] * 4
        + [arr(rows, z.c_wide), arr(z.n, 6 * q, LANES, dtype=BF)],
        [whole, sums, d_two, pre_w, pre_s, gain_w, gain_s, pre, st, gain, offset],
        [w],
        [
            pltpu.VMEM((rows, z.c_out), BF),
            pltpu.VMEM((6 * q, LANES), F32),
            pltpu.VMEM((rows, z.c_wide), F32),
        ],
        flops=2 * rows * z.c_wide * z.c_out,
        raw=[arr(rows, 2 * z.c_out // z.g, dtype=BF)] * z.g,
        n_raw=2 * z.g,
        scalars=[place],
        passes=passes,
    )


def back_start(refs, mates_ref, sum_ref, out_ref, q, n_rows, totals):
    got_ref, d_ref, pre_ref, st_ref, g_ref = refs
    merge_sums(got_ref, mates_ref, sum_ref, q, n_rows, totals)
    for m in range(MICRO):
        at = pl.ds(m * n_rows, n_rows)
        for c in range(q):
            out_ref[at, cols(c)] = back_rows(
                pre_ref[at, cols(c)], d_ref[at, cols(c)].astype(F32), st_ref, sum_ref, m, q, c, g_ref[:, cols(c)]
            ).astype(BF)


def k_back_stride(got, mates, d, pre_s, st_s, gain_s, pre, st, gain, offset, place, w, z, passes=()):
    q = z.q4

    def body(k):
        got_ref, mates_ref, d_ref, ps_ref, ss_ref, gs_ref, pre_ref, st_ref, g_ref, o_ref = k.i
        t_off, t_gain, d_next, pay_ref = k.o
        delta_ref, rows_ref, sum_ref, contrib = k.x
        back_start((got_ref, d_ref, ps_ref, ss_ref, gs_ref), mates_ref, sum_ref, delta_ref, q, z.half, (t_off, t_gain))
        some = z.c_wide // z.g
        for j in range(z.g):
            at = pl.ds(pl.multiple_of(((k.s[0][0] & (z.g - 1)) ^ j) * some, some), some)
            k.copy(delta_ref.at[:, at], k.raw[j])
        for tap in range(9):
            k.wait_w(chunk=tap)
            at = pl.ds(tap * z.c_wide, z.c_wide)
            contrib[:, at] = dot_nt(delta_ref[...], k.w[0][at])
        for m in range(MICRO):
            for c in range(q):
                phase = {}
                for r in range(3):
                    for k in range(3):
                        piece = contrib[pl.ds(m * z.half, z.half), pl.ds((r * 3 + k) * z.c_wide + c * LANES, LANES)]
                        piece = shift_x(shift_y(piece, 1 if r == 0 else 0), 1 if k == 0 else 0)
                        p = ((r + 1) % 2, (k + 1) % 2)
                        phase[p] = piece if p not in phase else phase[p] + piece
                first = second = 0.0
                mean, inverse = row(st_ref, m * q + c), row(st_ref, (MICRO + m) * q + c)
                for i, p in enumerate(PHASES):
                    at = pl.ds(m * z.rows + i * z.half, z.half)
                    hat = (pre_ref[at, cols(c)] - mean) * inverse
                    grad = gelu_slope(g_ref[:, cols(c)] * hat + o_ref[:, cols(c)]) * phase[p]
                    d_next[at, cols(c)] = grad
                    first = first + jnp.sum(grad, axis=0, keepdims=True)
                    second = second + jnp.sum(grad * hat, axis=0, keepdims=True)
                rows_ref[pl.ds(m * q + c, 1), :] = first
                rows_ref[pl.ds((MICRO + m) * q + c, 1), :] = second
        fill(pay_ref, rows_ref)

    rows = MICRO * z.half
    return kernel_call(
        body,
        [arr(q, LANES)] * 2
        + [arr(MICRO * z.rows, z.c_wide), arr(z.n, 6 * q, LANES, dtype=BF)],
        [got, mates, d, pre_s, st_s, gain_s, pre, st, gain, offset],
        [w],
        [
            pltpu.VMEM((rows, z.c_wide), BF),
            pltpu.VMEM((6 * q, LANES), F32),
            pltpu.VMEM((6 * q, LANES), F32),
            pltpu.VMEM((rows, 9 * z.c_wide), F32),
        ],
        flops=2 * rows * 9 * z.c_wide * z.c_wide,
        passes=passes,
        chunks=9,
        raw=[arr(rows, z.c_wide // z.g, dtype=BF)] * z.g,
        n_raw=z.g,
        scalars=[place],
    )


def k_back_narrow(got, mates, d, pre_n, st_n, gain_n, even, slope, pre, st, w, z, passes=()):
    q, qo = z.q4, z.q3

    def body(k):
        got_ref, mates_ref, d_ref, pn_ref, sn_ref, gn_ref, even_ref, slope_ref, pre_ref, st_ref = k.i
        delta_ref, t_off, t_gain, d_next, pay_ref = k.o
        rows_ref, sum_ref, tmp = k.x
        back_start((got_ref, d_ref, pn_ref, sn_ref, gn_ref), mates_ref, sum_ref, delta_ref, q, z.rows, (t_off, t_gain))
        k.send(0)
        k.wait_w()
        tmp[...] = dot_nt(delta_ref[...], k.w[0][...])
        for m in range(MICRO):
            at = pl.ds(m * z.rows, z.rows)
            some = pl.ds(m * z.rows, z.half)
            for c in range(qo):
                tmp[some, cols(c)] = tmp[some, cols(c)] + even_ref[pl.ds(m * z.half, z.half), cols(c)]
                d_join = tmp[at, cols(c)].astype(BF).astype(F32)
                one = slope_ref[at, cols(c)].astype(F32) * d_join
                hat = (pre_ref[at, cols(c)] - row(st_ref, m * qo + c)) * row(st_ref, (MICRO + m) * qo + c)
                d_next[at, cols(c)] = one.astype(BF)
                sum_rows(one, hat, rows_ref, m * qo + c, MICRO * qo)
        fill(pay_ref, rows_ref)

    rows = MICRO * z.rows
    return kernel_call(
        body,
        [arr(rows, z.c_wide, dtype=BF)] + [arr(q, LANES)] * 2 + [arr(rows, z.c_in, dtype=BF), arr(z.n, 6 * qo, LANES, dtype=BF)],
        [got, mates, d, pre_n, st_n, gain_n, even, slope, pre, st],
        [w],
        [
            pltpu.VMEM((6 * qo, LANES), F32),
            pltpu.VMEM((6 * q, LANES), F32),
            pltpu.VMEM((rows, z.c_in), F32),
        ],
        flops=2 * rows * z.c_in * z.c_wide,
        passes=passes,
    )


def k_back_expand(got, mates, d, pre_e, st_e, gain_e, pre, st, gain, offset, w, z, passes=()):
    q, qo = z.q3, z.q1

    def body(k):
        got_ref, mates_ref, d_ref, pe_ref, se_ref, ge_ref, pre_ref, st_ref, g_ref, o_ref = k.i
        delta_ref, t_off, t_gain, d_next, pay_ref = k.o
        rows_ref, sum_ref, tmp = k.x
        back_start((got_ref, d_ref, pe_ref, se_ref, ge_ref), mates_ref, sum_ref, delta_ref, q, z.rows, (t_off, t_gain))
        k.send(0)
        k.wait_w()
        tmp[...] = dot_nt(delta_ref[...], k.w[0][...])
        for m in range(MICRO):
            at = pl.ds(m * z.rows, z.rows)
            for c in range(qo):
                slope_and_sums(tmp[at, cols(c)], pre_ref, at, st_ref, m, qo, c, g_ref, o_ref, d_next, rows_ref)
        fill(pay_ref, rows_ref)

    rows = MICRO * z.rows
    return kernel_call(
        body,
        [arr(rows, z.c_in, dtype=BF)] + [arr(q, LANES)] * 2 + [arr(rows, z.c_mid), arr(z.n, 6 * qo, LANES, dtype=BF)],
        [got, mates, d, pre_e, st_e, gain_e, pre, st, gain, offset],
        [w],
        [
            pltpu.VMEM((6 * qo, LANES), F32),
            pltpu.VMEM((6 * q, LANES), F32),
            pltpu.VMEM((rows, z.c_mid), F32),
        ],
        flops=2 * rows * z.c_in * z.c_mid,
        passes=passes,
    )


def k_back_spatial(got, mates, d, pre_s, st_s, gain_s, pre, st, gain, offset, w, z, passes=()):
    q = z.q1

    def body(k):
        got_ref, mates_ref, d_ref, ps_ref, ss_ref, gs_ref, pre_ref, st_ref, g_ref, o_ref = k.i
        delta_ref, t_off, t_gain, d_next, pay_ref = k.o
        rows_ref, sum_ref, patch_ref, tmp = k.x
        merge_sums(got_ref, mates_ref, sum_ref, q, z.rows, (t_off, t_gain))
        for m in range(MICRO):
            for c in range(q):
                phase = {}
                for i, p in enumerate(PHASES):
                    at = pl.ds(m * z.rows + i * z.half, z.half)
                    phase[p] = back_rows(
                        ps_ref[at, cols(c)], d_ref[at, cols(c)], ss_ref, sum_ref, m, q, c, gs_ref[:, cols(c)]
                    )
                    delta_ref[at, cols(c)] = phase[p].astype(BF)
                write_patches(phase, patch_ref, m, z.half, c, z.c_mid, -1)
        k.send(0)
        k.wait_w()
        tmp[...] = dot(patch_ref[...], k.w[0][...])
        for m in range(MICRO):
            at = pl.ds(m * z.rows, z.rows)
            for c in range(q):
                slope_and_sums(tmp[at, cols(c)], pre_ref, at, st_ref, m, q, c, g_ref, o_ref, d_next, rows_ref)
        fill(pay_ref, rows_ref)

    rows = MICRO * z.rows
    return kernel_call(
        body,
        [arr(rows, z.c_mid, dtype=BF)] + [arr(q, LANES)] * 2 + [arr(rows, z.c_mid), arr(z.n, 6 * q, LANES, dtype=BF)],
        [got, mates, d, pre_s, st_s, gain_s, pre, st, gain, offset],
        [w],
        [
            pltpu.VMEM((6 * q, LANES), F32),
            pltpu.VMEM((6 * q, LANES), F32),
            pltpu.VMEM((rows, 9 * z.c_mid), BF),
            pltpu.VMEM((rows, z.c_mid), F32),
        ],
        flops=2 * rows * 9 * z.c_mid * z.c_mid,
        passes=passes,
    )


def k_back_reduce(got, mates, d, pre_r, st_r, gain_r, maps_in, place, z, passes=()):
    q, hi, r = z.q1, z.ns // z.slo, z.c_in // z.n

    def body(k):
        got_ref, mates_ref, d_ref, pr_ref, sr_ref, gr_ref, *maps = k.i
        delta_ref, t_off, t_gain = k.o
        sum_ref, *held = k.x
        back_start((got_ref, d_ref, pr_ref, sr_ref, gr_ref), mates_ref, sum_ref, delta_ref, q, z.rows, (t_off, t_gain))
        k.send(0)
        if maps:
            (held,) = held
            product = dot_tn(maps[0][...], delta_ref[...])
            held[...] = product.reshape(hi, z.slo, z.nb // 2, 2, r, z.c_mid).astype(BF)
            core = k.s[0][0] & 1
            k.copy(held.at[:, :, :, core], k.raw[0])
            k.copy(held.at[:, :, :, 1 - core], k.raw[1])

    rows = MICRO * z.rows
    maps = [] if maps_in is None else [maps_in]
    return kernel_call(
        body,
        [arr(rows, z.c_mid, dtype=BF)] + [arr(q, LANES)] * 2,
        [got, mates, d, pre_r, st_r, gain_r, *maps],
        scratch=[pltpu.VMEM((6 * q, LANES), F32)]
        + [pltpu.VMEM((hi, z.slo, z.nb // 2, 2, r, z.c_mid), BF) for _ in maps],
        passes=passes,
        scalars=[place],
        raw=[arr(hi, z.slo, z.nb // 2, r, z.c_mid, dtype=BF)] * (2 * len(maps)),
        n_raw=2 * len(maps),
        flops=2 * rows * z.c_in * z.c_mid,
    )


def k_input(delta, d_one, w, z, passes=()):
    def body(k):
        (delta_ref, one_ref), (out_ref,), (tmp, line) = k.i, k.o, k.x
        k.wait_w()
        tmp[...] = dot_nt(delta_ref[...], k.w[0][...])
        for m in range(MICRO):
            for y in range(z.height):
                for c in range(z.q3):
                    for px in range(2):
                        at = pl.ds(m * z.rows + (2 * (y % 2) + px) * z.half + (y // 2) * 8, 8)
                        line[c, pl.ds((y * MICRO + m) * z.cols + px, 8, stride=2), :] = (
                            one_ref[at, cols(c)].astype(F32) + tmp[at, cols(c)]
                        )
                    out_ref[y, m, :, cols(c)] = line[c, pl.ds((y * MICRO + m) * z.cols, z.cols), :].astype(BF)

    rows = MICRO * z.rows
    return kernel_call(
        body,
        [arr(z.height, MICRO, z.cols, z.c_in, dtype=BF)],
        [delta, d_one],
        [w],
        [pltpu.VMEM((rows, z.c_in), F32), pltpu.VMEM((z.q3, rows, LANES), F32)],
        flops=2 * rows * z.c_in * z.c_mid,
        passes=passes,
    )


def k_even(delta, w, z):
    def body(k):
        k.wait_w()
        k.o[0][...] = dot_nt(k.i[0][...], k.w[0][...])

    rows = delta.shape[0]
    return kernel_call(body, [arr(rows, z.c_in)], [delta], [w], flops=2 * rows * z.c_in * z.c_out)[0]


def k_first_grads(outs, evens, pieces, z):
    some = z.c_out // z.g
    a, b = z.c_wide // z.ns, z.c_in // z.ns

    def body(k):
        lhs_w, lhs_s, rhs = k.st
        held_w, held_s = k.x
        held_w[...] = dot_tn(lhs_w[...], rhs[:, :some]).astype(BF)
        for s in range(z.ns):
            k.copy(held_w.at[pl.ds(s * a, a)], k.raw[0].at[s % z.slo, s // z.slo, pl.ds(0, a)])
        held_s[...] = dot_tn(lhs_s[...], rhs[:, some:]).astype(BF)
        for s in range(z.ns):
            k.copy(held_s.at[pl.ds(s * b, b)], k.raw[0].at[s % z.slo, s // z.slo, pl.ds(a, b)])

    return kernel_call(
        body,
        [],
        [],
        scratch=[pltpu.VMEM((z.c_wide, some), BF), pltpu.VMEM((z.c_in, some), BF)],
        stacks=[outs, evens, pieces],
        raw=[arr(z.slo, z.ns // z.slo, a + b, some, dtype=BF)],
        n_raw=2 * z.ns,
        flops=2 * z.g * outs[0].shape[0] * (z.c_in + z.c_wide) * some,
    )[0]


def k_stride_grads(maps, pieces, z):
    few = z.c_wide // z.g
    c = 9 * z.c_wide // z.ns
    wide = z.c_out // z.c_wide
    d = c // wide
    rows = z.g * pieces[0].shape[0]

    def body(k):
        map_ref, rhs = k.st
        held, lhs = k.x
        for m in range(z.g * MICRO):
            for col in range(z.q4):
                phase = {}
                for i, p in enumerate(PHASES):
                    phase[p] = map_ref[pl.ds(m * z.rows + i * z.half, z.half), cols(col)].astype(F32)
                write_patches(phase, lhs, m, z.half, col, z.c_wide, 1, ((0, 0),))
        for t in range(9):
            at = pl.ds(t * z.c_wide, z.c_wide)
            held[at] = dot_tn(lhs[:, at], rhs[...]).astype(BF)
        for s in range(z.ns):
            for part in range(wide):
                k.copy(
                    held.at[pl.ds(s * c + part * d, d)],
                    k.raw[0].at[s % z.slo, s // z.slo, :, pl.ds(part * few, few)],
                )

    return kernel_call(
        body,
        [],
        [],
        scratch=[pltpu.VMEM((9 * z.c_wide, few), BF), pltpu.VMEM((rows, 9 * z.c_wide), BF)],
        stacks=[maps, pieces],
        raw=[arr(z.slo, z.ns // z.slo, d, wide * few, dtype=BF)],
        n_raw=wide * z.ns,
        flops=2 * rows * 9 * z.c_wide * few,
    )[0]


def k_products(pairs, place, z, passes=()):
    hi = z.ns // z.slo
    widths = [(o.shape[1], g.shape[1]) for o, g in pairs]
    rows = [r // z.n * c // 256 for r, c in widths]
    total = sum(rows)

    def body(k):
        (held,) = k.x
        at = 0
        for j, (r, c) in enumerate(widths):
            product = dot_tn(k.i[2 * j][...], k.i[2 * j + 1][...])
            blocks = product.reshape(hi, z.slo, z.nb // 2, 2, r // z.n, c).astype(BF)
            for part in range(c // 256):
                held[:, :, :, :, pl.ds(at, r // z.n), :] = blocks[..., part * 256 : (part + 1) * 256]
                at += r // z.n
        core = k.s[0][0] & 1
        k.copy(held.at[:, :, :, core], k.raw[0])
        k.copy(held.at[:, :, :, 1 - core], k.raw[1])

    return kernel_call(
        body,
        [],
        [a for pair in pairs for a in pair],
        scratch=[pltpu.VMEM((hi, z.slo, z.nb // 2, 2, total, 256), BF)],
        raw=[arr(hi, z.slo, z.nb // 2, total, 256, dtype=BF)] * 2,
        n_raw=2,
        scalars=[place],
        passes=passes,
        flops=sum(2 * pairs[j][0].shape[0] * r * c for j, (r, c) in enumerate(widths)),
    )


def k_sum_plane(groups, where, z, early=()):
    hi, high = z.ns // z.slo, z.nb // 2
    rows = [g[0].shape[3] for g in groups]

    tall = [e.shape[1] for e in early]

    def body(k):
        (held,) = k.x
        at = 0
        for j, r in enumerate(rows):
            both = k.i[2 * j][...].astype(F32) + k.i[2 * j + 1][...].astype(F32)
            held[:, :, :, pl.ds(at, r), :] = both.astype(BF)
            at += r
        for i in range(high):
            for j in range(z.slo):
                k.copy(held.at[:, k.s[0][0] ^ j, k.s[0][1] ^ i], k.raw[z.slo * i + j])
        top = 0
        for copy in k.coming:
            copy.wait()
        for e, r in zip(k.i[2 * len(groups) :], tall):
            k.copy(e, k.raw[-1].at[:, pl.ds(top, r)])
            top += r

    total = sum(rows)
    return kernel_call(
        body,
        [],
        [a for g in groups for a in g] + list(early),
        scratch=[pltpu.VMEM((hi, z.slo, high, total, 256), BF)],
        raw=[arr(hi, total, 256, dtype=BF)] * (z.slo * high)
        + ([arr(hi, sum(tall), early[0].shape[2], dtype=BF)] if early else []),
        n_raw=z.slo * high + len(early),
        scalars=[where],
        late=len(early),
    )


def k_sum_line(groups, where, z, passes=()):
    hi = z.ns // z.slo
    rows = [g[0].shape[1] for g in groups]
    n = len(groups[0])

    def body(k):
        (held,) = k.x
        at = 0
        for j, r in enumerate(rows):
            value = k.i[j * n][...].astype(F32)
            for other in range(1, n):
                value = value + k.i[j * n + other][...].astype(F32)
            held[:, pl.ds(at, r), :] = value.astype(BF)
            at += r
        for j in range(hi):
            k.copy(held.at[k.s[0][2] ^ j], k.raw[j])

    total = sum(rows)
    return kernel_call(
        body,
        [],
        [a for g in groups for a in g],
        scratch=[pltpu.VMEM((hi, total, 256), BF)],
        raw=[arr(total, 256, dtype=BF)] * hi,
        n_raw=hi,
        scalars=[where],
        passes=passes,
    )


def k_sum_last(parts, passes=()):
    def body(k):
        value = k.i[0][...].astype(F32)
        for other in k.i[1:]:
            value = value + other[...].astype(F32)
        k.o[0][...] = value.astype(BF)

    return kernel_call(body, [arr(*parts[0].shape, dtype=BF)], parts, passes=passes)


def k_late_shares(pieces, place, shapes, z, passes=()):
    n = z.nb
    total = pieces[0].shape[0]

    def body(k):
        (held,) = k.x
        for j in range(n):
            held[k.s[0][0] ^ j] = k.i[j][...]
        for j in range(n):
            value = held[j].astype(F32)
            at = 0
            for g, (r, c) in enumerate(shapes):
                r = r // z.n
                for part in range(c // 256):
                    k.o[g][pl.ds(j * r, r), pl.ds(part * 256, 256)] = value[at : at + r]
                    at += r

    return kernel_call(
        body,
        [arr(r // z.ns, c) for r, c in shapes],
        list(pieces),
        scratch=[pltpu.VMEM((n, total, 256), BF)],
        scalars=[place],
        limit=24,
        passes=passes,
    )


def k_early_shares(pieces, place, z):
    n = z.g
    some, few = z.c_out // n, z.c_wide // n
    a, b, c = z.c_wide // z.ns, z.c_in // z.ns, 9 * z.c_wide // z.ns
    d = c * few // some

    def body(k):
        (held,) = k.x
        for j in range(n):
            held[(k.s[0][0] & (n - 1)) ^ j] = k.i[j][...]
        for j in range(n):
            value = held[j].astype(F32)
            k.o[0][:, pl.ds(j * some, some)] = value[:a]
            k.o[1][:, pl.ds(j * some, some)] = value[a : a + b]
            for part in range(some // few):
                k.o[2][pl.ds(part * d, d), pl.ds(j * few, few)] = value[a + b :, part * few : (part + 1) * few]

    return kernel_call(
        body,
        [arr(a, z.c_out), arr(b, z.c_out), arr(c, z.c_wide)],
        list(pieces),
        scratch=[pltpu.VMEM((n, a + b + d, some), BF)],
        scalars=[place],
        limit=24,
    )


def on_device(
    features,
    view_ids,
    w_reduce,
    w_spatial,
    w_expand,
    w_narrow,
    w_stride,
    w_widen,
    w_shortcut,
    gain_reduce,
    offset_reduce,
    gain_spatial,
    offset_spatial,
    gain_expand,
    offset_expand,
    gain_narrow,
    offset_narrow,
    gain_stride,
    offset_stride,
    gain_widen,
    offset_widen,
    gain_shortcut,
    offset_shortcut,
    cotangent,
):
    z = Sizes()
    z.ns, z.nb = lax.axis_size(SPACE), lax.axis_size(BATCH)
    z.slo = lax.axis_size("slo")
    z.g = min(z.nb, 4)
    z.n = z.ns * z.nb
    z.maps, z.cols = features.shape[1], features.shape[3]
    z.height = z.ns
    z.rows = z.height * z.cols
    z.half = z.rows // 4
    z.c_in, z.c_mid = w_reduce.shape
    z.c_wide, z.c_out = w_widen.shape
    z.q1, z.q3, z.q4, z.q6 = (c // LANES for c in (z.c_mid, z.c_in, z.c_wide, z.c_out))
    z.q_product = -(-MICRO * (z.q3 + 2 * z.q1) // 8) * 8
    assert features.shape[2] == 1 and cotangent.shape[1] == 1 and z.maps == z.ns and z.cols == 16
    yh, xh = z.height // 2, z.cols // 2
    n, ns, nb = z.n, z.ns, z.nb
    s, b = lax.axis_index(SPACE), lax.axis_index(BATCH)
    place = b.astype(jnp.int32).reshape(1)

    def share(pay):
        return lax.all_to_all(pay, ALL, 0, 0, tiled=True)

    def exchange(block):
        return lax.all_to_all(block, SPACE, 0, 0, tiled=True)

    def swap(block, axis, distance):
        return lax.ppermute(block, axis, [(i, i ^ distance) for i in range(lax.axis_size(axis))])

    def trade(pieces):
        pairs = [(i, i ^ j) for j in range(z.g) for i in range(nb)]
        return [p if j == 0 else lax.ppermute(p, BATCH, pairs[j * nb : (j + 1) * nb]) for j, p in enumerate(pieces)]

    def everywhere(block, places):
        pieces = []
        for high in range(places // 2):
            other = swap(block, "bhi", high) if high else block
            pieces += [other, swap(other, "core", 1)]
        return pieces

    def over_groups(product):
        distance = z.g // 2
        while distance < nb // 2:
            product = (product.astype(F32) + swap(product, "bhi", distance).astype(F32)).astype(BF)
            distance *= 2
        return product

    def lines(vector):
        return vector.reshape(1, -1)

    vectors = {
        "reduce": (lines(gain_reduce), lines(offset_reduce)),
        "spatial": (lines(gain_spatial), lines(offset_spatial)),
        "expand": (lines(gain_expand), lines(offset_expand)),
        "narrow": (lines(gain_narrow), lines(offset_narrow)),
        "stride": (lines(gain_stride), lines(offset_stride)),
        "widen": (lines(gain_widen), lines(offset_widen)),
        "shortcut": (lines(gain_shortcut), lines(offset_shortcut)),
    }

    my_ids = lax.dynamic_slice_in_dim(view_ids, s, 1, 1).astype(F32)
    arrived = exchange(features.reshape(MICRO, z.maps, z.cols, z.c_in).transpose(1, 0, 2, 3))
    pre_reduce, pay = k_reduce(arrived, my_ids.reshape(MICRO), w_reduce, z)
    got = share(pay)
    ids = got[:, 9 * z.q1 : 9 * z.q1 + MICRO].astype(F32)
    same = (ids == my_ids[None]).astype(F32)
    mates = {q: jnp.repeat(same, q, axis=1) for q in (z.q3, z.q4)}
    id_rows = jnp.concatenate([ids, ids, jnp.zeros((n, 2, LANES), F32)], axis=1)

    maps_in = arrived.reshape(yh, 2, MICRO, xh, 2, z.c_in).transpose(2, 1, 4, 0, 3, 5)
    maps_in = maps_in.reshape(MICRO * z.rows, z.c_in)

    patch_reduce, pre_spatial, pay, st_reduce, mates[z.q1] = k_spatial(
        got, my_ids.reshape(MICRO), pre_reduce, *vectors["reduce"], w_spatial, z
    )
    got = share(pay)
    out_spatial, pre_expand, pay, st_spatial = k_expand(got, mates[z.q1], pre_spatial, *vectors["spatial"], w_expand, z)
    got = share(pay)
    slope_one, joined, even, pre_narrow, pay, st_expand = k_narrow(
        got, mates[z.q3], same.transpose(1, 0, 2), pre_expand, *vectors["expand"], maps_in, w_expand, w_narrow, z
    )
    evens = everywhere(even, z.g)
    got = share(pay)
    pre_shortcut, short_st = k_shortcut(even, w_shortcut, z)
    out_narrow, pre_stride, pay, st_narrow = k_stride(
        got, mates[z.q4], pre_narrow, *vectors["narrow"], w_stride, z
    )
    got = share(pay)
    outs_narrow = everywhere(out_narrow, z.g)
    out_stride, pre_widen, pay, st_stride = k_widen(
        got, mates[z.q4], pre_stride, *vectors["stride"], short_st, w_widen, z
    )
    outs_stride = everywhere(out_stride, z.g)
    whole = share(k_views(share(pay), id_rows, z))
    mapped, d_two, pay = k_mapped(
        whole,
        pre_widen,
        pre_shortcut,
        cotangent.reshape(-1, z.c_out),
        (*vectors["widen"], *vectors["shortcut"]),
        z,
    )

    sums = share(k_view_sums(share(pay), id_rows, z))
    delta_shortcut, go_widen, gg_widen, gg_shortcut, go_shortcut, d_stride, pay, *more = k_back_widen(
        whole, sums, d_two, pre_widen, pre_shortcut, vectors["widen"][0], vectors["shortcut"][0],
        pre_stride, st_stride, *vectors["stride"], place, w_widen, z, (*outs_narrow, *evens, *outs_stride),
    )
    got = share(pay)
    pieces, outs_narrow, evens, outs_stride = (more[j * z.g : (j + 1) * z.g] for j in range(4))
    d_even = k_even(delta_shortcut, w_shortcut, z)
    first_pieces = trade(pieces)
    go_stride, gg_stride, d_narrow, pay, *more = k_back_stride(
        got, mates[z.q4], d_stride, pre_stride, st_stride, vectors["stride"][0],
        pre_narrow, st_narrow, *vectors["narrow"], place, w_stride, z, (*first_pieces, d_even),
    )
    pieces, first_pieces, d_even = more[: z.g], more[z.g : 2 * z.g], more[2 * z.g]
    got = share(pay)
    first = k_first_grads(outs_stride, evens, first_pieces, z)
    first = over_groups(first)
    pieces = trade(pieces)
    delta_narrow, go_narrow, gg_narrow, d_one, pay, first, *pieces = k_back_narrow(
        got, mates[z.q4], d_narrow, pre_narrow, st_narrow, vectors["narrow"][0],
        d_even, slope_one, pre_expand, st_expand, w_narrow, z, (first, *pieces),
    )
    got = share(pay)
    first = lax.psum_scatter(first, "slo", scatter_dimension=0, tiled=True)
    second = over_groups(k_stride_grads(outs_narrow, pieces, z))

    delta_expand, go_expand, gg_expand, d_spatial, pay, second = k_back_expand(
        got, mates[z.q3], d_one, pre_expand, st_expand, vectors["expand"][0],
        pre_spatial, st_spatial, *vectors["spatial"], w_expand, z, (second,),
    )
    got = share(pay)
    second = lax.psum_scatter(second, "slo", scatter_dimension=0, tiled=True)
    blocks = all(w.shape[0] % (8 * n) == 0 for w in (w_reduce, w_spatial, w_expand, w_narrow))
    pairs_some = [(joined, delta_narrow), (out_spatial, delta_expand)]
    kept_some, sent_some = k_products(pairs_some, place, z) if blocks else (None, delta_expand)
    flipped = w_spatial.reshape(9, z.c_mid, z.c_mid).transpose(0, 2, 1).reshape(9 * z.c_mid, z.c_mid)
    delta_spatial, go_spatial, gg_spatial, d_reduce, pay, sent_some, first = k_back_spatial(
        got, mates[z.q1], d_spatial, pre_spatial, st_spatial, vectors["spatial"][0],
        pre_reduce, st_reduce, *vectors["reduce"], flipped, z, (sent_some, first),
    )
    got = share(pay)
    pairs_more = [(patch_reduce, delta_spatial)]
    kept_more, sent_more = k_products(pairs_more, place, z) if blocks else (None, delta_spatial)
    came_some = swap(sent_some, "core", 1) if blocks else sent_some
    where = jnp.stack([lax.axis_index("slo"), lax.axis_index("bhi"), lax.axis_index("shi")]).astype(jnp.int32)

    def over_plane(groups, early):
        high = nb // 2
        parts = k_sum_plane(groups, where, z, early)
        came = []
        for i in range(high):
            for j in range(z.slo):
                pairs = [(u * z.slo + v, (u ^ i) * z.slo + (v ^ j)) for u in range(high) for v in range(z.slo)]
                part = parts[i * z.slo + j]
                came.append(lax.ppermute(part, ("bhi", "slo"), pairs) if i or j else part)
        return came, parts[high * z.slo :]

    delta_reduce, go_reduce, gg_reduce, *more = k_back_reduce(
        got, mates[z.q1], d_reduce, pre_reduce, st_reduce, vectors["reduce"][0], maps_in if blocks else None, place, z,
        (sent_more, came_some, where),
    )
    pairs_last, passed = [(maps_in, delta_reduce)], ()
    if blocks:
        kept_last, sent_last, sent_more, came_some, where = more
        groups = [(kept_some, came_some), (kept_more, swap(sent_more, "core", 1)), (kept_last, swap(sent_last, "core", 1))]
        passed, (early,) = over_plane(groups, (first[0], second[0]))
    else:
        early = jnp.concatenate([first[0], second[0]], axis=1)
    left, *passed = k_input(delta_reduce, d_one, w_reduce, z, passed)
    left = exchange(left)
    early = lax.psum_scatter(early, "shi", scatter_dimension=0, tiled=True)
    if blocks:
        *parts, early = k_sum_line([passed], where, z, (early,))
        early = k_early_shares(everywhere(early[0], z.g), place, z)
        parts = [p if j == 0 else swap(p, "shi", j) for j, p in enumerate(parts)]
        late, *early = k_sum_last(parts, early)
        late = everywhere(late, nb)
        shapes = [w.shape for w in (w_narrow, w_expand, w_spatial, w_reduce)]
        late = k_late_shares(late, place, shapes, z)
        grad_w_narrow, grad_w_expand, grad_w_spatial, grad_w_reduce = late
    else:
        late = [dot_tn(o, g).astype(BF) for o, g in pairs_some + pairs_more + pairs_last]
        late = [lax.psum_scatter(w, SPACE, scatter_dimension=0, tiled=True) for w in late]
        late = [w.astype(F32) for w in lax.psum(late, BATCH)]
        grad_w_narrow, grad_w_expand, grad_w_spatial, grad_w_reduce = late
        early = k_early_shares(everywhere(early[0], z.g), place, z)
    grad_w_widen, grad_w_shortcut, grad_w_stride = early
    grad_features = left.transpose(1, 0, 2, 3).reshape(features.shape)

    flat = lambda block: block.reshape(-1)
    return (
        mapped.reshape(cotangent.shape),
        grad_features,
        grad_w_reduce,
        grad_w_spatial,
        grad_w_expand,
        grad_w_narrow,
        grad_w_stride,
        grad_w_widen,
        grad_w_shortcut,
        flat(gg_reduce),
        flat(go_reduce),
        flat(gg_spatial),
        flat(go_spatial),
        flat(gg_expand),
        flat(go_expand),
        flat(gg_narrow),
        flat(go_narrow),
        flat(gg_stride),
        flat(go_stride),
        flat(gg_widen),
        flat(go_widen),
        flat(gg_shortcut),
        flat(go_shortcut),
    )


def solution(mesh):
    nb, ns = mesh.shape["batch"], mesh.shape["space"]
    fine = Mesh(mesh.devices.reshape(nb // 2, 2, ns // 2, 2), ALL)
    maps = P(None, ALL, None, None, None)
    return jax.shard_map(
        on_device,
        mesh=fine,
        in_specs=(P(None, BATCH, SPACE, None, None), P(None, BATCH)) + (P(),) * 21 + (maps,),
        out_specs=(maps, P(None, BATCH, SPACE, None, None)) + (P(SPACE, None),) * 7 + (P(),) * 14,
        check_vma=False,
    )
```
